32 devices in a mesh: azim: 4 (over z), rad: 4 (over x, core), axial: 2 (over y).
Axes of the slice: x: 2, y: 2, z: 4, core: 2. Of those that a mesh axis runs over, the one named last changes fastest.
Arguments:
- adjoint_final: float32 [4, 48, 8, 8, 512], P(None, None, 'azim', 'axial', 'rad'), may hold values from -6 to 6
- state_start: bfloat16 [4, 48, 8, 8, 512], P(None, None, 'azim', 'axial', 'rad'), may hold values from 0.099609375 to 2
- state_middle: bfloat16 [4, 48, 8, 8, 512], P(None, None, 'azim', 'axial', 'rad'), may hold values from 0.099609375 to 2
- speeds: float32 [3, 8, 8, 512], P(None, 'azim', 'axial', 'rad'), may hold values from 0.04 to 0.25
- flags: int32 [3, 8, 8, 512], P(None, 'azim', 'axial', 'rad'), may hold values from 0 to 1
- zones: int32 [8, 8, 512], P('azim', 'axial', 'rad'), may hold values from 0 to 3
- growth_rate: float32 [48], replicated, may hold values from 0.05 to 0.5
- transfer_rate: float32 [48], replicated, may hold values from 0.05 to 0.5
- nucleation_rate: float32 [4], replicated, may hold values from 0.2 to 1
Outputs:
- adjoint_start: float32 [4, 48, 8, 8, 512], P(None, None, 'azim', 'axial', 'rad')
The draws below stay inside these ranges and needn't reach their ends.
All inputs are finite; a program needn't handle non-finite values.
Results may differ from the reference program's by a relative error of at most 0.0003.
Values sent between devices are 32-bit elements; how exact they have to be, the bound alone decides.
No kernel may reach another device: no remote copies, remote signals or barrier semaphores. Data moves between devices by JAX's collectives and lax.ppermute only.
A program may use at most 128 MiB of HBM per device.

```python
import math
import jax
import jax.numpy as jnp
from jax import lax

MOMS = 4
SECTIONS = 48
ZONES = 4
NA = 8
NZ = 8
NR = 512


def place_ends(result, rng, least, top_value):
    dims = result.shape
    spot = [jax.random.randint(jax.random.fold_in(rng, axis), (), 0, dims[axis]) for axis in range(len(dims))]
    result = result.at[tuple(spot)].set(least)
    longest = dims.index(max(dims))
    spot[longest] = (spot[longest] + 1) % dims[longest]
    return result.at[tuple(spot)].set(top_value)


def levels(stream_key, extent, cuts, low, largest):
    factor_of = 1.0
    for position, parts in cuts:
        heights = jax.random.uniform(jax.random.fold_in(jax.random.fold_in(stream_key, 6), position), (parts,), jnp.float32, low / len(cuts), largest / len(cuts))
        factor_of = factor_of * jnp.repeat(jnp.exp(heights), extent[position] // parts).reshape((-1,) + (1,) * (len(extent) - 1 - position))
    return factor_of


def normal_values(key, extent, deviation, most, cuts=(), held_as=jnp.bfloat16):
    values = jax.random.normal(key, extent, jnp.float32) * deviation
    if len(cuts) > 0:
        values = levels(key, extent, cuts, -0.22, 0.18) * values
    return jnp.clip(values, min=-most, max=most).astype(held_as)


def setup_inputs(seed: int = 0) -> dict:
    splits = jax.random.split(jax.random.key(seed), 10)
    return {
        "adjoint_final": normal_values(splits[0], (MOMS, SECTIONS, NA, NZ, NR), 1.0, 6.0, ((2, 4), (3, 2), (4, 4)), jnp.float32),
        "state_start": jnp.clip(jnp.exp(math.log(2.0) - 2.9996462 * jax.random.uniform(splits[1], (MOMS, SECTIONS, NA, NZ, NR), jnp.float32) ** levels(splits[1], (MOMS, SECTIONS, NA, NZ, NR), ((2, 4), (3, 2), (4, 4)), -0.2, 0.2)), 0.099609375, 2.0).astype(jnp.bfloat16),
        "state_middle": jnp.clip(jnp.exp(math.log(2.0) - 2.9996462 * jax.random.uniform(splits[2], (MOMS, SECTIONS, NA, NZ, NR), jnp.float32) ** levels(splits[2], (MOMS, SECTIONS, NA, NZ, NR), ((2, 4), (3, 2), (4, 4)), -0.2, 0.2)), 0.099609375, 2.0).astype(jnp.bfloat16),
        "speeds": jnp.clip(jnp.exp(math.log(0.25) - 1.8325815 * jax.random.uniform(splits[3], (3, NA, NZ, NR), jnp.float32) ** levels(splits[3], (3, NA, NZ, NR), ((1, 4), (2, 2), (3, 4)), -0.2, 0.2)), 0.04, 0.25),
        "flags": place_ends(jax.random.randint(splits[4], (3, NA, NZ, NR), 0, 2), jax.random.fold_in(splits[4], 1), 0, 1).astype(jnp.int32),
        "zones": place_ends(jax.random.randint(splits[5], (NA, NZ, NR), 0, ZONES), jax.random.fold_in(splits[5], 1), 0, ZONES - 1).astype(jnp.int32),
        "growth_rate": jnp.clip(jnp.exp(jax.random.uniform(splits[6], (SECTIONS,), jnp.float32, math.log(0.05), math.log(0.5))), 0.05, 0.5),
        "transfer_rate": jnp.clip(jnp.exp(jax.random.uniform(splits[7], (SECTIONS,), jnp.float32, math.log(0.05), math.log(0.5))), 0.05, 0.5),
        "nucleation_rate": jnp.clip(jnp.exp(jax.random.uniform(splits[8], (ZONES,), jnp.float32, math.log(0.2), math.log(1.0))), 0.2, 1.0),
    }


supersat_scale = 1.5
crowding = 0.02
nucleus_moments = (1.0, 0.5, 0.25, 0.125)

def source_term(state, growth_rate, transfer_rate, nucleation):
    extra = (1,) * (state.ndim - 2)
    growth = growth_rate.reshape((1, -1) + extra)
    transfer = transfer_rate.reshape((1, -1) + extra)
    third = state[3]
    sigma = supersat_scale / (1.0 + crowding * lax.optimization_barrier(jnp.sum(third * third, axis=0)))
    lower = jnp.concatenate([jnp.zeros_like(state[0:1]), state[:3]], axis=0)
    factors = jnp.array([0.0, 1.0, 2.0, 3.0], dtype=state.dtype).reshape((4, 1) + extra)
    outflow = transfer * state
    inflow = jnp.concatenate([jnp.zeros_like(outflow[:, 0:1]), outflow[:, :-1]], axis=1)
    first = (jnp.arange(state.shape[1]) == 0).astype(state.dtype).reshape((1, -1) + extra)
    nucleus = jnp.array(nucleus_moments, dtype=state.dtype).reshape((4, 1) + extra)
    birth = nucleus * first * (nucleation * sigma * sigma)[None, None]
    return sigma[None, None] * (factors * growth * lower + inflow - outflow) + birth

def source_adjoint(state, adjoint, growth_rate, transfer_rate, nucleation):
    _, pull = jax.vjp(lambda field: source_term(field, growth_rate, transfer_rate, nucleation), state)
    return pull(adjoint)[0]

def cut_region(field, direction, offset):
    lead = [slice(None)] * (field.ndim - 3)
    spatial = []
    for which in range(3):
        moved = offset if which == direction else 0
        length = field.shape[field.ndim - 3 + which]
        spatial.append(slice(1 + moved, length - 1 + moved))
    return field[tuple(lead + spatial)]

def transport_adjoint(adjoint_pad, coeff_pad):
    total = None
    for direction in range(3):
        centre = cut_region(adjoint_pad, direction, 0)
        higher = cut_region(adjoint_pad, direction, 1)
        lowerv = cut_region(adjoint_pad, direction, -1)
        p_high = cut_region(coeff_pad[direction], direction, 1)
        q_here = cut_region(coeff_pad[3 + direction], direction, 0)
        term = p_high * (higher - centre) + q_here * (lowerv - centre)
        total = term if total is None else total + term
    return total

def face_coefficients(speeds, flags):
    upwind = flags.astype(speeds.dtype)
    return jnp.concatenate([speeds * upwind, speeds * (1.0 - upwind)], axis=0)

def nucleation_field(zones, nucleation_rate):
    labels = jnp.arange(nucleation_rate.shape[0], dtype=jnp.int32).reshape((-1, 1, 1, 1))
    match = (zones[None] == labels).astype(nucleation_rate.dtype)
    return lax.optimization_barrier(jnp.sum(match * nucleation_rate.reshape((-1, 1, 1, 1)), axis=0))

def pad_field(field):
    count = field.ndim
    wrapped = jnp.pad(field, [(0, 0)] * (count - 3) + [(1, 1), (0, 0), (0, 0)], mode='wrap')
    return jnp.pad(wrapped, [(0, 0)] * (count - 2) + [(1, 1), (1, 1)])

def reference(adjoint_final, state_start, state_middle, speeds, flags, zones, growth_rate, transfer_rate, nucleation_rate):
    coeff_pad = pad_field(face_coefficients(speeds, flags))
    nucleation = nucleation_field(zones, nucleation_rate)
    start = state_start.astype(jnp.float32)
    middle = state_middle.astype(jnp.float32)
    later = adjoint_final
    adjoint_middle = 0.5 * later + 0.5 * (transport_adjoint(pad_field(later), coeff_pad) + source_adjoint(middle, later, growth_rate, transfer_rate, nucleation))
    return 0.5 * later + adjoint_middle + transport_adjoint(pad_field(adjoint_middle), coeff_pad) + source_adjoint(start, adjoint_middle, growth_rate, transfer_rate, nucleation)
```

```python
import functools

import jax
import jax.numpy as jnp
from jax import lax
from jax.experimental import pallas as pl
from jax.experimental.pallas import tpu as pltpu
from jax.sharding import PartitionSpec as P

supersat_scale = 1.5
crowding = 0.02
nucleus_moments = (1.0, 0.5, 0.25, 0.125)
f32 = jnp.float32
exact = lax.Precision.HIGHEST


def rows_of():
    return lax.broadcasted_iota(jnp.int32, (8, 128), 0)


def lanes_of():
    return lax.broadcasted_iota(jnp.int32, (8, 128), 1)


def faces(speeds_ref, flags_ref):
    p, q = [], []
    for d in range(3):
        speed, upwind = speeds_ref[d], flags_ref[d].astype(f32)
        p.append(speed * upwind)
        q.append(speed * (1.0 - upwind))
    return p, q


class Local:
    def __init__(self, p, q):
        row, lane = rows_of(), lanes_of()
        z, top = row % 4, row >= 4
        self.azim = jnp.where(top, q[0], pltpu.roll(p[0], 4, 0))
        self.ax_up = jnp.where(z == 3, 0.0, pltpu.roll(p[1], 7, 0))
        self.ax_dn = jnp.where(z == 0, 0.0, q[1])
        self.rad_up = jnp.where(lane == 127, 0.0, pltpu.roll(p[2], 127, 1))
        self.rad_dn = jnp.where(lane == 0, 0.0, q[2])
        self.centre = self.azim + self.ax_up + q[1] + self.rad_up + q[2] + jnp.where(top, 0.0, q[0])

    def __call__(self, x):
        return (
            self.azim * pltpu.roll(x, 4, 0)
            + self.ax_up * pltpu.roll(x, 7, 0)
            + self.ax_dn * pltpu.roll(x, 1, 0)
            + self.rad_up * pltpu.roll(x, 127, 1)
            + self.rad_dn * pltpu.roll(x, 1, 1)
            - self.centre * x
        )


def pair_rows(x, first, second):
    return jnp.where(
        rows_of() % 2 == 0,
        jnp.broadcast_to(x[first : first + 1], (8, 128)),
        jnp.broadcast_to(x[second : second + 1], (8, 128)),
    )


def pack(comps, x_ref, where_ref, dn_ref, up_ref, ax_ref, radup_ref, raddn_ref):
    for c in range(comps):
        dn_ref[4 * c : 4 * c + 4] = x_ref[8 * c : 8 * c + 4]
        up_ref[4 * c : 4 * c + 4] = x_ref[8 * c + 4 : 8 * c + 8]

    @pl.when(where_ref[0] == 0)
    def _():
        ax_ref[0 : 2 * comps] = x_ref[pl.ds(3, 2 * comps, stride=4)]

    @pl.when(where_ref[0] != 0)
    def _():
        ax_ref[0 : 2 * comps] = x_ref[pl.ds(0, 2 * comps, stride=4)]

    ends = columns(x_ref[...])
    radup_ref[:, 0 : 8 * comps] = ends[0:1]
    raddn_ref[:, 0 : 8 * comps] = ends[1:2]


def columns(x):
    row, lane = rows_of(), lanes_of()
    take = jnp.where(((row == 0) & (lane == 127)) | ((row == 1) & (lane == 0)), 1.0, 0.0)
    return lax.dot_general(take, x, (((1,), (1,)), ((), ())), precision=exact, preferred_element_type=f32)


def put_columns(lower, upper):
    n = lower.shape[1]
    row, lane = rows_of(), lanes_of()
    which = lax.broadcasted_iota(jnp.int32, (8, n), 0)
    both = jnp.where(which == 0, lower, jnp.where(which == 1, upper, 0.0))
    place = jnp.where(((row == 0) & (lane == 0)) | ((row == 1) & (lane == 127)), 1.0, 0.0)
    return lax.dot_general(both, place, (((0,), (0,)), ((), ())), precision=exact, preferred_element_type=f32)


def first_pack(comps, where_ref, a_ref, speeds_ref, flags_ref, dn_ref, up_ref, ax_ref, radup_ref, raddn_ref):
    p, _ = faces(speeds_ref, flags_ref)
    pack(comps, a_ref, where_ref, dn_ref, up_ref, ax_ref, radup_ref, raddn_ref)
    dn_ref[4 * comps : 4 * comps + 8] = p[0]
    ax_ref[2 * comps : 2 * comps + 8] = pair_rows(p[1], 0, 4)
    radup_ref[:, 8 * comps :] = jnp.zeros((1, 128), f32)
    raddn_ref[:, 8 * comps :] = jnp.zeros((1, 128), f32)
    raddn_ref[:, 8 * comps : 8 * comps + 8] = columns(p[2])[1:2]


def source(sections, x_ref, u_ref, growth_ref, transfer_ref, zones_ref, rate_ref, finish):
    def inner(k, s, x):
        term = transfer_ref[s] * ((x[k][1] - x[k][0]) if s + 1 < sections else -x[k][0])
        if k < 3:
            term = term + ((k + 1.0) * growth_ref[s]) * x[k + 1][0]
        return term

    def load(s):
        got = []
        for k in range(4):
            c = k * sections + s
            here = x_ref[8 * c : 8 * c + 8]
            got.append((here, x_ref[8 * c + 8 : 8 * c + 16] if s + 1 < sections else None))
        return got

    squares = jnp.zeros((8, 128), f32)
    product = jnp.zeros((8, 128), f32)
    for s in range(sections):
        x = load(s)
        for k in range(4):
            u = u_ref[k * sections + s].astype(f32)
            product = product + u * inner(k, s, x)
        squares = squares + u * u
    sigma = supersat_scale / (1.0 + crowding * squares)
    birth = jnp.zeros((8, 128), f32)
    for k in range(4):
        c = k * sections
        birth = birth + nucleus_moments[k] * x_ref[8 * c : 8 * c + 8]
    rate = jnp.zeros((8, 128), f32)
    for label in range(rate_ref.shape[0]):
        rate = jnp.where(zones_ref[...] == label, rate_ref[label], rate)
    slope = (-2.0 * crowding / supersat_scale) * sigma * sigma * (product + 2.0 * rate * sigma * birth)
    for s in range(sections):
        x = load(s)
        for k in range(4):
            c = k * sections + s
            term = sigma * inner(k, s, x)
            if k == 3:
                term = term + u_ref[c].astype(f32) * slope
            finish(c, x[k][0], term)


def first_local(sections, a_ref, u_ref, speeds_ref, flags_ref, zones_ref, growth_ref, transfer_ref, rate_ref, out_ref):
    local = Local(*faces(speeds_ref, flags_ref))

    def finish(c, x, term):
        out_ref[8 * c : 8 * c + 8] = 0.5 * (x + local(x) + term)

    source(sections, a_ref, u_ref, growth_ref, transfer_ref, zones_ref, rate_ref, finish)


def second_local(
    sections, m_ref, a_ref, u_ref, edge_ref, speeds_ref, flags_ref, zones_ref, growth_ref, transfer_ref, rate_ref, out_ref
):
    local = Local(*faces(speeds_ref, flags_ref))
    local.centre = local.centre + (edge_ref[3] - 1.0)

    def finish(c, x, term):
        out_ref[8 * c : 8 * c + 8] = 0.5 * a_ref[8 * c : 8 * c + 8] + (local(x) + term)

    source(sections, m_ref, u_ref, growth_ref, transfer_ref, zones_ref, rate_ref, finish)


def add_halo(comps, scale, where_ref, part, below_ref, above_ref, ax_ref, hrad, azim, axial, rad, out_ref):
    top = rows_of() >= 4
    for c in range(comps):
        pair = 8 * (c // 2)
        below, above = below_ref[pair : pair + 8], above_ref[pair : pair + 8]
        if c % 2 == 0:
            halo = jnp.where(top, pltpu.roll(above, 4, 0), below)
        else:
            halo = jnp.where(top, above, pltpu.roll(below, 4, 0))
        out_ref[8 * c : 8 * c + 8] = part(c) + scale * (azim * halo + rad * hrad[8 * c : 8 * c + 8])
    several = jnp.concatenate([scale * axial] * (2 * comps // 8), axis=0)
    for start, index in ((3, 0), (0, 1)):

        @pl.when(where_ref[0] == index)
        def _():
            spots = pl.ds(start, 2 * comps, stride=4)
            out_ref[spots] = out_ref[spots] + several * ax_ref[0 : 2 * comps]


def first_halo(
    comps,
    where_ref,
    part_ref,
    a_ref,
    below_ref,
    above_ref,
    ax_ref,
    radlo_ref,
    radhi_ref,
    speeds_ref,
    flags_ref,
    m_ref,
    edge_ref,
    dn_ref,
    up_ref,
    axo_ref,
    radup_ref,
    raddn_ref,
):
    _, q = faces(speeds_ref, flags_ref)
    row, lane = rows_of(), lanes_of()
    hrad = put_columns(radlo_ref[...], radhi_ref[...])
    lower_half = where_ref[0] == 0
    p_azim = jnp.where(row >= 4, pltpu.roll(above_ref[4 * comps : 4 * comps + 8], 4, 0), 0.0)
    pairs = jnp.where(lower_half, ax_ref[2 * comps : 2 * comps + 8], 0.0)
    p_axial = jnp.where(row == 3, pairs[0:1], jnp.where(row == 7, pairs[1:2], 0.0))
    p_rad = jnp.where(lane == 127, hrad[8 * comps : 8 * comps + 8], 0.0)
    azim = jnp.where(row >= 4, p_azim, q[0])
    axial = jnp.where(lower_half, pairs, pair_rows(q[1], 0, 4))
    rad = jnp.where(lane == 0, q[2], p_rad)
    centre = p_azim + p_axial + p_rad
    edge_ref[0] = azim
    edge_ref[1] = axial
    edge_ref[2] = rad
    edge_ref[3] = centre

    def part(c):
        return part_ref[8 * c : 8 * c + 8] - (0.5 * centre) * a_ref[8 * c : 8 * c + 8]

    add_halo(comps, 0.5, where_ref, part, below_ref, above_ref, ax_ref, hrad, azim, axial, rad, m_ref)
    pack(comps, m_ref, where_ref, dn_ref, up_ref, axo_ref, radup_ref, raddn_ref)


def second_halo(comps, where_ref, part_ref, below_ref, above_ref, ax_ref, radlo_ref, radhi_ref, edge_ref, out_ref):
    hrad = put_columns(radlo_ref[...], radhi_ref[...])

    def part(c):
        return part_ref[8 * c : 8 * c + 8]

    add_halo(
        comps, 1.0, where_ref, part, below_ref, above_ref, ax_ref, hrad, edge_ref[0], edge_ref[1], edge_ref[2], out_ref
    )


VMEM = pl.BlockSpec(memory_space=pltpu.VMEM)
SMEM = pl.BlockSpec(memory_space=pltpu.SMEM)


def call(body, specs, outs, cost, *operands):
    many = isinstance(outs, list)
    return pl.pallas_call(
        body,
        in_specs=[SMEM if s == "s" else VMEM for s in specs],
        out_specs=[VMEM] * len(outs) if many else VMEM,
        out_shape=[jax.ShapeDtypeStruct(o, f32) for o in outs] if many else jax.ShapeDtypeStruct(outs, f32),
        cost_estimate=pl.CostEstimate(flops=cost, bytes_accessed=cost // 10, transcendentals=0),
        compiler_params=pltpu.CompilerParams(vmem_limit_bytes=32 * 1024 * 1024),
    )(*operands)


def exchange(dn, up, ax, radup, raddn):
    def shift(x, axis, step, wrap):
        size = lax.axis_size(axis)
        pairs = [(i, (i + step) % size) for i in range(size) if wrap or 0 <= i + step < size]
        return lax.ppermute(x, axis, pairs)

    above = shift(dn, "azim", -1, True)
    below = shift(up, "azim", 1, True)
    ax = lax.ppermute(ax, "axial", [(0, 1), (1, 0)])
    radlo = shift(radup, "rad", 1, False)
    radhi = shift(raddn, "rad", -1, False)
    return below, above, ax, radlo, radhi


def shards(adjoint_final, state_start, state_middle, speeds, flags, zones, growth_rate, transfer_rate, nucleation_rate):
    shape = adjoint_final.shape
    moments, sections = shape[:2]
    comps = moments * sections
    assert moments == 4 and shape[2:] == (2, 4, 128) and comps % 4 == 0
    assert lax.axis_size("axial") == 2
    cells = 8 * comps
    a = adjoint_final.reshape(cells, 128)
    start = state_start.reshape(comps, 8, 128)
    middle = state_middle.reshape(comps, 8, 128)
    speeds = speeds.reshape(3, 8, 128)
    flags = flags.reshape(3, 8, 128)
    zones = zones.reshape(8, 128)
    where = lax.axis_index("axial").reshape(1)
    half, rows = cells // 2, cells // 4

    first = call(
        functools.partial(first_pack, comps),
        "svvv",
        [(half + 8, 128), (half, 128), (rows + 8, 128), (1, cells + 128), (1, cells + 128)],
        2_000_000,
        where,
        a,
        speeds,
        flags,
    )
    part = call(
        functools.partial(first_local, sections),
        "vvvvvsss",
        (cells, 128),
        8_000_000,
        a,
        middle,
        speeds,
        flags,
        zones,
        growth_rate,
        transfer_rate,
        nucleation_rate,
    )
    below, above, ax, radlo, radhi = exchange(*first)
    m, edge, *second = call(
        functools.partial(first_halo, comps),
        "s" + "v" * 9,
        [
            (cells, 128),
            (4, 8, 128),
            (half, 128),
            (half, 128),
            (rows, 128),
            (1, cells),
            (1, cells),
        ],
        4_000_000,
        where,
        part,
        a,
        below,
        above,
        ax,
        radlo,
        radhi,
        speeds,
        flags,
    )
    part = call(
        functools.partial(second_local, sections),
        "vvvvvvvsss",
        (cells, 128),
        8_000_000,
        m,
        a,
        start,
        edge,
        speeds,
        flags,
        zones,
        growth_rate,
        transfer_rate,
        nucleation_rate,
    )
    below, above, ax, radlo, radhi = exchange(*second)
    out = call(
        functools.partial(second_halo, comps),
        "s" + "v" * 7,
        (cells, 128),
        3_000_000,
        where,
        part,
        below,
        above,
        ax,
        radlo,
        radhi,
        edge,
    )
    return out.reshape(shape)


def solution(mesh):
    field = P(None, None, "azim", "axial", "rad")
    faces_spec = P(None, "azim", "axial", "rad")
    return jax.shard_map(
        shards,
        mesh=mesh,
        in_specs=(field, field, field, faces_spec, faces_spec, P("azim", "axial", "rad"), P(), P(), P()),
        out_specs=field,
        check_vma=False,
    )
```

```python
import functools

import jax
import jax.numpy as jnp
from jax import lax
from jax.experimental import pallas as pl
from jax.experimental.pallas import tpu as pltpu
from jax.sharding import PartitionSpec as P

supersat_scale = 1.5
crowding = 0.02
nucleus_moments = (1.0, 0.5, 0.25, 0.125)
f32 = jnp.float32
exact = lax.Precision.HIGHEST


def rows_of():
    return lax.broadcasted_iota(jnp.int32, (8, 128), 0)


def lanes_of():
    return lax.broadcasted_iota(jnp.int32, (8, 128), 1)


def faces(speeds_ref, flags_ref):
    p, q = [], []
    for d in range(3):
        speed, upwind = speeds_ref[d], flags_ref[d].astype(f32)
        p.append(speed * upwind)
        q.append(speed * (1.0 - upwind))
    return p, q


class Local:
    def __init__(self, p, q):
        row, lane = rows_of(), lanes_of()
        z, top = row % 4, row >= 4
        self.azim = jnp.where(top, q[0], pltpu.roll(p[0], 4, 0))
        self.ax_up = jnp.where(z == 3, 0.0, pltpu.roll(p[1], 7, 0))
        self.ax_dn = jnp.where(z == 0, 0.0, q[1])
        self.rad_up = jnp.where(lane == 127, 0.0, pltpu.roll(p[2], 127, 1))
        self.rad_dn = jnp.where(lane == 0, 0.0, q[2])
        self.centre = self.azim + self.ax_up + q[1] + self.rad_up + q[2] + jnp.where(top, 0.0, q[0])

    def __call__(self, x):
        return (
            self.azim * pltpu.roll(x, 4, 0)
            + self.ax_up * pltpu.roll(x, 7, 0)
            + self.ax_dn * pltpu.roll(x, 1, 0)
            + self.rad_up * pltpu.roll(x, 127, 1)
            + self.rad_dn * pltpu.roll(x, 1, 1)
            - self.centre * x
        )


def pair_rows(x, first, second):
    return jnp.where(
        rows_of() % 2 == 0,
        jnp.broadcast_to(x[first : first + 1], (8, 128)),
        jnp.broadcast_to(x[second : second + 1], (8, 128)),
    )


def copies(pairs, sems):
    made = [pltpu.make_async_copy(src, dst, sems.at[i]) for i, (src, dst) in enumerate(pairs)]
    for copy in made:
        copy.start()
    return made


def pack_sides(comps, x_ref, where_ref, ax_ref, radup_ref, raddn_ref):
    @pl.when(where_ref[0] == 0)
    def _():
        ax_ref[0 : 2 * comps] = x_ref[pl.ds(3, 2 * comps, stride=4)]

    @pl.when(where_ref[0] != 0)
    def _():
        ax_ref[0 : 2 * comps] = x_ref[pl.ds(0, 2 * comps, stride=4)]

    ends = columns(x_ref[...])
    radup_ref[:, 0 : 8 * comps] = ends[0:1]
    raddn_ref[:, 0 : 8 * comps] = ends[1:2]


def columns(x):
    row, lane = rows_of(), lanes_of()
    take = jnp.where(((row == 0) & (lane == 127)) | ((row == 1) & (lane == 0)), 1.0, 0.0)
    return lax.dot_general(take, x, (((1,), (1,)), ((), ())), precision=exact, preferred_element_type=f32)


def put_columns(lower, upper):
    n = lower.shape[1]
    row, lane = rows_of(), lanes_of()
    which = lax.broadcasted_iota(jnp.int32, (8, n), 0)
    both = jnp.where(which == 0, lower, jnp.where(which == 1, upper, 0.0))
    place = jnp.where(((row == 0) & (lane == 0)) | ((row == 1) & (lane == 127)), 1.0, 0.0)
    return lax.dot_general(both, place, (((0,), (0,)), ((), ())), precision=exact, preferred_element_type=f32)


def first_down(comps, a_ref, speeds_ref, flags_ref, dn_ref, speed_ref, flag_ref, sems):
    part = comps // 4
    made = copies(
        [(speeds_ref.at[0, 0], speed_ref), (flags_ref.at[0, 0], flag_ref)]
        + [(a_ref.at[pl.ds(i * part, part), 0], dn_ref.at[pl.ds(i * part, part)]) for i in range(4)],
        sems,
    )
    made[0].wait()
    made[1].wait()
    dn_ref[comps] = speed_ref[...] * flag_ref[...].astype(f32)
    dn_ref[comps + 1] = jnp.zeros((4, 128), f32)
    for copy in made[2:]:
        copy.wait()


def first_rest(comps, where_ref, a_ref, speeds_ref, flags_ref, up_ref, ax_ref, radup_ref, raddn_ref):
    p, _ = faces(speeds_ref, flags_ref)
    for c in range(comps):
        up_ref[4 * c : 4 * c + 4] = a_ref[8 * c + 4 : 8 * c + 8]
    pack_sides(comps, a_ref, where_ref, ax_ref, radup_ref, raddn_ref)
    ax_ref[2 * comps : 2 * comps + 8] = pair_rows(p[1], 0, 4)
    radup_ref[:, 8 * comps :] = jnp.zeros((1, 128), f32)
    raddn_ref[:, 8 * comps :] = jnp.zeros((1, 128), f32)
    raddn_ref[:, 8 * comps : 8 * comps + 8] = columns(p[2])[1:2]


def source(sections, x_ref, u_ref, growth_ref, transfer_ref, zones_ref, rate_ref, finish):
    def inner(k, s, x):
        term = transfer_ref[s] * ((x[k][1] - x[k][0]) if s + 1 < sections else -x[k][0])
        if k < 3:
            term = term + ((k + 1.0) * growth_ref[s]) * x[k + 1][0]
        return term

    def load(s):
        got = []
        for k in range(4):
            c = k * sections + s
            here = x_ref[8 * c : 8 * c + 8]
            got.append((here, x_ref[8 * c + 8 : 8 * c + 16] if s + 1 < sections else None))
        return got

    squares = jnp.zeros((8, 128), f32)
    product = jnp.zeros((8, 128), f32)
    for s in range(sections):
        x = load(s)
        for k in range(4):
            u = u_ref[k * sections + s].astype(f32)
            product = product + u * inner(k, s, x)
        squares = squares + u * u
    sigma = supersat_scale / (1.0 + crowding * squares)
    birth = jnp.zeros((8, 128), f32)
    for k in range(4):
        c = k * sections
        birth = birth + nucleus_moments[k] * x_ref[8 * c : 8 * c + 8]
    rate = jnp.zeros((8, 128), f32)
    for label in range(rate_ref.shape[0]):
        rate = jnp.where(zones_ref[...] == label, rate_ref[label], rate)
    slope = (-2.0 * crowding / supersat_scale) * sigma * sigma * (product + 2.0 * rate * sigma * birth)
    for s in range(sections):
        x = load(s)
        for k in range(4):
            c = k * sections + s
            term = sigma * inner(k, s, x)
            if k == 3:
                term = term + u_ref[c].astype(f32) * slope
            finish(c, x[k][0], term)


def first_local(sections, a_ref, u_ref, speeds_ref, flags_ref, zones_ref, growth_ref, transfer_ref, rate_ref, out_ref):
    local = Local(*faces(speeds_ref, flags_ref))

    def finish(c, x, term):
        out_ref[8 * c : 8 * c + 8] = 0.5 * (x + local(x) + term)

    source(sections, a_ref, u_ref, growth_ref, transfer_ref, zones_ref, rate_ref, finish)


def second_local(
    sections, m_ref, a_ref, u_ref, edge_ref, speeds_ref, flags_ref, zones_ref, growth_ref, transfer_ref, rate_ref, out_ref
):
    local = Local(*faces(speeds_ref, flags_ref))
    local.centre = local.centre + (edge_ref[3] - 1.0)

    def finish(c, x, term):
        out_ref[8 * c : 8 * c + 8] = 0.5 * a_ref[8 * c : 8 * c + 8] + (local(x) + term)

    source(sections, m_ref, u_ref, growth_ref, transfer_ref, zones_ref, rate_ref, finish)


def from_below(c, below_ref):
    pair = below_ref[8 * (c // 2) : 8 * (c // 2) + 8]
    return pair if c % 2 == 0 else pltpu.roll(pair, 4, 0)


def from_above(c, above_ref):
    pair = above_ref[8 * (c // 2) : 8 * (c // 2) + 8]
    return pair if c % 2 == 1 else pltpu.roll(pair, 4, 0)


def add_axial(comps, scale, where_ref, axial, ax_ref, out_ref):
    several = jnp.concatenate([scale * axial] * (2 * comps // 8), axis=0)
    for start, index in ((3, 0), (0, 1)):

        @pl.when(where_ref[0] == index)
        def _():
            spots = pl.ds(start, 2 * comps, stride=4)
            out_ref[spots] = out_ref[spots] + several * ax_ref[0 : 2 * comps]


def first_top(
    comps,
    where_ref,
    part_ref,
    a_ref,
    above_ref,
    ax_ref,
    radlo_ref,
    radhi_ref,
    speeds_ref,
    flags_ref,
    m_ref,
    edge_ref,
    up_ref,
):
    _, q = faces(speeds_ref, flags_ref)
    row, lane = rows_of(), lanes_of()
    top = row >= 4
    hrad = put_columns(radlo_ref[...], radhi_ref[...])
    lower_half = where_ref[0] == 0
    p_azim = jnp.where(top, pltpu.roll(above_ref[4 * comps : 4 * comps + 8], 4, 0), 0.0)
    pairs = jnp.where(lower_half, ax_ref[2 * comps : 2 * comps + 8], 0.0)
    p_axial = jnp.where(row == 3, pairs[0:1], jnp.where(row == 7, pairs[1:2], 0.0))
    p_rad = jnp.where(lane == 127, hrad[8 * comps : 8 * comps + 8], 0.0)
    axial = jnp.where(lower_half, pairs, pair_rows(q[1], 0, 4))
    rad = jnp.where(lane == 0, q[2], p_rad)
    centre = p_azim + p_axial + p_rad
    edge_ref[0] = jnp.where(top, p_azim, q[0])
    edge_ref[1] = axial
    edge_ref[2] = rad
    edge_ref[3] = centre
    for c in range(comps):
        spots = slice(8 * c, 8 * c + 8)
        m_ref[spots] = part_ref[spots] + 0.5 * (
            p_azim * from_above(c, above_ref) + rad * hrad[spots] - centre * a_ref[spots]
        )
    add_axial(comps, 0.5, where_ref, axial, ax_ref, m_ref)
    for c in range(comps):
        up_ref[4 * c : 4 * c + 4] = m_ref[8 * c + 4 : 8 * c + 8]


def first_bottom(comps, where_ref, part_ref, below_ref, edge_ref, m_ref, dn_ref, ax_ref, radup_ref, raddn_ref):
    azim = jnp.where(rows_of() >= 4, 0.0, 0.5 * edge_ref[0])
    for c in range(comps):
        m_ref[8 * c : 8 * c + 8] = part_ref[8 * c : 8 * c + 8] + azim * from_below(c, below_ref)
        dn_ref[4 * c : 4 * c + 4] = m_ref[8 * c : 8 * c + 4]
    pack_sides(comps, m_ref, where_ref, ax_ref, radup_ref, raddn_ref)


def second_bottom(
    comps, where_ref, part_ref, below_ref, ax_ref, radlo_ref, radhi_ref, edge_ref, out_ref, top_ref, full_ref, low_ref, sems
):
    hrad = put_columns(radlo_ref[...], radhi_ref[...])
    azim, rad = jnp.where(rows_of() >= 4, 0.0, edge_ref[0]), edge_ref[2]
    for c in range(comps):
        spots = slice(8 * c, 8 * c + 8)
        full_ref[spots] = part_ref[spots] + azim * from_below(c, below_ref) + rad * hrad[spots]
    add_axial(comps, 1.0, where_ref, edge_ref[1], ax_ref, full_ref)
    for c in range(comps):
        low_ref[c] = full_ref[8 * c : 8 * c + 4]
    made = copies([(low_ref, out_ref.at[:, 0])], sems)
    for c in range(comps):
        top_ref[c] = full_ref[8 * c + 4 : 8 * c + 8]
    made[0].wait()


def second_top(comps, parts, _, top_ref, above_ref, edge_ref, out_ref, high_ref, sems):
    azim = edge_ref[0][4:8]
    size = comps // parts
    made = []
    for i in range(parts):
        spots = pl.ds(i * size, size)
        high_ref[spots] = top_ref[spots] + azim[None] * above_ref[spots]
        made.append(pltpu.make_async_copy(high_ref.at[spots], out_ref.at[spots, 1], sems.at[i]))
        made[-1].start()
    for copy in made:
        copy.wait()


SPACES = {
    "v": pl.BlockSpec(memory_space=pltpu.VMEM),
    "s": pl.BlockSpec(memory_space=pltpu.SMEM),
    "h": pl.BlockSpec(memory_space=pltpu.HBM),
}


def call(body, ins, outs, shapes, cost, *operands, scratch=(), aliases={}, room=32):
    return pl.pallas_call(
        body,
        in_specs=[SPACES[s] for s in ins],
        out_specs=[SPACES[s] for s in outs],
        out_shape=[jax.ShapeDtypeStruct(shape, f32) for shape in shapes],
        scratch_shapes=scratch,
        input_output_aliases=aliases,
        cost_estimate=pl.CostEstimate(flops=cost, bytes_accessed=cost // 10, transcendentals=0),
        compiler_params=pltpu.CompilerParams(vmem_limit_bytes=room * 1024 * 1024),
    )(*operands)


def shift(x, axis, step, wrap):
    size = lax.axis_size(axis)
    pairs = [(i, (i + step) % size) for i in range(size) if wrap or 0 <= i + step < size]
    return lax.ppermute(x, axis, pairs)


def sides(ax, radup, raddn):
    ax = lax.ppermute(ax, "axial", [(0, 1), (1, 0)])
    return ax, shift(radup, "rad", 1, False), shift(raddn, "rad", -1, False)


def shards(adjoint_final, state_start, state_middle, speeds, flags, zones, growth_rate, transfer_rate, nucleation_rate):
    shape = adjoint_final.shape
    moments, sections = shape[:2]
    comps = moments * sections
    assert moments == 4 and shape[2:] == (2, 4, 128) and comps % 4 == 0
    assert lax.axis_size("axial") == 2
    cells = 8 * comps
    half, rows = cells // 2, cells // 4
    a = adjoint_final.reshape(cells, 128)
    speeds2 = speeds.reshape(3, 8, 128)
    flags2 = flags.reshape(3, 8, 128)
    where = lax.axis_index("axial").reshape(1)
    rates = (zones.reshape(8, 128), growth_rate, transfer_rate, nucleation_rate)
    dma = pltpu.SemaphoreType.DMA

    (dn,) = call(
        functools.partial(first_down, comps),
        "hhh",
        "v",
        [(comps + 2, 4, 128)],
        1_000_000,
        adjoint_final.reshape(comps, 2, 4, 128),
        speeds,
        flags,
        scratch=[pltpu.VMEM((4, 128), f32), pltpu.VMEM((4, 128), jnp.int32), dma((6,))],
        room=60,
    )
    above = shift(dn, "azim", -1, True).reshape(half + 8, 128)
    up, *edges = call(
        functools.partial(first_rest, comps),
        "svvv",
        "vvvv",
        [(half, 128), (rows + 8, 128), (1, cells + 128), (1, cells + 128)],
        2_000_000,
        where,
        a,
        speeds2,
        flags2,
    )
    below = shift(up, "azim", 1, True)
    edges = sides(*edges)
    (part,) = call(
        functools.partial(first_local, sections),
        "vvvvvsss",
        "v",
        [(cells, 128)],
        8_000_000,
        a,
        state_middle.reshape(comps, 8, 128),
        speeds2,
        flags2,
        *rates,
    )
    part, edge, up = call(
        functools.partial(first_top, comps),
        "s" + "v" * 8,
        "vvv",
        [(cells, 128), (4, 8, 128), (half, 128)],
        4_000_000,
        where,
        part,
        a,
        above,
        *edges,
        speeds2,
        flags2,
    )
    next_below = shift(up, "azim", 1, True)
    m, dn, *edges = call(
        functools.partial(first_bottom, comps),
        "svvv",
        "vvvvv",
        [(cells, 128), (half, 128), (rows, 128), (1, cells), (1, cells)],
        4_000_000,
        where,
        part,
        below,
        edge,
    )
    above = shift(dn, "azim", -1, True).reshape(comps, 4, 128)
    edges = sides(*edges)
    (part,) = call(
        functools.partial(second_local, sections),
        "vvvvvvvsss",
        "v",
        [(cells, 128)],
        8_000_000,
        m,
        a,
        state_start.reshape(comps, 8, 128),
        edge,
        speeds2,
        flags2,
        *rates,
    )
    out, top = call(
        functools.partial(second_bottom, comps),
        "s" + "v" * 6,
        "hv",
        [(comps, 2, 4, 128), (comps, 4, 128)],
        4_000_000,
        where,
        part,
        next_below,
        *edges,
        edge,
        scratch=[pltpu.VMEM((cells, 128), f32), pltpu.VMEM((comps, 4, 128), f32), dma((1,))],
    )
    (out,) = call(
        functools.partial(second_top, comps, 4),
        "hvvv",
        "h",
        [(comps, 2, 4, 128)],
        1_000_000,
        out,
        top,
        above,
        edge,
        scratch=[pltpu.VMEM((comps, 4, 128), f32), dma((4,))],
        aliases={0: 0},
    )
    return out.reshape(shape)


def solution(mesh):
    field = P(None, None, "azim", "axial", "rad")
    faces_spec = P(None, "azim", "axial", "rad")
    return jax.shard_map(
        shards,
        mesh=mesh,
        in_specs=(field, field, field, faces_spec, faces_spec, P("azim", "axial", "rad"), P(), P(), P()),
        out_specs=field,
        check_vma=False,
    )
```

```python
import functools

import jax
import jax.numpy as jnp
from jax import lax
from jax.experimental import pallas as pl
from jax.experimental.pallas import tpu as pltpu
from jax.sharding import PartitionSpec as P

supersat_scale = 1.5
crowding = 0.02
nucleus_moments = (1.0, 0.5, 0.25, 0.125)
f32 = jnp.float32
exact = lax.Precision.HIGHEST


def rows_of():
    return lax.broadcasted_iota(jnp.int32, (8, 128), 0)


def lanes_of():
    return lax.broadcasted_iota(jnp.int32, (8, 128), 1)


def faces(speeds_ref, flags_ref):
    p, q = [], []
    for d in range(3):
        speed, upwind = speeds_ref[d], flags_ref[d].astype(f32)
        p.append(speed * upwind)
        q.append(speed * (1.0 - upwind))
    return p, q


class Local:
    def __init__(self, p, q):
        row, lane = rows_of(), lanes_of()
        z, top = row % 4, row >= 4
        self.azim = jnp.where(top, q[0], pltpu.roll(p[0], 4, 0))
        self.ax_up = jnp.where(z == 3, 0.0, pltpu.roll(p[1], 7, 0))
        self.ax_dn = jnp.where(z == 0, 0.0, q[1])
        self.rad_up = jnp.where(lane == 127, 0.0, pltpu.roll(p[2], 127, 1))
        self.rad_dn = jnp.where(lane == 0, 0.0, q[2])
        self.centre = self.azim + self.ax_up + q[1] + self.rad_up + q[2] + jnp.where(top, 0.0, q[0])

    def __call__(self, x):
        return (
            self.azim * pltpu.roll(x, 4, 0)
            + self.ax_up * pltpu.roll(x, 7, 0)
            + self.ax_dn * pltpu.roll(x, 1, 0)
            + self.rad_up * pltpu.roll(x, 127, 1)
            + self.rad_dn * pltpu.roll(x, 1, 1)
            - self.centre * x
        )


def pair_rows(x, first, second):
    return jnp.where(
        rows_of() % 2 == 0,
        jnp.broadcast_to(x[first : first + 1], (8, 128)),
        jnp.broadcast_to(x[second : second + 1], (8, 128)),
    )


def copies(pairs, sems):
    made = [pltpu.make_async_copy(src, dst, sems.at[i]) for i, (src, dst) in enumerate(pairs)]
    for copy in made:
        copy.start()
    return made


def pack_sides(comps, x_ref, where_ref, ax_ref, radup_ref, raddn_ref):
    @pl.when(where_ref[0] == 0)
    def _():
        ax_ref[0 : 2 * comps] = x_ref[pl.ds(3, 2 * comps, stride=4)]

    @pl.when(where_ref[0] != 0)
    def _():
        ax_ref[0 : 2 * comps] = x_ref[pl.ds(0, 2 * comps, stride=4)]

    ends = columns(x_ref[...])
    radup_ref[:, 0 : 8 * comps] = ends[0:1]
    raddn_ref[:, 0 : 8 * comps] = ends[1:2]


def columns(x):
    row, lane = rows_of(), lanes_of()
    take = jnp.where(((row == 0) & (lane == 127)) | ((row == 1) & (lane == 0)), 1.0, 0.0)
    return lax.dot_general(take, x, (((1,), (1,)), ((), ())), precision=exact, preferred_element_type=f32)


def put_columns(lower, upper):
    n = lower.shape[1]
    row, lane = rows_of(), lanes_of()
    which = lax.broadcasted_iota(jnp.int32, (8, n), 0)
    both = jnp.where(which == 0, lower, jnp.where(which == 1, upper, 0.0))
    place = jnp.where(((row == 0) & (lane == 0)) | ((row == 1) & (lane == 127)), 1.0, 0.0)
    return lax.dot_general(both, place, (((0,), (0,)), ((), ())), precision=exact, preferred_element_type=f32)


def first_rest(comps, where_ref, a_ref, speeds_ref, flags_ref, up_ref, ax_ref, radup_ref, raddn_ref):
    p, _ = faces(speeds_ref, flags_ref)
    for c in range(comps):
        up_ref[4 * c : 4 * c + 4] = a_ref[8 * c + 4 : 8 * c + 8]
    pack_sides(comps, a_ref, where_ref, ax_ref, radup_ref, raddn_ref)
    ax_ref[2 * comps : 2 * comps + 8] = pair_rows(p[1], 0, 4)
    radup_ref[:, 8 * comps :] = jnp.zeros((1, 128), f32)
    raddn_ref[:, 8 * comps :] = jnp.zeros((1, 128), f32)
    raddn_ref[:, 8 * comps : 8 * comps + 8] = columns(p[2])[1:2]


def source(sections, x_ref, u_ref, growth_ref, transfer_ref, zones_ref, rate_ref, finish):
    def inner(k, s, x):
        term = transfer_ref[s] * ((x[k][1] - x[k][0]) if s + 1 < sections else -x[k][0])
        if k < 3:
            term = term + ((k + 1.0) * growth_ref[s]) * x[k + 1][0]
        return term

    def load(s):
        got = []
        for k in range(4):
            c = k * sections + s
            here = x_ref[8 * c : 8 * c + 8]
            got.append((here, x_ref[8 * c + 8 : 8 * c + 16] if s + 1 < sections else None))
        return got

    squares = jnp.zeros((8, 128), f32)
    product = jnp.zeros((8, 128), f32)
    for s in range(sections):
        x = load(s)
        for k in range(4):
            u = u_ref[k * sections + s].astype(f32)
            product = product + u * inner(k, s, x)
        squares = squares + u * u
    sigma = supersat_scale / (1.0 + crowding * squares)
    birth = jnp.zeros((8, 128), f32)
    for k in range(4):
        c = k * sections
        birth = birth + nucleus_moments[k] * x_ref[8 * c : 8 * c + 8]
    rate = jnp.zeros((8, 128), f32)
    for label in range(rate_ref.shape[0]):
        rate = jnp.where(zones_ref[...] == label, rate_ref[label], rate)
    slope = (-2.0 * crowding / supersat_scale) * sigma * sigma * (product + 2.0 * rate * sigma * birth)
    for s in range(sections):
        x = load(s)
        for k in range(4):
            c = k * sections + s
            term = sigma * inner(k, s, x)
            if k == 3:
                term = term + u_ref[c].astype(f32) * slope
            finish(c, x[k][0], term)


def first_local(sections, a_ref, u_ref, speeds_ref, flags_ref, zones_ref, growth_ref, transfer_ref, rate_ref, out_ref):
    local = Local(*faces(speeds_ref, flags_ref))

    def finish(c, x, term):
        out_ref[8 * c : 8 * c + 8] = 0.5 * (x + local(x) + term)

    source(sections, a_ref, u_ref, growth_ref, transfer_ref, zones_ref, rate_ref, finish)


def second_local(
    sections, m_ref, a_ref, u_ref, edge_ref, speeds_ref, flags_ref, zones_ref, growth_ref, transfer_ref, rate_ref, out_ref
):
    local = Local(*faces(speeds_ref, flags_ref))
    local.centre = local.centre + (edge_ref[3] - 1.0)

    def finish(c, x, term):
        out_ref[8 * c : 8 * c + 8] = 0.5 * a_ref[8 * c : 8 * c + 8] + (local(x) + term)

    source(sections, m_ref, u_ref, growth_ref, transfer_ref, zones_ref, rate_ref, finish)


def from_below(c, below_ref):
    pair = below_ref[8 * (c // 2) : 8 * (c // 2) + 8]
    return pair if c % 2 == 0 else pltpu.roll(pair, 4, 0)


def from_above(c, above_ref):
    pair = above_ref[8 * (c // 2) : 8 * (c // 2) + 8]
    return pair if c % 2 == 1 else pltpu.roll(pair, 4, 0)


def add_axial(comps, scale, where_ref, axial, ax_ref, out_ref):
    several = jnp.concatenate([scale * axial] * (2 * comps // 8), axis=0)
    for start, index in ((3, 0), (0, 1)):

        @pl.when(where_ref[0] == index)
        def _():
            spots = pl.ds(start, 2 * comps, stride=4)
            out_ref[spots] = out_ref[spots] + several * ax_ref[0 : 2 * comps]


def first_top(
    comps,
    where_ref,
    part_ref,
    a_ref,
    above_ref,
    ax_ref,
    radlo_ref,
    radhi_ref,
    speeds_ref,
    flags_ref,
    m_ref,
    edge_ref,
    up_ref,
):
    _, q = faces(speeds_ref, flags_ref)
    row, lane = rows_of(), lanes_of()
    top = row >= 4
    hrad = put_columns(radlo_ref[...], radhi_ref[...])
    lower_half = where_ref[0] == 0
    p_azim = jnp.concatenate([jnp.zeros((4, 128), f32), above_ref[4 * comps : 4 * comps + 4]], axis=0)
    pairs = jnp.where(lower_half, ax_ref[2 * comps : 2 * comps + 8], 0.0)
    p_axial = jnp.where(row == 3, pairs[0:1], jnp.where(row == 7, pairs[1:2], 0.0))
    p_rad = jnp.where(lane == 127, hrad[8 * comps : 8 * comps + 8], 0.0)
    axial = jnp.where(lower_half, pairs, pair_rows(q[1], 0, 4))
    rad = jnp.where(lane == 0, q[2], p_rad)
    centre = p_azim + p_axial + p_rad
    edge_ref[0] = jnp.where(top, p_azim, q[0])
    edge_ref[1] = axial
    edge_ref[2] = rad
    edge_ref[3] = centre
    for c in range(comps):
        spots = slice(8 * c, 8 * c + 8)
        m_ref[spots] = part_ref[spots] + 0.5 * (
            p_azim * from_above(c, above_ref) + rad * hrad[spots] - centre * a_ref[spots]
        )
    add_axial(comps, 0.5, where_ref, axial, ax_ref, m_ref)
    for c in range(comps):
        up_ref[4 * c : 4 * c + 4] = m_ref[8 * c + 4 : 8 * c + 8]


def first_bottom(comps, where_ref, part_ref, below_ref, edge_ref, m_ref, dn_ref, ax_ref, radup_ref, raddn_ref):
    azim = jnp.where(rows_of() >= 4, 0.0, 0.5 * edge_ref[0])
    for c in range(comps):
        m_ref[8 * c : 8 * c + 8] = part_ref[8 * c : 8 * c + 8] + azim * from_below(c, below_ref)
        dn_ref[4 * c : 4 * c + 4] = m_ref[8 * c : 8 * c + 4]
    pack_sides(comps, m_ref, where_ref, ax_ref, radup_ref, raddn_ref)


def second_bottom(
    comps, where_ref, part_ref, below_ref, ax_ref, radlo_ref, radhi_ref, edge_ref, out_ref, top_ref, full_ref, low_ref, sems
):
    hrad = put_columns(radlo_ref[...], radhi_ref[...])
    azim, rad = jnp.where(rows_of() >= 4, 0.0, edge_ref[0]), edge_ref[2]
    for c in range(comps):
        spots = slice(8 * c, 8 * c + 8)
        full_ref[spots] = part_ref[spots] + azim * from_below(c, below_ref) + rad * hrad[spots]
    add_axial(comps, 1.0, where_ref, edge_ref[1], ax_ref, full_ref)
    for c in range(comps):
        low_ref[c] = full_ref[8 * c : 8 * c + 4]
    made = copies([(low_ref, out_ref.at[:, 0])], sems)
    for c in range(comps):
        top_ref[c] = full_ref[8 * c + 4 : 8 * c + 8]
    made[0].wait()


def second_top(comps, parts, _, top_ref, above_ref, edge_ref, out_ref, high_ref, sems):
    azim = edge_ref[0][4:8]
    size = comps // parts
    made = []
    for i in range(parts):
        spots = pl.ds(i * size, size)
        high_ref[spots] = top_ref[spots] + azim[None] * above_ref[spots]
        made.append(pltpu.make_async_copy(high_ref.at[spots], out_ref.at[spots, 1], sems.at[i]))
        made[-1].start()
    for copy in made:
        copy.wait()


SPACES = {
    "v": pl.BlockSpec(memory_space=pltpu.VMEM),
    "s": pl.BlockSpec(memory_space=pltpu.SMEM),
    "h": pl.BlockSpec(memory_space=pltpu.HBM),
}


def call(body, ins, outs, shapes, cost, *operands, scratch=(), aliases={}, room=32):
    return pl.pallas_call(
        body,
        in_specs=[SPACES[s] for s in ins],
        out_specs=[SPACES[s] for s in outs],
        out_shape=[jax.ShapeDtypeStruct(shape, f32) for shape in shapes],
        scratch_shapes=scratch,
        input_output_aliases=aliases,
        cost_estimate=pl.CostEstimate(flops=cost, bytes_accessed=cost // 10, transcendentals=0),
        compiler_params=pltpu.CompilerParams(vmem_limit_bytes=room * 1024 * 1024),
    )(*operands)


def shift(x, axis, step, wrap):
    size = lax.axis_size(axis)
    pairs = [(i, (i + step) % size) for i in range(size) if wrap or 0 <= i + step < size]
    return lax.ppermute(x, axis, pairs)


def sides(ax, radup, raddn):
    ax = lax.ppermute(ax, "axial", [(0, 1), (1, 0)])
    return ax, shift(radup, "rad", 1, False), shift(raddn, "rad", -1, False)


def shards(adjoint_final, state_start, state_middle, speeds, flags, zones, growth_rate, transfer_rate, nucleation_rate):
    shape = adjoint_final.shape
    moments, sections = shape[:2]
    comps = moments * sections
    assert moments == 4 and shape[2:] == (2, 4, 128) and comps % 4 == 0
    assert lax.axis_size("axial") == 2
    cells = 8 * comps
    half, rows = cells // 2, cells // 4
    a = adjoint_final.reshape(cells, 128)
    speeds2 = speeds.reshape(3, 8, 128)
    flags2 = flags.reshape(3, 8, 128)
    where = lax.axis_index("axial").reshape(1)
    rates = (zones.reshape(8, 128), growth_rate, transfer_rate, nucleation_rate)
    dma = pltpu.SemaphoreType.DMA

    keep = ((0, 1, 0), (0, -1, 0), (0, 0, 0), (0, 0, 0))
    after = ((comps, -2, 0), (0, -1, 0), (0, 0, 0), (0, 0, 0))
    dn = lax.pad(adjoint_final.reshape(comps, 2, 4, 128), 0.0, keep)
    dn = dn + lax.pad(speeds, 0.0, after) * lax.pad(flags, 0, after).astype(f32)
    above = shift(dn, "azim", -1, True).reshape(half + 4, 128)
    up, *edges = call(
        functools.partial(first_rest, comps),
        "svvv",
        "vvvv",
        [(half, 128), (rows + 8, 128), (1, cells + 128), (1, cells + 128)],
        2_000_000,
        where,
        a,
        speeds2,
        flags2,
    )
    below = shift(up, "azim", 1, True)
    edges = sides(*edges)
    (part,) = call(
        functools.partial(first_local, sections),
        "vvvvvsss",
        "v",
        [(cells, 128)],
        8_000_000,
        a,
        state_middle.reshape(comps, 8, 128),
        speeds2,
        flags2,
        *rates,
    )
    part, edge, up = call(
        functools.partial(first_top, comps),
        "s" + "v" * 8,
        "vvv",
        [(cells, 128), (4, 8, 128), (half, 128)],
        4_000_000,
        where,
        part,
        a,
        above,
        *edges,
        speeds2,
        flags2,
    )
    next_below = shift(up, "azim", 1, True)
    m, dn, *edges = call(
        functools.partial(first_bottom, comps),
        "svvv",
        "vvvvv",
        [(cells, 128), (half, 128), (rows, 128), (1, cells), (1, cells)],
        4_000_000,
        where,
        part,
        below,
        edge,
    )
    above = shift(dn, "azim", -1, True).reshape(comps, 4, 128)
    edges = sides(*edges)
    (part,) = call(
        functools.partial(second_local, sections),
        "vvvvvvvsss",
        "v",
        [(cells, 128)],
        8_000_000,
        m,
        a,
        state_start.reshape(comps, 8, 128),
        edge,
        speeds2,
        flags2,
        *rates,
    )
    out, top = call(
        functools.partial(second_bottom, comps),
        "s" + "v" * 6,
        "hv",
        [(comps, 2, 4, 128), (comps, 4, 128)],
        4_000_000,
        where,
        part,
        next_below,
        *edges,
        edge,
        scratch=[pltpu.VMEM((cells, 128), f32), pltpu.VMEM((comps, 4, 128), f32), dma((1,))],
    )
    (out,) = call(
        functools.partial(second_top, comps, 4),
        "hvvv",
        "h",
        [(comps, 2, 4, 128)],
        1_000_000,
        out,
        top,
        above,
        edge,
        scratch=[pltpu.VMEM((comps, 4, 128), f32), dma((4,))],
        aliases={0: 0},
    )
    return out.reshape(shape)


def solution(mesh):
    field = P(None, None, "azim", "axial", "rad")
    faces_spec = P(None, "azim", "axial", "rad")
    return jax.shard_map(
        shards,
        mesh=mesh,
        in_specs=(field, field, field, faces_spec, faces_spec, P("azim", "axial", "rad"), P(), P(), P()),
        out_specs=field,
        check_vma=False,
    )
```

```python
import functools

import jax
import jax.numpy as jnp
from jax import lax
from jax.experimental import pallas as pl
from jax.experimental.pallas import tpu as pltpu
from jax.sharding import PartitionSpec as P

supersat_scale = 1.5
crowding = 0.02
nucleus_moments = (1.0, 0.5, 0.25, 0.125)
f32 = jnp.float32
bf16 = jnp.bfloat16
exact = lax.Precision.HIGHEST

slots = 320
extra = slots - 256


def rows_of():
    return lax.broadcasted_iota(jnp.int32, (8, 128), 0)


def lanes_of():
    return lax.broadcasted_iota(jnp.int32, (8, 128), 1)


def faces(speeds_ref, flags_ref):
    p, q = [], []
    for d in range(3):
        speed, upwind = speeds_ref[d], flags_ref[d].astype(f32)
        p.append(speed * upwind)
        q.append(speed * (1.0 - upwind))
    return p, q


class Local:
    def __init__(self, p, q):
        row, lane = rows_of(), lanes_of()
        z, top = row % 4, row >= 4
        self.azim = jnp.where(top, q[0], pltpu.roll(p[0], 4, 0))
        self.ax_up = jnp.where(z == 3, 0.0, pltpu.roll(p[1], 7, 0))
        self.ax_dn = jnp.where(z == 0, 0.0, q[1])
        self.rad_up = jnp.where(lane == 127, 0.0, pltpu.roll(p[2], 127, 1))
        self.rad_dn = jnp.where(lane == 0, 0.0, q[2])
        self.centre = self.azim + self.ax_up + q[1] + self.rad_up + q[2] + jnp.where(top, 0.0, q[0])

    def __call__(self, x):
        return (
            self.azim * pltpu.roll(x, 4, 0)
            + self.ax_up * pltpu.roll(x, 7, 0)
            + self.ax_dn * pltpu.roll(x, 1, 0)
            + self.rad_up * pltpu.roll(x, 127, 1)
            + self.rad_dn * pltpu.roll(x, 1, 1)
            - self.centre * x
        )


def pair_rows(x, first, second):
    return jnp.where(
        rows_of() % 2 == 0,
        jnp.broadcast_to(x[first : first + 1], (8, 128)),
        jnp.broadcast_to(x[second : second + 1], (8, 128)),
    )


def make_tables(p, where_zero, low_ref, high_ref):
    row, lane = rows_of(), lanes_of()
    taken = (p == 0.0) if where_zero else (p != 0.0)
    one = jnp.where(taken & (row < 4), 1.0, 0.0)
    before = lax.broadcasted_iota(jnp.int32, (128, 128), 0) < lax.broadcasted_iota(jnp.int32, (128, 128), 1)
    inside = jnp.dot(one.astype(bf16), jnp.where(before, 1.0, 0.0).astype(bf16), preferred_element_type=f32)
    total = jnp.sum(one, axis=1, keepdims=True)
    base = jnp.zeros((8, 1), f32)
    for step in (1, 2, 3):
        base = base + jnp.where(
            lax.broadcasted_iota(jnp.int32, (8, 1), 0) >= step, jnp.roll(total, step, axis=0), 0.0
        )
    slot = jnp.where(one > 0.0, inside + base, -1.0).astype(jnp.int32)
    here = lax.broadcasted_iota(jnp.int32, (128, 128), 0)
    first = jnp.where(here < extra, here + 256, -2)
    second = jnp.where(here >= extra, here + (256 - extra), -2)
    for z in range(4):
        cells = slice(128 * z, 128 * z + 128)
        want = jnp.broadcast_to(slot[z : z + 1], (128, 128))
        for ref, start, names in ((low_ref, 0, here), (low_ref, 128, here + 128), (high_ref, 0, first), (high_ref, 128, second)):
            ref[start : start + 128, cells] = jnp.where(names == want, 1.0, 0.0).astype(bf16)


def pieces(x):
    high = x.astype(bf16)
    rest = x - high.astype(f32)
    middle = rest.astype(bf16)
    return high, middle, (rest - middle.astype(f32)).astype(bf16)


def stacked(x, half):
    return jnp.concatenate([part[half * i : half * i + half] for i in range(2) for part in pieces(x)], axis=0)


def summed(x, half):
    parts = [x[half * i : half * i + half] for i in range(6)]
    return [parts[3 * i] + (parts[3 * i + 1] + parts[3 * i + 2]) for i in range(2)]


def encode(comps, x_ref, first_row, low_ref, high_ref, message_ref):
    half = comps // 2
    x = jnp.concatenate(
        [stacked(x_ref[pl.ds(first_row + z, comps, stride=8)], half) for z in range(4)], axis=1
    )
    over = (((1,), (1,)), ((), ()))
    low = lax.dot_general(x, low_ref[...], over, preferred_element_type=f32)
    high = [
        lax.dot_general(
            x[3 * half * i : 3 * half * (i + 1)], high_ref[128 * i : 128 * i + 128], over, preferred_element_type=f32
        )
        for i in range(2)
    ]
    tail = jnp.zeros((half, 128), f32)
    for i, part in enumerate(summed(low, half)):
        message_ref[half * i : half * i + half] = part[:, :128]
        message_ref[comps + half * i : comps + half * i + half] = part[:, 128:]
    for part in high:
        tail = tail + (part[:half] + (part[half : 2 * half] + part[2 * half :]))
    message_ref[2 * comps : 2 * comps + half] = tail


def decode(comps, message_ref, low_ref, high_ref):
    half = comps // 2
    x = jnp.concatenate([stacked(message_ref[comps * i : comps * i + comps], half) for i in range(2)], axis=1)
    low = jnp.dot(x, low_ref[...], preferred_element_type=f32)
    tail = jnp.concatenate(pieces(message_ref[2 * comps : 2 * comps + half]), axis=0)
    found = []
    for i, part in enumerate(summed(low, half)):
        high = jnp.dot(tail, high_ref[128 * i : 128 * i + 128], preferred_element_type=f32)
        found.append(part + (high[:half] + (high[half : 2 * half] + high[2 * half :])))
    return jnp.concatenate(found, axis=0)


def add_azimuthal(comps, halo, coefficient, first_row, out_ref):
    for z in range(4):
        spots = pl.ds(first_row + z, comps, stride=8)
        out_ref[spots] = out_ref[spots] + coefficient[first_row + z : first_row + z + 1] * halo[:, 128 * z : 128 * z + 128]


def pack_axial(comps, x_ref, where_ref, ax_ref):
    @pl.when(where_ref[0] == 0)
    def _():
        ax_ref[0 : 2 * comps] = x_ref[pl.ds(3, 2 * comps, stride=4)]

    @pl.when(where_ref[0] != 0)
    def _():
        ax_ref[0 : 2 * comps] = x_ref[pl.ds(0, 2 * comps, stride=4)]


def add_axial(comps, scale, where_ref, axial, ax_ref, out_ref):
    several = jnp.concatenate([scale * axial] * (2 * comps // 8), axis=0)
    for start, index in ((3, 0), (0, 1)):

        @pl.when(where_ref[0] == index)
        def _():
            spots = pl.ds(start, 2 * comps, stride=4)
            out_ref[spots] = out_ref[spots] + several * ax_ref[0 : 2 * comps]


def columns(x):
    row, lane = rows_of(), lanes_of()
    take = jnp.where(((row == 0) & (lane == 127)) | ((row == 1) & (lane == 0)), 1.0, 0.0)
    return lax.dot_general(take, x, (((1,), (1,)), ((), ())), precision=exact, preferred_element_type=f32)


def pack_radial(comps, x_ref, p, where_ref, one_ref, two_ref):
    even = where_ref[1] % 2 == 0
    used = 8 * comps
    ends = columns(x_ref[...])
    for ref, last in ((one_ref, even), (two_ref, jnp.logical_not(even))):
        ref[:, 0:used] = jnp.where(last, ends[0:1], ends[1:2])
        ref[:, used:] = jnp.zeros((1, 256), f32)
        if p is not None:
            ref[:, used : used + 8] = columns(p)[1:2]


def radial_halo(comps, where_ref, one_ref, two_ref):
    n = 8 * comps + 128
    even = where_ref[1] % 2 == 0
    one, two = one_ref[:, 0:n], two_ref[:, 0:n]
    lower = jnp.where(where_ref[1] > 0, jnp.where(even, two, one), 0.0)
    upper = jnp.where(where_ref[1] < where_ref[2] - 1, jnp.where(even, one, two), 0.0)
    row, lane = rows_of(), lanes_of()
    which = lax.broadcasted_iota(jnp.int32, (8, n), 0)
    both = jnp.where(which == 0, lower, jnp.where(which == 1, upper, 0.0))
    place = jnp.where(((row == 0) & (lane == 0)) | ((row == 1) & (lane == 127)), 1.0, 0.0)
    return lax.dot_general(both, place, (((0,), (0,)), ((), ())), precision=exact, preferred_element_type=f32)


def source(sections, x_ref, u_ref, growth_ref, transfer_ref, zones_ref, rate_ref, finish):
    def inner(k, s, x):
        term = transfer_ref[s] * ((x[k][1] - x[k][0]) if s + 1 < sections else -x[k][0])
        if k < 3:
            term = term + ((k + 1.0) * growth_ref[s]) * x[k + 1][0]
        return term

    def load(s):
        got = []
        for k in range(4):
            c = k * sections + s
            here = x_ref[8 * c : 8 * c + 8]
            got.append((here, x_ref[8 * c + 8 : 8 * c + 16] if s + 1 < sections else None))
        return got

    squares = jnp.zeros((8, 128), f32)
    product = jnp.zeros((8, 128), f32)
    for s in range(sections):
        x = load(s)
        for k in range(4):
            u = u_ref[k * sections + s].astype(f32)
            product = product + u * inner(k, s, x)
        squares = squares + u * u
    sigma = supersat_scale / (1.0 + crowding * squares)
    birth = jnp.zeros((8, 128), f32)
    for k in range(4):
        c = k * sections
        birth = birth + nucleus_moments[k] * x_ref[8 * c : 8 * c + 8]
    rate = jnp.zeros((8, 128), f32)
    for label in range(rate_ref.shape[0]):
        rate = jnp.where(zones_ref[...] == label, rate_ref[label], rate)
    slope = (-2.0 * crowding / supersat_scale) * sigma * sigma * (product + 2.0 * rate * sigma * birth)
    for s in range(sections):
        x = load(s)
        for k in range(4):
            c = k * sections + s
            term = sigma * inner(k, s, x)
            if k == 3:
                term = term + u_ref[c].astype(f32) * slope
            finish(c, x[k][0], term)


def first_down(comps, where_ref, a_ref, speeds_ref, flags_ref, dn_ref, ax_ref, low_ref, high_ref):
    p, _ = faces(speeds_ref, flags_ref)
    make_tables(p[0], False, low_ref, high_ref)
    encode(comps, a_ref, 0, low_ref, high_ref, dn_ref)
    dn_ref[5 * comps // 2 :] = jnp.zeros((8, 128), f32)
    pack_axial(comps, a_ref, where_ref, ax_ref)
    ax_ref[2 * comps : 2 * comps + 8] = pair_rows(p[1], 0, 4)


def first_up(comps, where_ref, a_ref, upper_ref, bad_ref, speeds_ref, flags_ref, up_ref, one_ref, two_ref, low_ref, high_ref):
    p, _ = faces(speeds_ref, flags_ref)
    make_tables(upper_ref[...], True, low_ref, high_ref)
    encode(comps, a_ref, 4, low_ref, high_ref, up_ref)
    up_ref[5 * comps // 2 :] = bad_ref[...]
    pack_radial(comps, a_ref, p[2], where_ref, one_ref, two_ref)


def first_local(sections, a_ref, u_ref, speeds_ref, flags_ref, zones_ref, growth_ref, transfer_ref, rate_ref, out_ref):
    local = Local(*faces(speeds_ref, flags_ref))

    def finish(c, x, term):
        out_ref[8 * c : 8 * c + 8] = 0.5 * (x + local(x) + term)

    source(sections, a_ref, u_ref, growth_ref, transfer_ref, zones_ref, rate_ref, finish)


def second_local(
    sections, m_ref, a_ref, u_ref, edge_ref, speeds_ref, flags_ref, zones_ref, growth_ref, transfer_ref, rate_ref, out_ref
):
    local = Local(*faces(speeds_ref, flags_ref))
    local.centre = local.centre + (edge_ref[3] - 1.0)

    def finish(c, x, term):
        out_ref[8 * c : 8 * c + 8] = 0.5 * a_ref[8 * c : 8 * c + 8] + (local(x) + term)

    source(sections, m_ref, u_ref, growth_ref, transfer_ref, zones_ref, rate_ref, finish)


def first_top(
    comps,
    where_ref,
    part_ref,
    a_ref,
    above_ref,
    ax_ref,
    one_ref,
    two_ref,
    upper_ref,
    speeds_ref,
    flags_ref,
    up_low_ref,
    up_high_ref,
    m_ref,
    edge_ref,
    up_ref,
    low_ref,
    high_ref,
):
    _, q = faces(speeds_ref, flags_ref)
    row, lane = rows_of(), lanes_of()
    top = row >= 4
    make_tables(upper_ref[...], False, low_ref, high_ref)
    hrad = radial_halo(comps, where_ref, one_ref, two_ref)
    lower_half = where_ref[0] == 0
    p_azim = jnp.where(top, pltpu.roll(upper_ref[...], 4, 0), 0.0)
    pairs = jnp.where(lower_half, ax_ref[2 * comps : 2 * comps + 8], 0.0)
    p_axial = jnp.where(row == 3, pairs[0:1], jnp.where(row == 7, pairs[1:2], 0.0))
    p_rad = jnp.where(lane == 127, hrad[8 * comps : 8 * comps + 8], 0.0)
    axial = jnp.where(lower_half, pairs, pair_rows(q[1], 0, 4))
    rad = jnp.where(lane == 0, q[2], p_rad)
    centre = p_azim + p_axial + p_rad
    edge_ref[0] = jnp.where(top, p_azim, q[0])
    edge_ref[1] = axial
    edge_ref[2] = rad
    edge_ref[3] = centre
    for c in range(comps):
        spots = slice(8 * c, 8 * c + 8)
        m_ref[spots] = part_ref[spots] + 0.5 * (rad * hrad[spots] - centre * a_ref[spots])
    add_axial(comps, 0.5, where_ref, axial, ax_ref, m_ref)
    add_azimuthal(comps, decode(comps, above_ref, low_ref, high_ref), 0.5 * p_azim, 4, m_ref)
    encode(comps, m_ref, 4, up_low_ref, up_high_ref, up_ref)


def first_bottom(
    comps,
    where_ref,
    part_ref,
    below_ref,
    above_ref,
    bad_ref,
    edge_ref,
    speeds_ref,
    flags_ref,
    dn_low_ref,
    dn_high_ref,
    m_ref,
    dn_ref,
    ax_ref,
    one_ref,
    two_ref,
    worse_ref,
    low_ref,
    high_ref,
):
    p, _ = faces(speeds_ref, flags_ref)
    make_tables(p[0], True, low_ref, high_ref)
    m_ref[...] = part_ref[...]
    add_azimuthal(comps, decode(comps, below_ref, low_ref, high_ref), 0.5 * edge_ref[0], 0, m_ref)
    encode(comps, m_ref, 0, dn_low_ref, dn_high_ref, dn_ref)
    pack_axial(comps, m_ref, where_ref, ax_ref)
    pack_radial(comps, m_ref, None, where_ref, one_ref, two_ref)
    worse_ref[...] = bad_ref[...] + below_ref[5 * comps // 2 :] + above_ref[5 * comps // 2 :]


def second_bottom(
    comps, where_ref, part_ref, below_ref, ax_ref, one_ref, two_ref, edge_ref, low_ref, high_ref, full_ref
):
    hrad = radial_halo(comps, where_ref, one_ref, two_ref)
    rad = edge_ref[2]
    for c in range(comps):
        spots = slice(8 * c, 8 * c + 8)
        full_ref[spots] = part_ref[spots] + rad * hrad[spots]
    add_axial(comps, 1.0, where_ref, edge_ref[1], ax_ref, full_ref)
    add_azimuthal(comps, decode(comps, below_ref, low_ref, high_ref), edge_ref[0], 0, full_ref)


def second_top(comps, parts, full_ref, above_ref, edge_ref, low_ref, high_ref, out_ref, done_ref, sems):
    halo = decode(comps, above_ref, low_ref, high_ref)
    edge = edge_ref[0]
    size = comps // parts
    made = []
    for i in range(parts):
        spots = pl.ds(8 * size * i, 8 * size)
        done_ref[spots] = full_ref[spots]
        for z in range(4):
            some = pl.ds(8 * size * i + 4 + z, size, stride=8)
            done_ref[some] = (
                done_ref[some] + edge[4 + z : 5 + z] * halo[size * i : size * i + size, 128 * z : 128 * z + 128]
            )
        made.append(pltpu.make_async_copy(done_ref.at[spots], out_ref.at[spots], sems.at[i]))
        made[-1].start()
    for copy in made:
        copy.wait()


SPACES = {
    "v": pl.BlockSpec(memory_space=pltpu.VMEM),
    "s": pl.BlockSpec(memory_space=pltpu.SMEM),
    "h": pl.BlockSpec(memory_space=pltpu.HBM),
}


def call(body, ins, outs, shapes, cost, *operands, scratch=()):
    shapes = [shape if isinstance(shape, jax.ShapeDtypeStruct) else jax.ShapeDtypeStruct(shape, f32) for shape in shapes]
    return pl.pallas_call(
        body,
        in_specs=[SPACES[s] for s in ins],
        out_specs=[SPACES[s] for s in outs],
        out_shape=shapes,
        scratch_shapes=scratch,
        cost_estimate=pl.CostEstimate(flops=cost, bytes_accessed=cost // 10, transcendentals=0),
        compiler_params=pltpu.CompilerParams(vmem_limit_bytes=32 * 1024 * 1024),
    )(*operands)


def shift(x, axis, step):
    size = lax.axis_size(axis)
    return lax.ppermute(x, axis, [(i, (i + step) % size) for i in range(size)])


def swap_axial(x):
    return lax.ppermute(x, "axial", [(0, 1), (1, 0)])


def swap_radial(x, first):
    size = lax.axis_size("rad")
    pairs = [(i, (i + 1) % size) for i in range(first, size, 2)]
    return lax.ppermute(x, "rad", pairs + [(j, i) for i, j in pairs])


def packed_step(
    adjoint_final, state_start, state_middle, speeds, flags, zones, growth_rate, transfer_rate, nucleation_rate
):
    shape = adjoint_final.shape
    moments, sections = shape[:2]
    comps = moments * sections
    assert moments == 4 and shape[2:] == (2, 4, 128) and comps % 32 == 0
    assert lax.axis_size("axial") == 2 and lax.axis_size("rad") == 4
    cells = 8 * comps
    rows, message = cells // 4, 5 * comps // 2 + 8
    a = adjoint_final.reshape(cells, 128)
    speeds = speeds.reshape(3, 8, 128)
    flags = flags.reshape(3, 8, 128)
    where = jnp.stack([lax.axis_index("axial"), lax.axis_index("rad"), lax.axis_size("rad")]).astype(jnp.int32)
    rates = (zones.reshape(8, 128), growth_rate, transfer_rate, nucleation_rate)
    tables = [jax.ShapeDtypeStruct((256, 512), bf16)] * 2

    lower = speeds[0] * flags[0].astype(f32)
    upper = shift(lower, "azim", -1)

    def crowded(p):
        taken = jnp.sum((p[:4] != 0.0).astype(f32))
        return jnp.maximum(taken - slots, 512.0 - slots - taken) > 0.0

    dn, ax, *dn_tables = call(
        functools.partial(first_down, comps),
        "svvv",
        "vvvv",
        [(message, 128), (rows + 8, 128)] + tables,
        2_000_000,
        where,
        a,
        speeds,
        flags,
    )
    bad = (crowded(lower) | crowded(upper)).astype(f32)
    if lax.axis_size("azim") > 4:
        bad = lax.pmax(bad, "azim")
    bad = jnp.broadcast_to(bad, (8, 128))
    dn = lax.dynamic_update_slice(dn, bad, (message - 8, 0))
    above = shift(dn, "azim", -1)
    up, one, two, *up_tables = call(
        functools.partial(first_up, comps),
        "s" + "v" * 5,
        "vvvvv",
        [(message, 128), (1, cells + 256), (1, cells + 256)] + tables,
        3_000_000,
        where,
        a,
        upper,
        bad,
        speeds,
        flags,
    )
    ax = swap_axial(ax)
    below = shift(up, "azim", 1)
    one, two = swap_radial(one, 0), swap_radial(two, 1)
    (part,) = call(
        functools.partial(first_local, sections),
        "vvvvvsss",
        "v",
        [(cells, 128)],
        8_000_000,
        a,
        state_middle.reshape(comps, 8, 128),
        speeds,
        flags,
        *rates,
    )
    part, edge, up, *above_tables = call(
        functools.partial(first_top, comps),
        "s" + "v" * 11,
        "vvvvv",
        [(cells, 128), (4, 8, 128), (message - 8, 128)] + tables,
        4_000_000,
        where,
        part,
        a,
        above,
        ax,
        one,
        two,
        upper,
        speeds,
        flags,
        *up_tables,
    )
    next_below = shift(up, "azim", 1)
    m, dn, ax, one, two, bad, *below_tables = call(
        functools.partial(first_bottom, comps),
        "s" + "v" * 9,
        "v" * 8,
        [(cells, 128), (message - 8, 128), (rows, 128), (1, cells + 256), (1, cells + 256), (8, 128)] + tables,
        4_000_000,
        where,
        part,
        below,
        above,
        bad,
        edge,
        speeds,
        flags,
        *dn_tables,
    )
    above = shift(dn, "azim", -1)

    def told(message_, count):
        return message_ + lax.pad(count, 0.0, ((0, 0, 0), (cells + 128, 0, 0)))

    bad = (bad + swap_axial(bad))[:1]
    ax = swap_axial(ax)
    one = swap_radial(told(one, bad), 0)
    bad = bad + one[:, cells + 128 :]
    two = swap_radial(told(two, bad), 1)
    bad = bad + two[:, cells + 128 :]
    (part,) = call(
        functools.partial(second_local, sections),
        "vvvvvvvsss",
        "v",
        [(cells, 128)],
        8_000_000,
        m,
        a,
        state_start.reshape(comps, 8, 128),
        edge,
        speeds,
        flags,
        *rates,
    )
    (full,) = call(
        functools.partial(second_bottom, comps),
        "s" + "v" * 8,
        "v",
        [(cells, 128)],
        4_000_000,
        where,
        part,
        next_below,
        ax,
        one,
        two,
        edge,
        *below_tables,
    )
    (out,) = call(
        functools.partial(second_top, comps, 4),
        "vvvvv",
        "h",
        [(cells, 128)],
        2_000_000,
        full,
        above,
        edge,
        *above_tables,
        scratch=[pltpu.VMEM((cells, 128), f32), pltpu.SemaphoreType.DMA((4,))],
    )
    return out.reshape(shape), bad[0, 0]


def extended(x, sides, width, wrap):
    for axis, dim in sides:
        size, length = (lax.axis_size(axis), x.shape[dim])
        up = [(i, (i + 1) % size) for i in range(size if wrap else size - 1)]
        down = [(j, i) for i, j in up]
        last = lax.slice_in_dim(x, length - width, length, axis=dim)
        first = lax.slice_in_dim(x, 0, width, axis=dim)
        before = lax.ppermute(last, axis, up)
        after = lax.ppermute(first, axis, down)
        x = jnp.concatenate([before, x, after], axis=dim)
    return x


def source_term(state, growth_rate, transfer_rate, nucleation):
    extra = (1,) * (state.ndim - 2)
    growth = growth_rate.reshape((1, -1) + extra)
    transfer = transfer_rate.reshape((1, -1) + extra)
    third = state[3]
    sigma = supersat_scale / (1.0 + crowding * jnp.sum(third * third, axis=0))
    lower = jnp.concatenate([jnp.zeros_like(state[0:1]), state[:3]], axis=0)
    factors = jnp.array([0.0, 1.0, 2.0, 3.0], dtype=state.dtype).reshape((4, 1) + extra)
    outflow = transfer * state
    inflow = jnp.concatenate([jnp.zeros_like(outflow[:, 0:1]), outflow[:, :-1]], axis=1)
    first = (jnp.arange(state.shape[1]) == 0).astype(state.dtype).reshape((1, -1) + extra)
    nucleus = jnp.array(nucleus_moments, dtype=state.dtype).reshape((4, 1) + extra)
    birth = nucleus * first * (nucleation * sigma * sigma)[None, None]
    return sigma[None, None] * (factors * growth * lower + inflow - outflow) + birth


def source_adjoint(state, adjoint, growth_rate, transfer_rate, nucleation):
    _, pull = jax.vjp(
        lambda field: source_term(field, growth_rate, transfer_rate, nucleation), state
    )
    return pull(adjoint)[0]


def cut_region(field, direction, offset):
    lead = [slice(None)] * (field.ndim - 3)
    spatial = []
    for which in range(3):
        moved = offset if which == direction else 0
        length = field.shape[field.ndim - 3 + which]
        spatial.append(slice(1 + moved, length - 1 + moved))
    return field[tuple(lead + spatial)]


def transport_adjoint(adjoint_pad, coeff_pad):
    total = None
    for direction in range(3):
        centre = cut_region(adjoint_pad, direction, 0)
        higher = cut_region(adjoint_pad, direction, 1)
        lowerv = cut_region(adjoint_pad, direction, -1)
        p_high = cut_region(coeff_pad[direction], direction, 1)
        q_here = cut_region(coeff_pad[3 + direction], direction, 0)
        term = p_high * (higher - centre) + q_here * (lowerv - centre)
        total = term if total is None else total + term
    return total


def face_coefficients(speeds, flags):
    upwind = flags.astype(speeds.dtype)
    return jnp.concatenate([speeds * upwind, speeds * (1.0 - upwind)], axis=0)


def nucleation_field(zones, nucleation_rate):
    labels = jnp.arange(nucleation_rate.shape[0], dtype=jnp.int32).reshape((-1, 1, 1, 1))
    match = (zones[None] == labels).astype(nucleation_rate.dtype)
    return jnp.sum(match * nucleation_rate.reshape((-1, 1, 1, 1)), axis=0)


def whole_step(
    adjoint_final,
    state_start,
    state_middle,
    speeds,
    flags,
    zones,
    growth_rate,
    transfer_rate,
    nucleation_rate,
):
    coeffs = face_coefficients(speeds, flags)
    nucleation = nucleation_field(zones, nucleation_rate)
    start = state_start.astype(jnp.float32)
    middle = state_middle.astype(jnp.float32)
    dims = adjoint_final.shape
    comps = dims[0] * dims[1]
    packed = jnp.concatenate([adjoint_final.reshape((comps,) + dims[2:]), coeffs], axis=0)
    packed = extended(packed, (("azim", 1),), 1, True)
    packed = extended(packed, (("rad", 3), ("axial", 2)), 1, False)
    later_pad = packed[:comps].reshape(dims[:2] + packed.shape[1:])
    coeff_pad = packed[comps:]
    adjoint_middle = 0.5 * adjoint_final + 0.5 * (
        transport_adjoint(later_pad, coeff_pad)
        + source_adjoint(middle, adjoint_final, growth_rate, transfer_rate, nucleation)
    )
    flat = adjoint_middle.reshape((comps,) + dims[2:])
    flat = extended(flat, (("azim", 1),), 1, True)
    flat = extended(flat, (("rad", 3), ("axial", 2)), 1, False)
    middle_pad = flat.reshape(dims[:2] + flat.shape[1:])
    return (
        0.5 * adjoint_final
        + adjoint_middle
        + transport_adjoint(middle_pad, coeff_pad)
        + source_adjoint(start, adjoint_middle, growth_rate, transfer_rate, nucleation)
    )


def shards(*arguments):
    out, bad = packed_step(*arguments)
    return lax.cond(bad > 0.0, lambda _: whole_step(*arguments), lambda quick: quick, out)


def solution(mesh):
    field = P(None, None, "azim", "axial", "rad")
    faces_spec = P(None, "azim", "axial", "rad")
    return jax.shard_map(
        shards,
        mesh=mesh,
        in_specs=(field, field, field, faces_spec, faces_spec, P("azim", "axial", "rad"), P(), P(), P()),
        out_specs=field,
        check_vma=False,
    )
```

```python
import functools

import jax
import jax.numpy as jnp
from jax import lax
from jax.experimental import pallas as pl
from jax.experimental.pallas import tpu as pltpu
from jax.sharding import PartitionSpec as P

supersat_scale = 1.5
crowding = 0.02
nucleus_moments = (1.0, 0.5, 0.25, 0.125)
f32 = jnp.float32
bf16 = jnp.bfloat16
exact = lax.Precision.HIGHEST

slots = 320
extra = slots - 256


def rows_of():
    return lax.broadcasted_iota(jnp.int32, (8, 128), 0)


def lanes_of():
    return lax.broadcasted_iota(jnp.int32, (8, 128), 1)


def faces(speeds_ref, flags_ref):
    p, q = [], []
    for d in range(3):
        speed, upwind = speeds_ref[d], flags_ref[d].astype(f32)
        p.append(speed * upwind)
        q.append(speed * (1.0 - upwind))
    return p, q


class Local:
    def __init__(self, p, q):
        row, lane = rows_of(), lanes_of()
        z, top = row % 4, row >= 4
        self.azim = jnp.where(top, q[0], pltpu.roll(p[0], 4, 0))
        self.ax_up = jnp.where(z == 3, 0.0, pltpu.roll(p[1], 7, 0))
        self.ax_dn = jnp.where(z == 0, 0.0, q[1])
        self.rad_up = jnp.where(lane == 127, 0.0, pltpu.roll(p[2], 127, 1))
        self.rad_dn = jnp.where(lane == 0, 0.0, q[2])
        self.centre = self.azim + self.ax_up + q[1] + self.rad_up + q[2] + jnp.where(top, 0.0, q[0])

    def __call__(self, x):
        return (
            self.azim * pltpu.roll(x, 4, 0)
            + self.ax_up * pltpu.roll(x, 7, 0)
            + self.ax_dn * pltpu.roll(x, 1, 0)
            + self.rad_up * pltpu.roll(x, 127, 1)
            + self.rad_dn * pltpu.roll(x, 1, 1)
            - self.centre * x
        )


def pair_rows(x, first, second):
    return jnp.where(
        rows_of() % 2 == 0,
        jnp.broadcast_to(x[first : first + 1], (8, 128)),
        jnp.broadcast_to(x[second : second + 1], (8, 128)),
    )


def make_tables(p, low_ref, high_ref):
    row, lane = rows_of(), lanes_of()
    one = jnp.where((p != 0.0) & (row < 4), 1.0, 0.0)
    before = lax.broadcasted_iota(jnp.int32, (128, 128), 0) < lax.broadcasted_iota(jnp.int32, (128, 128), 1)
    inside = jnp.dot(one.astype(bf16), jnp.where(before, 1.0, 0.0).astype(bf16), preferred_element_type=f32)
    total = jnp.sum(one, axis=1, keepdims=True)
    base = jnp.zeros((8, 1), f32)
    for step in (1, 2, 3):
        base = base + jnp.where(
            lax.broadcasted_iota(jnp.int32, (8, 1), 0) >= step, jnp.roll(total, step, axis=0), 0.0
        )
    slot = jnp.where(one > 0.0, inside + base, -1.0).astype(jnp.int32)
    here = lax.broadcasted_iota(jnp.int32, (128, 128), 0)
    first = jnp.where(here < extra, here + 256, -2)
    second = jnp.where(here >= extra, here + (256 - extra), -2)
    for z in range(4):
        cells = slice(128 * z, 128 * z + 128)
        want = jnp.broadcast_to(slot[z : z + 1], (128, 128))
        for ref, start, names in ((low_ref, 0, here), (low_ref, 128, here + 128), (high_ref, 0, first), (high_ref, 128, second)):
            ref[start : start + 128, cells] = jnp.where(names == want, 1.0, 0.0).astype(bf16)
    return jnp.sum(total, axis=0, keepdims=True)


def crowded(count):
    return jnp.where(jnp.broadcast_to(count, (8, 128)) > slots, 1.0, 0.0)


def pieces(x):
    high = x.astype(bf16)
    rest = x - high.astype(f32)
    middle = rest.astype(bf16)
    return high, middle, (rest - middle.astype(f32)).astype(bf16)


def stacked(x, half):
    return jnp.concatenate([part[half * i : half * i + half] for i in range(2) for part in pieces(x)], axis=0)


def summed(x, half):
    parts = [x[half * i : half * i + half] for i in range(6)]
    return [parts[3 * i] + (parts[3 * i + 1] + parts[3 * i + 2]) for i in range(2)]


def encode(comps, x_ref, first_row, low_ref, high_ref, message_ref):
    half = comps // 2
    x = jnp.concatenate(
        [stacked(x_ref[pl.ds(first_row + z, comps, stride=8)], half) for z in range(4)], axis=1
    )
    over = (((1,), (1,)), ((), ()))
    low = lax.dot_general(x, low_ref[...], over, preferred_element_type=f32)
    high = [
        lax.dot_general(
            x[3 * half * i : 3 * half * (i + 1)], high_ref[128 * i : 128 * i + 128], over, preferred_element_type=f32
        )
        for i in range(2)
    ]
    tail = jnp.zeros((half, 128), f32)
    for i, part in enumerate(summed(low, half)):
        message_ref[half * i : half * i + half] = part[:, :128]
        message_ref[comps + half * i : comps + half * i + half] = part[:, 128:]
    for part in high:
        tail = tail + (part[:half] + (part[half : 2 * half] + part[2 * half :]))
    message_ref[2 * comps : 2 * comps + half] = tail


def decode(comps, message_ref, low_ref, high_ref):
    half = comps // 2
    x = jnp.concatenate([stacked(message_ref[comps * i : comps * i + comps], half) for i in range(2)], axis=1)
    low = jnp.dot(x, low_ref[...], preferred_element_type=f32)
    tail = jnp.concatenate(pieces(message_ref[2 * comps : 2 * comps + half]), axis=0)
    found = []
    for i, part in enumerate(summed(low, half)):
        high = jnp.dot(tail, high_ref[128 * i : 128 * i + 128], preferred_element_type=f32)
        found.append(part + (high[:half] + (high[half : 2 * half] + high[2 * half :])))
    return jnp.concatenate(found, axis=0)


def add_azimuthal(comps, halo, coefficient, first_row, out_ref):
    for z in range(4):
        spots = pl.ds(first_row + z, comps, stride=8)
        out_ref[spots] = out_ref[spots] + coefficient[first_row + z : first_row + z + 1] * halo[:, 128 * z : 128 * z + 128]


def pack_axial(comps, x_ref, axial_ref, ax_ref):
    @pl.when(axial_ref[0] == 0)
    def _():
        ax_ref[0 : 2 * comps] = x_ref[pl.ds(3, 2 * comps, stride=4)]

    @pl.when(axial_ref[0] != 0)
    def _():
        ax_ref[0 : 2 * comps] = x_ref[pl.ds(0, 2 * comps, stride=4)]


def add_axial(comps, scale, axial_ref, axial, ax_ref, out_ref):
    several = jnp.concatenate([scale * axial] * (2 * comps // 8), axis=0)
    for start, index in ((3, 0), (0, 1)):

        @pl.when(axial_ref[0] == index)
        def _():
            spots = pl.ds(start, 2 * comps, stride=4)
            out_ref[spots] = out_ref[spots] + several * ax_ref[0 : 2 * comps]


def columns(x):
    row, lane = rows_of(), lanes_of()
    take = jnp.where(((row == 0) & (lane == 127)) | ((row == 1) & (lane == 0)), 1.0, 0.0)
    return lax.dot_general(take, x, (((1,), (1,)), ((), ())), precision=exact, preferred_element_type=f32)


def pack_radial(comps, x_ref, p, rad_ref, one_ref, two_ref):
    even = rad_ref[0] % 2 == 0
    used = 8 * comps
    ends = columns(x_ref[...])
    for ref, last in ((one_ref, even), (two_ref, jnp.logical_not(even))):
        ref[:, 0:used] = jnp.where(last, ends[0:1], ends[1:2])
        ref[:, used:] = jnp.zeros((1, 256), f32)
        if p is not None:
            ref[:, used : used + 8] = columns(p)[1:2]


def radial_halo(comps, rad_ref, one_ref, two_ref):
    n = 8 * comps + 128
    even = rad_ref[0] % 2 == 0
    one, two = one_ref[:, 0:n], two_ref[:, 0:n]
    lower = jnp.where(rad_ref[0] > 0, jnp.where(even, two, one), 0.0)
    upper = jnp.where(rad_ref[0] < 3, jnp.where(even, one, two), 0.0)
    row, lane = rows_of(), lanes_of()
    which = lax.broadcasted_iota(jnp.int32, (8, n), 0)
    both = jnp.where(which == 0, lower, jnp.where(which == 1, upper, 0.0))
    place = jnp.where(((row == 0) & (lane == 0)) | ((row == 1) & (lane == 127)), 1.0, 0.0)
    return lax.dot_general(both, place, (((0,), (0,)), ((), ())), precision=exact, preferred_element_type=f32)


def source(sections, x_ref, u_ref, growth_ref, transfer_ref, zones_ref, rate_ref, finish):
    def inner(k, s, x):
        term = transfer_ref[s] * ((x[k][1] - x[k][0]) if s + 1 < sections else -x[k][0])
        if k < 3:
            term = term + ((k + 1.0) * growth_ref[s]) * x[k + 1][0]
        return term

    def load(s):
        got = []
        for k in range(4):
            c = k * sections + s
            here = x_ref[8 * c : 8 * c + 8]
            got.append((here, x_ref[8 * c + 8 : 8 * c + 16] if s + 1 < sections else None))
        return got

    squares = jnp.zeros((8, 128), f32)
    product = jnp.zeros((8, 128), f32)
    for s in range(sections):
        x = load(s)
        for k in range(4):
            u = u_ref[k * sections + s].astype(f32)
            product = product + u * inner(k, s, x)
        squares = squares + u * u
    sigma = supersat_scale / (1.0 + crowding * squares)
    birth = jnp.zeros((8, 128), f32)
    for k in range(4):
        c = k * sections
        birth = birth + nucleus_moments[k] * x_ref[8 * c : 8 * c + 8]
    rate = jnp.zeros((8, 128), f32)
    for label in range(rate_ref.shape[0]):
        rate = jnp.where(zones_ref[...] == label, rate_ref[label], rate)
    slope = (-2.0 * crowding / supersat_scale) * sigma * sigma * (product + 2.0 * rate * sigma * birth)
    for s in range(sections):
        x = load(s)
        for k in range(4):
            c = k * sections + s
            term = sigma * inner(k, s, x)
            if k == 3:
                term = term + u_ref[c].astype(f32) * slope
            finish(c, x[k][0], term)


def first_down(
    comps, axial_ref, rad_ref, a_ref, speeds_ref, flags_ref, dn_ref, ax_ref, one_ref, two_ref, bad_ref, low_ref, high_ref
):
    p, _ = faces(speeds_ref, flags_ref)
    count = make_tables(p[0], low_ref, high_ref)
    bad_ref[...] = crowded(count)
    encode(comps, a_ref, 0, low_ref, high_ref, dn_ref)
    dn_ref[5 * comps // 2 :] = p[0]
    pack_axial(comps, a_ref, axial_ref, ax_ref)
    ax_ref[2 * comps : 2 * comps + 8] = pair_rows(p[1], 0, 4)
    pack_radial(comps, a_ref, p[2], rad_ref, one_ref, two_ref)


def first_local(sections, a_ref, u_ref, speeds_ref, flags_ref, zones_ref, growth_ref, transfer_ref, rate_ref, out_ref):
    local = Local(*faces(speeds_ref, flags_ref))

    def finish(c, x, term):
        out_ref[8 * c : 8 * c + 8] = 0.5 * (x + local(x) + term)

    source(sections, a_ref, u_ref, growth_ref, transfer_ref, zones_ref, rate_ref, finish)


def second_local(
    sections,
    m_ref,
    a_ref,
    u_ref,
    above_ref,
    edge_ref,
    low_ref,
    high_ref,
    bad_ref,
    axial_bad_ref,
    speeds_ref,
    flags_ref,
    zones_ref,
    growth_ref,
    transfer_ref,
    rate_ref,
    out_ref,
    worse_ref,
):
    local = Local(*faces(speeds_ref, flags_ref))
    local.centre = local.centre + (edge_ref[3] - 1.0)
    worse_ref[...] = (bad_ref[...] + axial_bad_ref[...])[0:1]

    def finish(c, x, term):
        out_ref[8 * c : 8 * c + 8] = 0.5 * a_ref[8 * c : 8 * c + 8] + (local(x) + term)

    source(sections, m_ref, u_ref, growth_ref, transfer_ref, zones_ref, rate_ref, finish)
    add_azimuthal(4 * sections, decode(4 * sections, above_ref, low_ref, high_ref), edge_ref[0], 4, out_ref)


def from_below(c, below_ref):
    pair = below_ref[8 * (c // 2) : 8 * (c // 2) + 8]
    return pair if c % 2 == 0 else pltpu.roll(pair, 4, 0)


def first_bottom(
    comps,
    axial_ref,
    rad_ref,
    part_ref,
    a_ref,
    below_ref,
    ax_ref,
    one_ref,
    two_ref,
    bad_ref,
    speeds_ref,
    flags_ref,
    low_ref,
    high_ref,
    m_ref,
    edge_ref,
    dn_ref,
    worse_ref,
):
    _, q = faces(speeds_ref, flags_ref)
    row, lane = rows_of(), lanes_of()
    hrad = radial_halo(comps, rad_ref, one_ref, two_ref)
    lower_half = axial_ref[0] == 0
    pairs = jnp.where(lower_half, ax_ref[2 * comps : 2 * comps + 8], 0.0)
    p_axial = jnp.where(row == 3, pairs[0:1], jnp.where(row == 7, pairs[1:2], 0.0))
    p_rad = jnp.where(lane == 127, hrad[8 * comps : 8 * comps + 8], 0.0)
    axial = jnp.where(lower_half, pairs, pair_rows(q[1], 0, 4))
    rad = jnp.where(lane == 0, q[2], p_rad)
    centre = p_axial + p_rad
    azim = jnp.where(row >= 4, 0.0, q[0])
    edge_ref[0] = azim
    edge_ref[1] = axial
    edge_ref[2] = rad
    edge_ref[3] = centre
    for c in range(comps):
        spots = slice(8 * c, 8 * c + 8)
        m_ref[spots] = part_ref[spots] + 0.5 * (
            azim * from_below(c, below_ref) + rad * hrad[spots] - centre * a_ref[spots]
        )
    add_axial(comps, 0.5, axial_ref, axial, ax_ref, m_ref)
    encode(comps, m_ref, 0, low_ref, high_ref, dn_ref)
    below_p = jnp.where((row < 4) & (below_ref[4 * comps :] != 0.0), 1.0, 0.0)
    count = jnp.sum(jnp.sum(below_p, axis=1, keepdims=True), axis=0, keepdims=True)
    worse_ref[...] = bad_ref[...] + crowded(count)


def first_top(
    comps,
    axial_ref,
    rad_ref,
    part_ref,
    a_ref,
    above_ref,
    edge_ref,
    bad_ref,
    far_ref,
    m_ref,
    edges_ref,
    up_ref,
    ax_ref,
    one_ref,
    two_ref,
    worse_ref,
    low_ref,
    high_ref,
):
    upper = above_ref[5 * comps // 2 :]
    count = make_tables(upper, low_ref, high_ref)
    worse_ref[...] = bad_ref[...] + far_ref[...] + crowded(count)
    azim = jnp.where(rows_of() >= 4, pltpu.roll(upper, 4, 0), 0.0)
    edges_ref[0] = edge_ref[0] + azim
    edges_ref[1] = edge_ref[1]
    edges_ref[2] = edge_ref[2]
    edges_ref[3] = edge_ref[3] + azim
    half_azim = 0.5 * azim
    for c in range(comps):
        spots = slice(8 * c, 8 * c + 8)
        m_ref[spots] = part_ref[spots] - half_azim * a_ref[spots]
    add_azimuthal(comps, decode(comps, above_ref, low_ref, high_ref), half_azim, 4, m_ref)
    for c in range(comps):
        up_ref[4 * c : 4 * c + 4] = m_ref[8 * c + 4 : 8 * c + 8]
    pack_axial(comps, m_ref, axial_ref, ax_ref)
    pack_radial(comps, m_ref, None, rad_ref, one_ref, two_ref)


def second_top(
    comps,
    axial_ref,
    rad_ref,
    part_ref,
    ax_ref,
    one_ref,
    two_ref,
    edge_ref,
    bad_ref,
    far_ref,
    out_ref,
    bottom_ref,
    worse_ref,
    full_ref,
    high_half_ref,
    sems,
):
    hrad = radial_halo(comps, rad_ref, one_ref, two_ref)
    rad = edge_ref[2]
    for c in range(comps):
        spots = slice(8 * c, 8 * c + 8)
        full_ref[spots] = part_ref[spots] + rad * hrad[spots]
    add_axial(comps, 1.0, axial_ref, edge_ref[1], ax_ref, full_ref)
    for c in range(comps):
        high_half_ref[c] = full_ref[8 * c + 4 : 8 * c + 8]
    copy = pltpu.make_async_copy(high_half_ref, out_ref.at[:, 1], sems.at[0])
    copy.start()
    for c in range(comps):
        bottom_ref[c] = full_ref[8 * c : 8 * c + 4]
    ends = slice(8 * comps + 128, 8 * comps + 256)
    worse_ref[...] = bad_ref[...] + far_ref[...] + (one_ref[:, ends] + two_ref[:, ends])
    copy.wait()


def second_bottom(comps, parts, _, bottom_ref, below_ref, edge_ref, out_ref, low_half_ref, sems):
    azim = edge_ref[0][0:4]
    size = comps // parts
    made = []
    for i in range(parts):
        spots = pl.ds(i * size, size)
        low_half_ref[spots] = bottom_ref[spots] + azim[None] * below_ref[spots]
        made.append(pltpu.make_async_copy(low_half_ref.at[spots], out_ref.at[spots, 0], sems.at[i]))
        made[-1].start()
    for copy in made:
        copy.wait()


SPACES = {
    "v": pl.BlockSpec(memory_space=pltpu.VMEM),
    "s": pl.BlockSpec(memory_space=pltpu.SMEM),
    "h": pl.BlockSpec(memory_space=pltpu.HBM),
}


def call(body, ins, outs, shapes, *operands, scratch=(), aliases={}):
    shapes = [shape if isinstance(shape, jax.ShapeDtypeStruct) else jax.ShapeDtypeStruct(shape, f32) for shape in shapes]
    return pl.pallas_call(
        body,
        in_specs=[SPACES[s] for s in ins],
        out_specs=[SPACES[s] for s in outs],
        out_shape=shapes,
        scratch_shapes=scratch,
        input_output_aliases=aliases,
        cost_estimate=pl.CostEstimate(flops=4000000, bytes_accessed=400000, transcendentals=0),
        compiler_params=pltpu.CompilerParams(vmem_limit_bytes=32 * 1024 * 1024),
    )(*operands)


def shift(x, axis, step):
    size = lax.axis_size(axis)
    return lax.ppermute(x, axis, [(i, (i + step) % size) for i in range(size)])


def swap_axial(x):
    return lax.ppermute(x, "axial", [(0, 1), (1, 0)])


def swap_radial(x, first):
    size = lax.axis_size("rad")
    pairs = [(i, (i + 1) % size) for i in range(first, size, 2)]
    return lax.ppermute(x, "rad", pairs + [(j, i) for i, j in pairs])


def packed_step(
    adjoint_final, state_start, state_middle, speeds, flags, zones, growth_rate, transfer_rate, nucleation_rate
):
    shape = adjoint_final.shape
    moments, sections = shape[:2]
    comps = moments * sections
    assert moments == 4 and shape[2:] == (2, 4, 128) and comps % 32 == 0
    assert lax.axis_size("axial") == 2 and lax.axis_size("rad") == 4
    cells = 8 * comps
    half, rows, message = cells // 2, cells // 4, 5 * comps // 2 + 8
    a = adjoint_final.reshape(cells, 128)
    speeds_, speeds = speeds, speeds.reshape(3, 8, 128)
    flags_, flags = flags, flags.reshape(3, 8, 128)
    place = (lax.axis_index("axial").reshape(1), lax.axis_index("rad").reshape(1))
    rates = (zones.reshape(8, 128), growth_rate, transfer_rate, nucleation_rate)
    tables = [jax.ShapeDtypeStruct((256, 512), bf16)] * 2

    keep = ((0, 2, 0), (-1, 0, 0), (0, 0, 0), (0, 0, 0))
    after = ((comps, 1, 0), (0, -1, 0), (0, 0, 0), (0, 0, 0))
    up = lax.pad(adjoint_final.reshape(comps, 2, 4, 128), 0.0, keep)
    up = up + lax.pad(speeds_[:1], 0.0, after) * lax.pad(flags_[:1], 0, after).astype(f32)
    below = shift(up.reshape(half + 8, 128), "azim", 1)
    dn, ax, one, two, bad, *dn_tables = call(
        functools.partial(first_down, comps),
        "ssvvv",
        "v" * 7,
        [(message, 128), (rows + 8, 128), (1, cells + 256), (1, cells + 256), (8, 128)] + tables,
        *place,
        a,
        speeds,
        flags,
    )
    above = shift(dn, "azim", -1)
    far = shift(bad, "azim", 2)
    if lax.axis_size("azim") > 4:
        far = lax.pmax(far, "azim")
    ax = swap_axial(ax)
    one, two = swap_radial(one, 0), swap_radial(two, 1)
    (part,) = call(
        functools.partial(first_local, sections),
        "vvvvvsss",
        "v",
        [(cells, 128)],
        a,
        state_middle.reshape(comps, 8, 128),
        speeds,
        flags,
        *rates,
    )
    part, edge, dn, bad = call(
        functools.partial(first_bottom, comps),
        "ss" + "v" * 11,
        "vvvv",
        [(cells, 128), (4, 8, 128), (message - 8, 128), (8, 128)],
        *place,
        part,
        a,
        below,
        ax,
        one,
        two,
        bad,
        speeds,
        flags,
        *dn_tables,
    )
    next_above = shift(dn, "azim", -1)
    m, edge, up, ax, one, two, bad, *tables = call(
        functools.partial(first_top, comps),
        "ss" + "v" * 6,
        "v" * 9,
        [
            (cells, 128),
            (4, 8, 128),
            (half, 128),
            (rows, 128),
            (1, cells + 256),
            (1, cells + 256),
            (8, 128),
        ]
        + tables,
        *place,
        part,
        a,
        above,
        edge,
        bad,
        far,
    )
    below = shift(up, "azim", 1).reshape(comps, 4, 128)
    ax = swap_axial(ax)
    part, bad = call(
        functools.partial(second_local, sections),
        "v" * 12 + "sss",
        "vv",
        [(cells, 128), (1, 128)],
        m,
        a,
        state_start.reshape(comps, 8, 128),
        next_above,
        edge,
        *tables,
        bad,
        swap_axial(bad),
        speeds,
        flags,
        *rates,
    )

    def told(columns_):
        return columns_ + lax.pad(bad, 0.0, ((0, 0, 0), (cells + 128, 0, 0)))

    one, two = swap_radial(told(one), 0), swap_radial(told(two), 1)
    far = shift(bad, "rad", 2)
    out, bottom, bad = call(
        functools.partial(second_top, comps),
        "ss" + "v" * 7,
        "hvv",
        [(comps, 2, 4, 128), (comps, 4, 128), (1, 128)],
        *place,
        part,
        ax,
        one,
        two,
        edge,
        bad,
        far,
        scratch=[pltpu.VMEM((cells, 128), f32), pltpu.VMEM((comps, 4, 128), f32), pltpu.SemaphoreType.DMA((1,))],
    )

    def finish():
        (whole,) = call(
            functools.partial(second_bottom, comps, 4),
            "hvvv",
            "h",
            [(comps, 2, 4, 128)],
            out,
            bottom,
            below,
            edge,
            scratch=[pltpu.VMEM((comps, 4, 128), f32), pltpu.SemaphoreType.DMA((4,))],
            aliases={0: 0},
        )
        return whole.reshape(shape)

    return finish, bad[0, 0]


def extended(x, sides, width, wrap):
    for axis, dim in sides:
        size, length = (lax.axis_size(axis), x.shape[dim])
        up = [(i, (i + 1) % size) for i in range(size if wrap else size - 1)]
        down = [(j, i) for i, j in up]
        last = lax.slice_in_dim(x, length - width, length, axis=dim)
        first = lax.slice_in_dim(x, 0, width, axis=dim)
        before = lax.ppermute(last, axis, up)
        after = lax.ppermute(first, axis, down)
        x = jnp.concatenate([before, x, after], axis=dim)
    return x


def source_term(state, growth_rate, transfer_rate, nucleation):
    extra = (1,) * (state.ndim - 2)
    growth = growth_rate.reshape((1, -1) + extra)
    transfer = transfer_rate.reshape((1, -1) + extra)
    third = state[3]
    sigma = supersat_scale / (1.0 + crowding * jnp.sum(third * third, axis=0))
    lower = jnp.concatenate([jnp.zeros_like(state[0:1]), state[:3]], axis=0)
    factors = jnp.array([0.0, 1.0, 2.0, 3.0], dtype=state.dtype).reshape((4, 1) + extra)
    outflow = transfer * state
    inflow = jnp.concatenate([jnp.zeros_like(outflow[:, 0:1]), outflow[:, :-1]], axis=1)
    first = (jnp.arange(state.shape[1]) == 0).astype(state.dtype).reshape((1, -1) + extra)
    nucleus = jnp.array(nucleus_moments, dtype=state.dtype).reshape((4, 1) + extra)
    birth = nucleus * first * (nucleation * sigma * sigma)[None, None]
    return sigma[None, None] * (factors * growth * lower + inflow - outflow) + birth


def source_adjoint(state, adjoint, growth_rate, transfer_rate, nucleation):
    _, pull = jax.vjp(
        lambda field: source_term(field, growth_rate, transfer_rate, nucleation), state
    )
    return pull(adjoint)[0]


def cut_region(field, direction, offset):
    lead = [slice(None)] * (field.ndim - 3)
    spatial = []
    for which in range(3):
        moved = offset if which == direction else 0
        length = field.shape[field.ndim - 3 + which]
        spatial.append(slice(1 + moved, length - 1 + moved))
    return field[tuple(lead + spatial)]


def transport_adjoint(adjoint_pad, coeff_pad):
    total = None
    for direction in range(3):
        centre = cut_region(adjoint_pad, direction, 0)
        higher = cut_region(adjoint_pad, direction, 1)
        lowerv = cut_region(adjoint_pad, direction, -1)
        p_high = cut_region(coeff_pad[direction], direction, 1)
        q_here = cut_region(coeff_pad[3 + direction], direction, 0)
        term = p_high * (higher - centre) + q_here * (lowerv - centre)
        total = term if total is None else total + term
    return total


def face_coefficients(speeds, flags):
    upwind = flags.astype(speeds.dtype)
    return jnp.concatenate([speeds * upwind, speeds * (1.0 - upwind)], axis=0)


def nucleation_field(zones, nucleation_rate):
    labels = jnp.arange(nucleation_rate.shape[0], dtype=jnp.int32).reshape((-1, 1, 1, 1))
    match = (zones[None] == labels).astype(nucleation_rate.dtype)
    return jnp.sum(match * nucleation_rate.reshape((-1, 1, 1, 1)), axis=0)


def whole_step(
    adjoint_final,
    state_start,
    state_middle,
    speeds,
    flags,
    zones,
    growth_rate,
    transfer_rate,
    nucleation_rate,
):
    coeffs = face_coefficients(speeds, flags)
    nucleation = nucleation_field(zones, nucleation_rate)
    start = state_start.astype(jnp.float32)
    middle = state_middle.astype(jnp.float32)
    dims = adjoint_final.shape
    comps = dims[0] * dims[1]
    packed = jnp.concatenate([adjoint_final.reshape((comps,) + dims[2:]), coeffs], axis=0)
    packed = extended(packed, (("azim", 1),), 1, True)
    packed = extended(packed, (("rad", 3), ("axial", 2)), 1, False)
    later_pad = packed[:comps].reshape(dims[:2] + packed.shape[1:])
    coeff_pad = packed[comps:]
    adjoint_middle = 0.5 * adjoint_final + 0.5 * (
        transport_adjoint(later_pad, coeff_pad)
        + source_adjoint(middle, adjoint_final, growth_rate, transfer_rate, nucleation)
    )
    flat = adjoint_middle.reshape((comps,) + dims[2:])
    flat = extended(flat, (("azim", 1),), 1, True)
    flat = extended(flat, (("rad", 3), ("axial", 2)), 1, False)
    middle_pad = flat.reshape(dims[:2] + flat.shape[1:])
    return (
        0.5 * adjoint_final
        + adjoint_middle
        + transport_adjoint(middle_pad, coeff_pad)
        + source_adjoint(start, adjoint_middle, growth_rate, transfer_rate, nucleation)
    )


def shards(*arguments):
    finish, bad = packed_step(*arguments)
    return lax.cond(bad > 0.0, lambda: whole_step(*arguments), finish)


def solution(mesh):
    field = P(None, None, "azim", "axial", "rad")
    faces_spec = P(None, "azim", "axial", "rad")
    return jax.shard_map(
        shards,
        mesh=mesh,
        in_specs=(field, field, field, faces_spec, faces_spec, P("azim", "axial", "rad"), P(), P(), P()),
        out_specs=field,
        check_vma=False,
    )
```

```python
import functools

import jax
import jax.numpy as jnp
from jax import lax
from jax.experimental import pallas as pl
from jax.experimental.pallas import tpu as pltpu
from jax.sharding import PartitionSpec as P

supersat_scale = 1.5
crowding = 0.02
nucleus_moments = (1.0, 0.5, 0.25, 0.125)
f32 = jnp.float32
bf16 = jnp.bfloat16
exact = lax.Precision.HIGHEST

slots = 320
extra = slots - 256


def rows_of():
    return lax.broadcasted_iota(jnp.int32, (8, 128), 0)


def lanes_of():
    return lax.broadcasted_iota(jnp.int32, (8, 128), 1)


def faces(speeds_ref, flags_ref):
    p, q = [], []
    for d in range(3):
        speed, upwind = speeds_ref[d], flags_ref[d].astype(f32)
        p.append(speed * upwind)
        q.append(speed * (1.0 - upwind))
    return p, q


class Local:
    def __init__(self, p, q):
        row, lane = rows_of(), lanes_of()
        z, top = row % 4, row >= 4
        self.azim = jnp.where(top, q[0], pltpu.roll(p[0], 4, 0))
        self.ax_up = jnp.where(z == 3, 0.0, pltpu.roll(p[1], 7, 0))
        self.ax_dn = jnp.where(z == 0, 0.0, q[1])
        self.rad_up = jnp.where(lane == 127, 0.0, pltpu.roll(p[2], 127, 1))
        self.rad_dn = jnp.where(lane == 0, 0.0, q[2])
        self.centre = self.azim + self.ax_up + q[1] + self.rad_up + q[2] + jnp.where(top, 0.0, q[0])

    def __call__(self, x):
        return (
            self.azim * pltpu.roll(x, 4, 0)
            + self.ax_up * pltpu.roll(x, 7, 0)
            + self.ax_dn * pltpu.roll(x, 1, 0)
            + self.rad_up * pltpu.roll(x, 127, 1)
            + self.rad_dn * pltpu.roll(x, 1, 1)
            - self.centre * x
        )


def pair_rows(x, first, second):
    return jnp.where(
        rows_of() % 2 == 0,
        jnp.broadcast_to(x[first : first + 1], (8, 128)),
        jnp.broadcast_to(x[second : second + 1], (8, 128)),
    )


def make_tables(p, low_ref, high_ref):
    row, lane = rows_of(), lanes_of()
    one = jnp.where((p != 0.0) & (row < 4), 1.0, 0.0)
    before = lax.broadcasted_iota(jnp.int32, (128, 128), 0) < lax.broadcasted_iota(jnp.int32, (128, 128), 1)
    inside = jnp.dot(one.astype(bf16), jnp.where(before, 1.0, 0.0).astype(bf16), preferred_element_type=f32)
    total = jnp.sum(one, axis=1, keepdims=True)
    base = jnp.zeros((8, 1), f32)
    for step in (1, 2, 3):
        base = base + jnp.where(
            lax.broadcasted_iota(jnp.int32, (8, 1), 0) >= step, jnp.roll(total, step, axis=0), 0.0
        )
    slot = jnp.where(one > 0.0, inside + base, -1.0).astype(jnp.int32)
    here = lax.broadcasted_iota(jnp.int32, (128, 128), 0)
    first = jnp.where(here < extra, here + 256, -2)
    second = jnp.where(here >= extra, here + (256 - extra), -2)
    for z in range(4):
        cells = slice(128 * z, 128 * z + 128)
        want = jnp.broadcast_to(slot[z : z + 1], (128, 128))
        for ref, start, names in ((low_ref, 0, here), (low_ref, 128, here + 128), (high_ref, 0, first), (high_ref, 128, second)):
            ref[start : start + 128, cells] = jnp.where(names == want, 1.0, 0.0).astype(bf16)


def crowded(p):
    taken = jnp.where((rows_of() < 4) & (p != 0.0), 1.0, 0.0)
    count = jnp.sum(jnp.sum(taken, axis=1, keepdims=True), axis=0, keepdims=True)
    return jnp.where(jnp.broadcast_to(count, (8, 128)) > slots, 1.0, 0.0)


def pieces(x):
    high = x.astype(bf16)
    rest = x - high.astype(f32)
    middle = rest.astype(bf16)
    return high, middle, (rest - middle.astype(f32)).astype(bf16)


def stacked(x, half):
    return jnp.concatenate([part[half * i : half * i + half] for i in range(2) for part in pieces(x)], axis=0)


def summed(x, half):
    parts = [x[half * i : half * i + half] for i in range(6)]
    return [parts[3 * i] + (parts[3 * i + 1] + parts[3 * i + 2]) for i in range(2)]


def encode(comps, x_ref, first_row, low_ref, high_ref, message_ref):
    half = comps // 2
    x = jnp.concatenate(
        [stacked(x_ref[pl.ds(first_row + z, comps, stride=8)], half) for z in range(4)], axis=1
    )
    over = (((1,), (1,)), ((), ()))
    low = lax.dot_general(x, low_ref[...], over, preferred_element_type=f32)
    high = [
        lax.dot_general(
            x[3 * half * i : 3 * half * (i + 1)], high_ref[128 * i : 128 * i + 128], over, preferred_element_type=f32
        )
        for i in range(2)
    ]
    tail = jnp.zeros((half, 128), f32)
    for i, part in enumerate(summed(low, half)):
        message_ref[half * i : half * i + half] = part[:, :128]
        message_ref[comps + half * i : comps + half * i + half] = part[:, 128:]
    for part in high:
        tail = tail + (part[:half] + (part[half : 2 * half] + part[2 * half :]))
    message_ref[2 * comps : 2 * comps + half] = tail


def decode(comps, message_ref, low_ref, high_ref):
    half = comps // 2
    x = jnp.concatenate([stacked(message_ref[comps * i : comps * i + comps], half) for i in range(2)], axis=1)
    low = jnp.dot(x, low_ref[...], preferred_element_type=f32)
    tail = jnp.concatenate(pieces(message_ref[2 * comps : 2 * comps + half]), axis=0)
    found = []
    for i, part in enumerate(summed(low, half)):
        high = jnp.dot(tail, high_ref[128 * i : 128 * i + 128], preferred_element_type=f32)
        found.append(part + (high[:half] + (high[half : 2 * half] + high[2 * half :])))
    return jnp.concatenate(found, axis=0)


def add_azimuthal(comps, halo, coefficient, first_row, out_ref):
    for z in range(4):
        spots = pl.ds(first_row + z, comps, stride=8)
        out_ref[spots] = out_ref[spots] + coefficient[first_row + z : first_row + z + 1] * halo[:, 128 * z : 128 * z + 128]


def pack_axial(comps, x_ref, axial_ref, ax_ref):
    @pl.when(axial_ref[0] == 0)
    def _():
        ax_ref[0 : 2 * comps] = x_ref[pl.ds(3, 2 * comps, stride=4)]

    @pl.when(axial_ref[0] != 0)
    def _():
        ax_ref[0 : 2 * comps] = x_ref[pl.ds(0, 2 * comps, stride=4)]


def add_axial(comps, scale, axial_ref, axial, ax_ref, out_ref):
    several = jnp.concatenate([scale * axial] * (2 * comps // 8), axis=0)
    for start, index in ((3, 0), (0, 1)):

        @pl.when(axial_ref[0] == index)
        def _():
            spots = pl.ds(start, 2 * comps, stride=4)
            out_ref[spots] = out_ref[spots] + several * ax_ref[0 : 2 * comps]


def columns(x):
    row, lane = rows_of(), lanes_of()
    take = jnp.where(((row == 0) & (lane == 127)) | ((row == 1) & (lane == 0)), 1.0, 0.0)
    return lax.dot_general(take, x, (((1,), (1,)), ((), ())), precision=exact, preferred_element_type=f32)


def pack_radial(comps, x_ref, p, rad_ref, one_ref, two_ref):
    even = rad_ref[0] % 2 == 0
    used = 8 * comps
    ends = columns(x_ref[...])
    for ref, last in ((one_ref, even), (two_ref, jnp.logical_not(even))):
        ref[:, 0:used] = jnp.where(last, ends[0:1], ends[1:2])
        ref[:, used:] = jnp.zeros((1, 256), f32)
        if p is not None:
            ref[:, used : used + 8] = columns(p)[1:2]


def radial_halo(comps, rad_ref, one_ref, two_ref):
    n = 8 * comps + 128
    even = rad_ref[0] % 2 == 0
    one, two = one_ref[:, 0:n], two_ref[:, 0:n]
    lower = jnp.where(rad_ref[0] > 0, jnp.where(even, two, one), 0.0)
    upper = jnp.where(rad_ref[0] < 3, jnp.where(even, one, two), 0.0)
    row, lane = rows_of(), lanes_of()
    which = lax.broadcasted_iota(jnp.int32, (8, n), 0)
    both = jnp.where(which == 0, lower, jnp.where(which == 1, upper, 0.0))
    place = jnp.where(((row == 0) & (lane == 0)) | ((row == 1) & (lane == 127)), 1.0, 0.0)
    return lax.dot_general(both, place, (((0,), (0,)), ((), ())), precision=exact, preferred_element_type=f32)


def source(sections, x_ref, u_ref, growth_ref, transfer_ref, zones_ref, rate_ref, finish):
    def inner(k, s, x):
        term = transfer_ref[s] * ((x[k][1] - x[k][0]) if s + 1 < sections else -x[k][0])
        if k < 3:
            term = term + ((k + 1.0) * growth_ref[s]) * x[k + 1][0]
        return term

    def load(s):
        got = []
        for k in range(4):
            c = k * sections + s
            here = x_ref[8 * c : 8 * c + 8]
            got.append((here, x_ref[8 * c + 8 : 8 * c + 16] if s + 1 < sections else None))
        return got

    squares = jnp.zeros((8, 128), f32)
    product = jnp.zeros((8, 128), f32)
    for s in range(sections):
        x = load(s)
        for k in range(4):
            u = u_ref[k * sections + s].astype(f32)
            product = product + u * inner(k, s, x)
        squares = squares + u * u
    sigma = supersat_scale / (1.0 + crowding * squares)
    birth = jnp.zeros((8, 128), f32)
    for k in range(4):
        c = k * sections
        birth = birth + nucleus_moments[k] * x_ref[8 * c : 8 * c + 8]
    rate = jnp.zeros((8, 128), f32)
    for label in range(rate_ref.shape[0]):
        rate = jnp.where(zones_ref[...] == label, rate_ref[label], rate)
    slope = (-2.0 * crowding / supersat_scale) * sigma * sigma * (product + 2.0 * rate * sigma * birth)
    for s in range(sections):
        x = load(s)
        for k in range(4):
            c = k * sections + s
            term = sigma * inner(k, s, x)
            if k == 3:
                term = term + u_ref[c].astype(f32) * slope
            finish(c, x[k][0], term)


def first_down(
    comps, axial_ref, rad_ref, a_ref, speeds_ref, flags_ref, dn_ref, ax_ref, one_ref, two_ref, bad_ref, low_ref, high_ref
):
    p, _ = faces(speeds_ref, flags_ref)
    make_tables(p[0], low_ref, high_ref)
    bad_ref[...] = crowded(p[0])
    encode(comps, a_ref, 0, low_ref, high_ref, dn_ref)
    dn_ref[5 * comps // 2 : 5 * comps // 2 + 8] = p[0]
    dn_ref[5 * comps // 2 + 8 :] = jnp.zeros((8, 128), f32)
    pack_axial(comps, a_ref, axial_ref, ax_ref)
    ax_ref[2 * comps : 2 * comps + 8] = pair_rows(p[1], 0, 4)
    pack_radial(comps, a_ref, p[2], rad_ref, one_ref, two_ref)


def first_local(sections, a_ref, u_ref, speeds_ref, flags_ref, zones_ref, growth_ref, transfer_ref, rate_ref, out_ref):
    local = Local(*faces(speeds_ref, flags_ref))

    def finish(c, x, term):
        out_ref[8 * c : 8 * c + 8] = 0.5 * (x + local(x) + term)

    source(sections, a_ref, u_ref, growth_ref, transfer_ref, zones_ref, rate_ref, finish)


def second_local(
    sections,
    m_ref,
    a_ref,
    u_ref,
    above_ref,
    edge_ref,
    low_ref,
    high_ref,
    bad_ref,
    axial_bad_ref,
    speeds_ref,
    flags_ref,
    zones_ref,
    growth_ref,
    transfer_ref,
    rate_ref,
    out_ref,
    worse_ref,
):
    local = Local(*faces(speeds_ref, flags_ref))
    local.centre = local.centre + (edge_ref[3] - 1.0)
    worse_ref[...] = (bad_ref[...] + axial_bad_ref[...])[0:1]

    def finish(c, x, term):
        out_ref[8 * c : 8 * c + 8] = 0.5 * a_ref[8 * c : 8 * c + 8] + (local(x) + term)

    source(sections, m_ref, u_ref, growth_ref, transfer_ref, zones_ref, rate_ref, finish)
    add_azimuthal(4 * sections, decode(4 * sections, above_ref, low_ref, high_ref), edge_ref[0], 4, out_ref)


def from_below(c, below_ref):
    pair = below_ref[8 * (c // 2) : 8 * (c // 2) + 8]
    return pair if c % 2 == 0 else pltpu.roll(pair, 4, 0)


def first_bottom(
    comps,
    axial_ref,
    rad_ref,
    part_ref,
    a_ref,
    below_ref,
    ax_ref,
    one_ref,
    two_ref,
    bad_ref,
    speeds_ref,
    flags_ref,
    low_ref,
    high_ref,
    m_ref,
    edge_ref,
    dn_ref,
    worse_ref,
):
    _, q = faces(speeds_ref, flags_ref)
    row, lane = rows_of(), lanes_of()
    hrad = radial_halo(comps, rad_ref, one_ref, two_ref)
    lower_half = axial_ref[0] == 0
    pairs = jnp.where(lower_half, ax_ref[2 * comps : 2 * comps + 8], 0.0)
    p_axial = jnp.where(row == 3, pairs[0:1], jnp.where(row == 7, pairs[1:2], 0.0))
    p_rad = jnp.where(lane == 127, hrad[8 * comps : 8 * comps + 8], 0.0)
    axial = jnp.where(lower_half, pairs, pair_rows(q[1], 0, 4))
    rad = jnp.where(lane == 0, q[2], p_rad)
    centre = p_axial + p_rad
    azim = jnp.where(row >= 4, 0.0, q[0])
    edge_ref[0] = azim
    edge_ref[1] = axial
    edge_ref[2] = rad
    edge_ref[3] = centre
    for c in range(comps):
        spots = slice(8 * c, 8 * c + 8)
        m_ref[spots] = part_ref[spots] + 0.5 * (
            azim * from_below(c, below_ref) + rad * hrad[spots] - centre * a_ref[spots]
        )
    add_axial(comps, 0.5, axial_ref, axial, ax_ref, m_ref)
    encode(comps, m_ref, 0, low_ref, high_ref, dn_ref)
    worse_ref[...] = bad_ref[...] + crowded(below_ref[4 * comps :])


def first_top(
    comps,
    axial_ref,
    rad_ref,
    part_ref,
    a_ref,
    above_ref,
    edge_ref,
    bad_ref,
    m_ref,
    edges_ref,
    up_ref,
    ax_ref,
    one_ref,
    two_ref,
    worse_ref,
    low_ref,
    high_ref,
):
    upper = above_ref[5 * comps // 2 : 5 * comps // 2 + 8]
    make_tables(upper, low_ref, high_ref)
    worse_ref[...] = bad_ref[...] + crowded(upper) + crowded(above_ref[5 * comps // 2 + 8 :])
    azim = jnp.where(rows_of() >= 4, pltpu.roll(upper, 4, 0), 0.0)
    edges_ref[0] = edge_ref[0] + azim
    edges_ref[1] = edge_ref[1]
    edges_ref[2] = edge_ref[2]
    edges_ref[3] = edge_ref[3] + azim
    half_azim = 0.5 * azim
    for c in range(comps):
        spots = slice(8 * c, 8 * c + 8)
        m_ref[spots] = part_ref[spots] - half_azim * a_ref[spots]
    add_azimuthal(comps, decode(comps, above_ref, low_ref, high_ref), half_azim, 4, m_ref)
    for c in range(comps):
        up_ref[4 * c : 4 * c + 4] = m_ref[8 * c + 4 : 8 * c + 8]
    pack_axial(comps, m_ref, axial_ref, ax_ref)
    pack_radial(comps, m_ref, None, rad_ref, one_ref, two_ref)


def second_top(
    comps,
    axial_ref,
    rad_ref,
    part_ref,
    ax_ref,
    one_ref,
    two_ref,
    edge_ref,
    bad_ref,
    far_ref,
    out_ref,
    bottom_ref,
    worse_ref,
    full_ref,
    high_half_ref,
    sems,
):
    hrad = radial_halo(comps, rad_ref, one_ref, two_ref)
    rad = edge_ref[2]
    for c in range(comps):
        spots = slice(8 * c, 8 * c + 8)
        full_ref[spots] = part_ref[spots] + rad * hrad[spots]
    add_axial(comps, 1.0, axial_ref, edge_ref[1], ax_ref, full_ref)
    for c in range(comps):
        high_half_ref[c] = full_ref[8 * c + 4 : 8 * c + 8]
    copy = pltpu.make_async_copy(high_half_ref, out_ref.at[:, 1], sems.at[0])
    copy.start()
    for c in range(comps):
        bottom_ref[c] = full_ref[8 * c : 8 * c + 4]
    ends = slice(8 * comps + 128, 8 * comps + 256)
    worse_ref[...] = bad_ref[...] + far_ref[...] + (one_ref[:, ends] + two_ref[:, ends])
    copy.wait()


def second_bottom(comps, parts, _, bottom_ref, below_ref, edge_ref, out_ref, low_half_ref, sems):
    azim = edge_ref[0][0:4]
    size = comps // parts
    made = []
    for i in range(parts):
        spots = pl.ds(i * size, size)
        low_half_ref[spots] = bottom_ref[spots] + azim[None] * below_ref[spots]
        made.append(pltpu.make_async_copy(low_half_ref.at[spots], out_ref.at[spots, 0], sems.at[i]))
        made[-1].start()
    for copy in made:
        copy.wait()


SPACES = {
    "v": pl.BlockSpec(memory_space=pltpu.VMEM),
    "s": pl.BlockSpec(memory_space=pltpu.SMEM),
    "h": pl.BlockSpec(memory_space=pltpu.HBM),
}


def call(body, ins, outs, shapes, *operands, scratch=(), aliases={}, room=32):
    shapes = [shape if isinstance(shape, jax.ShapeDtypeStruct) else jax.ShapeDtypeStruct(shape, f32) for shape in shapes]
    return pl.pallas_call(
        body,
        in_specs=[SPACES[s] for s in ins],
        out_specs=[SPACES[s] for s in outs],
        out_shape=shapes,
        scratch_shapes=scratch,
        input_output_aliases=aliases,
        cost_estimate=pl.CostEstimate(flops=4000000, bytes_accessed=400000, transcendentals=0),
        compiler_params=pltpu.CompilerParams(vmem_limit_bytes=room * 1024 * 1024),
    )(*operands)


def shift(x, axis, step):
    size = lax.axis_size(axis)
    return lax.ppermute(x, axis, [(i, (i + step) % size) for i in range(size)])


def swap_axial(x):
    return lax.ppermute(x, "axial", [(0, 1), (1, 0)])


def swap_radial(x, first):
    size = lax.axis_size("rad")
    pairs = [(i, (i + 1) % size) for i in range(first, size, 2)]
    return lax.ppermute(x, "rad", pairs + [(j, i) for i, j in pairs])


def packed_step(
    adjoint_final, state_start, state_middle, speeds, flags, zones, growth_rate, transfer_rate, nucleation_rate
):
    shape = adjoint_final.shape
    moments, sections = shape[:2]
    comps = moments * sections
    assert moments == 4 and shape[2:] == (2, 4, 128) and comps % 32 == 0
    assert lax.axis_size("axial") == 2 and lax.axis_size("rad") == 4
    cells = 8 * comps
    half, rows, message = cells // 2, cells // 4, 5 * comps // 2
    a = adjoint_final.reshape(cells, 128)
    speeds_, speeds = speeds, speeds.reshape(3, 8, 128)
    flags_, flags = flags, flags.reshape(3, 8, 128)
    place = (lax.axis_index("axial").reshape(1), lax.axis_index("rad").reshape(1))
    rates = (zones.reshape(8, 128), growth_rate, transfer_rate, nucleation_rate)
    tables = [jax.ShapeDtypeStruct((256, 512), bf16)] * 2

    keep = ((0, 2, 0), (-1, 0, 0), (0, 0, 0), (0, 0, 0))
    after = ((comps, -1, 0), (0, -1, 0), (0, 0, 0), (0, 0, 0))
    up = lax.pad(adjoint_final.reshape(comps, 2, 4, 128), 0.0, keep)
    up = up + lax.pad(speeds_, 0.0, after) * lax.pad(flags_, 0, after).astype(f32)
    below = shift(up.reshape(half + 8, 128), "azim", 1)
    upper = shift(speeds[0] * flags[0].astype(f32), "azim", -1)
    dn, ax, one, two, bad, *dn_tables = call(
        functools.partial(first_down, comps),
        "ssvvv",
        "v" * 7,
        [(message + 16, 128), (rows + 8, 128), (1, cells + 256), (1, cells + 256), (8, 128)] + tables,
        *place,
        a,
        speeds,
        flags,
    )
    above = shift(lax.dynamic_update_slice(dn, upper, (message + 8, 0)), "azim", -1)
    if lax.axis_size("azim") > 4:
        bad = lax.pmax(bad, "azim")
    ax = swap_axial(ax)
    one, two = swap_radial(one, 0), swap_radial(two, 1)
    (part,) = call(
        functools.partial(first_local, sections),
        "vvvvvsss",
        "v",
        [(cells, 128)],
        a,
        state_middle.reshape(comps, 8, 128),
        speeds,
        flags,
        *rates,
    )
    part, edge, dn, bad = call(
        functools.partial(first_bottom, comps),
        "ss" + "v" * 11,
        "vvvv",
        [(cells, 128), (4, 8, 128), (message, 128), (8, 128)],
        *place,
        part,
        a,
        below,
        ax,
        one,
        two,
        bad,
        speeds,
        flags,
        *dn_tables,
    )
    next_above = shift(dn, "azim", -1)
    m, edge, up, ax, one, two, bad, *tables = call(
        functools.partial(first_top, comps),
        "ss" + "v" * 5,
        "v" * 9,
        [
            (cells, 128),
            (4, 8, 128),
            (half, 128),
            (rows, 128),
            (1, cells + 256),
            (1, cells + 256),
            (8, 128),
        ]
        + tables,
        *place,
        part,
        a,
        above,
        edge,
        bad,
    )
    below = shift(up, "azim", 1).reshape(comps, 4, 128)
    ax = swap_axial(ax)
    part, bad = call(
        functools.partial(second_local, sections),
        "v" * 12 + "sss",
        "vv",
        [(cells, 128), (1, 128)],
        m,
        a,
        state_start.reshape(comps, 8, 128),
        next_above,
        edge,
        *tables,
        bad,
        swap_axial(bad),
        speeds,
        flags,
        *rates,
    )

    def told(columns_):
        return columns_ + lax.pad(bad, 0.0, ((0, 0, 0), (cells + 128, 0, 0)))

    one, two = swap_radial(told(one), 0), swap_radial(told(two), 1)
    far = shift(bad, "rad", 2)
    out, bottom, bad = call(
        functools.partial(second_top, comps),
        "ss" + "v" * 7,
        "hvv",
        [(comps, 2, 4, 128), (comps, 4, 128), (1, 128)],
        *place,
        part,
        ax,
        one,
        two,
        edge,
        bad,
        far,
        scratch=[pltpu.VMEM((cells, 128), f32), pltpu.VMEM((comps, 4, 128), f32), pltpu.SemaphoreType.DMA((1,))],
    )

    def finish():
        (whole,) = call(
            functools.partial(second_bottom, comps, 4),
            "hvvv",
            "h",
            [(comps, 2, 4, 128)],
            out,
            bottom,
            below,
            edge,
            scratch=[pltpu.VMEM((comps, 4, 128), f32), pltpu.SemaphoreType.DMA((4,))],
            aliases={0: 0},
            room=63,
        )
        return whole.reshape(shape)

    return finish, bad[0, 0]


def extended(x, sides, width, wrap):
    for axis, dim in sides:
        size, length = (lax.axis_size(axis), x.shape[dim])
        up = [(i, (i + 1) % size) for i in range(size if wrap else size - 1)]
        down = [(j, i) for i, j in up]
        last = lax.slice_in_dim(x, length - width, length, axis=dim)
        first = lax.slice_in_dim(x, 0, width, axis=dim)
        before = lax.ppermute(last, axis, up)
        after = lax.ppermute(first, axis, down)
        x = jnp.concatenate([before, x, after], axis=dim)
    return x


def source_term(state, growth_rate, transfer_rate, nucleation):
    extra = (1,) * (state.ndim - 2)
    growth = growth_rate.reshape((1, -1) + extra)
    transfer = transfer_rate.reshape((1, -1) + extra)
    third = state[3]
    sigma = supersat_scale / (1.0 + crowding * jnp.sum(third * third, axis=0))
    lower = jnp.concatenate([jnp.zeros_like(state[0:1]), state[:3]], axis=0)
    factors = jnp.array([0.0, 1.0, 2.0, 3.0], dtype=state.dtype).reshape((4, 1) + extra)
    outflow = transfer * state
    inflow = jnp.concatenate([jnp.zeros_like(outflow[:, 0:1]), outflow[:, :-1]], axis=1)
    first = (jnp.arange(state.shape[1]) == 0).astype(state.dtype).reshape((1, -1) + extra)
    nucleus = jnp.array(nucleus_moments, dtype=state.dtype).reshape((4, 1) + extra)
    birth = nucleus * first * (nucleation * sigma * sigma)[None, None]
    return sigma[None, None] * (factors * growth * lower + inflow - outflow) + birth


def source_adjoint(state, adjoint, growth_rate, transfer_rate, nucleation):
    _, pull = jax.vjp(
        lambda field: source_term(field, growth_rate, transfer_rate, nucleation), state
    )
    return pull(adjoint)[0]


def cut_region(field, direction, offset):
    lead = [slice(None)] * (field.ndim - 3)
    spatial = []
    for which in range(3):
        moved = offset if which == direction else 0
        length = field.shape[field.ndim - 3 + which]
        spatial.append(slice(1 + moved, length - 1 + moved))
    return field[tuple(lead + spatial)]


def transport_adjoint(adjoint_pad, coeff_pad):
    total = None
    for direction in range(3):
        centre = cut_region(adjoint_pad, direction, 0)
        higher = cut_region(adjoint_pad, direction, 1)
        lowerv = cut_region(adjoint_pad, direction, -1)
        p_high = cut_region(coeff_pad[direction], direction, 1)
        q_here = cut_region(coeff_pad[3 + direction], direction, 0)
        term = p_high * (higher - centre) + q_here * (lowerv - centre)
        total = term if total is None else total + term
    return total


def face_coefficients(speeds, flags):
    upwind = flags.astype(speeds.dtype)
    return jnp.concatenate([speeds * upwind, speeds * (1.0 - upwind)], axis=0)


def nucleation_field(zones, nucleation_rate):
    labels = jnp.arange(nucleation_rate.shape[0], dtype=jnp.int32).reshape((-1, 1, 1, 1))
    match = (zones[None] == labels).astype(nucleation_rate.dtype)
    return jnp.sum(match * nucleation_rate.reshape((-1, 1, 1, 1)), axis=0)


def whole_step(
    adjoint_final,
    state_start,
    state_middle,
    speeds,
    flags,
    zones,
    growth_rate,
    transfer_rate,
    nucleation_rate,
):
    coeffs = face_coefficients(speeds, flags)
    nucleation = nucleation_field(zones, nucleation_rate)
    start = state_start.astype(jnp.float32)
    middle = state_middle.astype(jnp.float32)
    dims = adjoint_final.shape
    comps = dims[0] * dims[1]
    packed = jnp.concatenate([adjoint_final.reshape((comps,) + dims[2:]), coeffs], axis=0)
    packed = extended(packed, (("azim", 1),), 1, True)
    packed = extended(packed, (("rad", 3), ("axial", 2)), 1, False)
    later_pad = packed[:comps].reshape(dims[:2] + packed.shape[1:])
    coeff_pad = packed[comps:]
    adjoint_middle = 0.5 * adjoint_final + 0.5 * (
        transport_adjoint(later_pad, coeff_pad)
        + source_adjoint(middle, adjoint_final, growth_rate, transfer_rate, nucleation)
    )
    flat = adjoint_middle.reshape((comps,) + dims[2:])
    flat = extended(flat, (("azim", 1),), 1, True)
    flat = extended(flat, (("rad", 3), ("axial", 2)), 1, False)
    middle_pad = flat.reshape(dims[:2] + flat.shape[1:])
    return (
        0.5 * adjoint_final
        + adjoint_middle
        + transport_adjoint(middle_pad, coeff_pad)
        + source_adjoint(start, adjoint_middle, growth_rate, transfer_rate, nucleation)
    )


def shards(*arguments):
    finish, bad = packed_step(*arguments)
    return lax.cond(bad > 0.0, lambda: whole_step(*arguments), finish)


def solution(mesh):
    field = P(None, None, "azim", "axial", "rad")
    faces_spec = P(None, "azim", "axial", "rad")
    return jax.shard_map(
        shards,
        mesh=mesh,
        in_specs=(field, field, field, faces_spec, faces_spec, P("azim", "axial", "rad"), P(), P(), P()),
        out_specs=field,
        check_vma=False,
    )
```

```python
import functools

import jax
import jax.numpy as jnp
from jax import lax
from jax.experimental import pallas as pl
from jax.experimental.pallas import tpu as pltpu
from jax.sharding import PartitionSpec as P

supersat_scale = 1.5
crowding = 0.02
nucleus_moments = (1.0, 0.5, 0.25, 0.125)
f32 = jnp.float32
bf16 = jnp.bfloat16
exact = lax.Precision.HIGHEST

slots = 320
extra = slots - 256


def rows_of():
    return lax.broadcasted_iota(jnp.int32, (8, 128), 0)


def lanes_of():
    return lax.broadcasted_iota(jnp.int32, (8, 128), 1)


def faces(speeds_ref, flags_ref):
    p, q = [], []
    for d in range(3):
        speed, upwind = speeds_ref[d], flags_ref[d].astype(f32)
        p.append(speed * upwind)
        q.append(speed * (1.0 - upwind))
    return p, q


class Local:
    def __init__(self, p, q):
        row, lane = rows_of(), lanes_of()
        z, top = row % 4, row >= 4
        self.azim = jnp.where(top, q[0], pltpu.roll(p[0], 4, 0))
        self.ax_up = jnp.where(z == 3, 0.0, pltpu.roll(p[1], 7, 0))
        self.ax_dn = jnp.where(z == 0, 0.0, q[1])
        self.rad_up = jnp.where(lane == 127, 0.0, pltpu.roll(p[2], 127, 1))
        self.rad_dn = jnp.where(lane == 0, 0.0, q[2])
        self.centre = self.azim + self.ax_up + q[1] + self.rad_up + q[2] + jnp.where(top, 0.0, q[0])

    def __call__(self, x):
        return (
            self.azim * pltpu.roll(x, 4, 0)
            + self.ax_up * pltpu.roll(x, 7, 0)
            + self.ax_dn * pltpu.roll(x, 1, 0)
            + self.rad_up * pltpu.roll(x, 127, 1)
            + self.rad_dn * pltpu.roll(x, 1, 1)
            - self.centre * x
        )


def pair_rows(x, first, second):
    return jnp.where(
        rows_of() % 2 == 0,
        jnp.broadcast_to(x[first : first + 1], (8, 128)),
        jnp.broadcast_to(x[second : second + 1], (8, 128)),
    )


def make_tables(p, where_zero, low_ref, high_ref):
    row, lane = rows_of(), lanes_of()
    taken = (p == 0.0) if where_zero else (p != 0.0)
    one = jnp.where(taken & (row < 4), 1.0, 0.0)
    before = lax.broadcasted_iota(jnp.int32, (128, 128), 0) < lax.broadcasted_iota(jnp.int32, (128, 128), 1)
    inside = jnp.dot(one.astype(bf16), jnp.where(before, 1.0, 0.0).astype(bf16), preferred_element_type=f32)
    total = jnp.sum(one, axis=1, keepdims=True)
    base = jnp.zeros((8, 1), f32)
    for step in (1, 2, 3):
        base = base + jnp.where(
            lax.broadcasted_iota(jnp.int32, (8, 1), 0) >= step, jnp.roll(total, step, axis=0), 0.0
        )
    slot = jnp.where(one > 0.0, inside + base, -1.0).astype(jnp.int32)
    here = lax.broadcasted_iota(jnp.int32, (128, 128), 0)
    first = jnp.where(here < extra, here + 256, -2)
    second = jnp.where(here >= extra, here + (256 - extra), -2)
    for z in range(4):
        cells = slice(128 * z, 128 * z + 128)
        want = jnp.broadcast_to(slot[z : z + 1], (128, 128))
        for ref, start, names in ((low_ref, 0, here), (low_ref, 128, here + 128), (high_ref, 0, first), (high_ref, 128, second)):
            ref[start : start + 128, cells] = jnp.where(names == want, 1.0, 0.0).astype(bf16)


def crowded(p):
    taken = jnp.where((rows_of() < 4) & (p != 0.0), 1.0, 0.0)
    count = jnp.sum(jnp.sum(taken, axis=1, keepdims=True), axis=0, keepdims=True)
    count = jnp.broadcast_to(count, (8, 128))
    return jnp.where(jnp.maximum(count, 512.0 - count) > slots, 1.0, 0.0)


def pieces(x):
    high = x.astype(bf16)
    rest = x - high.astype(f32)
    middle = rest.astype(bf16)
    return high, middle, (rest - middle.astype(f32)).astype(bf16)


def stacked(x, half):
    return jnp.concatenate([part[half * i : half * i + half] for i in range(2) for part in pieces(x)], axis=0)


def summed(x, half):
    parts = [x[half * i : half * i + half] for i in range(6)]
    return [parts[3 * i] + (parts[3 * i + 1] + parts[3 * i + 2]) for i in range(2)]


def encode(comps, x_ref, first_row, low_ref, high_ref, message_ref):
    half = comps // 2
    x = jnp.concatenate(
        [stacked(x_ref[pl.ds(first_row + z, comps, stride=8)], half) for z in range(4)], axis=1
    )
    over = (((1,), (1,)), ((), ()))
    low = lax.dot_general(x, low_ref[...], over, preferred_element_type=f32)
    high = [
        lax.dot_general(
            x[3 * half * i : 3 * half * (i + 1)], high_ref[128 * i : 128 * i + 128], over, preferred_element_type=f32
        )
        for i in range(2)
    ]
    tail = jnp.zeros((half, 128), f32)
    for i, part in enumerate(summed(low, half)):
        message_ref[half * i : half * i + half] = part[:, :128]
        message_ref[comps + half * i : comps + half * i + half] = part[:, 128:]
    for part in high:
        tail = tail + (part[:half] + (part[half : 2 * half] + part[2 * half :]))
    message_ref[2 * comps : 2 * comps + half] = tail


def decode(comps, message_ref, low_ref, high_ref):
    half = comps // 2
    x = jnp.concatenate([stacked(message_ref[comps * i : comps * i + comps], half) for i in range(2)], axis=1)
    low = jnp.dot(x, low_ref[...], preferred_element_type=f32)
    tail = jnp.concatenate(pieces(message_ref[2 * comps : 2 * comps + half]), axis=0)
    found = []
    for i, part in enumerate(summed(low, half)):
        high = jnp.dot(tail, high_ref[128 * i : 128 * i + 128], preferred_element_type=f32)
        found.append(part + (high[:half] + (high[half : 2 * half] + high[2 * half :])))
    return jnp.concatenate(found, axis=0)


def add_azimuthal(comps, halo, coefficient, first_row, out_ref):
    for z in range(4):
        spots = pl.ds(first_row + z, comps, stride=8)
        out_ref[spots] = out_ref[spots] + coefficient[first_row + z : first_row + z + 1] * halo[:, 128 * z : 128 * z + 128]


def pack_sides(comps, x_ref, where_ref, ax_ref, radup_ref, raddn_ref):
    @pl.when(where_ref[0] == 0)
    def _():
        ax_ref[0 : 2 * comps] = x_ref[pl.ds(3, 2 * comps, stride=4)]

    @pl.when(where_ref[0] != 0)
    def _():
        ax_ref[0 : 2 * comps] = x_ref[pl.ds(0, 2 * comps, stride=4)]

    ends = columns(x_ref[...])
    radup_ref[:, 0 : 8 * comps] = ends[0:1]
    raddn_ref[:, 0 : 8 * comps] = ends[1:2]


def columns(x):
    row, lane = rows_of(), lanes_of()
    take = jnp.where(((row == 0) & (lane == 127)) | ((row == 1) & (lane == 0)), 1.0, 0.0)
    return lax.dot_general(take, x, (((1,), (1,)), ((), ())), precision=exact, preferred_element_type=f32)


def put_columns(lower, upper):
    n = lower.shape[1]
    row, lane = rows_of(), lanes_of()
    which = lax.broadcasted_iota(jnp.int32, (8, n), 0)
    both = jnp.where(which == 0, lower, jnp.where(which == 1, upper, 0.0))
    place = jnp.where(((row == 0) & (lane == 0)) | ((row == 1) & (lane == 127)), 1.0, 0.0)
    return lax.dot_general(both, place, (((0,), (0,)), ((), ())), precision=exact, preferred_element_type=f32)


def first_rest(comps, where_ref, a_ref, speeds_ref, flags_ref, up_ref, ax_ref, radup_ref, raddn_ref):
    p, _ = faces(speeds_ref, flags_ref)
    for c in range(comps):
        up_ref[4 * c : 4 * c + 4] = a_ref[8 * c + 4 : 8 * c + 8]
    up_ref[4 * comps :] = p[0]
    pack_sides(comps, a_ref, where_ref, ax_ref, radup_ref, raddn_ref)
    ax_ref[2 * comps : 2 * comps + 8] = pair_rows(p[1], 0, 4)
    radup_ref[:, 8 * comps :] = jnp.zeros((1, 128), f32)
    raddn_ref[:, 8 * comps :] = jnp.zeros((1, 128), f32)
    raddn_ref[:, 8 * comps : 8 * comps + 8] = columns(p[2])[1:2]


def source(sections, x_ref, u_ref, growth_ref, transfer_ref, zones_ref, rate_ref, finish):
    def inner(k, s, x):
        term = transfer_ref[s] * ((x[k][1] - x[k][0]) if s + 1 < sections else -x[k][0])
        if k < 3:
            term = term + ((k + 1.0) * growth_ref[s]) * x[k + 1][0]
        return term

    def load(s):
        got = []
        for k in range(4):
            c = k * sections + s
            here = x_ref[8 * c : 8 * c + 8]
            got.append((here, x_ref[8 * c + 8 : 8 * c + 16] if s + 1 < sections else None))
        return got

    squares = jnp.zeros((8, 128), f32)
    product = jnp.zeros((8, 128), f32)
    for s in range(sections):
        x = load(s)
        for k in range(4):
            u = u_ref[k * sections + s].astype(f32)
            product = product + u * inner(k, s, x)
        squares = squares + u * u
    sigma = supersat_scale / (1.0 + crowding * squares)
    birth = jnp.zeros((8, 128), f32)
    for k in range(4):
        c = k * sections
        birth = birth + nucleus_moments[k] * x_ref[8 * c : 8 * c + 8]
    rate = jnp.zeros((8, 128), f32)
    for label in range(rate_ref.shape[0]):
        rate = jnp.where(zones_ref[...] == label, rate_ref[label], rate)
    slope = (-2.0 * crowding / supersat_scale) * sigma * sigma * (product + 2.0 * rate * sigma * birth)
    for s in range(sections):
        x = load(s)
        for k in range(4):
            c = k * sections + s
            term = sigma * inner(k, s, x)
            if k == 3:
                term = term + u_ref[c].astype(f32) * slope
            finish(c, x[k][0], term)


def first_local(
    sections,
    a_ref,
    u_ref,
    speeds_ref,
    flags_ref,
    zones_ref,
    growth_ref,
    transfer_ref,
    rate_ref,
    out_ref,
    dn_low_ref,
    dn_high_ref,
    up_low_ref,
    up_high_ref,
):
    p, q = faces(speeds_ref, flags_ref)
    local = Local(p, q)
    make_tables(p[0], False, dn_low_ref, dn_high_ref)
    make_tables(p[0], True, up_low_ref, up_high_ref)

    def finish(c, x, term):
        out_ref[8 * c : 8 * c + 8] = 0.5 * (x + local(x) + term)

    source(sections, a_ref, u_ref, growth_ref, transfer_ref, zones_ref, rate_ref, finish)


def second_local(
    sections, m_ref, a_ref, u_ref, edge_ref, speeds_ref, flags_ref, zones_ref, growth_ref, transfer_ref, rate_ref, out_ref
):
    local = Local(*faces(speeds_ref, flags_ref))
    local.centre = local.centre + (edge_ref[3] - 1.0)

    def finish(c, x, term):
        out_ref[8 * c : 8 * c + 8] = 0.5 * a_ref[8 * c : 8 * c + 8] + (local(x) + term)

    source(sections, m_ref, u_ref, growth_ref, transfer_ref, zones_ref, rate_ref, finish)


def from_below(c, below_ref):
    pair = below_ref[8 * (c // 2) : 8 * (c // 2) + 8]
    return pair if c % 2 == 0 else pltpu.roll(pair, 4, 0)


def from_above(c, above_ref):
    pair = above_ref[8 * (c // 2) : 8 * (c // 2) + 8]
    return pair if c % 2 == 1 else pltpu.roll(pair, 4, 0)


def add_axial(comps, scale, where_ref, axial, ax_ref, out_ref):
    several = jnp.concatenate([scale * axial] * (2 * comps // 8), axis=0)
    for start, index in ((3, 0), (0, 1)):

        @pl.when(where_ref[0] == index)
        def _():
            spots = pl.ds(start, 2 * comps, stride=4)
            out_ref[spots] = out_ref[spots] + several * ax_ref[0 : 2 * comps]


def first_top(
    comps,
    where_ref,
    part_ref,
    a_ref,
    above_ref,
    ax_ref,
    radlo_ref,
    radhi_ref,
    far_ref,
    speeds_ref,
    flags_ref,
    m_ref,
    edge_ref,
    up_ref,
    bad_ref,
    dn_low_ref,
    dn_high_ref,
    up_low_ref,
    up_high_ref,
):
    p, q = faces(speeds_ref, flags_ref)
    row, lane = rows_of(), lanes_of()
    upper = above_ref[4 * comps :]
    make_tables(upper, True, up_low_ref, up_high_ref)
    make_tables(upper, False, dn_low_ref, dn_high_ref)
    bad_ref[...] = crowded(p[0]) + crowded(upper) + crowded(far_ref[...])
    hrad = put_columns(radlo_ref[...], radhi_ref[...])
    lower_half = where_ref[0] == 0
    p_azim = jnp.where(row >= 4, pltpu.roll(upper, 4, 0), 0.0)
    pairs = jnp.where(lower_half, ax_ref[2 * comps : 2 * comps + 8], 0.0)
    p_axial = jnp.where(row == 3, pairs[0:1], jnp.where(row == 7, pairs[1:2], 0.0))
    p_rad = jnp.where(lane == 127, hrad[8 * comps : 8 * comps + 8], 0.0)
    axial = jnp.where(lower_half, pairs, pair_rows(q[1], 0, 4))
    rad = jnp.where(lane == 0, q[2], p_rad)
    centre = p_azim + p_axial + p_rad
    edge_ref[0] = jnp.where(row >= 4, p_azim, q[0])
    edge_ref[1] = axial
    edge_ref[2] = rad
    edge_ref[3] = centre
    for c in range(comps):
        spots = slice(8 * c, 8 * c + 8)
        m_ref[spots] = part_ref[spots] + 0.5 * (
            p_azim * from_above(c, above_ref) + rad * hrad[spots] - centre * a_ref[spots]
        )
    add_axial(comps, 0.5, where_ref, axial, ax_ref, m_ref)
    encode(comps, m_ref, 4, up_low_ref, up_high_ref, up_ref)


def first_bottom(
    comps,
    where_ref,
    part_ref,
    below_ref,
    edge_ref,
    bad_ref,
    low_ref,
    high_ref,
    m_ref,
    dn_ref,
    ax_ref,
    radup_ref,
    raddn_ref,
    worse_ref,
):
    azim = jnp.where(rows_of() >= 4, 0.0, 0.5 * edge_ref[0])
    for c in range(comps):
        m_ref[8 * c : 8 * c + 8] = part_ref[8 * c : 8 * c + 8] + azim * from_below(c, below_ref)
    encode(comps, m_ref, 0, low_ref, high_ref, dn_ref)
    worse_ref[...] = bad_ref[...] + crowded(below_ref[4 * comps :])
    pack_sides(comps, m_ref, where_ref, ax_ref, radup_ref, raddn_ref)


def second_bottom(
    comps, where_ref, part_ref, below_ref, ax_ref, radlo_ref, radhi_ref, edge_ref, low_ref, high_ref, base_ref, full_ref
):
    hrad = put_columns(radlo_ref[...], radhi_ref[...])
    rad = edge_ref[2]
    for c in range(comps):
        spots = slice(8 * c, 8 * c + 8)
        base_ref[spots] = part_ref[spots] + rad * hrad[spots]
    add_axial(comps, 1.0, where_ref, edge_ref[1], ax_ref, base_ref)
    full_ref[...] = base_ref[...]
    add_azimuthal(comps, decode(comps, below_ref, low_ref, high_ref), edge_ref[0], 0, full_ref)


def second_top(comps, full_ref, above_ref, edge_ref, low_ref, high_ref, out_ref):
    out_ref[...] = full_ref[...]
    add_azimuthal(comps, decode(comps, above_ref, low_ref, high_ref), edge_ref[0], 4, out_ref)


SPACES = {
    "v": pl.BlockSpec(memory_space=pltpu.VMEM),
    "s": pl.BlockSpec(memory_space=pltpu.SMEM),
    "h": pl.BlockSpec(memory_space=pltpu.HBM),
}


def call(body, ins, outs, shapes, cost, *operands):
    return pl.pallas_call(
        body,
        in_specs=[SPACES[s] for s in ins],
        out_specs=[SPACES[s] for s in outs],
        out_shape=[s if isinstance(s, jax.ShapeDtypeStruct) else jax.ShapeDtypeStruct(s, f32) for s in shapes],
        cost_estimate=pl.CostEstimate(flops=cost, bytes_accessed=cost // 10, transcendentals=0),
        compiler_params=pltpu.CompilerParams(vmem_limit_bytes=32 * 1024 * 1024),
    )(*operands)


def shift(x, axis, step, wrap):
    size = lax.axis_size(axis)
    pairs = [(i, (i + step) % size) for i in range(size) if wrap or 0 <= i + step < size]
    return lax.ppermute(x, axis, pairs)


def sides(ax, radup, raddn):
    ax = lax.ppermute(ax, "axial", [(0, 1), (1, 0)])
    return ax, shift(radup, "rad", 1, False), shift(raddn, "rad", -1, False)


def shards(adjoint_final, state_start, state_middle, speeds, flags, zones, growth_rate, transfer_rate, nucleation_rate):
    shape = adjoint_final.shape
    moments, sections = shape[:2]
    comps = moments * sections
    assert moments == 4 and shape[2:] == (2, 4, 128) and comps % 4 == 0
    assert lax.axis_size("axial") == 2
    cells = 8 * comps
    half, rows = cells // 2, cells // 4
    a = adjoint_final.reshape(cells, 128)
    speeds2 = speeds.reshape(3, 8, 128)
    flags2 = flags.reshape(3, 8, 128)
    where = lax.axis_index("axial").reshape(1)
    rates = (zones.reshape(8, 128), growth_rate, transfer_rate, nucleation_rate)
    message = 5 * comps // 2
    tables = [jax.ShapeDtypeStruct((256, 512), bf16)] * 2

    keep = ((0, 2, 0), (0, -1, 0), (0, 0, 0), (0, 0, 0))
    after = ((comps, -1, 0), (0, -1, 0), (0, 0, 0), (0, 0, 0))
    dn = lax.pad(adjoint_final.reshape(comps, 2, 4, 128), 0.0, keep)
    dn = dn + lax.pad(speeds, 0.0, after) * lax.pad(flags, 0, after).astype(f32)
    above = shift(dn.reshape(half + 8, 128), "azim", -1, True)
    up, *edges = call(
        functools.partial(first_rest, comps),
        "svvv",
        "vvvv",
        [(half + 8, 128), (rows + 8, 128), (1, cells + 128), (1, cells + 128)],
        2_000_000,
        where,
        a,
        speeds2,
        flags2,
    )
    below = shift(up, "azim", 1, True)
    far = shift(speeds2[0] * flags2[0].astype(f32), "azim", 2, True)
    edges = sides(*edges)
    part, *lower_tables = call(
        functools.partial(first_local, sections),
        "vvvvvsss",
        "vvvvv",
        [(cells, 128)] + 2 * tables,
        8_000_000,
        a,
        state_middle.reshape(comps, 8, 128),
        speeds2,
        flags2,
        *rates,
    )
    part, edge, up, bad, *upper_tables = call(
        functools.partial(first_top, comps),
        "s" + "v" * 9,
        "v" * 8,
        [(cells, 128), (4, 8, 128), (message, 128), (8, 128)] + 2 * tables,
        4_000_000,
        where,
        part,
        a,
        above,
        *edges,
        far,
        speeds2,
        flags2,
    )
    next_below = shift(up, "azim", 1, True)
    m, dn, *edges, bad = call(
        functools.partial(first_bottom, comps),
        "s" + "v" * 6,
        "v" * 6,
        [(cells, 128), (message, 128), (rows, 128), (1, cells), (1, cells), (8, 128)],
        4_000_000,
        where,
        part,
        below,
        edge,
        bad,
        *lower_tables[:2],
    )
    next_above = shift(dn, "azim", -1, True)
    edges = sides(*edges)
    (part,) = call(
        functools.partial(second_local, sections),
        "vvvvvvvsss",
        "v",
        [(cells, 128)],
        8_000_000,
        m,
        a,
        state_start.reshape(comps, 8, 128),
        edge,
        speeds2,
        flags2,
        *rates,
    )
    base, full = call(
        functools.partial(second_bottom, comps),
        "s" + "v" * 8,
        "vv",
        [(cells, 128), (cells, 128)],
        4_000_000,
        where,
        part,
        next_below,
        *edges,
        edge,
        *lower_tables[2:],
    )

    def quick():
        (out,) = call(
            functools.partial(second_top, comps),
            "vvvvv",
            "v",
            [(cells, 128)],
            1_000_000,
            full,
            next_above,
            edge,
            *upper_tables[:2],
        )
        return out

    def whole():
        rows_ = m.reshape(comps, 2, 4, 128)
        halo = jnp.stack([shift(rows_[:, 1], "azim", 1, True), shift(rows_[:, 0], "azim", -1, True)], axis=1)
        return base + (edge[0].reshape(1, 2, 4, 128) * halo).reshape(cells, 128)

    worst = bad[0, 0]
    if lax.axis_size("azim") != 4:
        worst = lax.pmax(worst, "azim")
    return lax.cond(worst > 0.0, whole, quick).reshape(shape)


def solution(mesh):
    field = P(None, None, "azim", "axial", "rad")
    faces_spec = P(None, "azim", "axial", "rad")
    return jax.shard_map(
        shards,
        mesh=mesh,
        in_specs=(field, field, field, faces_spec, faces_spec, P("azim", "axial", "rad"), P(), P(), P()),
        out_specs=field,
        check_vma=False,
    )
```

```python
import functools

import jax
import jax.numpy as jnp
from jax import lax
from jax.experimental import pallas as pl
from jax.experimental.pallas import tpu as pltpu
from jax.sharding import PartitionSpec as P

supersat_scale = 1.5
crowding = 0.02
nucleus_moments = (1.0, 0.5, 0.25, 0.125)
f32 = jnp.float32
bf16 = jnp.bfloat16
exact = lax.Precision.HIGHEST

slots = 320
extra = slots - 256


def rows_of():
    return lax.broadcasted_iota(jnp.int32, (8, 128), 0)


def lanes_of():
    return lax.broadcasted_iota(jnp.int32, (8, 128), 1)


def faces(speeds_ref, flags_ref):
    p, q = [], []
    for d in range(3):
        speed, upwind = speeds_ref[d], flags_ref[d].astype(f32)
        p.append(speed * upwind)
        q.append(speed * (1.0 - upwind))
    return p, q


class Local:
    def __init__(self, p, q):
        row, lane = rows_of(), lanes_of()
        z, top = row % 4, row >= 4
        self.azim = jnp.where(top, q[0], pltpu.roll(p[0], 4, 0))
        self.ax_up = jnp.where(z == 3, 0.0, pltpu.roll(p[1], 7, 0))
        self.ax_dn = jnp.where(z == 0, 0.0, q[1])
        self.rad_up = jnp.where(lane == 127, 0.0, pltpu.roll(p[2], 127, 1))
        self.rad_dn = jnp.where(lane == 0, 0.0, q[2])
        self.centre = self.azim + self.ax_up + q[1] + self.rad_up + q[2] + jnp.where(top, 0.0, q[0])

    def __call__(self, x):
        return (
            self.azim * pltpu.roll(x, 4, 0)
            + self.ax_up * pltpu.roll(x, 7, 0)
            + self.ax_dn * pltpu.roll(x, 1, 0)
            + self.rad_up * pltpu.roll(x, 127, 1)
            + self.rad_dn * pltpu.roll(x, 1, 1)
            - self.centre * x
        )


def pair_rows(x, first, second):
    return jnp.where(
        rows_of() % 2 == 0,
        jnp.broadcast_to(x[first : first + 1], (8, 128)),
        jnp.broadcast_to(x[second : second + 1], (8, 128)),
    )


def make_tables(p, where_zero, low_ref, high_ref):
    row, lane = rows_of(), lanes_of()
    taken = (p == 0.0) if where_zero else (p != 0.0)
    one = jnp.where(taken & (row < 4), 1.0, 0.0)
    before = lax.broadcasted_iota(jnp.int32, (128, 128), 0) < lax.broadcasted_iota(jnp.int32, (128, 128), 1)
    inside = jnp.dot(one.astype(bf16), jnp.where(before, 1.0, 0.0).astype(bf16), preferred_element_type=f32)
    total = jnp.sum(one, axis=1, keepdims=True)
    base = jnp.zeros((8, 1), f32)
    for step in (1, 2, 3):
        base = base + jnp.where(
            lax.broadcasted_iota(jnp.int32, (8, 1), 0) >= step, jnp.roll(total, step, axis=0), 0.0
        )
    slot = jnp.where(one > 0.0, inside + base, -1.0).astype(jnp.int32)
    here = lax.broadcasted_iota(jnp.int32, (128, 128), 0)
    first = jnp.where(here < extra, here + 256, -2)
    second = jnp.where(here >= extra, here + (256 - extra), -2)
    for z in range(4):
        cells = slice(128 * z, 128 * z + 128)
        want = jnp.broadcast_to(slot[z : z + 1], (128, 128))
        for ref, start, names in ((low_ref, 0, here), (low_ref, 128, here + 128), (high_ref, 0, first), (high_ref, 128, second)):
            ref[start : start + 128, cells] = jnp.where(names == want, 1.0, 0.0).astype(bf16)


def crowded(p):
    taken = jnp.where((rows_of() < 4) & (p != 0.0), 1.0, 0.0)
    count = jnp.sum(jnp.sum(taken, axis=1, keepdims=True), axis=0, keepdims=True)
    count = jnp.broadcast_to(count, (8, 128))
    return jnp.where(jnp.maximum(count, 512.0 - count) > slots, 1.0, 0.0)


def pieces(x):
    high = x.astype(bf16)
    rest = x - high.astype(f32)
    middle = rest.astype(bf16)
    return high, middle, (rest - middle.astype(f32)).astype(bf16)


def stacked(x, half):
    return jnp.concatenate([part[half * i : half * i + half] for i in range(2) for part in pieces(x)], axis=0)


def summed(x, half):
    parts = [x[half * i : half * i + half] for i in range(6)]
    return [parts[3 * i] + (parts[3 * i + 1] + parts[3 * i + 2]) for i in range(2)]


def encode(comps, x_ref, first_row, low_ref, high_ref, message_ref):
    half = comps // 2
    x = jnp.concatenate(
        [stacked(x_ref[pl.ds(first_row + z, comps, stride=8)], half) for z in range(4)], axis=1
    )
    over = (((1,), (1,)), ((), ()))
    low = lax.dot_general(x, low_ref[...], over, preferred_element_type=f32)
    high = [
        lax.dot_general(
            x[3 * half * i : 3 * half * (i + 1)], high_ref[128 * i : 128 * i + 128], over, preferred_element_type=f32
        )
        for i in range(2)
    ]
    tail = jnp.zeros((half, 128), f32)
    for i, part in enumerate(summed(low, half)):
        message_ref[half * i : half * i + half] = part[:, :128]
        message_ref[comps + half * i : comps + half * i + half] = part[:, 128:]
    for part in high:
        tail = tail + (part[:half] + (part[half : 2 * half] + part[2 * half :]))
    message_ref[2 * comps : 2 * comps + half] = tail


def decode(comps, message_ref, low_ref, high_ref):
    half = comps // 2
    x = jnp.concatenate([stacked(message_ref[comps * i : comps * i + comps], half) for i in range(2)], axis=1)
    low = jnp.dot(x, low_ref[...], preferred_element_type=f32)
    tail = jnp.concatenate(pieces(message_ref[2 * comps : 2 * comps + half]), axis=0)
    found = []
    for i, part in enumerate(summed(low, half)):
        high = jnp.dot(tail, high_ref[128 * i : 128 * i + 128], preferred_element_type=f32)
        found.append(part + (high[:half] + (high[half : 2 * half] + high[2 * half :])))
    return jnp.concatenate(found, axis=0)


def add_azimuthal(comps, halo, coefficient, first_row, out_ref):
    for z in range(4):
        spots = pl.ds(first_row + z, comps, stride=8)
        out_ref[spots] = out_ref[spots] + coefficient[first_row + z : first_row + z + 1] * halo[:, 128 * z : 128 * z + 128]


def pack_sides(comps, x_ref, where_ref, ax_ref, radup_ref, raddn_ref):
    @pl.when(where_ref[0] == 0)
    def _():
        ax_ref[0 : 2 * comps] = x_ref[pl.ds(3, 2 * comps, stride=4)]

    @pl.when(where_ref[0] != 0)
    def _():
        ax_ref[0 : 2 * comps] = x_ref[pl.ds(0, 2 * comps, stride=4)]

    ends = columns(x_ref[...])
    radup_ref[:, 0 : 8 * comps] = ends[0:1]
    raddn_ref[:, 0 : 8 * comps] = ends[1:2]


def columns(x):
    row, lane = rows_of(), lanes_of()
    take = jnp.where(((row == 0) & (lane == 127)) | ((row == 1) & (lane == 0)), 1.0, 0.0)
    return lax.dot_general(take, x, (((1,), (1,)), ((), ())), precision=exact, preferred_element_type=f32)


def put_columns(lower, upper):
    n = lower.shape[1]
    row, lane = rows_of(), lanes_of()
    which = lax.broadcasted_iota(jnp.int32, (8, n), 0)
    both = jnp.where(which == 0, lower, jnp.where(which == 1, upper, 0.0))
    place = jnp.where(((row == 0) & (lane == 0)) | ((row == 1) & (lane == 127)), 1.0, 0.0)
    return lax.dot_general(both, place, (((0,), (0,)), ((), ())), precision=exact, preferred_element_type=f32)


def first_rest(comps, where_ref, a_ref, speeds_ref, flags_ref, up_ref, ax_ref, radup_ref, raddn_ref):
    p, _ = faces(speeds_ref, flags_ref)
    for c in range(comps):
        up_ref[4 * c : 4 * c + 4] = a_ref[8 * c + 4 : 8 * c + 8]
    up_ref[4 * comps :] = p[0]
    pack_sides(comps, a_ref, where_ref, ax_ref, radup_ref, raddn_ref)
    ax_ref[2 * comps : 2 * comps + 8] = pair_rows(p[1], 0, 4)
    radup_ref[:, 8 * comps :] = jnp.zeros((1, 128), f32)
    raddn_ref[:, 8 * comps :] = jnp.zeros((1, 128), f32)
    raddn_ref[:, 8 * comps : 8 * comps + 8] = columns(p[2])[1:2]


def source(sections, x_ref, u_ref, growth_ref, transfer_ref, zones_ref, rate_ref, finish):
    def inner(k, s, x):
        term = transfer_ref[s] * ((x[k][1] - x[k][0]) if s + 1 < sections else -x[k][0])
        if k < 3:
            term = term + ((k + 1.0) * growth_ref[s]) * x[k + 1][0]
        return term

    def load(s):
        got = []
        for k in range(4):
            c = k * sections + s
            here = x_ref[8 * c : 8 * c + 8]
            got.append((here, x_ref[8 * c + 8 : 8 * c + 16] if s + 1 < sections else None))
        return got

    squares = jnp.zeros((8, 128), f32)
    product = jnp.zeros((8, 128), f32)
    for s in range(sections):
        x = load(s)
        for k in range(4):
            u = u_ref[k * sections + s].astype(f32)
            product = product + u * inner(k, s, x)
        squares = squares + u * u
    sigma = supersat_scale / (1.0 + crowding * squares)
    birth = jnp.zeros((8, 128), f32)
    for k in range(4):
        c = k * sections
        birth = birth + nucleus_moments[k] * x_ref[8 * c : 8 * c + 8]
    rate = jnp.zeros((8, 128), f32)
    for label in range(rate_ref.shape[0]):
        rate = jnp.where(zones_ref[...] == label, rate_ref[label], rate)
    slope = (-2.0 * crowding / supersat_scale) * sigma * sigma * (product + 2.0 * rate * sigma * birth)
    for s in range(sections):
        x = load(s)
        for k in range(4):
            c = k * sections + s
            term = sigma * inner(k, s, x)
            if k == 3:
                term = term + u_ref[c].astype(f32) * slope
            finish(c, x[k][0], term)


def first_local(
    sections,
    a_ref,
    u_ref,
    speeds_ref,
    flags_ref,
    zones_ref,
    growth_ref,
    transfer_ref,
    rate_ref,
    out_ref,
    dn_low_ref,
    dn_high_ref,
    up_low_ref,
    up_high_ref,
):
    p, q = faces(speeds_ref, flags_ref)
    local = Local(p, q)
    make_tables(p[0], False, dn_low_ref, dn_high_ref)
    make_tables(p[0], True, up_low_ref, up_high_ref)

    def finish(c, x, term):
        out_ref[8 * c : 8 * c + 8] = 0.5 * (x + local(x) + term)

    source(sections, a_ref, u_ref, growth_ref, transfer_ref, zones_ref, rate_ref, finish)


def second_local(
    sections, m_ref, a_ref, u_ref, edge_ref, speeds_ref, flags_ref, zones_ref, growth_ref, transfer_ref, rate_ref, out_ref
):
    local = Local(*faces(speeds_ref, flags_ref))
    local.centre = local.centre + (edge_ref[3] - 1.0)

    def finish(c, x, term):
        out_ref[8 * c : 8 * c + 8] = 0.5 * a_ref[8 * c : 8 * c + 8] + (local(x) + term)

    source(sections, m_ref, u_ref, growth_ref, transfer_ref, zones_ref, rate_ref, finish)


def from_below(c, below_ref):
    pair = below_ref[8 * (c // 2) : 8 * (c // 2) + 8]
    return pair if c % 2 == 0 else pltpu.roll(pair, 4, 0)


def from_above(c, above_ref):
    pair = above_ref[8 * (c // 2) : 8 * (c // 2) + 8]
    return pair if c % 2 == 1 else pltpu.roll(pair, 4, 0)


def add_axial(comps, scale, where_ref, axial, ax_ref, out_ref):
    several = jnp.concatenate([scale * axial] * (2 * comps // 8), axis=0)
    for start, index in ((3, 0), (0, 1)):

        @pl.when(where_ref[0] == index)
        def _():
            spots = pl.ds(start, 2 * comps, stride=4)
            out_ref[spots] = out_ref[spots] + several * ax_ref[0 : 2 * comps]


def first_top(
    comps,
    where_ref,
    part_ref,
    a_ref,
    above_ref,
    ax_ref,
    radlo_ref,
    radhi_ref,
    speeds_ref,
    flags_ref,
    m_ref,
    edge_ref,
    up_ref,
    bad_ref,
    dn_low_ref,
    dn_high_ref,
    up_low_ref,
    up_high_ref,
):
    p, q = faces(speeds_ref, flags_ref)
    row, lane = rows_of(), lanes_of()
    upper = above_ref[4 * comps :]
    make_tables(upper, True, up_low_ref, up_high_ref)
    make_tables(upper, False, dn_low_ref, dn_high_ref)
    bad_ref[...] = crowded(p[0]) + crowded(upper)
    hrad = put_columns(radlo_ref[...], radhi_ref[...])
    lower_half = where_ref[0] == 0
    p_azim = jnp.where(row >= 4, pltpu.roll(upper, 4, 0), 0.0)
    pairs = jnp.where(lower_half, ax_ref[2 * comps : 2 * comps + 8], 0.0)
    p_axial = jnp.where(row == 3, pairs[0:1], jnp.where(row == 7, pairs[1:2], 0.0))
    p_rad = jnp.where(lane == 127, hrad[8 * comps : 8 * comps + 8], 0.0)
    axial = jnp.where(lower_half, pairs, pair_rows(q[1], 0, 4))
    rad = jnp.where(lane == 0, q[2], p_rad)
    centre = p_azim + p_axial + p_rad
    edge_ref[0] = jnp.where(row >= 4, p_azim, q[0])
    edge_ref[1] = axial
    edge_ref[2] = rad
    edge_ref[3] = centre
    for c in range(comps):
        spots = slice(8 * c, 8 * c + 8)
        m_ref[spots] = part_ref[spots] + 0.5 * (
            p_azim * from_above(c, above_ref) + rad * hrad[spots] - centre * a_ref[spots]
        )
    add_axial(comps, 0.5, where_ref, axial, ax_ref, m_ref)
    encode(comps, m_ref, 4, up_low_ref, up_high_ref, up_ref)


def first_bottom(
    comps,
    where_ref,
    part_ref,
    below_ref,
    edge_ref,
    bad_ref,
    low_ref,
    high_ref,
    m_ref,
    dn_ref,
    ax_ref,
    radup_ref,
    raddn_ref,
    worse_ref,
):
    azim = jnp.where(rows_of() >= 4, 0.0, 0.5 * edge_ref[0])
    for c in range(comps):
        m_ref[8 * c : 8 * c + 8] = part_ref[8 * c : 8 * c + 8] + azim * from_below(c, below_ref)
    encode(comps, m_ref, 0, low_ref, high_ref, dn_ref)
    worse_ref[...] = bad_ref[...] + crowded(below_ref[4 * comps :])
    dn_ref[5 * comps // 2 :] = worse_ref[...]
    pack_sides(comps, m_ref, where_ref, ax_ref, radup_ref, raddn_ref)


def second_bottom(
    comps, where_ref, part_ref, below_ref, ax_ref, radlo_ref, radhi_ref, edge_ref, low_ref, high_ref, base_ref, full_ref
):
    hrad = put_columns(radlo_ref[...], radhi_ref[...])
    rad = edge_ref[2]
    for c in range(comps):
        spots = slice(8 * c, 8 * c + 8)
        base_ref[spots] = part_ref[spots] + rad * hrad[spots]
    add_axial(comps, 1.0, where_ref, edge_ref[1], ax_ref, base_ref)
    full_ref[...] = base_ref[...]
    add_azimuthal(comps, decode(comps, below_ref, low_ref, high_ref), edge_ref[0], 0, full_ref)


def second_top(comps, full_ref, above_ref, edge_ref, bad_ref, low_ref, high_ref, out_ref, again_ref):
    again_ref[0] = (jnp.max(bad_ref[...] + above_ref[5 * comps // 2 :]) > 0.0).astype(jnp.int32)
    out_ref[...] = full_ref[...]
    add_azimuthal(comps, decode(comps, above_ref, low_ref, high_ref), edge_ref[0], 4, out_ref)


SPACES = {
    "v": pl.BlockSpec(memory_space=pltpu.VMEM),
    "s": pl.BlockSpec(memory_space=pltpu.SMEM),
    "h": pl.BlockSpec(memory_space=pltpu.HBM),
}


def call(body, ins, outs, shapes, cost, *operands):
    return pl.pallas_call(
        body,
        in_specs=[SPACES[s] for s in ins],
        out_specs=[SPACES[s] for s in outs],
        out_shape=[s if isinstance(s, jax.ShapeDtypeStruct) else jax.ShapeDtypeStruct(s, f32) for s in shapes],
        cost_estimate=pl.CostEstimate(flops=cost, bytes_accessed=cost // 10, transcendentals=0),
        compiler_params=pltpu.CompilerParams(vmem_limit_bytes=32 * 1024 * 1024),
    )(*operands)


def shift(x, axis, step, wrap):
    size = lax.axis_size(axis)
    pairs = [(i, (i + step) % size) for i in range(size) if wrap or 0 <= i + step < size]
    return lax.ppermute(x, axis, pairs)


def sides(ax, radup, raddn):
    ax = lax.ppermute(ax, "axial", [(0, 1), (1, 0)])
    return ax, shift(radup, "rad", 1, False), shift(raddn, "rad", -1, False)


def shards(adjoint_final, state_start, state_middle, speeds, flags, zones, growth_rate, transfer_rate, nucleation_rate):
    shape = adjoint_final.shape
    moments, sections = shape[:2]
    comps = moments * sections
    assert moments == 4 and shape[2:] == (2, 4, 128) and comps % 4 == 0
    assert lax.axis_size("axial") == 2
    cells = 8 * comps
    half, rows = cells // 2, cells // 4
    a = adjoint_final.reshape(cells, 128)
    speeds2 = speeds.reshape(3, 8, 128)
    flags2 = flags.reshape(3, 8, 128)
    where = lax.axis_index("axial").reshape(1)
    rates = (zones.reshape(8, 128), growth_rate, transfer_rate, nucleation_rate)
    message = 5 * comps // 2
    tables = [jax.ShapeDtypeStruct((256, 512), bf16)] * 2

    keep = ((0, 2, 0), (0, -1, 0), (0, 0, 0), (0, 0, 0))
    after = ((comps, -1, 0), (0, -1, 0), (0, 0, 0), (0, 0, 0))
    dn = lax.pad(adjoint_final.reshape(comps, 2, 4, 128), 0.0, keep)
    dn = dn + lax.pad(speeds, 0.0, after) * lax.pad(flags, 0, after).astype(f32)
    above = shift(dn.reshape(half + 8, 128), "azim", -1, True)
    up, *edges = call(
        functools.partial(first_rest, comps),
        "svvv",
        "vvvv",
        [(half + 8, 128), (rows + 8, 128), (1, cells + 128), (1, cells + 128)],
        2_000_000,
        where,
        a,
        speeds2,
        flags2,
    )
    below = shift(up, "azim", 1, True)
    edges = sides(*edges)
    part, *lower_tables = call(
        functools.partial(first_local, sections),
        "vvvvvsss",
        "vvvvv",
        [(cells, 128)] + 2 * tables,
        8_000_000,
        a,
        state_middle.reshape(comps, 8, 128),
        speeds2,
        flags2,
        *rates,
    )
    part, edge, up, bad, *upper_tables = call(
        functools.partial(first_top, comps),
        "s" + "v" * 8,
        "v" * 8,
        [(cells, 128), (4, 8, 128), (message, 128), (8, 128)] + 2 * tables,
        4_000_000,
        where,
        part,
        a,
        above,
        *edges,
        speeds2,
        flags2,
    )
    next_below = shift(up, "azim", 1, True)
    m, dn, *edges, bad = call(
        functools.partial(first_bottom, comps),
        "s" + "v" * 6,
        "v" * 6,
        [(cells, 128), (message + 8, 128), (rows, 128), (1, cells), (1, cells), (8, 128)],
        4_000_000,
        where,
        part,
        below,
        edge,
        bad,
        *lower_tables[:2],
    )
    next_above = shift(dn, "azim", -1, True)
    edges = sides(*edges)
    (part,) = call(
        functools.partial(second_local, sections),
        "vvvvvvvsss",
        "v",
        [(cells, 128)],
        8_000_000,
        m,
        a,
        state_start.reshape(comps, 8, 128),
        edge,
        speeds2,
        flags2,
        *rates,
    )
    base, full = call(
        functools.partial(second_bottom, comps),
        "s" + "v" * 8,
        "vv",
        [(cells, 128), (cells, 128)],
        4_000_000,
        where,
        part,
        next_below,
        *edges,
        edge,
        *lower_tables[2:],
    )

    out, again = call(
        functools.partial(second_top, comps),
        "vvvvvv",
        "vs",
        [(cells, 128), jax.ShapeDtypeStruct((1,), jnp.int32)],
        1_000_000,
        full,
        next_above,
        edge,
        bad,
        *upper_tables[:2],
    )

    def whole():
        rows_ = m.reshape(comps, 2, 4, 128)
        halo = jnp.stack([shift(rows_[:, 1], "azim", 1, True), shift(rows_[:, 0], "azim", -1, True)], axis=1)
        return base + (edge[0].reshape(1, 2, 4, 128) * halo).reshape(cells, 128)

    again = again[0]
    if lax.axis_size("azim") != 4:
        again = lax.pmax(again.astype(f32), "azim").astype(jnp.int32)
    return lax.cond(again > 0, whole, lambda: out).reshape(shape)


def solution(mesh):
    field = P(None, None, "azim", "axial", "rad")
    faces_spec = P(None, "azim", "axial", "rad")
    return jax.shard_map(
        shards,
        mesh=mesh,
        in_specs=(field, field, field, faces_spec, faces_spec, P("azim", "axial", "rad"), P(), P(), P()),
        out_specs=field,
        check_vma=False,
    )
```

```python
import functools

import jax
import jax.numpy as jnp
from jax import lax
from jax.experimental import pallas as pl
from jax.experimental.pallas import tpu as pltpu
from jax.sharding import PartitionSpec as P

supersat_scale = 1.5
crowding = 0.02
nucleus_moments = (1.0, 0.5, 0.25, 0.125)
f32 = jnp.float32
bf16 = jnp.bfloat16
exact = lax.Precision.HIGHEST

slots = 320
extra = slots - 256


def rows_of():
    return lax.broadcasted_iota(jnp.int32, (8, 128), 0)


def lanes_of():
    return lax.broadcasted_iota(jnp.int32, (8, 128), 1)


def faces(speeds_ref, flags_ref):
    p, q = [], []
    for d in range(3):
        speed, upwind = speeds_ref[d], flags_ref[d].astype(f32)
        p.append(speed * upwind)
        q.append(speed * (1.0 - upwind))
    return p, q


class Local:
    def __init__(self, p, q):
        row, lane = rows_of(), lanes_of()
        z, top = row % 4, row >= 4
        self.azim = jnp.where(top, q[0], pltpu.roll(p[0], 4, 0))
        self.ax_up = jnp.where(z == 3, 0.0, pltpu.roll(p[1], 7, 0))
        self.ax_dn = jnp.where(z == 0, 0.0, q[1])
        self.rad_up = jnp.where(lane == 127, 0.0, pltpu.roll(p[2], 127, 1))
        self.rad_dn = jnp.where(lane == 0, 0.0, q[2])
        self.centre = self.azim + self.ax_up + q[1] + self.rad_up + q[2] + jnp.where(top, 0.0, q[0])

    def __call__(self, x):
        return (
            self.azim * pltpu.roll(x, 4, 0)
            + self.ax_up * pltpu.roll(x, 7, 0)
            + self.ax_dn * pltpu.roll(x, 1, 0)
            + self.rad_up * pltpu.roll(x, 127, 1)
            + self.rad_dn * pltpu.roll(x, 1, 1)
            - self.centre * x
        )


def pair_rows(x, first, second):
    return jnp.where(
        rows_of() % 2 == 0,
        jnp.broadcast_to(x[first : first + 1], (8, 128)),
        jnp.broadcast_to(x[second : second + 1], (8, 128)),
    )


def make_tables(p, where_zero, low_ref, high_ref):
    row, lane = rows_of(), lanes_of()
    taken = (p == 0.0) if where_zero else (p != 0.0)
    one = jnp.where(taken & (row < 4), 1.0, 0.0)
    before = lax.broadcasted_iota(jnp.int32, (128, 128), 0) < lax.broadcasted_iota(jnp.int32, (128, 128), 1)
    inside = jnp.dot(one.astype(bf16), jnp.where(before, 1.0, 0.0).astype(bf16), preferred_element_type=f32)
    total = jnp.sum(one, axis=1, keepdims=True)
    base = jnp.zeros((8, 1), f32)
    for step in (1, 2, 3):
        base = base + jnp.where(
            lax.broadcasted_iota(jnp.int32, (8, 1), 0) >= step, jnp.roll(total, step, axis=0), 0.0
        )
    slot = jnp.where(one > 0.0, inside + base, -1.0).astype(jnp.int32)
    here = lax.broadcasted_iota(jnp.int32, (128, 128), 0)
    first = jnp.where(here < extra, here + 256, -2)
    second = jnp.where(here >= extra, here + (256 - extra), -2)
    for z in range(4):
        cells = slice(128 * z, 128 * z + 128)
        want = jnp.broadcast_to(slot[z : z + 1], (128, 128))
        for ref, start, names in ((low_ref, 0, here), (low_ref, 128, here + 128), (high_ref, 0, first), (high_ref, 128, second)):
            ref[start : start + 128, cells] = jnp.where(names == want, 1.0, 0.0).astype(bf16)


def crowded(p):
    taken = jnp.where((rows_of() < 4) & (p != 0.0), 1.0, 0.0)
    count = jnp.sum(jnp.sum(taken, axis=1, keepdims=True), axis=0, keepdims=True)
    count = jnp.broadcast_to(count, (8, 128))
    return jnp.where(jnp.maximum(count, 512.0 - count) > slots, 1.0, 0.0)


def pieces(x):
    high = x.astype(bf16)
    rest = x - high.astype(f32)
    middle = rest.astype(bf16)
    return high, middle, (rest - middle.astype(f32)).astype(bf16)


def stacked(x, half):
    return jnp.concatenate([part[half * i : half * i + half] for i in range(2) for part in pieces(x)], axis=0)


def summed(x, half):
    parts = [x[half * i : half * i + half] for i in range(6)]
    return [parts[3 * i] + (parts[3 * i + 1] + parts[3 * i + 2]) for i in range(2)]


def encode(comps, x_ref, first_row, low_ref, high_ref, message_ref):
    half = comps // 2
    x = jnp.concatenate(
        [stacked(x_ref[pl.ds(first_row + z, comps, stride=8)], half) for z in range(4)], axis=1
    )
    over = (((1,), (1,)), ((), ()))
    low = lax.dot_general(x, low_ref[...], over, preferred_element_type=f32)
    high = [
        lax.dot_general(
            x[3 * half * i : 3 * half * (i + 1)], high_ref[128 * i : 128 * i + 128], over, preferred_element_type=f32
        )
        for i in range(2)
    ]
    tail = jnp.zeros((half, 128), f32)
    for i, part in enumerate(summed(low, half)):
        message_ref[half * i : half * i + half] = part[:, :128]
        message_ref[comps + half * i : comps + half * i + half] = part[:, 128:]
    for part in high:
        tail = tail + (part[:half] + (part[half : 2 * half] + part[2 * half :]))
    message_ref[2 * comps : 2 * comps + half] = tail


def decode(comps, message_ref, low_ref, high_ref):
    half = comps // 2
    x = jnp.concatenate([stacked(message_ref[comps * i : comps * i + comps], half) for i in range(2)], axis=1)
    low = jnp.dot(x, low_ref[...], preferred_element_type=f32)
    tail = jnp.concatenate(pieces(message_ref[2 * comps : 2 * comps + half]), axis=0)
    found = []
    for i, part in enumerate(summed(low, half)):
        high = jnp.dot(tail, high_ref[128 * i : 128 * i + 128], preferred_element_type=f32)
        found.append(part + (high[:half] + (high[half : 2 * half] + high[2 * half :])))
    return jnp.concatenate(found, axis=0)


def add_azimuthal(comps, halo, coefficient, first_row, out_ref):
    for z in range(4):
        spots = pl.ds(first_row + z, comps, stride=8)
        out_ref[spots] = out_ref[spots] + coefficient[first_row + z : first_row + z + 1] * halo[:, 128 * z : 128 * z + 128]


def pack_sides(comps, x_ref, where_ref, ax_ref, radup_ref, raddn_ref):
    @pl.when(where_ref[0] == 0)
    def _():
        ax_ref[0 : 2 * comps] = x_ref[pl.ds(3, 2 * comps, stride=4)]

    @pl.when(where_ref[0] != 0)
    def _():
        ax_ref[0 : 2 * comps] = x_ref[pl.ds(0, 2 * comps, stride=4)]

    ends = columns(x_ref[...])
    radup_ref[:, 0 : 8 * comps] = ends[0:1]
    raddn_ref[:, 0 : 8 * comps] = ends[1:2]


def columns(x):
    row, lane = rows_of(), lanes_of()
    take = jnp.where(((row == 0) & (lane == 127)) | ((row == 1) & (lane == 0)), 1.0, 0.0)
    return lax.dot_general(take, x, (((1,), (1,)), ((), ())), precision=exact, preferred_element_type=f32)


def put_columns(lower, upper):
    n = lower.shape[1]
    row, lane = rows_of(), lanes_of()
    which = lax.broadcasted_iota(jnp.int32, (8, n), 0)
    both = jnp.where(which == 0, lower, jnp.where(which == 1, upper, 0.0))
    place = jnp.where(((row == 0) & (lane == 0)) | ((row == 1) & (lane == 127)), 1.0, 0.0)
    return lax.dot_general(both, place, (((0,), (0,)), ((), ())), precision=exact, preferred_element_type=f32)


def first_rest(comps, where_ref, a_ref, speeds_ref, flags_ref, up_ref, ax_ref, radup_ref, raddn_ref):
    p, _ = faces(speeds_ref, flags_ref)
    for c in range(comps):
        up_ref[4 * c : 4 * c + 4] = a_ref[8 * c + 4 : 8 * c + 8]
    up_ref[4 * comps :] = p[0]
    pack_sides(comps, a_ref, where_ref, ax_ref, radup_ref, raddn_ref)
    ax_ref[2 * comps : 2 * comps + 8] = pair_rows(p[1], 0, 4)
    radup_ref[:, 8 * comps :] = jnp.zeros((1, 128), f32)
    raddn_ref[:, 8 * comps :] = jnp.zeros((1, 128), f32)
    raddn_ref[:, 8 * comps : 8 * comps + 8] = columns(p[2])[1:2]


def source(sections, x_ref, u_ref, growth_ref, transfer_ref, zones_ref, rate_ref, finish):
    def inner(k, s, x):
        term = transfer_ref[s] * ((x[k][1] - x[k][0]) if s + 1 < sections else -x[k][0])
        if k < 3:
            term = term + ((k + 1.0) * growth_ref[s]) * x[k + 1][0]
        return term

    def load(s):
        got = []
        for k in range(4):
            c = k * sections + s
            here = x_ref[8 * c : 8 * c + 8]
            got.append((here, x_ref[8 * c + 8 : 8 * c + 16] if s + 1 < sections else None))
        return got

    squares = jnp.zeros((8, 128), f32)
    product = jnp.zeros((8, 128), f32)
    for s in range(sections):
        x = load(s)
        for k in range(4):
            u = u_ref[k * sections + s].astype(f32)
            product = product + u * inner(k, s, x)
        squares = squares + u * u
    sigma = supersat_scale / (1.0 + crowding * squares)
    birth = jnp.zeros((8, 128), f32)
    for k in range(4):
        c = k * sections
        birth = birth + nucleus_moments[k] * x_ref[8 * c : 8 * c + 8]
    rate = jnp.zeros((8, 128), f32)
    for label in range(rate_ref.shape[0]):
        rate = jnp.where(zones_ref[...] == label, rate_ref[label], rate)
    slope = (-2.0 * crowding / supersat_scale) * sigma * sigma * (product + 2.0 * rate * sigma * birth)
    for s in range(sections):
        x = load(s)
        for k in range(4):
            c = k * sections + s
            term = sigma * inner(k, s, x)
            if k == 3:
                term = term + u_ref[c].astype(f32) * slope
            finish(c, x[k][0], term)


def first_local(
    sections,
    a_ref,
    u_ref,
    speeds_ref,
    flags_ref,
    zones_ref,
    growth_ref,
    transfer_ref,
    rate_ref,
    out_ref,
    dn_low_ref,
    dn_high_ref,
    up_low_ref,
    up_high_ref,
):
    p, q = faces(speeds_ref, flags_ref)
    local = Local(p, q)
    make_tables(p[0], False, dn_low_ref, dn_high_ref)
    make_tables(p[0], True, up_low_ref, up_high_ref)

    def finish(c, x, term):
        out_ref[8 * c : 8 * c + 8] = 0.5 * (x + local(x) + term)

    source(sections, a_ref, u_ref, growth_ref, transfer_ref, zones_ref, rate_ref, finish)


def second_local(
    sections,
    m_ref,
    a_ref,
    u_ref,
    below_ref,
    edge_ref,
    low_ref,
    high_ref,
    speeds_ref,
    flags_ref,
    zones_ref,
    growth_ref,
    transfer_ref,
    rate_ref,
    out_ref,
    bottom_ref,
):
    local = Local(*faces(speeds_ref, flags_ref))
    local.centre = local.centre + (edge_ref[3] - 1.0)

    def finish(c, x, term):
        out_ref[8 * c : 8 * c + 8] = 0.5 * a_ref[8 * c : 8 * c + 8] + (local(x) + term)

    source(sections, m_ref, u_ref, growth_ref, transfer_ref, zones_ref, rate_ref, finish)
    bottom_ref[...] = out_ref[...]
    add_azimuthal(4 * sections, decode(4 * sections, below_ref, low_ref, high_ref), edge_ref[0], 0, bottom_ref)


def from_below(c, below_ref):
    pair = below_ref[8 * (c // 2) : 8 * (c // 2) + 8]
    return pair if c % 2 == 0 else pltpu.roll(pair, 4, 0)


def from_above(c, above_ref):
    pair = above_ref[8 * (c // 2) : 8 * (c // 2) + 8]
    return pair if c % 2 == 1 else pltpu.roll(pair, 4, 0)


def add_axial(comps, scale, where_ref, axial, ax_ref, out_ref):
    several = jnp.concatenate([scale * axial] * (2 * comps // 8), axis=0)
    for start, index in ((3, 0), (0, 1)):

        @pl.when(where_ref[0] == index)
        def _():
            spots = pl.ds(start, 2 * comps, stride=4)
            out_ref[spots] = out_ref[spots] + several * ax_ref[0 : 2 * comps]


def first_top(
    comps,
    where_ref,
    part_ref,
    a_ref,
    above_ref,
    ax_ref,
    radlo_ref,
    radhi_ref,
    speeds_ref,
    flags_ref,
    m_ref,
    edge_ref,
    up_ref,
    bad_ref,
    dn_low_ref,
    dn_high_ref,
    up_low_ref,
    up_high_ref,
):
    p, q = faces(speeds_ref, flags_ref)
    row, lane = rows_of(), lanes_of()
    upper = above_ref[4 * comps :]
    make_tables(upper, True, up_low_ref, up_high_ref)
    make_tables(upper, False, dn_low_ref, dn_high_ref)
    bad_ref[...] = crowded(p[0]) + crowded(upper)
    hrad = put_columns(radlo_ref[...], radhi_ref[...])
    lower_half = where_ref[0] == 0
    p_azim = jnp.where(row >= 4, pltpu.roll(upper, 4, 0), 0.0)
    pairs = jnp.where(lower_half, ax_ref[2 * comps : 2 * comps + 8], 0.0)
    p_axial = jnp.where(row == 3, pairs[0:1], jnp.where(row == 7, pairs[1:2], 0.0))
    p_rad = jnp.where(lane == 127, hrad[8 * comps : 8 * comps + 8], 0.0)
    axial = jnp.where(lower_half, pairs, pair_rows(q[1], 0, 4))
    rad = jnp.where(lane == 0, q[2], p_rad)
    centre = p_azim + p_axial + p_rad
    edge_ref[0] = jnp.where(row >= 4, p_azim, q[0])
    edge_ref[1] = axial
    edge_ref[2] = rad
    edge_ref[3] = centre
    for c in range(comps):
        spots = slice(8 * c, 8 * c + 8)
        m_ref[spots] = part_ref[spots] + 0.5 * (
            p_azim * from_above(c, above_ref) + rad * hrad[spots] - centre * a_ref[spots]
        )
    add_axial(comps, 0.5, where_ref, axial, ax_ref, m_ref)
    encode(comps, m_ref, 4, up_low_ref, up_high_ref, up_ref)


def first_bottom(
    comps,
    where_ref,
    part_ref,
    below_ref,
    edge_ref,
    bad_ref,
    low_ref,
    high_ref,
    m_ref,
    dn_ref,
    ax_ref,
    radup_ref,
    raddn_ref,
    worse_ref,
):
    azim = jnp.where(rows_of() >= 4, 0.0, 0.5 * edge_ref[0])
    for c in range(comps):
        m_ref[8 * c : 8 * c + 8] = part_ref[8 * c : 8 * c + 8] + azim * from_below(c, below_ref)
    encode(comps, m_ref, 0, low_ref, high_ref, dn_ref)
    worse_ref[...] = bad_ref[...] + crowded(below_ref[4 * comps :])
    dn_ref[5 * comps // 2 :] = worse_ref[...]
    pack_sides(comps, m_ref, where_ref, ax_ref, radup_ref, raddn_ref)


def second_sides(
    comps, where_ref, part_ref, bottom_ref, ax_ref, radlo_ref, radhi_ref, edge_ref, base_ref, full_ref
):
    hrad = put_columns(radlo_ref[...], radhi_ref[...])
    rad = edge_ref[2]
    for c in range(comps):
        spots = slice(8 * c, 8 * c + 8)
        halo = rad * hrad[spots]
        base_ref[spots] = part_ref[spots] + halo
        full_ref[spots] = bottom_ref[spots] + halo
    for ref in (base_ref, full_ref):
        add_axial(comps, 1.0, where_ref, edge_ref[1], ax_ref, ref)


def second_top(comps, full_ref, above_ref, edge_ref, bad_ref, low_ref, high_ref, out_ref, again_ref):
    again_ref[0] = (jnp.max(bad_ref[...] + above_ref[5 * comps // 2 :]) > 0.0).astype(jnp.int32)
    out_ref[...] = full_ref[...]
    add_azimuthal(comps, decode(comps, above_ref, low_ref, high_ref), edge_ref[0], 4, out_ref)


SPACES = {
    "v": pl.BlockSpec(memory_space=pltpu.VMEM),
    "s": pl.BlockSpec(memory_space=pltpu.SMEM),
    "h": pl.BlockSpec(memory_space=pltpu.HBM),
}


def call(body, ins, outs, shapes, cost, *operands):
    return pl.pallas_call(
        body,
        in_specs=[SPACES[s] for s in ins],
        out_specs=[SPACES[s] for s in outs],
        out_shape=[s if isinstance(s, jax.ShapeDtypeStruct) else jax.ShapeDtypeStruct(s, f32) for s in shapes],
        cost_estimate=pl.CostEstimate(flops=cost, bytes_accessed=cost // 10, transcendentals=0),
        compiler_params=pltpu.CompilerParams(vmem_limit_bytes=32 * 1024 * 1024),
    )(*operands)


def shift(x, axis, step, wrap):
    size = lax.axis_size(axis)
    pairs = [(i, (i + step) % size) for i in range(size) if wrap or 0 <= i + step < size]
    return lax.ppermute(x, axis, pairs)


def sides(ax, radup, raddn):
    ax = lax.ppermute(ax, "axial", [(0, 1), (1, 0)])
    return ax, shift(radup, "rad", 1, False), shift(raddn, "rad", -1, False)


def shards(adjoint_final, state_start, state_middle, speeds, flags, zones, growth_rate, transfer_rate, nucleation_rate):
    shape = adjoint_final.shape
    moments, sections = shape[:2]
    comps = moments * sections
    assert moments == 4 and shape[2:] == (2, 4, 128) and comps % 4 == 0
    assert lax.axis_size("axial") == 2
    cells = 8 * comps
    half, rows = cells // 2, cells // 4
    a = adjoint_final.reshape(cells, 128)
    speeds2 = speeds.reshape(3, 8, 128)
    flags2 = flags.reshape(3, 8, 128)
    where = lax.axis_index("axial").reshape(1)
    rates = (zones.reshape(8, 128), growth_rate, transfer_rate, nucleation_rate)
    message = 5 * comps // 2
    tables = [jax.ShapeDtypeStruct((256, 512), bf16)] * 2

    keep = ((0, 2, 0), (0, -1, 0), (0, 0, 0), (0, 0, 0))
    after = ((comps, -1, 0), (0, -1, 0), (0, 0, 0), (0, 0, 0))
    dn = lax.pad(adjoint_final.reshape(comps, 2, 4, 128), 0.0, keep)
    dn = dn + lax.pad(speeds, 0.0, after) * lax.pad(flags, 0, after).astype(f32)
    above = shift(dn.reshape(half + 8, 128), "azim", -1, True)
    up, *edges = call(
        functools.partial(first_rest, comps),
        "svvv",
        "vvvv",
        [(half + 8, 128), (rows + 8, 128), (1, cells + 128), (1, cells + 128)],
        2_000_000,
        where,
        a,
        speeds2,
        flags2,
    )
    below = shift(up, "azim", 1, True)
    edges = sides(*edges)
    part, *lower_tables = call(
        functools.partial(first_local, sections),
        "vvvvvsss",
        "vvvvv",
        [(cells, 128)] + 2 * tables,
        8_000_000,
        a,
        state_middle.reshape(comps, 8, 128),
        speeds2,
        flags2,
        *rates,
    )
    part, edge, up, bad, *upper_tables = call(
        functools.partial(first_top, comps),
        "s" + "v" * 8,
        "v" * 8,
        [(cells, 128), (4, 8, 128), (message, 128), (8, 128)] + 2 * tables,
        4_000_000,
        where,
        part,
        a,
        above,
        *edges,
        speeds2,
        flags2,
    )
    next_below = shift(up, "azim", 1, True)
    m, dn, *edges, bad = call(
        functools.partial(first_bottom, comps),
        "s" + "v" * 6,
        "v" * 6,
        [(cells, 128), (message + 8, 128), (rows, 128), (1, cells), (1, cells), (8, 128)],
        10_000,
        where,
        part,
        below,
        edge,
        bad,
        *lower_tables[:2],
    )
    next_above = shift(dn, "azim", -1, True)
    edges = sides(*edges)
    part, bottom = call(
        functools.partial(second_local, sections),
        "v" * 10 + "sss",
        "vv",
        [(cells, 128), (cells, 128)],
        300_000_000,
        m,
        a,
        state_start.reshape(comps, 8, 128),
        next_below,
        edge,
        *lower_tables[2:],
        speeds2,
        flags2,
        *rates,
    )
    base, full = call(
        functools.partial(second_sides, comps),
        "s" + "v" * 6,
        "vv",
        [(cells, 128), (cells, 128)],
        10_000,
        where,
        part,
        bottom,
        *edges,
        edge,
    )

    out, again = call(
        functools.partial(second_top, comps),
        "vvvvvv",
        "vs",
        [(cells, 128), jax.ShapeDtypeStruct((1,), jnp.int32)],
        1_000_000,
        full,
        next_above,
        edge,
        bad,
        *upper_tables[:2],
    )

    def whole():
        rows_ = m.reshape(comps, 2, 4, 128)
        halo = jnp.stack([shift(rows_[:, 1], "azim", 1, True), shift(rows_[:, 0], "azim", -1, True)], axis=1)
        return base + (edge[0].reshape(1, 2, 4, 128) * halo).reshape(cells, 128)

    again = again[0]
    if lax.axis_size("azim") != 4:
        again = lax.pmax(again.astype(f32), "azim").astype(jnp.int32)
    return lax.cond(again > 0, whole, lambda: out).reshape(shape)


def solution(mesh):
    field = P(None, None, "azim", "axial", "rad")
    faces_spec = P(None, "azim", "axial", "rad")
    return jax.shard_map(
        shards,
        mesh=mesh,
        in_specs=(field, field, field, faces_spec, faces_spec, P("azim", "axial", "rad"), P(), P(), P()),
        out_specs=field,
        check_vma=False,
    )
```

```python
import functools

import jax
import jax.numpy as jnp
from jax import lax
from jax.experimental import pallas as pl
from jax.experimental.pallas import tpu as pltpu
from jax.sharding import PartitionSpec as P

supersat_scale = 1.5
crowding = 0.02
nucleus_moments = (1.0, 0.5, 0.25, 0.125)
f32 = jnp.float32
bf16 = jnp.bfloat16
exact = lax.Precision.HIGHEST

slots = 320
extra = slots - 256


def rows_of():
    return lax.broadcasted_iota(jnp.int32, (8, 128), 0)


def lanes_of():
    return lax.broadcasted_iota(jnp.int32, (8, 128), 1)


def faces(speeds_ref, flags_ref):
    p, q = [], []
    for d in range(3):
        speed, upwind = speeds_ref[d], flags_ref[d].astype(f32)
        p.append(speed * upwind)
        q.append(speed * (1.0 - upwind))
    return p, q


class Local:
    def __init__(self, p, q):
        row, lane = rows_of(), lanes_of()
        z, top = row % 4, row >= 4
        self.azim = jnp.where(top, q[0], pltpu.roll(p[0], 4, 0))
        self.ax_up = jnp.where(z == 3, 0.0, pltpu.roll(p[1], 7, 0))
        self.ax_dn = jnp.where(z == 0, 0.0, q[1])
        self.rad_up = jnp.where(lane == 127, 0.0, pltpu.roll(p[2], 127, 1))
        self.rad_dn = jnp.where(lane == 0, 0.0, q[2])
        self.centre = self.azim + self.ax_up + q[1] + self.rad_up + q[2] + jnp.where(top, 0.0, q[0])

    def __call__(self, x):
        return (
            self.azim * pltpu.roll(x, 4, 0)
            + self.ax_up * pltpu.roll(x, 7, 0)
            + self.ax_dn * pltpu.roll(x, 1, 0)
            + self.rad_up * pltpu.roll(x, 127, 1)
            + self.rad_dn * pltpu.roll(x, 1, 1)
            - self.centre * x
        )


def pair_rows(x, first, second):
    return jnp.where(
        rows_of() % 2 == 0,
        jnp.broadcast_to(x[first : first + 1], (8, 128)),
        jnp.broadcast_to(x[second : second + 1], (8, 128)),
    )


def make_tables(p, where_zero, low_ref, high_ref):
    row, lane = rows_of(), lanes_of()
    taken = (p == 0.0) if where_zero else (p != 0.0)
    one = jnp.where(taken & (row < 4), 1.0, 0.0)
    before = lax.broadcasted_iota(jnp.int32, (128, 128), 0) < lax.broadcasted_iota(jnp.int32, (128, 128), 1)
    inside = jnp.dot(one.astype(bf16), jnp.where(before, 1.0, 0.0).astype(bf16), preferred_element_type=f32)
    total = jnp.sum(one, axis=1, keepdims=True)
    base = jnp.zeros((8, 1), f32)
    for step in (1, 2, 3):
        base = base + jnp.where(
            lax.broadcasted_iota(jnp.int32, (8, 1), 0) >= step, jnp.roll(total, step, axis=0), 0.0
        )
    slot = jnp.where(one > 0.0, inside + base, -1.0).astype(jnp.int32)
    here = lax.broadcasted_iota(jnp.int32, (128, 128), 0)
    first = jnp.where(here < extra, here + 256, -2)
    second = jnp.where(here >= extra, here + (256 - extra), -2)
    for z in range(4):
        cells = slice(128 * z, 128 * z + 128)
        want = jnp.broadcast_to(slot[z : z + 1], (128, 128))
        for ref, start, names in ((low_ref, 0, here), (low_ref, 128, here + 128), (high_ref, 0, first), (high_ref, 128, second)):
            ref[start : start + 128, cells] = jnp.where(names == want, 1.0, 0.0).astype(bf16)


def crowded(p):
    taken = jnp.where((rows_of() < 4) & (p != 0.0), 1.0, 0.0)
    count = jnp.sum(jnp.sum(taken, axis=1, keepdims=True), axis=0, keepdims=True)
    count = jnp.broadcast_to(count, (8, 128))
    return jnp.where(jnp.maximum(count, 512.0 - count) > slots, 1.0, 0.0)


def pieces(x):
    high = x.astype(bf16)
    rest = x - high.astype(f32)
    middle = rest.astype(bf16)
    return high, middle, (rest - middle.astype(f32)).astype(bf16)


def stacked(x, half):
    return jnp.concatenate([part[half * i : half * i + half] for i in range(2) for part in pieces(x)], axis=0)


def summed(x, half):
    parts = [x[half * i : half * i + half] for i in range(6)]
    return [parts[3 * i] + (parts[3 * i + 1] + parts[3 * i + 2]) for i in range(2)]


def encode(comps, x_ref, first_row, low_ref, high_ref, message_ref):
    half = comps // 2
    x = jnp.concatenate(
        [stacked(x_ref[pl.ds(first_row + z, comps, stride=8)], half) for z in range(4)], axis=1
    )
    over = (((1,), (1,)), ((), ()))
    low = lax.dot_general(x, low_ref[...], over, preferred_element_type=f32)
    high = [
        lax.dot_general(
            x[3 * half * i : 3 * half * (i + 1)], high_ref[128 * i : 128 * i + 128], over, preferred_element_type=f32
        )
        for i in range(2)
    ]
    tail = jnp.zeros((half, 128), f32)
    for i, part in enumerate(summed(low, half)):
        message_ref[half * i : half * i + half] = part[:, :128]
        message_ref[comps + half * i : comps + half * i + half] = part[:, 128:]
    for part in high:
        tail = tail + (part[:half] + (part[half : 2 * half] + part[2 * half :]))
    message_ref[2 * comps : 2 * comps + half] = tail


def decode(comps, message_ref, low_ref, high_ref):
    half = comps // 2
    x = jnp.concatenate([stacked(message_ref[comps * i : comps * i + comps], half) for i in range(2)], axis=1)
    low = jnp.dot(x, low_ref[...], preferred_element_type=f32)
    tail = jnp.concatenate(pieces(message_ref[2 * comps : 2 * comps + half]), axis=0)
    found = []
    for i, part in enumerate(summed(low, half)):
        high = jnp.dot(tail, high_ref[128 * i : 128 * i + 128], preferred_element_type=f32)
        found.append(part + (high[:half] + (high[half : 2 * half] + high[2 * half :])))
    return jnp.concatenate(found, axis=0)


def add_azimuthal(comps, halo, coefficient, first_row, out_ref):
    for z in range(4):
        spots = pl.ds(first_row + z, comps, stride=8)
        out_ref[spots] = out_ref[spots] + coefficient[first_row + z : first_row + z + 1] * halo[:, 128 * z : 128 * z + 128]


def pack_sides(comps, x_ref, where_ref, ax_ref, radup_ref, raddn_ref):
    @pl.when(where_ref[0] == 0)
    def _():
        ax_ref[0 : 2 * comps] = x_ref[pl.ds(3, 2 * comps, stride=4)]

    @pl.when(where_ref[0] != 0)
    def _():
        ax_ref[0 : 2 * comps] = x_ref[pl.ds(0, 2 * comps, stride=4)]

    ends = columns(x_ref[...])
    radup_ref[:, 0 : 8 * comps] = ends[0:1]
    raddn_ref[:, 0 : 8 * comps] = ends[1:2]


def columns(x):
    row, lane = rows_of(), lanes_of()
    take = jnp.where(((row == 0) & (lane == 127)) | ((row == 1) & (lane == 0)), 1.0, 0.0)
    return lax.dot_general(take, x, (((1,), (1,)), ((), ())), precision=exact, preferred_element_type=f32)


def put_columns(lower, upper):
    n = lower.shape[1]
    row, lane = rows_of(), lanes_of()
    which = lax.broadcasted_iota(jnp.int32, (8, n), 0)
    both = jnp.where(which == 0, lower, jnp.where(which == 1, upper, 0.0))
    place = jnp.where(((row == 0) & (lane == 0)) | ((row == 1) & (lane == 127)), 1.0, 0.0)
    return lax.dot_general(both, place, (((0,), (0,)), ((), ())), precision=exact, preferred_element_type=f32)


def first_rest(comps, where_ref, a_ref, speeds_ref, flags_ref, up_ref, ax_ref, radup_ref, raddn_ref):
    p, _ = faces(speeds_ref, flags_ref)
    for c in range(comps):
        up_ref[4 * c : 4 * c + 4] = a_ref[8 * c + 4 : 8 * c + 8]
    up_ref[4 * comps :] = p[0]
    pack_sides(comps, a_ref, where_ref, ax_ref, radup_ref, raddn_ref)
    ax_ref[2 * comps : 2 * comps + 8] = pair_rows(p[1], 0, 4)
    ax_ref[2 * comps + 8 :] = jnp.zeros((8, 128), f32)
    radup_ref[:, 8 * comps :] = jnp.zeros((1, 128), f32)
    raddn_ref[:, 8 * comps :] = jnp.zeros((1, 128), f32)
    raddn_ref[:, 8 * comps : 8 * comps + 8] = columns(p[2])[1:2]


def source(sections, x_ref, u_ref, growth_ref, transfer_ref, zones_ref, rate_ref, finish):
    def inner(k, s, x):
        term = transfer_ref[s] * ((x[k][1] - x[k][0]) if s + 1 < sections else -x[k][0])
        if k < 3:
            term = term + ((k + 1.0) * growth_ref[s]) * x[k + 1][0]
        return term

    def load(s):
        got = []
        for k in range(4):
            c = k * sections + s
            here = x_ref[8 * c : 8 * c + 8]
            got.append((here, x_ref[8 * c + 8 : 8 * c + 16] if s + 1 < sections else None))
        return got

    squares = jnp.zeros((8, 128), f32)
    product = jnp.zeros((8, 128), f32)
    for s in range(sections):
        x = load(s)
        for k in range(4):
            u = u_ref[k * sections + s].astype(f32)
            product = product + u * inner(k, s, x)
        squares = squares + u * u
    sigma = supersat_scale / (1.0 + crowding * squares)
    birth = jnp.zeros((8, 128), f32)
    for k in range(4):
        c = k * sections
        birth = birth + nucleus_moments[k] * x_ref[8 * c : 8 * c + 8]
    rate = jnp.zeros((8, 128), f32)
    for label in range(rate_ref.shape[0]):
        rate = jnp.where(zones_ref[...] == label, rate_ref[label], rate)
    slope = (-2.0 * crowding / supersat_scale) * sigma * sigma * (product + 2.0 * rate * sigma * birth)
    for s in range(sections):
        x = load(s)
        for k in range(4):
            c = k * sections + s
            term = sigma * inner(k, s, x)
            if k == 3:
                term = term + u_ref[c].astype(f32) * slope
            finish(c, x[k][0], term)


def first_local(
    sections,
    a_ref,
    u_ref,
    radlo_ref,
    radhi_ref,
    speeds_ref,
    flags_ref,
    zones_ref,
    growth_ref,
    transfer_ref,
    rate_ref,
    out_ref,
    rad_ref,
    dn_low_ref,
    dn_high_ref,
    up_low_ref,
    up_high_ref,
):
    p, q = faces(speeds_ref, flags_ref)
    local = Local(p, q)
    hrad = put_columns(radlo_ref[...], radhi_ref[...])
    p_rad = jnp.where(lanes_of() == 127, hrad[32 * sections : 32 * sections + 8], 0.0)
    rad = jnp.where(lanes_of() == 0, q[2], p_rad)
    rad_ref[...] = rad
    local.centre = local.centre + p_rad
    make_tables(p[0], False, dn_low_ref, dn_high_ref)
    make_tables(p[0], True, up_low_ref, up_high_ref)

    def finish(c, x, term):
        out_ref[8 * c : 8 * c + 8] = 0.5 * (x + local(x) + rad * hrad[8 * c : 8 * c + 8] + term)

    source(sections, a_ref, u_ref, growth_ref, transfer_ref, zones_ref, rate_ref, finish)


def second_local(
    sections,
    m_ref,
    a_ref,
    u_ref,
    below_ref,
    radlo_ref,
    radhi_ref,
    edge_ref,
    low_ref,
    high_ref,
    speeds_ref,
    flags_ref,
    zones_ref,
    growth_ref,
    transfer_ref,
    rate_ref,
    out_ref,
    bottom_ref,
):
    local = Local(*faces(speeds_ref, flags_ref))
    local.centre = local.centre + (edge_ref[3] - 1.0)
    hrad = put_columns(radlo_ref[...], radhi_ref[...])
    rad = edge_ref[2]

    def finish(c, x, term):
        spots = slice(8 * c, 8 * c + 8)
        out_ref[spots] = 0.5 * a_ref[spots] + (local(x) + rad * hrad[spots] + term)

    source(sections, m_ref, u_ref, growth_ref, transfer_ref, zones_ref, rate_ref, finish)
    bottom_ref[...] = out_ref[...]
    add_azimuthal(4 * sections, decode(4 * sections, below_ref, low_ref, high_ref), edge_ref[0], 0, bottom_ref)


def from_below(c, below_ref):
    pair = below_ref[8 * (c // 2) : 8 * (c // 2) + 8]
    return pair if c % 2 == 0 else pltpu.roll(pair, 4, 0)


def from_above(c, above_ref):
    pair = above_ref[8 * (c // 2) : 8 * (c // 2) + 8]
    return pair if c % 2 == 1 else pltpu.roll(pair, 4, 0)


def add_axial(comps, scale, where_ref, axial, ax_ref, out_ref):
    several = jnp.concatenate([scale * axial] * (2 * comps // 8), axis=0)
    for start, index in ((3, 0), (0, 1)):

        @pl.when(where_ref[0] == index)
        def _():
            spots = pl.ds(start, 2 * comps, stride=4)
            out_ref[spots] = out_ref[spots] + several * ax_ref[0 : 2 * comps]


def first_top(
    comps,
    where_ref,
    part_ref,
    a_ref,
    above_ref,
    ax_ref,
    rad_ref,
    speeds_ref,
    flags_ref,
    m_ref,
    edge_ref,
    up_ref,
    bad_ref,
    dn_low_ref,
    dn_high_ref,
    up_low_ref,
    up_high_ref,
):
    p, q = faces(speeds_ref, flags_ref)
    row, lane = rows_of(), lanes_of()
    upper = above_ref[4 * comps :]
    make_tables(upper, True, up_low_ref, up_high_ref)
    make_tables(upper, False, dn_low_ref, dn_high_ref)
    bad_ref[...] = crowded(p[0]) + crowded(upper)
    lower_half = where_ref[0] == 0
    p_azim = jnp.where(row >= 4, pltpu.roll(upper, 4, 0), 0.0)
    pairs = jnp.where(lower_half, ax_ref[2 * comps : 2 * comps + 8], 0.0)
    p_axial = jnp.where(row == 3, pairs[0:1], jnp.where(row == 7, pairs[1:2], 0.0))
    axial = jnp.where(lower_half, pairs, pair_rows(q[1], 0, 4))
    centre = p_azim + p_axial
    edge_ref[0] = jnp.where(row >= 4, p_azim, q[0])
    edge_ref[1] = axial
    edge_ref[2] = rad_ref[...]
    edge_ref[3] = centre + jnp.where(lane == 127, rad_ref[...], 0.0)
    for c in range(comps):
        spots = slice(8 * c, 8 * c + 8)
        m_ref[spots] = part_ref[spots] + 0.5 * (
            p_azim * from_above(c, above_ref) - centre * a_ref[spots]
        )
    add_axial(comps, 0.5, where_ref, axial, ax_ref, m_ref)
    encode(comps, m_ref, 4, up_low_ref, up_high_ref, up_ref)


def first_bottom(
    comps,
    where_ref,
    part_ref,
    below_ref,
    edge_ref,
    bad_ref,
    low_ref,
    high_ref,
    m_ref,
    dn_ref,
    ax_ref,
    radup_ref,
    raddn_ref,
    worse_ref,
):
    azim = jnp.where(rows_of() >= 4, 0.0, 0.5 * edge_ref[0])
    for c in range(comps):
        m_ref[8 * c : 8 * c + 8] = part_ref[8 * c : 8 * c + 8] + azim * from_below(c, below_ref)
    encode(comps, m_ref, 0, low_ref, high_ref, dn_ref)
    worse_ref[...] = bad_ref[...] + crowded(below_ref[4 * comps :])
    ax_ref[2 * comps :] = jnp.zeros((8, 128), f32)
    dn_ref[5 * comps // 2 :] = worse_ref[...]
    pack_sides(comps, m_ref, where_ref, ax_ref, radup_ref, raddn_ref)


def second_rest(comps, where_ref, bottom_ref, above_ref, ax_ref, edge_ref, bad_ref, low_ref, high_ref, out_ref, again_ref):
    again_ref[0] = (jnp.max(bad_ref[...] + above_ref[5 * comps // 2 :]) > 0.0).astype(jnp.int32)
    out_ref[...] = bottom_ref[...]
    add_axial(comps, 1.0, where_ref, edge_ref[1], ax_ref, out_ref)
    add_azimuthal(comps, decode(comps, above_ref, low_ref, high_ref), edge_ref[0], 4, out_ref)


SPACES = {
    "v": pl.BlockSpec(memory_space=pltpu.VMEM),
    "s": pl.BlockSpec(memory_space=pltpu.SMEM),
    "h": pl.BlockSpec(memory_space=pltpu.HBM),
}


def call(body, ins, outs, shapes, cost, *operands):
    return pl.pallas_call(
        body,
        in_specs=[SPACES[s] for s in ins],
        out_specs=[SPACES[s] for s in outs],
        out_shape=[s if isinstance(s, jax.ShapeDtypeStruct) else jax.ShapeDtypeStruct(s, f32) for s in shapes],
        cost_estimate=pl.CostEstimate(flops=cost, bytes_accessed=cost // 10, transcendentals=0),
        compiler_params=pltpu.CompilerParams(vmem_limit_bytes=32 * 1024 * 1024),
    )(*operands)


def shift(x, axis, step, wrap):
    size = lax.axis_size(axis)
    pairs = [(i, (i + step) % size) for i in range(size) if wrap or 0 <= i + step < size]
    return lax.ppermute(x, axis, pairs)


def sides(ax, radup, raddn):
    radlo, radhi = shift(radup, "rad", 1, False), shift(raddn, "rad", -1, False)
    for row, came in enumerate((radlo, radhi)):
        ax = lax.dynamic_update_slice(ax, came[:, :128], (ax.shape[0] - 8 + row, 0))
    return lax.ppermute(ax, "axial", [(0, 1), (1, 0)]), radlo, radhi


def shards(adjoint_final, state_start, state_middle, speeds, flags, zones, growth_rate, transfer_rate, nucleation_rate):
    shape = adjoint_final.shape
    moments, sections = shape[:2]
    comps = moments * sections
    assert moments == 4 and shape[2:] == (2, 4, 128) and comps % 4 == 0
    assert lax.axis_size("axial") == 2
    cells = 8 * comps
    half, rows = cells // 2, cells // 4
    a = adjoint_final.reshape(cells, 128)
    speeds2 = speeds.reshape(3, 8, 128)
    flags2 = flags.reshape(3, 8, 128)
    where = lax.axis_index("axial").reshape(1)
    rates = (zones.reshape(8, 128), growth_rate, transfer_rate, nucleation_rate)
    message = 5 * comps // 2
    tables = [jax.ShapeDtypeStruct((256, 512), bf16)] * 2

    keep = ((0, 2, 0), (0, -1, 0), (0, 0, 0), (0, 0, 0))
    after = ((comps, -1, 0), (0, -1, 0), (0, 0, 0), (0, 0, 0))
    dn = lax.pad(adjoint_final.reshape(comps, 2, 4, 128), 0.0, keep)
    dn = dn + lax.pad(speeds, 0.0, after) * lax.pad(flags, 0, after).astype(f32)
    above = shift(dn.reshape(half + 8, 128), "azim", -1, True)
    up, *edges = call(
        functools.partial(first_rest, comps),
        "svvv",
        "vvvv",
        [(half + 8, 128), (rows + 16, 128), (1, cells + 128), (1, cells + 128)],
        2_000_000,
        where,
        a,
        speeds2,
        flags2,
    )
    below = shift(up, "azim", 1, True)
    ax, *edges = sides(*edges)
    part, rad, *lower_tables = call(
        functools.partial(first_local, sections),
        "vvvvvvvsss",
        "vvvvvv",
        [(cells, 128), (8, 128)] + 2 * tables,
        8_000_000,
        a,
        state_middle.reshape(comps, 8, 128),
        *edges,
        speeds2,
        flags2,
        *rates,
    )
    part, edge, up, bad, *upper_tables = call(
        functools.partial(first_top, comps),
        "s" + "v" * 7,
        "v" * 8,
        [(cells, 128), (4, 8, 128), (message, 128), (8, 128)] + 2 * tables,
        4_000_000,
        where,
        part,
        a,
        above,
        ax,
        rad,
        speeds2,
        flags2,
    )
    next_below = shift(up, "azim", 1, True)
    m, dn, *edges, bad = call(
        functools.partial(first_bottom, comps),
        "s" + "v" * 6,
        "v" * 6,
        [(cells, 128), (message + 8, 128), (rows + 8, 128), (1, cells), (1, cells), (8, 128)],
        10_000,
        where,
        part,
        below,
        edge,
        bad,
        *lower_tables[:2],
    )
    next_above = shift(dn, "azim", -1, True)
    ax, *edges = sides(*edges)
    part, bottom = call(
        functools.partial(second_local, sections),
        "v" * 12 + "sss",
        "vv",
        [(cells, 128), (cells, 128)],
        300_000_000,
        m,
        a,
        state_start.reshape(comps, 8, 128),
        next_below,
        *edges,
        edge,
        *lower_tables[2:],
        speeds2,
        flags2,
        *rates,
    )
    out, again = call(
        functools.partial(second_rest, comps),
        "s" + "v" * 7,
        "vs",
        [(cells, 128), jax.ShapeDtypeStruct((1,), jnp.int32)],
        1_000_000,
        where,
        bottom,
        next_above,
        ax,
        edge,
        bad,
        *upper_tables[:2],
    )

    def whole():
        rows_ = m.reshape(comps, 2, 4, 128)
        halo = jnp.stack([shift(rows_[:, 1], "azim", 1, True), shift(rows_[:, 0], "azim", -1, True)], axis=1)
        azimuthal = edge[0].reshape(1, 2, 4, 128) * halo
        outer = jnp.arange(4).reshape(1, 1, 4, 1) == 3 * (1 - where[0])
        axial = jnp.where(outer, edge[1, :2].reshape(1, 2, 1, 128) * ax[:rows].reshape(comps, 2, 1, 128), 0.0)
        return (part.reshape(comps, 2, 4, 128) + axial + azimuthal).reshape(cells, 128)

    again = again[0]
    if lax.axis_size("azim") != 4:
        again = lax.pmax(again.astype(f32), "azim").astype(jnp.int32)
    return lax.cond(again > 0, whole, lambda: out).reshape(shape)


def solution(mesh):
    field = P(None, None, "azim", "axial", "rad")
    faces_spec = P(None, "azim", "axial", "rad")
    return jax.shard_map(
        shards,
        mesh=mesh,
        in_specs=(field, field, field, faces_spec, faces_spec, P("azim", "axial", "rad"), P(), P(), P()),
        out_specs=field,
        check_vma=False,
    )
```

```python
import functools

import jax
import jax.numpy as jnp
from jax import lax
from jax.experimental import pallas as pl
from jax.experimental.pallas import tpu as pltpu
from jax.sharding import PartitionSpec as P

supersat_scale = 1.5
crowding = 0.02
nucleus_moments = (1.0, 0.5, 0.25, 0.125)
f32 = jnp.float32
bf16 = jnp.bfloat16
exact = lax.Precision.HIGHEST

slots = 320
extra = slots - 256


def rows_of():
    return lax.broadcasted_iota(jnp.int32, (8, 128), 0)


def lanes_of():
    return lax.broadcasted_iota(jnp.int32, (8, 128), 1)


def faces(speeds_ref, flags_ref):
    p, q = [], []
    for d in range(3):
        speed, upwind = speeds_ref[d], flags_ref[d].astype(f32)
        p.append(speed * upwind)
        q.append(speed * (1.0 - upwind))
    return p, q


class Local:
    def __init__(self, p, q):
        row, lane = rows_of(), lanes_of()
        z, top = row % 4, row >= 4
        self.azim = jnp.where(top, q[0], pltpu.roll(p[0], 4, 0))
        self.ax_up = jnp.where(z == 3, 0.0, pltpu.roll(p[1], 7, 0))
        self.ax_dn = jnp.where(z == 0, 0.0, q[1])
        self.rad_up = jnp.where(lane == 127, 0.0, pltpu.roll(p[2], 127, 1))
        self.rad_dn = jnp.where(lane == 0, 0.0, q[2])
        self.centre = self.azim + self.ax_up + q[1] + self.rad_up + q[2] + jnp.where(top, 0.0, q[0])

    def __call__(self, x):
        return (
            self.azim * pltpu.roll(x, 4, 0)
            + self.ax_up * pltpu.roll(x, 7, 0)
            + self.ax_dn * pltpu.roll(x, 1, 0)
            + self.rad_up * pltpu.roll(x, 127, 1)
            + self.rad_dn * pltpu.roll(x, 1, 1)
            - self.centre * x
        )


def pair_rows(x, first, second):
    return jnp.where(
        rows_of() % 2 == 0,
        jnp.broadcast_to(x[first : first + 1], (8, 128)),
        jnp.broadcast_to(x[second : second + 1], (8, 128)),
    )


def make_tables(p, where_zero, low_ref, high_ref):
    row, lane = rows_of(), lanes_of()
    taken = (p == 0.0) if where_zero else (p != 0.0)
    one = jnp.where(taken & (row < 4), 1.0, 0.0)
    before = lax.broadcasted_iota(jnp.int32, (128, 128), 0) < lax.broadcasted_iota(jnp.int32, (128, 128), 1)
    inside = jnp.dot(one.astype(bf16), jnp.where(before, 1.0, 0.0).astype(bf16), preferred_element_type=f32)
    total = jnp.sum(one, axis=1, keepdims=True)
    base = jnp.zeros((8, 1), f32)
    for step in (1, 2, 3):
        base = base + jnp.where(
            lax.broadcasted_iota(jnp.int32, (8, 1), 0) >= step, jnp.roll(total, step, axis=0), 0.0
        )
    slot = jnp.where(one > 0.0, inside + base, -1.0).astype(jnp.int32)
    here = lax.broadcasted_iota(jnp.int32, (128, 128), 0)
    first = jnp.where(here < extra, here + 256, -2)
    second = jnp.where(here >= extra, here + (256 - extra), -2)
    for z in range(4):
        cells = slice(128 * z, 128 * z + 128)
        want = jnp.broadcast_to(slot[z : z + 1], (128, 128))
        for ref, start, names in ((low_ref, 0, here), (low_ref, 128, here + 128), (high_ref, 0, first), (high_ref, 128, second)):
            ref[start : start + 128, cells] = jnp.where(names == want, 1.0, 0.0).astype(bf16)


def crowded(p):
    taken = jnp.where((rows_of() < 4) & (p != 0.0), 1.0, 0.0)
    count = jnp.sum(jnp.sum(taken, axis=1, keepdims=True), axis=0, keepdims=True)
    count = jnp.broadcast_to(count, (8, 128))
    return jnp.where(jnp.maximum(count, 512.0 - count) > slots, 1.0, 0.0)


def pieces(x):
    high = x.astype(bf16)
    rest = x - high.astype(f32)
    middle = rest.astype(bf16)
    return high, middle, (rest - middle.astype(f32)).astype(bf16)


def stacked(x, half):
    return jnp.concatenate([part[half * i : half * i + half] for i in range(2) for part in pieces(x)], axis=0)


def summed(x, half):
    parts = [x[half * i : half * i + half] for i in range(6)]
    return [parts[3 * i] + (parts[3 * i + 1] + parts[3 * i + 2]) for i in range(2)]


def encode(comps, x_ref, first_row, low_ref, high_ref, message_ref):
    half = comps // 2
    x = jnp.concatenate(
        [stacked(x_ref[pl.ds(first_row + z, comps, stride=8)], half) for z in range(4)], axis=1
    )
    over = (((1,), (1,)), ((), ()))
    low = lax.dot_general(x, low_ref[...], over, preferred_element_type=f32)
    high = [
        lax.dot_general(
            x[3 * half * i : 3 * half * (i + 1)], high_ref[128 * i : 128 * i + 128], over, preferred_element_type=f32
        )
        for i in range(2)
    ]
    tail = jnp.zeros((half, 128), f32)
    for i, part in enumerate(summed(low, half)):
        message_ref[half * i : half * i + half] = part[:, :128]
        message_ref[comps + half * i : comps + half * i + half] = part[:, 128:]
    for part in high:
        tail = tail + (part[:half] + (part[half : 2 * half] + part[2 * half :]))
    message_ref[2 * comps : 2 * comps + half] = tail


def decode(comps, message_ref, low_ref, high_ref):
    half = comps // 2
    x = jnp.concatenate([stacked(message_ref[comps * i : comps * i + comps], half) for i in range(2)], axis=1)
    low = jnp.dot(x, low_ref[...], preferred_element_type=f32)
    tail = jnp.concatenate(pieces(message_ref[2 * comps : 2 * comps + half]), axis=0)
    found = []
    for i, part in enumerate(summed(low, half)):
        high = jnp.dot(tail, high_ref[128 * i : 128 * i + 128], preferred_element_type=f32)
        found.append(part + (high[:half] + (high[half : 2 * half] + high[2 * half :])))
    return jnp.concatenate(found, axis=0)


def add_azimuthal(comps, halo, coefficient, first_row, out_ref):
    for z in range(4):
        spots = pl.ds(first_row + z, comps, stride=8)
        out_ref[spots] = out_ref[spots] + coefficient[first_row + z : first_row + z + 1] * halo[:, 128 * z : 128 * z + 128]


def pack_sides(comps, last, x_ref, where_ref, rad_ref, ax_ref, radup_ref, raddn_ref):
    @pl.when(where_ref[0] == 0)
    def _():
        ax_ref[0 : 2 * comps] = x_ref[pl.ds(3, 2 * comps, stride=4)]

    @pl.when(where_ref[0] != 0)
    def _():
        ax_ref[0 : 2 * comps] = x_ref[pl.ds(0, 2 * comps, stride=4)]

    ends = columns(x_ref[...])
    radup_ref[:, 0 : 8 * comps] = jnp.where(rad_ref[0] < last, ends[0:1], 0.0)
    raddn_ref[:, 0 : 8 * comps] = jnp.where(rad_ref[0] > 0, ends[1:2], 0.0)


def columns(x):
    row, lane = rows_of(), lanes_of()
    take = jnp.where(((row == 0) & (lane == 127)) | ((row == 1) & (lane == 0)), 1.0, 0.0)
    return lax.dot_general(take, x, (((1,), (1,)), ((), ())), precision=exact, preferred_element_type=f32)


def put_columns(lower, upper):
    n = lower.shape[1]
    row, lane = rows_of(), lanes_of()
    which = lax.broadcasted_iota(jnp.int32, (8, n), 0)
    both = jnp.where(which == 0, lower, jnp.where(which == 1, upper, 0.0))
    place = jnp.where(((row == 0) & (lane == 0)) | ((row == 1) & (lane == 127)), 1.0, 0.0)
    return lax.dot_general(both, place, (((0,), (0,)), ((), ())), precision=exact, preferred_element_type=f32)


def first_rest(comps, last, where_ref, rad_ref, a_ref, speeds_ref, flags_ref, up_ref, ax_ref, radup_ref, raddn_ref):
    p, _ = faces(speeds_ref, flags_ref)
    for c in range(comps):
        up_ref[4 * c : 4 * c + 4] = a_ref[8 * c + 4 : 8 * c + 8]
    up_ref[4 * comps :] = p[0]
    pack_sides(comps, last, a_ref, where_ref, rad_ref, ax_ref, radup_ref, raddn_ref)
    ax_ref[2 * comps : 2 * comps + 8] = pair_rows(p[1], 0, 4)
    radup_ref[:, 8 * comps :] = jnp.zeros((1, 128), f32)
    raddn_ref[:, 8 * comps :] = jnp.zeros((1, 128), f32)
    raddn_ref[:, 8 * comps : 8 * comps + 8] = jnp.where(rad_ref[0] > 0, columns(p[2])[1:2], 0.0)


def source(sections, x_ref, u_ref, growth_ref, transfer_ref, zones_ref, rate_ref, finish):
    def inner(k, s, x):
        term = transfer_ref[s] * ((x[k][1] - x[k][0]) if s + 1 < sections else -x[k][0])
        if k < 3:
            term = term + ((k + 1.0) * growth_ref[s]) * x[k + 1][0]
        return term

    def load(s):
        got = []
        for k in range(4):
            c = k * sections + s
            here = x_ref[8 * c : 8 * c + 8]
            got.append((here, x_ref[8 * c + 8 : 8 * c + 16] if s + 1 < sections else None))
        return got

    squares = jnp.zeros((8, 128), f32)
    product = jnp.zeros((8, 128), f32)
    for s in range(sections):
        x = load(s)
        for k in range(4):
            u = u_ref[k * sections + s].astype(f32)
            product = product + u * inner(k, s, x)
        squares = squares + u * u
    sigma = supersat_scale / (1.0 + crowding * squares)
    birth = jnp.zeros((8, 128), f32)
    for k in range(4):
        c = k * sections
        birth = birth + nucleus_moments[k] * x_ref[8 * c : 8 * c + 8]
    rate = jnp.zeros((8, 128), f32)
    for label in range(rate_ref.shape[0]):
        rate = jnp.where(zones_ref[...] == label, rate_ref[label], rate)
    slope = (-2.0 * crowding / supersat_scale) * sigma * sigma * (product + 2.0 * rate * sigma * birth)
    for s in range(sections):
        x = load(s)
        for k in range(4):
            c = k * sections + s
            term = sigma * inner(k, s, x)
            if k == 3:
                term = term + u_ref[c].astype(f32) * slope
            finish(c, x[k][0], term)


def first_local(
    sections,
    a_ref,
    u_ref,
    speeds_ref,
    flags_ref,
    zones_ref,
    growth_ref,
    transfer_ref,
    rate_ref,
    out_ref,
    dn_low_ref,
    dn_high_ref,
    up_low_ref,
    up_high_ref,
):
    p, q = faces(speeds_ref, flags_ref)
    local = Local(p, q)
    make_tables(p[0], False, dn_low_ref, dn_high_ref)
    make_tables(p[0], True, up_low_ref, up_high_ref)

    def finish(c, x, term):
        out_ref[8 * c : 8 * c + 8] = 0.5 * (x + local(x) + term)

    source(sections, a_ref, u_ref, growth_ref, transfer_ref, zones_ref, rate_ref, finish)


def second_local(
    sections,
    m_ref,
    a_ref,
    u_ref,
    below_ref,
    edge_ref,
    low_ref,
    high_ref,
    speeds_ref,
    flags_ref,
    zones_ref,
    growth_ref,
    transfer_ref,
    rate_ref,
    out_ref,
    bottom_ref,
):
    local = Local(*faces(speeds_ref, flags_ref))
    local.centre = local.centre + (edge_ref[3] - 1.0)

    def finish(c, x, term):
        out_ref[8 * c : 8 * c + 8] = 0.5 * a_ref[8 * c : 8 * c + 8] + (local(x) + term)

    source(sections, m_ref, u_ref, growth_ref, transfer_ref, zones_ref, rate_ref, finish)
    bottom_ref[...] = out_ref[...]
    add_azimuthal(4 * sections, decode(4 * sections, below_ref, low_ref, high_ref), edge_ref[0], 0, bottom_ref)


def from_below(c, below_ref):
    pair = below_ref[8 * (c // 2) : 8 * (c // 2) + 8]
    return pair if c % 2 == 0 else pltpu.roll(pair, 4, 0)


def from_above(c, above_ref):
    pair = above_ref[8 * (c // 2) : 8 * (c // 2) + 8]
    return pair if c % 2 == 1 else pltpu.roll(pair, 4, 0)


def add_axial(comps, scale, where_ref, axial, ax_ref, out_ref):
    several = jnp.concatenate([scale * axial] * (2 * comps // 8), axis=0)
    for start, index in ((3, 0), (0, 1)):

        @pl.when(where_ref[0] == index)
        def _():
            spots = pl.ds(start, 2 * comps, stride=4)
            out_ref[spots] = out_ref[spots] + several * ax_ref[0 : 2 * comps]


def first_top(
    comps,
    where_ref,
    part_ref,
    a_ref,
    above_ref,
    ax_ref,
    radlo_ref,
    radhi_ref,
    speeds_ref,
    flags_ref,
    m_ref,
    edge_ref,
    up_ref,
    bad_ref,
    dn_low_ref,
    dn_high_ref,
    up_low_ref,
    up_high_ref,
):
    p, q = faces(speeds_ref, flags_ref)
    row, lane = rows_of(), lanes_of()
    upper = above_ref[4 * comps :]
    make_tables(upper, True, up_low_ref, up_high_ref)
    make_tables(upper, False, dn_low_ref, dn_high_ref)
    bad_ref[...] = crowded(p[0]) + crowded(upper)
    hrad = put_columns(radlo_ref[...], radhi_ref[...])
    lower_half = where_ref[0] == 0
    p_azim = jnp.where(row >= 4, pltpu.roll(upper, 4, 0), 0.0)
    pairs = jnp.where(lower_half, ax_ref[2 * comps : 2 * comps + 8], 0.0)
    p_axial = jnp.where(row == 3, pairs[0:1], jnp.where(row == 7, pairs[1:2], 0.0))
    p_rad = jnp.where(lane == 127, hrad[8 * comps : 8 * comps + 8], 0.0)
    axial = jnp.where(lower_half, pairs, pair_rows(q[1], 0, 4))
    rad = jnp.where(lane == 0, q[2], p_rad)
    centre = p_azim + p_axial + p_rad
    edge_ref[0] = jnp.where(row >= 4, p_azim, q[0])
    edge_ref[1] = axial
    edge_ref[2] = rad
    edge_ref[3] = centre
    for c in range(comps):
        spots = slice(8 * c, 8 * c + 8)
        m_ref[spots] = part_ref[spots] + 0.5 * (
            p_azim * from_above(c, above_ref) + rad * hrad[spots] - centre * a_ref[spots]
        )
    add_axial(comps, 0.5, where_ref, axial, ax_ref, m_ref)
    encode(comps, m_ref, 4, up_low_ref, up_high_ref, up_ref)


def first_bottom(
    comps,
    last,
    where_ref,
    rad_ref,
    part_ref,
    below_ref,
    edge_ref,
    bad_ref,
    low_ref,
    high_ref,
    m_ref,
    dn_ref,
    ax_ref,
    radup_ref,
    raddn_ref,
    worse_ref,
):
    azim = jnp.where(rows_of() >= 4, 0.0, 0.5 * edge_ref[0])
    for c in range(comps):
        m_ref[8 * c : 8 * c + 8] = part_ref[8 * c : 8 * c + 8] + azim * from_below(c, below_ref)
    encode(comps, m_ref, 0, low_ref, high_ref, dn_ref)
    worse_ref[...] = bad_ref[...] + crowded(below_ref[4 * comps :])
    dn_ref[5 * comps // 2 :] = worse_ref[...]
    pack_sides(comps, last, m_ref, where_ref, rad_ref, ax_ref, radup_ref, raddn_ref)


def second_sides(
    comps, where_ref, part_ref, bottom_ref, ax_ref, radlo_ref, radhi_ref, edge_ref, base_ref, full_ref
):
    hrad = put_columns(radlo_ref[...], radhi_ref[...])
    rad = edge_ref[2]
    for c in range(comps):
        spots = slice(8 * c, 8 * c + 8)
        halo = rad * hrad[spots]
        base_ref[spots] = part_ref[spots] + halo
        full_ref[spots] = bottom_ref[spots] + halo
    for ref in (base_ref, full_ref):
        add_axial(comps, 1.0, where_ref, edge_ref[1], ax_ref, ref)


def second_top(comps, full_ref, above_ref, edge_ref, bad_ref, low_ref, high_ref, out_ref, again_ref):
    again_ref[0] = (jnp.max(bad_ref[...] + above_ref[5 * comps // 2 :]) > 0.0).astype(jnp.int32)
    out_ref[...] = full_ref[...]
    add_azimuthal(comps, decode(comps, above_ref, low_ref, high_ref), edge_ref[0], 4, out_ref)


SPACES = {
    "v": pl.BlockSpec(memory_space=pltpu.VMEM),
    "s": pl.BlockSpec(memory_space=pltpu.SMEM),
    "h": pl.BlockSpec(memory_space=pltpu.HBM),
}


def call(body, ins, outs, shapes, cost, *operands):
    return pl.pallas_call(
        body,
        in_specs=[SPACES[s] for s in ins],
        out_specs=[SPACES[s] for s in outs],
        out_shape=[s if isinstance(s, jax.ShapeDtypeStruct) else jax.ShapeDtypeStruct(s, f32) for s in shapes],
        cost_estimate=pl.CostEstimate(flops=cost, bytes_accessed=cost // 10, transcendentals=0),
        compiler_params=pltpu.CompilerParams(vmem_limit_bytes=32 * 1024 * 1024),
    )(*operands)


def shift(x, axis, step, wrap):
    size = lax.axis_size(axis)
    pairs = [(i, (i + step) % size) for i in range(size) if wrap or 0 <= i + step < size]
    return lax.ppermute(x, axis, pairs)


def sides(ax, radup, raddn):
    ax = lax.ppermute(ax, "axial", [(0, 1), (1, 0)])
    return ax, shift(radup, "rad", 1, True), shift(raddn, "rad", -1, True)


def shards(adjoint_final, state_start, state_middle, speeds, flags, zones, growth_rate, transfer_rate, nucleation_rate):
    shape = adjoint_final.shape
    moments, sections = shape[:2]
    comps = moments * sections
    assert moments == 4 and shape[2:] == (2, 4, 128) and comps % 4 == 0
    assert lax.axis_size("axial") == 2
    cells = 8 * comps
    half, rows = cells // 2, cells // 4
    a = adjoint_final.reshape(cells, 128)
    speeds2 = speeds.reshape(3, 8, 128)
    flags2 = flags.reshape(3, 8, 128)
    where = lax.axis_index("axial").reshape(1)
    place = (where, lax.axis_index("rad").reshape(1))
    last = lax.axis_size("rad") - 1
    rates = (zones.reshape(8, 128), growth_rate, transfer_rate, nucleation_rate)
    message = 5 * comps // 2
    tables = [jax.ShapeDtypeStruct((256, 512), bf16)] * 2

    keep = ((0, 2, 0), (0, -1, 0), (0, 0, 0), (0, 0, 0))
    after = ((comps, -1, 0), (0, -1, 0), (0, 0, 0), (0, 0, 0))
    dn = lax.pad(adjoint_final.reshape(comps, 2, 4, 128), 0.0, keep)
    dn = dn + lax.pad(speeds, 0.0, after) * lax.pad(flags, 0, after).astype(f32)
    above = shift(dn.reshape(half + 8, 128), "azim", -1, True)
    up, *edges = call(
        functools.partial(first_rest, comps, last),
        "ssvvv",
        "vvvv",
        [(half + 8, 128), (rows + 8, 128), (1, cells + 128), (1, cells + 128)],
        2_000_000,
        *place,
        a,
        speeds2,
        flags2,
    )
    below = shift(up, "azim", 1, True)
    edges = sides(*edges)
    part, *lower_tables = call(
        functools.partial(first_local, sections),
        "vvvvvsss",
        "vvvvv",
        [(cells, 128)] + 2 * tables,
        8_000_000,
        a,
        state_middle.reshape(comps, 8, 128),
        speeds2,
        flags2,
        *rates,
    )
    part, edge, up, bad, *upper_tables = call(
        functools.partial(first_top, comps),
        "s" + "v" * 8,
        "v" * 8,
        [(cells, 128), (4, 8, 128), (message, 128), (8, 128)] + 2 * tables,
        4_000_000,
        where,
        part,
        a,
        above,
        *edges,
        speeds2,
        flags2,
    )
    next_below = shift(up, "azim", 1, True)
    m, dn, *edges, bad = call(
        functools.partial(first_bottom, comps, last),
        "ss" + "v" * 6,
        "v" * 6,
        [(cells, 128), (message + 8, 128), (rows, 128), (1, cells), (1, cells), (8, 128)],
        10_000,
        *place,
        part,
        below,
        edge,
        bad,
        *lower_tables[:2],
    )
    next_above = shift(dn, "azim", -1, True)
    edges = sides(*edges)
    part, bottom = call(
        functools.partial(second_local, sections),
        "v" * 10 + "sss",
        "vv",
        [(cells, 128), (cells, 128)],
        300_000_000,
        m,
        a,
        state_start.reshape(comps, 8, 128),
        next_below,
        edge,
        *lower_tables[2:],
        speeds2,
        flags2,
        *rates,
    )
    base, full = call(
        functools.partial(second_sides, comps),
        "s" + "v" * 6,
        "vv",
        [(cells, 128), (cells, 128)],
        10_000,
        where,
        part,
        bottom,
        *edges,
        edge,
    )

    out, again = call(
        functools.partial(second_top, comps),
        "vvvvvv",
        "vs",
        [(cells, 128), jax.ShapeDtypeStruct((1,), jnp.int32)],
        1_000_000,
        full,
        next_above,
        edge,
        bad,
        *upper_tables[:2],
    )

    def whole():
        rows_ = m.reshape(comps, 2, 4, 128)
        halo = jnp.stack([shift(rows_[:, 1], "azim", 1, True), shift(rows_[:, 0], "azim", -1, True)], axis=1)
        return base + (edge[0].reshape(1, 2, 4, 128) * halo).reshape(cells, 128)

    again = again[0]
    if lax.axis_size("azim") != 4:
        again = lax.pmax(again.astype(f32), "azim").astype(jnp.int32)
    return lax.cond(again > 0, whole, lambda: out).reshape(shape)


def solution(mesh):
    field = P(None, None, "azim", "axial", "rad")
    faces_spec = P(None, "azim", "axial", "rad")
    return jax.shard_map(
        shards,
        mesh=mesh,
        in_specs=(field, field, field, faces_spec, faces_spec, P("azim", "axial", "rad"), P(), P(), P()),
        out_specs=field,
        check_vma=False,
    )
```

```python
import functools

import jax
import jax.numpy as jnp
from jax import lax
from jax.experimental import pallas as pl
from jax.experimental.pallas import tpu as pltpu
from jax.sharding import PartitionSpec as P

supersat_scale = 1.5
crowding = 0.02
nucleus_moments = (1.0, 0.5, 0.25, 0.125)
f32 = jnp.float32
bf16 = jnp.bfloat16
exact = lax.Precision.HIGHEST

slots = 320
extra = slots - 256


def rows_of():
    return lax.broadcasted_iota(jnp.int32, (8, 128), 0)


def lanes_of():
    return lax.broadcasted_iota(jnp.int32, (8, 128), 1)


def faces(speeds_ref, flags_ref):
    p, q = [], []
    for d in range(3):
        speed, upwind = speeds_ref[d], flags_ref[d].astype(f32)
        p.append(speed * upwind)
        q.append(speed * (1.0 - upwind))
    return p, q


class Local:
    def __init__(self, p, q):
        row, lane = rows_of(), lanes_of()
        z, top = row % 4, row >= 4
        self.azim = jnp.where(top, q[0], pltpu.roll(p[0], 4, 0))
        self.ax_up = jnp.where(z == 3, 0.0, pltpu.roll(p[1], 7, 0))
        self.ax_dn = jnp.where(z == 0, 0.0, q[1])
        self.rad_up = jnp.where(lane == 127, 0.0, pltpu.roll(p[2], 127, 1))
        self.rad_dn = jnp.where(lane == 0, 0.0, q[2])
        self.centre = self.azim + self.ax_up + q[1] + self.rad_up + q[2] + jnp.where(top, 0.0, q[0])

    def __call__(self, x):
        return (
            self.azim * pltpu.roll(x, 4, 0)
            + self.ax_up * pltpu.roll(x, 7, 0)
            + self.ax_dn * pltpu.roll(x, 1, 0)
            + self.rad_up * pltpu.roll(x, 127, 1)
            + self.rad_dn * pltpu.roll(x, 1, 1)
            - self.centre * x
        )


def pair_rows(x, first, second):
    return jnp.where(
        rows_of() % 2 == 0,
        jnp.broadcast_to(x[first : first + 1], (8, 128)),
        jnp.broadcast_to(x[second : second + 1], (8, 128)),
    )


def make_tables(p, where_zero, low_ref, high_ref):
    row, lane = rows_of(), lanes_of()
    taken = (p == 0.0) if where_zero else (p != 0.0)
    one = jnp.where(taken & (row < 4), 1.0, 0.0)
    before = lax.broadcasted_iota(jnp.int32, (128, 128), 0) < lax.broadcasted_iota(jnp.int32, (128, 128), 1)
    inside = jnp.dot(one.astype(bf16), jnp.where(before, 1.0, 0.0).astype(bf16), preferred_element_type=f32)
    total = jnp.sum(one, axis=1, keepdims=True)
    base = jnp.zeros((8, 1), f32)
    for step in (1, 2, 3):
        base = base + jnp.where(
            lax.broadcasted_iota(jnp.int32, (8, 1), 0) >= step, jnp.roll(total, step, axis=0), 0.0
        )
    slot = jnp.where(one > 0.0, inside + base, -1.0).astype(jnp.int32)
    here = lax.broadcasted_iota(jnp.int32, (128, 128), 0)
    first = jnp.where(here < extra, here + 256, -2)
    second = jnp.where(here >= extra, here + (256 - extra), -2)
    for z in range(4):
        cells = slice(128 * z, 128 * z + 128)
        want = jnp.broadcast_to(slot[z : z + 1], (128, 128))
        for ref, start, names in ((low_ref, 0, here), (low_ref, 128, here + 128), (high_ref, 0, first), (high_ref, 128, second)):
            ref[start : start + 128, cells] = jnp.where(names == want, 1.0, 0.0).astype(bf16)


def crowded(p):
    taken = jnp.where((rows_of() < 4) & (p != 0.0), 1.0, 0.0)
    count = jnp.sum(jnp.sum(taken, axis=1, keepdims=True), axis=0, keepdims=True)
    count = jnp.broadcast_to(count, (8, 128))
    return jnp.where(jnp.maximum(count, 512.0 - count) > slots, 1.0, 0.0)


def pieces(x):
    high = x.astype(bf16)
    rest = x - high.astype(f32)
    middle = rest.astype(bf16)
    return high, middle, (rest - middle.astype(f32)).astype(bf16)


def stacked(x, half):
    return jnp.concatenate([part[half * i : half * i + half] for i in range(2) for part in pieces(x)], axis=0)


def summed(x, half):
    parts = [x[half * i : half * i + half] for i in range(6)]
    return [parts[3 * i] + (parts[3 * i + 1] + parts[3 * i + 2]) for i in range(2)]


def encode(comps, x_ref, first_row, low_ref, high_ref, message_ref):
    half = comps // 2
    x = jnp.concatenate(
        [stacked(x_ref[pl.ds(first_row + z, comps, stride=8)], half) for z in range(4)], axis=1
    )
    over = (((1,), (1,)), ((), ()))
    low = lax.dot_general(x, low_ref[...], over, preferred_element_type=f32)
    high = [
        lax.dot_general(
            x[3 * half * i : 3 * half * (i + 1)], high_ref[128 * i : 128 * i + 128], over, preferred_element_type=f32
        )
        for i in range(2)
    ]
    tail = jnp.zeros((half, 128), f32)
    for i, part in enumerate(summed(low, half)):
        message_ref[half * i : half * i + half] = part[:, :128]
        message_ref[comps + half * i : comps + half * i + half] = part[:, 128:]
    for part in high:
        tail = tail + (part[:half] + (part[half : 2 * half] + part[2 * half :]))
    message_ref[2 * comps : 2 * comps + half] = tail


def decode(comps, message_ref, low_ref, high_ref):
    half = comps // 2
    x = jnp.concatenate([stacked(message_ref[comps * i : comps * i + comps], half) for i in range(2)], axis=1)
    low = jnp.dot(x, low_ref[...], preferred_element_type=f32)
    tail = jnp.concatenate(pieces(message_ref[2 * comps : 2 * comps + half]), axis=0)
    found = []
    for i, part in enumerate(summed(low, half)):
        high = jnp.dot(tail, high_ref[128 * i : 128 * i + 128], preferred_element_type=f32)
        found.append(part + (high[:half] + (high[half : 2 * half] + high[2 * half :])))
    return jnp.concatenate(found, axis=0)


def add_azimuthal(comps, halo, coefficient, first_row, out_ref):
    for z in range(4):
        spots = pl.ds(first_row + z, comps, stride=8)
        out_ref[spots] = out_ref[spots] + coefficient[first_row + z : first_row + z + 1] * halo[:, 128 * z : 128 * z + 128]


def pack_sides(comps, last, x_ref, where_ref, rad_ref, ax_ref, radup_ref, raddn_ref):
    @pl.when(where_ref[0] == 0)
    def _():
        ax_ref[0 : 2 * comps] = x_ref[pl.ds(3, 2 * comps, stride=4)]

    @pl.when(where_ref[0] != 0)
    def _():
        ax_ref[0 : 2 * comps] = x_ref[pl.ds(0, 2 * comps, stride=4)]

    ends = columns(x_ref[...])
    radup_ref[:, 0 : 8 * comps] = jnp.where(rad_ref[0] < last, ends[0:1], 0.0)
    raddn_ref[:, 0 : 8 * comps] = jnp.where(rad_ref[0] > 0, ends[1:2], 0.0)


def columns(x):
    row, lane = rows_of(), lanes_of()
    take = jnp.where(((row == 0) & (lane == 127)) | ((row == 1) & (lane == 0)), 1.0, 0.0)
    return lax.dot_general(take, x, (((1,), (1,)), ((), ())), precision=exact, preferred_element_type=f32)


def put_columns(lower, upper):
    n = lower.shape[1]
    row, lane = rows_of(), lanes_of()
    which = lax.broadcasted_iota(jnp.int32, (8, n), 0)
    both = jnp.where(which == 0, lower, jnp.where(which == 1, upper, 0.0))
    place = jnp.where(((row == 0) & (lane == 0)) | ((row == 1) & (lane == 127)), 1.0, 0.0)
    return lax.dot_general(both, place, (((0,), (0,)), ((), ())), precision=exact, preferred_element_type=f32)


def first_rest(comps, last, where_ref, rad_ref, a_ref, speeds_ref, flags_ref, up_ref, ax_ref, radup_ref, raddn_ref):
    p, _ = faces(speeds_ref, flags_ref)
    for c in range(comps):
        up_ref[4 * c : 4 * c + 4] = a_ref[8 * c + 4 : 8 * c + 8]
    up_ref[4 * comps :] = p[0]
    pack_sides(comps, last, a_ref, where_ref, rad_ref, ax_ref, radup_ref, raddn_ref)
    ax_ref[2 * comps : 2 * comps + 8] = pair_rows(p[1], 0, 4)
    radup_ref[:, 8 * comps :] = jnp.zeros((1, 128), f32)
    raddn_ref[:, 8 * comps :] = jnp.zeros((1, 128), f32)
    raddn_ref[:, 8 * comps : 8 * comps + 8] = jnp.where(rad_ref[0] > 0, columns(p[2])[1:2], 0.0)


def source(sections, x_ref, u_ref, growth_ref, transfer_ref, zones_ref, rate_ref, finish):
    def inner(k, s, x):
        term = transfer_ref[s] * ((x[k][1] - x[k][0]) if s + 1 < sections else -x[k][0])
        if k < 3:
            term = term + ((k + 1.0) * growth_ref[s]) * x[k + 1][0]
        return term

    def load(s):
        got = []
        for k in range(4):
            c = k * sections + s
            here = x_ref[8 * c : 8 * c + 8]
            got.append((here, x_ref[8 * c + 8 : 8 * c + 16] if s + 1 < sections else None))
        return got

    squares = jnp.zeros((8, 128), f32)
    product = jnp.zeros((8, 128), f32)
    for s in range(sections):
        x = load(s)
        for k in range(4):
            u = u_ref[k * sections + s].astype(f32)
            product = product + u * inner(k, s, x)
        squares = squares + u * u
    sigma = supersat_scale / (1.0 + crowding * squares)
    birth = jnp.zeros((8, 128), f32)
    for k in range(4):
        c = k * sections
        birth = birth + nucleus_moments[k] * x_ref[8 * c : 8 * c + 8]
    rate = jnp.zeros((8, 128), f32)
    for label in range(rate_ref.shape[0]):
        rate = jnp.where(zones_ref[...] == label, rate_ref[label], rate)
    slope = (-2.0 * crowding / supersat_scale) * sigma * sigma * (product + 2.0 * rate * sigma * birth)
    for s in range(sections):
        x = load(s)
        for k in range(4):
            c = k * sections + s
            term = sigma * inner(k, s, x)
            if k == 3:
                term = term + u_ref[c].astype(f32) * slope
            finish(c, x[k][0], term)


def first_local(
    sections,
    a_ref,
    u_ref,
    speeds_ref,
    flags_ref,
    zones_ref,
    growth_ref,
    transfer_ref,
    rate_ref,
    out_ref,
    dn_low_ref,
    dn_high_ref,
    up_low_ref,
    up_high_ref,
):
    p, q = faces(speeds_ref, flags_ref)
    local = Local(p, q)
    make_tables(p[0], False, dn_low_ref, dn_high_ref)
    make_tables(p[0], True, up_low_ref, up_high_ref)

    def finish(c, x, term):
        out_ref[8 * c : 8 * c + 8] = 0.5 * (x + local(x) + term)

    source(sections, a_ref, u_ref, growth_ref, transfer_ref, zones_ref, rate_ref, finish)


def second_local(
    sections,
    m_ref,
    a_ref,
    u_ref,
    below_ref,
    edge_ref,
    low_ref,
    high_ref,
    speeds_ref,
    flags_ref,
    zones_ref,
    growth_ref,
    transfer_ref,
    rate_ref,
    out_ref,
    bottom_ref,
):
    local = Local(*faces(speeds_ref, flags_ref))
    local.centre = local.centre + (edge_ref[3] - 1.0)

    def finish(c, x, term):
        out_ref[8 * c : 8 * c + 8] = 0.5 * a_ref[8 * c : 8 * c + 8] + (local(x) + term)

    source(sections, m_ref, u_ref, growth_ref, transfer_ref, zones_ref, rate_ref, finish)
    bottom_ref[...] = out_ref[...]
    add_azimuthal(4 * sections, decode(4 * sections, below_ref, low_ref, high_ref), edge_ref[0], 0, bottom_ref)


def from_below(c, below_ref):
    pair = below_ref[8 * (c // 2) : 8 * (c // 2) + 8]
    return pair if c % 2 == 0 else pltpu.roll(pair, 4, 0)


def from_above(c, above_ref):
    pair = above_ref[8 * (c // 2) : 8 * (c // 2) + 8]
    return pair if c % 2 == 1 else pltpu.roll(pair, 4, 0)


def add_axial(comps, scale, where_ref, axial, ax_ref, out_ref):
    several = jnp.concatenate([scale * axial] * (2 * comps // 8), axis=0)
    for start, index in ((3, 0), (0, 1)):

        @pl.when(where_ref[0] == index)
        def _():
            spots = pl.ds(start, 2 * comps, stride=4)
            out_ref[spots] = out_ref[spots] + several * ax_ref[0 : 2 * comps]


def first_top(
    comps,
    where_ref,
    part_ref,
    a_ref,
    above_ref,
    ax_ref,
    radlo_ref,
    radhi_ref,
    speeds_ref,
    flags_ref,
    m_ref,
    edge_ref,
    up_ref,
    bad_ref,
    dn_low_ref,
    dn_high_ref,
    up_low_ref,
    up_high_ref,
):
    p, q = faces(speeds_ref, flags_ref)
    row, lane = rows_of(), lanes_of()
    upper = above_ref[4 * comps :]
    make_tables(upper, True, up_low_ref, up_high_ref)
    make_tables(upper, False, dn_low_ref, dn_high_ref)
    bad_ref[...] = crowded(p[0]) + crowded(upper)
    hrad = put_columns(radlo_ref[...], radhi_ref[...])
    lower_half = where_ref[0] == 0
    p_azim = jnp.where(row >= 4, pltpu.roll(upper, 4, 0), 0.0)
    pairs = jnp.where(lower_half, ax_ref[2 * comps : 2 * comps + 8], 0.0)
    p_axial = jnp.where(row == 3, pairs[0:1], jnp.where(row == 7, pairs[1:2], 0.0))
    p_rad = jnp.where(lane == 127, hrad[8 * comps : 8 * comps + 8], 0.0)
    axial = jnp.where(lower_half, pairs, pair_rows(q[1], 0, 4))
    rad = jnp.where(lane == 0, q[2], p_rad)
    centre = p_azim + p_axial + p_rad
    edge_ref[0] = jnp.where(row >= 4, p_azim, q[0])
    edge_ref[1] = axial
    edge_ref[2] = rad
    edge_ref[3] = centre
    for c in range(comps):
        spots = slice(8 * c, 8 * c + 8)
        m_ref[spots] = part_ref[spots] + 0.5 * (
            p_azim * from_above(c, above_ref) + rad * hrad[spots] - centre * a_ref[spots]
        )
    add_axial(comps, 0.5, where_ref, axial, ax_ref, m_ref)
    encode(comps, m_ref, 4, up_low_ref, up_high_ref, up_ref)


def first_bottom(
    comps,
    last,
    where_ref,
    rad_ref,
    part_ref,
    below_ref,
    edge_ref,
    bad_ref,
    low_ref,
    high_ref,
    m_ref,
    dn_ref,
    ax_ref,
    radup_ref,
    raddn_ref,
    worse_ref,
):
    azim = jnp.where(rows_of() >= 4, 0.0, 0.5 * edge_ref[0])
    for c in range(comps):
        m_ref[8 * c : 8 * c + 8] = part_ref[8 * c : 8 * c + 8] + azim * from_below(c, below_ref)
    encode(comps, m_ref, 0, low_ref, high_ref, dn_ref)
    worse_ref[...] = bad_ref[...] + crowded(below_ref[4 * comps :])
    dn_ref[5 * comps // 2 :] = worse_ref[...]
    pack_sides(comps, last, m_ref, where_ref, rad_ref, ax_ref, radup_ref, raddn_ref)


def second_rest(
    comps,
    parts,
    where_ref,
    bottom_ref,
    above_ref,
    ax_ref,
    radlo_ref,
    radhi_ref,
    edge_ref,
    bad_ref,
    low_ref,
    high_ref,
    out_ref,
    again_ref,
    done_ref,
    sems,
):
    again_ref[0] = (jnp.max(bad_ref[...] + above_ref[5 * comps // 2 :]) > 0.0).astype(jnp.int32)
    hrad = put_columns(radlo_ref[...], radhi_ref[...])
    halo = decode(comps, above_ref, low_ref, high_ref)
    azim, rad = edge_ref[0], edge_ref[2]
    for c in range(comps):
        spots = slice(8 * c, 8 * c + 8)
        done_ref[spots] = bottom_ref[spots] + rad * hrad[spots]
    add_axial(comps, 1.0, where_ref, edge_ref[1], ax_ref, done_ref)
    size = comps // parts
    made = []
    for i in range(parts):
        for z in range(4):
            some = pl.ds(8 * size * i + 4 + z, size, stride=8)
            done_ref[some] = (
                done_ref[some] + azim[4 + z : 5 + z] * halo[size * i : size * i + size, 128 * z : 128 * z + 128]
            )
        spots = pl.ds(8 * size * i, 8 * size)
        made.append(pltpu.make_async_copy(done_ref.at[spots], out_ref.at[spots], sems.at[i]))
        made[-1].start()
    for copy in made:
        copy.wait()


SPACES = {
    "v": pl.BlockSpec(memory_space=pltpu.VMEM),
    "s": pl.BlockSpec(memory_space=pltpu.SMEM),
    "h": pl.BlockSpec(memory_space=pltpu.HBM),
}


def call(body, ins, outs, shapes, cost, *operands, scratch=()):
    return pl.pallas_call(
        body,
        in_specs=[SPACES[s] for s in ins],
        out_specs=[SPACES[s] for s in outs],
        out_shape=[jax.ShapeDtypeStruct(s, f32) if isinstance(s, tuple) else s for s in shapes],
        scratch_shapes=scratch,
        cost_estimate=pl.CostEstimate(flops=cost, bytes_accessed=cost // 10, transcendentals=0),
        compiler_params=pltpu.CompilerParams(vmem_limit_bytes=32 * 1024 * 1024),
    )(*operands)


def shift(x, axis, step, wrap):
    size = lax.axis_size(axis)
    pairs = [(i, (i + step) % size) for i in range(size) if wrap or 0 <= i + step < size]
    return lax.ppermute(x, axis, pairs)


def sides(ax, radup, raddn):
    ax = lax.ppermute(ax, "axial", [(0, 1), (1, 0)])
    return ax, shift(radup, "rad", 1, True), shift(raddn, "rad", -1, True)


def shards(adjoint_final, state_start, state_middle, speeds, flags, zones, growth_rate, transfer_rate, nucleation_rate):
    shape = adjoint_final.shape
    moments, sections = shape[:2]
    comps = moments * sections
    assert moments == 4 and shape[2:] == (2, 4, 128) and comps % 4 == 0
    assert lax.axis_size("axial") == 2
    cells = 8 * comps
    half, rows = cells // 2, cells // 4
    a = adjoint_final.reshape(cells, 128)
    speeds2 = speeds.reshape(3, 8, 128)
    flags2 = flags.reshape(3, 8, 128)
    where = lax.axis_index("axial").reshape(1)
    place = (where, lax.axis_index("rad").reshape(1))
    last = lax.axis_size("rad") - 1
    rates = (zones.reshape(8, 128), growth_rate, transfer_rate, nucleation_rate)
    message = 5 * comps // 2
    tables = [jax.ShapeDtypeStruct((256, 512), bf16)] * 2

    keep = ((0, 2, 0), (0, -1, 0), (0, 0, 0), (0, 0, 0))
    after = ((comps, -1, 0), (0, -1, 0), (0, 0, 0), (0, 0, 0))
    dn = lax.pad(adjoint_final.reshape(comps, 2, 4, 128), 0.0, keep)
    dn = dn + lax.pad(speeds, 0.0, after) * lax.pad(flags, 0, after).astype(f32)
    above = shift(dn.reshape(half + 8, 128), "azim", -1, True)
    up, *edges = call(
        functools.partial(first_rest, comps, last),
        "ssvvv",
        "vvvv",
        [(half + 8, 128), (rows + 8, 128), (1, cells + 128), (1, cells + 128)],
        2_000_000,
        *place,
        a,
        speeds2,
        flags2,
    )
    below = shift(up, "azim", 1, True)
    edges = sides(*edges)
    part, *lower_tables = call(
        functools.partial(first_local, sections),
        "vvvvvsss",
        "vvvvv",
        [(cells, 128)] + 2 * tables,
        8_000_000,
        a,
        state_middle.reshape(comps, 8, 128),
        speeds2,
        flags2,
        *rates,
    )
    part, edge, up, bad, *upper_tables = call(
        functools.partial(first_top, comps),
        "s" + "v" * 8,
        "v" * 8,
        [(cells, 128), (4, 8, 128), (message, 128), (8, 128)] + 2 * tables,
        4_000_000,
        where,
        part,
        a,
        above,
        *edges,
        speeds2,
        flags2,
    )
    next_below = shift(up, "azim", 1, True)
    m, dn, *edges, bad = call(
        functools.partial(first_bottom, comps, last),
        "ss" + "v" * 6,
        "v" * 6,
        [(cells, 128), (message + 8, 128), (rows, 128), (1, cells), (1, cells), (8, 128)],
        10_000,
        *place,
        part,
        below,
        edge,
        bad,
        *lower_tables[:2],
    )
    next_above = shift(dn, "azim", -1, True)
    ax, radlo, radhi = sides(*edges)
    part, bottom = call(
        functools.partial(second_local, sections),
        "v" * 10 + "sss",
        "vv",
        [(cells, 128), (cells, 128)],
        300_000_000,
        m,
        a,
        state_start.reshape(comps, 8, 128),
        next_below,
        edge,
        *lower_tables[2:],
        speeds2,
        flags2,
        *rates,
    )
    out, again = call(
        functools.partial(second_rest, comps, 4),
        "s" + "v" * 9,
        "hs",
        [pltpu.HBM((cells, 128), f32), jax.ShapeDtypeStruct((1,), jnp.int32)],
        1_000_000,
        where,
        bottom,
        next_above,
        ax,
        radlo,
        radhi,
        edge,
        bad,
        *upper_tables[:2],
        scratch=[pltpu.VMEM((cells, 128), f32), pltpu.SemaphoreType.DMA((4,))],
    )

    def whole():
        rows_ = m.reshape(comps, 2, 4, 128)
        halo = jnp.stack([shift(rows_[:, 1], "azim", 1, True), shift(rows_[:, 0], "azim", -1, True)], axis=1)
        azimuthal = (edge[0].reshape(1, 2, 4, 128) * halo).reshape(comps, 8, 128)
        row, lane = jnp.arange(8).reshape(1, 8, 1), jnp.arange(128).reshape(1, 1, 128)
        two = jnp.repeat(ax.reshape(comps, 2, 128) * edge[1, :2], 4, axis=1)
        axial = jnp.where(row % 4 == 3 * (1 - where[0]), two, 0.0)
        lower, upper = radlo.reshape(comps, 8, 1), radhi.reshape(comps, 8, 1)
        radial = edge[2] * jnp.where(lane == 0, lower, jnp.where(lane == 127, upper, 0.0))
        return part + (azimuthal + axial + radial).reshape(cells, 128)

    again = again[0]
    if lax.axis_size("azim") != 4:
        again = lax.pmax(again.astype(f32), "azim").astype(jnp.int32)
    return lax.switch(again, (lambda: out, whole)).reshape(shape)


def solution(mesh):
    field = P(None, None, "azim", "axial", "rad")
    faces_spec = P(None, "azim", "axial", "rad")
    return jax.shard_map(
        shards,
        mesh=mesh,
        in_specs=(field, field, field, faces_spec, faces_spec, P("azim", "axial", "rad"), P(), P(), P()),
        out_specs=field,
        check_vma=False,
    )
```

```python
import functools

import jax
import jax.numpy as jnp
from jax import lax
from jax.experimental import pallas as pl
from jax.experimental.pallas import tpu as pltpu
from jax.sharding import PartitionSpec as P

supersat_scale = 1.5
crowding = 0.02
nucleus_moments = (1.0, 0.5, 0.25, 0.125)
f32 = jnp.float32
bf16 = jnp.bfloat16
exact = lax.Precision.HIGHEST

slots = 320
extra = slots - 256


def rows_of():
    return lax.broadcasted_iota(jnp.int32, (8, 128), 0)


def lanes_of():
    return lax.broadcasted_iota(jnp.int32, (8, 128), 1)


def faces(speeds_ref, flags_ref):
    p, q = [], []
    for d in range(3):
        speed, upwind = speeds_ref[d], flags_ref[d].astype(f32)
        p.append(speed * upwind)
        q.append(speed * (1.0 - upwind))
    return p, q


class Local:
    def __init__(self, p, q):
        row, lane = rows_of(), lanes_of()
        z, top = row % 4, row >= 4
        self.azim = jnp.where(top, q[0], pltpu.roll(p[0], 4, 0))
        self.ax_up = jnp.where(z == 3, 0.0, pltpu.roll(p[1], 7, 0))
        self.ax_dn = jnp.where(z == 0, 0.0, q[1])
        self.rad_up = jnp.where(lane == 127, 0.0, pltpu.roll(p[2], 127, 1))
        self.rad_dn = jnp.where(lane == 0, 0.0, q[2])
        self.centre = self.azim + self.ax_up + q[1] + self.rad_up + q[2] + jnp.where(top, 0.0, q[0])

    def __call__(self, x):
        return (
            self.azim * pltpu.roll(x, 4, 0)
            + self.ax_up * pltpu.roll(x, 7, 0)
            + self.ax_dn * pltpu.roll(x, 1, 0)
            + self.rad_up * pltpu.roll(x, 127, 1)
            + self.rad_dn * pltpu.roll(x, 1, 1)
            - self.centre * x
        )


def pair_rows(x, first, second):
    return jnp.where(
        rows_of() % 2 == 0,
        jnp.broadcast_to(x[first : first + 1], (8, 128)),
        jnp.broadcast_to(x[second : second + 1], (8, 128)),
    )


def make_tables(p, where_zero, low_ref, high_ref):
    row, lane = rows_of(), lanes_of()
    taken = (p == 0.0) if where_zero else (p != 0.0)
    one = jnp.where(taken & (row < 4), 1.0, 0.0)
    before = lax.broadcasted_iota(jnp.int32, (128, 128), 0) < lax.broadcasted_iota(jnp.int32, (128, 128), 1)
    inside = jnp.dot(one.astype(bf16), jnp.where(before, 1.0, 0.0).astype(bf16), preferred_element_type=f32)
    total = jnp.sum(one, axis=1, keepdims=True)
    base = jnp.zeros((8, 1), f32)
    for step in (1, 2, 3):
        base = base + jnp.where(
            lax.broadcasted_iota(jnp.int32, (8, 1), 0) >= step, jnp.roll(total, step, axis=0), 0.0
        )
    slot = jnp.where(one > 0.0, inside + base, -1.0).astype(jnp.int32)
    here = lax.broadcasted_iota(jnp.int32, (128, 128), 0)
    first = jnp.where(here < extra, here + 256, -2)
    second = jnp.where(here >= extra, here + (256 - extra), -2)
    for z in range(4):
        cells = slice(128 * z, 128 * z + 128)
        want = jnp.broadcast_to(slot[z : z + 1], (128, 128))
        for ref, start, names in ((low_ref, 0, here), (low_ref, 128, here + 128), (high_ref, 0, first), (high_ref, 128, second)):
            ref[start : start + 128, cells] = jnp.where(names == want, 1.0, 0.0).astype(bf16)


def crowded(p):
    taken = jnp.where((rows_of() < 4) & (p != 0.0), 1.0, 0.0)
    count = jnp.sum(jnp.sum(taken, axis=1, keepdims=True), axis=0, keepdims=True)
    count = jnp.broadcast_to(count, (8, 128))
    return jnp.where(jnp.maximum(count, 512.0 - count) > slots, 1.0, 0.0)


def pieces(x):
    high = x.astype(bf16)
    rest = x - high.astype(f32)
    middle = rest.astype(bf16)
    return high, middle, (rest - middle.astype(f32)).astype(bf16)


def stacked(x, half):
    return jnp.concatenate([part[half * i : half * i + half] for i in range(2) for part in pieces(x)], axis=0)


def summed(x, half):
    parts = [x[half * i : half * i + half] for i in range(6)]
    return [parts[3 * i] + (parts[3 * i + 1] + parts[3 * i + 2]) for i in range(2)]


def encode(comps, x_ref, first_row, low_ref, high_ref, message_ref):
    half = comps // 2
    x = jnp.concatenate(
        [stacked(x_ref[pl.ds(first_row + z, comps, stride=8)], half) for z in range(4)], axis=1
    )
    over = (((1,), (1,)), ((), ()))
    low = lax.dot_general(x, low_ref[...], over, preferred_element_type=f32)
    high = [
        lax.dot_general(
            x[3 * half * i : 3 * half * (i + 1)], high_ref[128 * i : 128 * i + 128], over, preferred_element_type=f32
        )
        for i in range(2)
    ]
    tail = jnp.zeros((half, 128), f32)
    for i, part in enumerate(summed(low, half)):
        message_ref[half * i : half * i + half] = part[:, :128]
        message_ref[comps + half * i : comps + half * i + half] = part[:, 128:]
    for part in high:
        tail = tail + (part[:half] + (part[half : 2 * half] + part[2 * half :]))
    message_ref[2 * comps : 2 * comps + half] = tail


def decode(comps, message_ref, low_ref, high_ref):
    half = comps // 2
    x = jnp.concatenate([stacked(message_ref[comps * i : comps * i + comps], half) for i in range(2)], axis=1)
    low = jnp.dot(x, low_ref[...], preferred_element_type=f32)
    tail = jnp.concatenate(pieces(message_ref[2 * comps : 2 * comps + half]), axis=0)
    found = []
    for i, part in enumerate(summed(low, half)):
        high = jnp.dot(tail, high_ref[128 * i : 128 * i + 128], preferred_element_type=f32)
        found.append(part + (high[:half] + (high[half : 2 * half] + high[2 * half :])))
    return jnp.concatenate(found, axis=0)


def add_azimuthal(comps, halo, coefficient, first_row, out_ref):
    for z in range(4):
        spots = pl.ds(first_row + z, comps, stride=8)
        out_ref[spots] = out_ref[spots] + coefficient[first_row + z : first_row + z + 1] * halo[:, 128 * z : 128 * z + 128]


def pack_sides(comps, last, x_ref, where_ref, rad_ref, ax_ref, radup_ref, raddn_ref):
    @pl.when(where_ref[0] == 0)
    def _():
        ax_ref[0 : 2 * comps] = x_ref[pl.ds(3, 2 * comps, stride=4)]

    @pl.when(where_ref[0] != 0)
    def _():
        ax_ref[0 : 2 * comps] = x_ref[pl.ds(0, 2 * comps, stride=4)]

    ends = columns(x_ref[...])
    radup_ref[:, 0 : 8 * comps] = jnp.where(rad_ref[0] < last, ends[0:1], 0.0)
    raddn_ref[:, 0 : 8 * comps] = jnp.where(rad_ref[0] > 0, ends[1:2], 0.0)


def columns(x):
    row, lane = rows_of(), lanes_of()
    take = jnp.where(((row == 0) & (lane == 127)) | ((row == 1) & (lane == 0)), 1.0, 0.0)
    return lax.dot_general(take, x, (((1,), (1,)), ((), ())), precision=exact, preferred_element_type=f32)


def put_columns(lower, upper):
    n = lower.shape[1]
    row, lane = rows_of(), lanes_of()
    which = lax.broadcasted_iota(jnp.int32, (8, n), 0)
    both = jnp.where(which == 0, lower, jnp.where(which == 1, upper, 0.0))
    place = jnp.where(((row == 0) & (lane == 0)) | ((row == 1) & (lane == 127)), 1.0, 0.0)
    return lax.dot_general(both, place, (((0,), (0,)), ((), ())), precision=exact, preferred_element_type=f32)


def first_rest(comps, last, where_ref, rad_ref, a_ref, speeds_ref, flags_ref, up_ref, ax_ref, radup_ref, raddn_ref):
    p, _ = faces(speeds_ref, flags_ref)
    for c in range(comps):
        up_ref[4 * c : 4 * c + 4] = a_ref[8 * c + 4 : 8 * c + 8]
    up_ref[4 * comps :] = p[0]
    pack_sides(comps, last, a_ref, where_ref, rad_ref, ax_ref, radup_ref, raddn_ref)
    ax_ref[2 * comps : 2 * comps + 8] = pair_rows(p[1], 0, 4)
    radup_ref[:, 8 * comps :] = jnp.zeros((1, 128), f32)
    raddn_ref[:, 8 * comps :] = jnp.zeros((1, 128), f32)
    raddn_ref[:, 8 * comps : 8 * comps + 8] = jnp.where(rad_ref[0] > 0, columns(p[2])[1:2], 0.0)


def source(sections, x_ref, u_ref, growth_ref, transfer_ref, zones_ref, rate_ref, finish):
    def inner(k, s, x):
        term = transfer_ref[s] * ((x[k][1] - x[k][0]) if s + 1 < sections else -x[k][0])
        if k < 3:
            term = term + ((k + 1.0) * growth_ref[s]) * x[k + 1][0]
        return term

    def load(s):
        got = []
        for k in range(4):
            c = k * sections + s
            here = x_ref[8 * c : 8 * c + 8]
            got.append((here, x_ref[8 * c + 8 : 8 * c + 16] if s + 1 < sections else None))
        return got

    squares = jnp.zeros((8, 128), f32)
    product = jnp.zeros((8, 128), f32)
    for s in range(sections):
        x = load(s)
        for k in range(4):
            u = u_ref[k * sections + s].astype(f32)
            product = product + u * inner(k, s, x)
        squares = squares + u * u
    sigma = supersat_scale / (1.0 + crowding * squares)
    birth = jnp.zeros((8, 128), f32)
    for k in range(4):
        c = k * sections
        birth = birth + nucleus_moments[k] * x_ref[8 * c : 8 * c + 8]
    rate = jnp.zeros((8, 128), f32)
    for label in range(rate_ref.shape[0]):
        rate = jnp.where(zones_ref[...] == label, rate_ref[label], rate)
    slope = (-2.0 * crowding / supersat_scale) * sigma * sigma * (product + 2.0 * rate * sigma * birth)
    for s in range(sections):
        x = load(s)
        for k in range(4):
            c = k * sections + s
            term = sigma * inner(k, s, x)
            if k == 3:
                term = term + u_ref[c].astype(f32) * slope
            finish(c, x[k][0], term)


def first_local(
    sections,
    a_ref,
    u_ref,
    speeds_ref,
    flags_ref,
    zones_ref,
    growth_ref,
    transfer_ref,
    rate_ref,
    out_ref,
    dn_low_ref,
    dn_high_ref,
    up_low_ref,
    up_high_ref,
):
    p, q = faces(speeds_ref, flags_ref)
    local = Local(p, q)
    make_tables(p[0], False, dn_low_ref, dn_high_ref)
    make_tables(p[0], True, up_low_ref, up_high_ref)

    def finish(c, x, term):
        out_ref[8 * c : 8 * c + 8] = 0.5 * (x + local(x) + term)

    source(sections, a_ref, u_ref, growth_ref, transfer_ref, zones_ref, rate_ref, finish)


def second_local(
    sections,
    m_ref,
    a_ref,
    u_ref,
    below_ref,
    edge_ref,
    low_ref,
    high_ref,
    speeds_ref,
    flags_ref,
    zones_ref,
    growth_ref,
    transfer_ref,
    rate_ref,
    out_ref,
    bottom_ref,
):
    local = Local(*faces(speeds_ref, flags_ref))
    local.centre = local.centre + (edge_ref[3] - 1.0)

    def finish(c, x, term):
        out_ref[8 * c : 8 * c + 8] = 0.5 * a_ref[8 * c : 8 * c + 8] + (local(x) + term)

    source(sections, m_ref, u_ref, growth_ref, transfer_ref, zones_ref, rate_ref, finish)
    bottom_ref[...] = out_ref[...]
    add_azimuthal(4 * sections, decode(4 * sections, below_ref, low_ref, high_ref), edge_ref[0], 0, bottom_ref)


def from_below(c, below_ref):
    pair = below_ref[8 * (c // 2) : 8 * (c // 2) + 8]
    return pair if c % 2 == 0 else pltpu.roll(pair, 4, 0)


def from_above(c, above_ref):
    pair = above_ref[8 * (c // 2) : 8 * (c // 2) + 8]
    return pair if c % 2 == 1 else pltpu.roll(pair, 4, 0)


def add_axial(comps, scale, where_ref, axial, ax_ref, out_ref):
    several = jnp.concatenate([scale * axial] * (2 * comps // 8), axis=0)
    for start, index in ((3, 0), (0, 1)):

        @pl.when(where_ref[0] == index)
        def _():
            spots = pl.ds(start, 2 * comps, stride=4)
            out_ref[spots] = out_ref[spots] + several * ax_ref[0 : 2 * comps]


def first_top(
    comps,
    where_ref,
    part_ref,
    a_ref,
    above_ref,
    ax_ref,
    radlo_ref,
    radhi_ref,
    speeds_ref,
    flags_ref,
    m_ref,
    edge_ref,
    up_ref,
    bad_ref,
    dn_low_ref,
    dn_high_ref,
    up_low_ref,
    up_high_ref,
):
    p, q = faces(speeds_ref, flags_ref)
    row, lane = rows_of(), lanes_of()
    upper = above_ref[4 * comps :]
    make_tables(upper, True, up_low_ref, up_high_ref)
    make_tables(upper, False, dn_low_ref, dn_high_ref)
    bad_ref[...] = crowded(p[0]) + crowded(upper)
    hrad = put_columns(radlo_ref[...], radhi_ref[...])
    lower_half = where_ref[0] == 0
    p_azim = jnp.where(row >= 4, pltpu.roll(upper, 4, 0), 0.0)
    pairs = jnp.where(lower_half, ax_ref[2 * comps : 2 * comps + 8], 0.0)
    p_axial = jnp.where(row == 3, pairs[0:1], jnp.where(row == 7, pairs[1:2], 0.0))
    p_rad = jnp.where(lane == 127, hrad[8 * comps : 8 * comps + 8], 0.0)
    axial = jnp.where(lower_half, pairs, pair_rows(q[1], 0, 4))
    rad = jnp.where(lane == 0, q[2], p_rad)
    centre = p_azim + p_axial + p_rad
    edge_ref[0] = jnp.where(row >= 4, p_azim, q[0])
    edge_ref[1] = axial
    edge_ref[2] = rad
    edge_ref[3] = centre
    for c in range(comps):
        spots = slice(8 * c, 8 * c + 8)
        m_ref[spots] = part_ref[spots] + 0.5 * (
            p_azim * from_above(c, above_ref) + rad * hrad[spots] - centre * a_ref[spots]
        )
    add_axial(comps, 0.5, where_ref, axial, ax_ref, m_ref)
    encode(comps, m_ref, 4, up_low_ref, up_high_ref, up_ref)


def first_bottom(
    comps,
    last,
    where_ref,
    rad_ref,
    part_ref,
    below_ref,
    edge_ref,
    bad_ref,
    low_ref,
    high_ref,
    m_ref,
    dn_ref,
    ax_ref,
    radup_ref,
    raddn_ref,
    worse_ref,
):
    azim = jnp.where(rows_of() >= 4, 0.0, 0.5 * edge_ref[0])
    for c in range(comps):
        m_ref[8 * c : 8 * c + 8] = part_ref[8 * c : 8 * c + 8] + azim * from_below(c, below_ref)
    encode(comps, m_ref, 0, low_ref, high_ref, dn_ref)
    worse_ref[...] = bad_ref[...] + crowded(below_ref[4 * comps :])
    dn_ref[5 * comps // 2 :] = worse_ref[...]
    pack_sides(comps, last, m_ref, where_ref, rad_ref, ax_ref, radup_ref, raddn_ref)


def second_radial(comps, bottom_ref, radlo_ref, radhi_ref, edge_ref, full_ref):
    hrad = put_columns(radlo_ref[...], radhi_ref[...])
    rad = edge_ref[2]
    for c in range(comps):
        spots = slice(8 * c, 8 * c + 8)
        full_ref[spots] = bottom_ref[spots] + rad * hrad[spots]


def second_rest(
    comps,
    parts,
    where_ref,
    full_ref,
    above_ref,
    ax_ref,
    edge_ref,
    bad_ref,
    low_ref,
    high_ref,
    out_ref,
    again_ref,
    done_ref,
    sems,
):
    again_ref[0] = (jnp.max(bad_ref[...] + above_ref[5 * comps // 2 :]) > 0.0).astype(jnp.int32)
    halo = decode(comps, above_ref, low_ref, high_ref)
    azim = edge_ref[0]
    done_ref[...] = full_ref[...]
    add_axial(comps, 1.0, where_ref, edge_ref[1], ax_ref, done_ref)
    size = comps // parts
    made = []
    for i in range(parts):
        for z in range(4):
            some = pl.ds(8 * size * i + 4 + z, size, stride=8)
            done_ref[some] = (
                done_ref[some] + azim[4 + z : 5 + z] * halo[size * i : size * i + size, 128 * z : 128 * z + 128]
            )
        spots = pl.ds(8 * size * i, 8 * size)
        made.append(pltpu.make_async_copy(done_ref.at[spots], out_ref.at[spots], sems.at[i]))
        made[-1].start()
    for copy in made:
        copy.wait()


SPACES = {
    "v": pl.BlockSpec(memory_space=pltpu.VMEM),
    "s": pl.BlockSpec(memory_space=pltpu.SMEM),
    "h": pl.BlockSpec(memory_space=pltpu.HBM),
}


def call(body, ins, outs, shapes, cost, *operands, scratch=()):
    return pl.pallas_call(
        body,
        in_specs=[SPACES[s] for s in ins],
        out_specs=[SPACES[s] for s in outs],
        out_shape=[jax.ShapeDtypeStruct(s, f32) if isinstance(s, tuple) else s for s in shapes],
        scratch_shapes=scratch,
        cost_estimate=pl.CostEstimate(flops=cost, bytes_accessed=cost // 10, transcendentals=0),
        compiler_params=pltpu.CompilerParams(vmem_limit_bytes=32 * 1024 * 1024),
    )(*operands)


def shift(x, axis, step, wrap):
    size = lax.axis_size(axis)
    pairs = [(i, (i + step) % size) for i in range(size) if wrap or 0 <= i + step < size]
    return lax.ppermute(x, axis, pairs)


def sides(ax, radup, raddn):
    ax = lax.ppermute(ax, "axial", [(0, 1), (1, 0)])
    return ax, shift(radup, "rad", 1, True), shift(raddn, "rad", -1, True)


def shards(adjoint_final, state_start, state_middle, speeds, flags, zones, growth_rate, transfer_rate, nucleation_rate):
    shape = adjoint_final.shape
    moments, sections = shape[:2]
    comps = moments * sections
    assert moments == 4 and shape[2:] == (2, 4, 128) and comps % 4 == 0
    assert lax.axis_size("axial") == 2
    cells = 8 * comps
    half, rows = cells // 2, cells // 4
    a = adjoint_final.reshape(cells, 128)
    speeds2 = speeds.reshape(3, 8, 128)
    flags2 = flags.reshape(3, 8, 128)
    where = lax.axis_index("axial").reshape(1)
    place = (where, lax.axis_index("rad").reshape(1))
    last = lax.axis_size("rad") - 1
    rates = (zones.reshape(8, 128), growth_rate, transfer_rate, nucleation_rate)
    message = 5 * comps // 2
    tables = [jax.ShapeDtypeStruct((256, 512), bf16)] * 2

    keep = ((0, 2, 0), (0, -1, 0), (0, 0, 0), (0, 0, 0))
    after = ((comps, -1, 0), (0, -1, 0), (0, 0, 0), (0, 0, 0))
    dn = lax.pad(adjoint_final.reshape(comps, 2, 4, 128), 0.0, keep)
    dn = dn + lax.pad(speeds, 0.0, after) * lax.pad(flags, 0, after).astype(f32)
    above = shift(dn.reshape(half + 8, 128), "azim", -1, True)
    up, *edges = call(
        functools.partial(first_rest, comps, last),
        "ssvvv",
        "vvvv",
        [(half + 8, 128), (rows + 8, 128), (1, cells + 128), (1, cells + 128)],
        2_000_000,
        *place,
        a,
        speeds2,
        flags2,
    )
    below = shift(up, "azim", 1, True)
    edges = sides(*edges)
    part, *lower_tables = call(
        functools.partial(first_local, sections),
        "vvvvvsss",
        "vvvvv",
        [(cells, 128)] + 2 * tables,
        8_000_000,
        a,
        state_middle.reshape(comps, 8, 128),
        speeds2,
        flags2,
        *rates,
    )
    part, edge, up, bad, *upper_tables = call(
        functools.partial(first_top, comps),
        "s" + "v" * 8,
        "v" * 8,
        [(cells, 128), (4, 8, 128), (message, 128), (8, 128)] + 2 * tables,
        4_000_000,
        where,
        part,
        a,
        above,
        *edges,
        speeds2,
        flags2,
    )
    next_below = shift(up, "azim", 1, True)
    m, dn, *edges, bad = call(
        functools.partial(first_bottom, comps, last),
        "ss" + "v" * 6,
        "v" * 6,
        [(cells, 128), (message + 8, 128), (rows, 128), (1, cells), (1, cells), (8, 128)],
        10_000,
        *place,
        part,
        below,
        edge,
        bad,
        *lower_tables[:2],
    )
    next_above = shift(dn, "azim", -1, True)
    ax, radlo, radhi = sides(*edges)
    part, bottom = call(
        functools.partial(second_local, sections),
        "v" * 10 + "sss",
        "vv",
        [(cells, 128), (cells, 128)],
        300_000_000,
        m,
        a,
        state_start.reshape(comps, 8, 128),
        next_below,
        edge,
        *lower_tables[2:],
        speeds2,
        flags2,
        *rates,
    )
    (full,) = call(
        functools.partial(second_radial, comps),
        "v" * 4,
        "v",
        [(cells, 128)],
        1_000_000,
        bottom,
        radlo,
        radhi,
        edge,
    )
    out, again = call(
        functools.partial(second_rest, comps, 4),
        "s" + "v" * 7,
        "hs",
        [pltpu.HBM((cells, 128), f32), jax.ShapeDtypeStruct((1,), jnp.int32)],
        1_000_000,
        where,
        full,
        next_above,
        ax,
        edge,
        bad,
        *upper_tables[:2],
        scratch=[pltpu.VMEM((cells, 128), f32), pltpu.SemaphoreType.DMA((4,))],
    )

    def whole():
        rows_ = m.reshape(comps, 2, 4, 128)
        halo = jnp.stack([shift(rows_[:, 1], "azim", 1, True), shift(rows_[:, 0], "azim", -1, True)], axis=1)
        azimuthal = (edge[0].reshape(1, 2, 4, 128) * halo).reshape(comps, 8, 128)
        row, lane = jnp.arange(8).reshape(1, 8, 1), jnp.arange(128).reshape(1, 1, 128)
        two = jnp.repeat(ax.reshape(comps, 2, 128) * edge[1, :2], 4, axis=1)
        axial = jnp.where(row % 4 == 3 * (1 - where[0]), two, 0.0)
        lower, upper = radlo.reshape(comps, 8, 1), radhi.reshape(comps, 8, 1)
        radial = edge[2] * jnp.where(lane == 0, lower, jnp.where(lane == 127, upper, 0.0))
        return part + (azimuthal + axial + radial).reshape(cells, 128)

    again = again[0]
    if lax.axis_size("azim") != 4:
        again = lax.pmax(again.astype(f32), "azim").astype(jnp.int32)
    return lax.switch(again, (lambda: out, whole)).reshape(shape)


def solution(mesh):
    field = P(None, None, "azim", "axial", "rad")
    faces_spec = P(None, "azim", "axial", "rad")
    return jax.shard_map(
        shards,
        mesh=mesh,
        in_specs=(field, field, field, faces_spec, faces_spec, P("azim", "axial", "rad"), P(), P(), P()),
        out_specs=field,
        check_vma=False,
    )
```

```python
import functools

import jax
import jax.numpy as jnp
from jax import lax
from jax.experimental import pallas as pl
from jax.experimental.pallas import tpu as pltpu
from jax.sharding import PartitionSpec as P

supersat_scale = 1.5
crowding = 0.02
nucleus_moments = (1.0, 0.5, 0.25, 0.125)
f32 = jnp.float32
bf16 = jnp.bfloat16
exact = lax.Precision.HIGHEST

slots = 320
extra = slots - 256


def rows_of():
    return lax.broadcasted_iota(jnp.int32, (8, 128), 0)


def lanes_of():
    return lax.broadcasted_iota(jnp.int32, (8, 128), 1)


def faces(speeds_ref, flags_ref):
    p, q = [], []
    for d in range(3):
        speed, upwind = speeds_ref[d], flags_ref[d].astype(f32)
        p.append(speed * upwind)
        q.append(speed * (1.0 - upwind))
    return p, q


class Local:
    def __init__(self, p, q):
        row, lane = rows_of(), lanes_of()
        z, top = row % 4, row >= 4
        self.azim = jnp.where(top, q[0], pltpu.roll(p[0], 4, 0))
        self.ax_up = jnp.where(z == 3, 0.0, pltpu.roll(p[1], 7, 0))
        self.ax_dn = jnp.where(z == 0, 0.0, q[1])
        self.rad_up = jnp.where(lane == 127, 0.0, pltpu.roll(p[2], 127, 1))
        self.rad_dn = jnp.where(lane == 0, 0.0, q[2])
        self.centre = self.azim + self.ax_up + q[1] + self.rad_up + q[2] + jnp.where(top, 0.0, q[0])

    def __call__(self, x):
        return (
            self.azim * pltpu.roll(x, 4, 0)
            + self.ax_up * pltpu.roll(x, 7, 0)
            + self.ax_dn * pltpu.roll(x, 1, 0)
            + self.rad_up * pltpu.roll(x, 127, 1)
            + self.rad_dn * pltpu.roll(x, 1, 1)
            - self.centre * x
        )


def pair_rows(x, first, second):
    return jnp.where(
        rows_of() % 2 == 0,
        jnp.broadcast_to(x[first : first + 1], (8, 128)),
        jnp.broadcast_to(x[second : second + 1], (8, 128)),
    )


def make_tables(p, where_zero, low_ref, high_ref):
    row, lane = rows_of(), lanes_of()
    taken = (p == 0.0) if where_zero else (p != 0.0)
    one = jnp.where(taken & (row < 4), 1.0, 0.0)
    before = lax.broadcasted_iota(jnp.int32, (128, 128), 0) < lax.broadcasted_iota(jnp.int32, (128, 128), 1)
    inside = jnp.dot(one.astype(bf16), jnp.where(before, 1.0, 0.0).astype(bf16), preferred_element_type=f32)
    total = jnp.sum(one, axis=1, keepdims=True)
    base = jnp.zeros((8, 1), f32)
    for step in (1, 2, 3):
        base = base + jnp.where(
            lax.broadcasted_iota(jnp.int32, (8, 1), 0) >= step, jnp.roll(total, step, axis=0), 0.0
        )
    slot = jnp.where(one > 0.0, inside + base, -1.0).astype(jnp.int32)
    here = lax.broadcasted_iota(jnp.int32, (128, 128), 0)
    first = jnp.where(here < extra, here + 256, -2)
    second = jnp.where(here >= extra, here + (256 - extra), -2)
    for z in range(4):
        cells = slice(128 * z, 128 * z + 128)
        want = jnp.broadcast_to(slot[z : z + 1], (128, 128))
        for ref, start, names in ((low_ref, 0, here), (low_ref, 128, here + 128), (high_ref, 0, first), (high_ref, 128, second)):
            ref[start : start + 128, cells] = jnp.where(names == want, 1.0, 0.0).astype(bf16)


def crowded(p):
    taken = jnp.where((rows_of() < 4) & (p != 0.0), 1.0, 0.0)
    count = jnp.sum(jnp.sum(taken, axis=1, keepdims=True), axis=0, keepdims=True)
    count = jnp.broadcast_to(count, (8, 128))
    return jnp.where(jnp.maximum(count, 512.0 - count) > slots, 1.0, 0.0)


def pieces(x):
    high = x.astype(bf16)
    rest = x - high.astype(f32)
    middle = rest.astype(bf16)
    return high, middle, (rest - middle.astype(f32)).astype(bf16)


def stacked(x, half):
    return jnp.concatenate([part[half * i : half * i + half] for i in range(2) for part in pieces(x)], axis=0)


def summed(x, half):
    parts = [x[half * i : half * i + half] for i in range(6)]
    return [parts[3 * i] + (parts[3 * i + 1] + parts[3 * i + 2]) for i in range(2)]


def encode(comps, x_ref, first_row, low_ref, high_ref, message_ref):
    half = comps // 2
    x = jnp.concatenate(
        [stacked(x_ref[pl.ds(first_row + z, comps, stride=8)], half) for z in range(4)], axis=1
    )
    over = (((1,), (1,)), ((), ()))
    low = lax.dot_general(x, low_ref[...], over, preferred_element_type=f32)
    high = [
        lax.dot_general(
            x[3 * half * i : 3 * half * (i + 1)], high_ref[128 * i : 128 * i + 128], over, preferred_element_type=f32
        )
        for i in range(2)
    ]
    tail = jnp.zeros((half, 128), f32)
    for i, part in enumerate(summed(low, half)):
        message_ref[half * i : half * i + half] = part[:, :128]
        message_ref[comps + half * i : comps + half * i + half] = part[:, 128:]
    for part in high:
        tail = tail + (part[:half] + (part[half : 2 * half] + part[2 * half :]))
    message_ref[2 * comps : 2 * comps + half] = tail


def decode(comps, message_ref, low_ref, high_ref):
    half = comps // 2
    x = jnp.concatenate([stacked(message_ref[comps * i : comps * i + comps], half) for i in range(2)], axis=1)
    low = jnp.dot(x, low_ref[...], preferred_element_type=f32)
    tail = jnp.concatenate(pieces(message_ref[2 * comps : 2 * comps + half]), axis=0)
    found = []
    for i, part in enumerate(summed(low, half)):
        high = jnp.dot(tail, high_ref[128 * i : 128 * i + 128], preferred_element_type=f32)
        found.append(part + (high[:half] + (high[half : 2 * half] + high[2 * half :])))
    return jnp.concatenate(found, axis=0)


def add_azimuthal(comps, halo, coefficient, first_row, out_ref):
    for z in range(4):
        spots = pl.ds(first_row + z, comps, stride=8)
        out_ref[spots] = out_ref[spots] + coefficient[first_row + z : first_row + z + 1] * halo[:, 128 * z : 128 * z + 128]


def pack_sides(comps, last, x_ref, where_ref, rad_ref, ax_ref, radup_ref, raddn_ref):
    @pl.when(where_ref[0] == 0)
    def _():
        ax_ref[0 : 2 * comps] = x_ref[pl.ds(3, 2 * comps, stride=4)]

    @pl.when(where_ref[0] != 0)
    def _():
        ax_ref[0 : 2 * comps] = x_ref[pl.ds(0, 2 * comps, stride=4)]

    ends = columns(x_ref[...])
    radup_ref[:, 0 : 8 * comps] = jnp.where(rad_ref[0] < last, ends[0:1], 0.0)
    raddn_ref[:, 0 : 8 * comps] = jnp.where(rad_ref[0] > 0, ends[1:2], 0.0)


def columns(x):
    row, lane = rows_of(), lanes_of()
    take = jnp.where(((row == 0) & (lane == 127)) | ((row == 1) & (lane == 0)), 1.0, 0.0)
    return lax.dot_general(take, x, (((1,), (1,)), ((), ())), precision=exact, preferred_element_type=f32)


def put_columns(lower, upper):
    n = lower.shape[1]
    row, lane = rows_of(), lanes_of()
    which = lax.broadcasted_iota(jnp.int32, (8, n), 0)
    both = jnp.where(which == 0, lower, jnp.where(which == 1, upper, 0.0))
    place = jnp.where(((row == 0) & (lane == 0)) | ((row == 1) & (lane == 127)), 1.0, 0.0)
    return lax.dot_general(both, place, (((0,), (0,)), ((), ())), precision=exact, preferred_element_type=f32)


def first_rest(comps, last, where_ref, rad_ref, a_ref, speeds_ref, flags_ref, up_ref, ax_ref, radup_ref, raddn_ref):
    p, _ = faces(speeds_ref, flags_ref)
    for c in range(comps):
        up_ref[4 * c : 4 * c + 4] = a_ref[8 * c + 4 : 8 * c + 8]
    up_ref[4 * comps :] = p[0]
    pack_sides(comps, last, a_ref, where_ref, rad_ref, ax_ref, radup_ref, raddn_ref)
    ax_ref[2 * comps : 2 * comps + 8] = pair_rows(p[1], 0, 4)
    radup_ref[:, 8 * comps :] = jnp.zeros((1, 128), f32)
    raddn_ref[:, 8 * comps :] = jnp.zeros((1, 128), f32)
    raddn_ref[:, 8 * comps : 8 * comps + 8] = jnp.where(rad_ref[0] > 0, columns(p[2])[1:2], 0.0)


def source(sections, x_ref, u_ref, growth_ref, transfer_ref, zones_ref, rate_ref, finish):
    def inner(k, s, x):
        term = transfer_ref[s] * ((x[k][1] - x[k][0]) if s + 1 < sections else -x[k][0])
        if k < 3:
            term = term + ((k + 1.0) * growth_ref[s]) * x[k + 1][0]
        return term

    def load(s):
        got = []
        for k in range(4):
            c = k * sections + s
            here = x_ref[8 * c : 8 * c + 8]
            got.append((here, x_ref[8 * c + 8 : 8 * c + 16] if s + 1 < sections else None))
        return got

    squares = jnp.zeros((8, 128), f32)
    product = jnp.zeros((8, 128), f32)
    for s in range(sections):
        x = load(s)
        for k in range(4):
            u = u_ref[k * sections + s].astype(f32)
            product = product + u * inner(k, s, x)
        squares = squares + u * u
    sigma = supersat_scale / (1.0 + crowding * squares)
    birth = jnp.zeros((8, 128), f32)
    for k in range(4):
        c = k * sections
        birth = birth + nucleus_moments[k] * x_ref[8 * c : 8 * c + 8]
    rate = jnp.zeros((8, 128), f32)
    for label in range(rate_ref.shape[0]):
        rate = jnp.where(zones_ref[...] == label, rate_ref[label], rate)
    slope = (-2.0 * crowding / supersat_scale) * sigma * sigma * (product + 2.0 * rate * sigma * birth)
    for s in range(sections):
        x = load(s)
        for k in range(4):
            c = k * sections + s
            term = sigma * inner(k, s, x)
            if k == 3:
                term = term + u_ref[c].astype(f32) * slope
            finish(c, x[k][0], term)


def first_local(
    sections,
    a_ref,
    u_ref,
    speeds_ref,
    flags_ref,
    zones_ref,
    growth_ref,
    transfer_ref,
    rate_ref,
    out_ref,
    dn_low_ref,
    dn_high_ref,
    up_low_ref,
    up_high_ref,
):
    p, q = faces(speeds_ref, flags_ref)
    local = Local(p, q)
    make_tables(p[0], False, dn_low_ref, dn_high_ref)
    make_tables(p[0], True, up_low_ref, up_high_ref)

    def finish(c, x, term):
        out_ref[8 * c : 8 * c + 8] = 0.5 * (x + local(x) + term)

    source(sections, a_ref, u_ref, growth_ref, transfer_ref, zones_ref, rate_ref, finish)


def second_local(
    sections,
    m_ref,
    a_ref,
    u_ref,
    below_ref,
    edge_ref,
    low_ref,
    high_ref,
    speeds_ref,
    flags_ref,
    zones_ref,
    growth_ref,
    transfer_ref,
    rate_ref,
    out_ref,
    bottom_ref,
):
    local = Local(*faces(speeds_ref, flags_ref))
    local.centre = local.centre + (edge_ref[3] - 1.0)

    def finish(c, x, term):
        out_ref[8 * c : 8 * c + 8] = 0.5 * a_ref[8 * c : 8 * c + 8] + (local(x) + term)

    source(sections, m_ref, u_ref, growth_ref, transfer_ref, zones_ref, rate_ref, finish)
    bottom_ref[...] = out_ref[...]
    add_azimuthal(4 * sections, decode(4 * sections, below_ref, low_ref, high_ref), edge_ref[0], 0, bottom_ref)


def from_below(c, below_ref):
    pair = below_ref[8 * (c // 2) : 8 * (c // 2) + 8]
    return pair if c % 2 == 0 else pltpu.roll(pair, 4, 0)


def from_above(c, above_ref):
    pair = above_ref[8 * (c // 2) : 8 * (c // 2) + 8]
    return pair if c % 2 == 1 else pltpu.roll(pair, 4, 0)


def add_axial(comps, scale, where_ref, axial, ax_ref, out_ref):
    several = jnp.concatenate([scale * axial] * (2 * comps // 8), axis=0)
    for start, index in ((3, 0), (0, 1)):

        @pl.when(where_ref[0] == index)
        def _():
            spots = pl.ds(start, 2 * comps, stride=4)
            out_ref[spots] = out_ref[spots] + several * ax_ref[0 : 2 * comps]


def first_top(
    comps,
    where_ref,
    part_ref,
    a_ref,
    above_ref,
    ax_ref,
    radlo_ref,
    radhi_ref,
    speeds_ref,
    flags_ref,
    m_ref,
    edge_ref,
    up_ref,
    bad_ref,
    dn_low_ref,
    dn_high_ref,
    up_low_ref,
    up_high_ref,
):
    p, q = faces(speeds_ref, flags_ref)
    row, lane = rows_of(), lanes_of()
    upper = above_ref[4 * comps :]
    make_tables(upper, True, up_low_ref, up_high_ref)
    make_tables(upper, False, dn_low_ref, dn_high_ref)
    bad_ref[...] = crowded(p[0]) + crowded(upper)
    hrad = put_columns(radlo_ref[...], radhi_ref[...])
    lower_half = where_ref[0] == 0
    p_azim = jnp.where(row >= 4, pltpu.roll(upper, 4, 0), 0.0)
    pairs = jnp.where(lower_half, ax_ref[2 * comps : 2 * comps + 8], 0.0)
    p_axial = jnp.where(row == 3, pairs[0:1], jnp.where(row == 7, pairs[1:2], 0.0))
    p_rad = jnp.where(lane == 127, hrad[8 * comps : 8 * comps + 8], 0.0)
    axial = jnp.where(lower_half, pairs, pair_rows(q[1], 0, 4))
    rad = jnp.where(lane == 0, q[2], p_rad)
    centre = p_azim + p_axial + p_rad
    edge_ref[0] = jnp.where(row >= 4, p_azim, q[0])
    edge_ref[1] = axial
    edge_ref[2] = rad
    edge_ref[3] = centre
    for c in range(comps):
        spots = slice(8 * c, 8 * c + 8)
        m_ref[spots] = part_ref[spots] + 0.5 * (
            p_azim * from_above(c, above_ref) + rad * hrad[spots] - centre * a_ref[spots]
        )
    add_axial(comps, 0.5, where_ref, axial, ax_ref, m_ref)
    encode(comps, m_ref, 4, up_low_ref, up_high_ref, up_ref)


def first_bottom(
    comps,
    last,
    where_ref,
    rad_ref,
    part_ref,
    below_ref,
    edge_ref,
    bad_ref,
    low_ref,
    high_ref,
    m_ref,
    dn_ref,
    ax_ref,
    radup_ref,
    raddn_ref,
    worse_ref,
):
    azim = jnp.where(rows_of() >= 4, 0.0, 0.5 * edge_ref[0])
    for c in range(comps):
        m_ref[8 * c : 8 * c + 8] = part_ref[8 * c : 8 * c + 8] + azim * from_below(c, below_ref)
    encode(comps, m_ref, 0, low_ref, high_ref, dn_ref)
    worse_ref[...] = bad_ref[...] + crowded(below_ref[4 * comps :])
    dn_ref[5 * comps // 2 :] = worse_ref[...]
    pack_sides(comps, last, m_ref, where_ref, rad_ref, ax_ref, radup_ref, raddn_ref)


def second_radial(comps, bottom_ref, radlo_ref, radhi_ref, edge_ref, full_ref):
    hrad = put_columns(radlo_ref[...], radhi_ref[...])
    rad = edge_ref[2]
    for c in range(comps):
        spots = slice(8 * c, 8 * c + 8)
        full_ref[spots] = bottom_ref[spots] + rad * hrad[spots]


def second_rest(
    comps,
    parts,
    where_ref,
    full_ref,
    above_ref,
    ax_ref,
    edge_ref,
    bad_ref,
    low_ref,
    high_ref,
    out_ref,
    again_ref,
    done_ref,
    sems,
):
    again_ref[0] = (jnp.max(bad_ref[...] + above_ref[5 * comps // 2 :]) > 0.0).astype(jnp.int32)
    halo = decode(comps, above_ref, low_ref, high_ref)
    azim = edge_ref[0]
    done_ref[...] = full_ref[...]
    add_axial(comps, 1.0, where_ref, edge_ref[1], ax_ref, done_ref)
    size = comps // parts
    made = []
    for i in range(parts):
        for z in range(4):
            some = pl.ds(8 * size * i + 4 + z, size, stride=8)
            done_ref[some] = (
                done_ref[some] + azim[4 + z : 5 + z] * halo[size * i : size * i + size, 128 * z : 128 * z + 128]
            )
        spots = pl.ds(8 * size * i, 8 * size)
        made.append(pltpu.make_async_copy(done_ref.at[spots], out_ref.at[spots], sems.at[i]))
        made[-1].start()
    for copy in made:
        copy.wait()


SPACES = {
    "v": pl.BlockSpec(memory_space=pltpu.VMEM),
    "s": pl.BlockSpec(memory_space=pltpu.SMEM),
    "h": pl.BlockSpec(memory_space=pltpu.HBM),
}


def call(body, ins, outs, shapes, cost, *operands, scratch=()):
    return pl.pallas_call(
        body,
        in_specs=[SPACES[s] for s in ins],
        out_specs=[SPACES[s] for s in outs],
        out_shape=[jax.ShapeDtypeStruct(s, f32) if isinstance(s, tuple) else s for s in shapes],
        scratch_shapes=scratch,
        cost_estimate=pl.CostEstimate(flops=cost, bytes_accessed=cost // 10, transcendentals=0),
        compiler_params=pltpu.CompilerParams(vmem_limit_bytes=32 * 1024 * 1024),
    )(*operands)


def shift(x, axis, step, wrap):
    size = lax.axis_size(axis)
    pairs = [(i, (i + step) % size) for i in range(size) if wrap or 0 <= i + step < size]
    return lax.ppermute(x, axis, pairs)


def sides(ax, radup, raddn):
    ax = lax.ppermute(ax, "axial", [(0, 1), (1, 0)])
    return ax, shift(radup, "rad", 1, True), shift(raddn, "rad", -1, True)


def shards(adjoint_final, state_start, state_middle, speeds, flags, zones, growth_rate, transfer_rate, nucleation_rate):
    shape = adjoint_final.shape
    moments, sections = shape[:2]
    comps = moments * sections
    assert moments == 4 and shape[2:] == (2, 4, 128) and comps % 4 == 0
    assert lax.axis_size("axial") == 2
    cells = 8 * comps
    half, rows = cells // 2, cells // 4
    a = adjoint_final.reshape(cells, 128)
    speeds2 = speeds.reshape(3, 8, 128)
    flags2 = flags.reshape(3, 8, 128)
    where = lax.axis_index("axial").reshape(1)
    place = (where, lax.axis_index("rad").reshape(1))
    last = lax.axis_size("rad") - 1
    rates = (zones.reshape(8, 128), growth_rate, transfer_rate, nucleation_rate)
    message = 5 * comps // 2
    tables = [jax.ShapeDtypeStruct((256, 512), bf16)] * 2

    keep = ((0, 2, 0), (0, -1, 0), (0, 0, 0), (0, 0, 0))
    after = ((comps, -1, 0), (0, -1, 0), (0, 0, 0), (0, 0, 0))
    dn = lax.pad(adjoint_final.reshape(comps, 2, 4, 128), 0.0, keep)
    dn = dn + lax.pad(speeds, 0.0, after) * lax.pad(flags, 0, after).astype(f32)
    above = shift(dn.reshape(half + 8, 128), "azim", -1, True)
    up, *edges = call(
        functools.partial(first_rest, comps, last),
        "ssvvv",
        "vvvv",
        [(half + 8, 128), (rows + 8, 128), (1, cells + 128), (1, cells + 128)],
        2_000_000,
        *place,
        a,
        speeds2,
        flags2,
    )
    below = shift(up, "azim", 1, True)
    edges = sides(*edges)
    part, *lower_tables = call(
        functools.partial(first_local, sections),
        "vvvvvsss",
        "vvvvv",
        [(cells, 128)] + 2 * tables,
        8_000_000,
        a,
        state_middle.reshape(comps, 8, 128),
        speeds2,
        flags2,
        *rates,
    )
    part, edge, up, bad, *upper_tables = call(
        functools.partial(first_top, comps),
        "s" + "v" * 8,
        "v" * 8,
        [(cells, 128), (4, 8, 128), (message, 128), (8, 128)] + 2 * tables,
        4_000_000,
        where,
        part,
        a,
        above,
        *edges,
        speeds2,
        flags2,
    )
    next_below = shift(up, "azim", 1, True)
    m, dn, *edges, bad = call(
        functools.partial(first_bottom, comps, last),
        "ss" + "v" * 6,
        "v" * 6,
        [(cells, 128), (message + 8, 128), (rows, 128), (1, cells), (1, cells), (8, 128)],
        10_000,
        *place,
        part,
        below,
        edge,
        bad,
        *lower_tables[:2],
    )
    next_above = shift(dn, "azim", -1, True)
    ax, radlo, radhi = sides(*edges)
    part, bottom = call(
        functools.partial(second_local, sections),
        "v" * 10 + "sss",
        "vv",
        [(cells, 128), (cells, 128)],
        300_000_000,
        m,
        a,
        state_start.reshape(comps, 8, 128),
        next_below,
        edge,
        *lower_tables[2:],
        speeds2,
        flags2,
        *rates,
    )
    (full,) = call(
        functools.partial(second_radial, comps),
        "v" * 4,
        "v",
        [(cells, 128)],
        1_000,
        bottom,
        radlo,
        radhi,
        edge,
    )
    out, again = call(
        functools.partial(second_rest, comps, 4),
        "s" + "v" * 7,
        "hs",
        [pltpu.HBM((cells, 128), f32), jax.ShapeDtypeStruct((1,), jnp.int32)],
        1_000_000,
        where,
        full,
        next_above,
        ax,
        edge,
        bad,
        *upper_tables[:2],
        scratch=[pltpu.VMEM((cells, 128), f32), pltpu.SemaphoreType.DMA((4,))],
    )

    def whole():
        rows_ = m.reshape(comps, 2, 4, 128)
        halo = jnp.stack([shift(rows_[:, 1], "azim", 1, True), shift(rows_[:, 0], "azim", -1, True)], axis=1)
        azimuthal = (edge[0].reshape(1, 2, 4, 128) * halo).reshape(comps, 8, 128)
        row, lane = jnp.arange(8).reshape(1, 8, 1), jnp.arange(128).reshape(1, 1, 128)
        two = jnp.repeat(ax.reshape(comps, 2, 128) * edge[1, :2], 4, axis=1)
        axial = jnp.where(row % 4 == 3 * (1 - where[0]), two, 0.0)
        lower, upper = radlo.reshape(comps, 8, 1), radhi.reshape(comps, 8, 1)
        radial = edge[2] * jnp.where(lane == 0, lower, jnp.where(lane == 127, upper, 0.0))
        return part + (azimuthal + axial + radial).reshape(cells, 128)

    again = again[0]
    if lax.axis_size("azim") != 4:
        again = lax.pmax(again.astype(f32), "azim").astype(jnp.int32)
    return lax.switch(again, (lambda: out, whole)).reshape(shape)


def solution(mesh):
    field = P(None, None, "azim", "axial", "rad")
    faces_spec = P(None, "azim", "axial", "rad")
    return jax.shard_map(
        shards,
        mesh=mesh,
        in_specs=(field, field, field, faces_spec, faces_spec, P("azim", "axial", "rad"), P(), P(), P()),
        out_specs=field,
        check_vma=False,
    )
```

```python
import functools

import jax
import jax.numpy as jnp
from jax import lax
from jax.experimental import pallas as pl
from jax.experimental.pallas import tpu as pltpu
from jax.sharding import PartitionSpec as P

supersat_scale = 1.5
crowding = 0.02
nucleus_moments = (1.0, 0.5, 0.25, 0.125)
f32 = jnp.float32
bf16 = jnp.bfloat16
exact = lax.Precision.HIGHEST

slots = 320
extra = slots - 256


def rows_of():
    return lax.broadcasted_iota(jnp.int32, (8, 128), 0)


def lanes_of():
    return lax.broadcasted_iota(jnp.int32, (8, 128), 1)


def faces(speeds_ref, flags_ref):
    p, q = [], []
    for d in range(3):
        speed, upwind = speeds_ref[d], flags_ref[d].astype(f32)
        p.append(speed * upwind)
        q.append(speed * (1.0 - upwind))
    return p, q


class Local:
    def __init__(self, p, q):
        row, lane = rows_of(), lanes_of()
        z, top = row % 4, row >= 4
        self.azim = jnp.where(top, q[0], pltpu.roll(p[0], 4, 0))
        self.ax_up = jnp.where(z == 3, 0.0, pltpu.roll(p[1], 7, 0))
        self.ax_dn = jnp.where(z == 0, 0.0, q[1])
        self.rad_up = jnp.where(lane == 127, 0.0, pltpu.roll(p[2], 127, 1))
        self.rad_dn = jnp.where(lane == 0, 0.0, q[2])
        self.centre = self.azim + self.ax_up + q[1] + self.rad_up + q[2] + jnp.where(top, 0.0, q[0])

    def __call__(self, x):
        return (
            self.azim * pltpu.roll(x, 4, 0)
            + self.ax_up * pltpu.roll(x, 7, 0)
            + self.ax_dn * pltpu.roll(x, 1, 0)
            + self.rad_up * pltpu.roll(x, 127, 1)
            + self.rad_dn * pltpu.roll(x, 1, 1)
            - self.centre * x
        )


def pair_rows(x, first, second):
    return jnp.where(
        rows_of() % 2 == 0,
        jnp.broadcast_to(x[first : first + 1], (8, 128)),
        jnp.broadcast_to(x[second : second + 1], (8, 128)),
    )


def make_tables(p, where_zero, low_ref, high_ref):
    row, lane = rows_of(), lanes_of()
    taken = (p == 0.0) if where_zero else (p != 0.0)
    one = jnp.where(taken & (row < 4), 1.0, 0.0)
    before = lax.broadcasted_iota(jnp.int32, (128, 128), 0) < lax.broadcasted_iota(jnp.int32, (128, 128), 1)
    inside = jnp.dot(one.astype(bf16), jnp.where(before, 1.0, 0.0).astype(bf16), preferred_element_type=f32)
    total = jnp.sum(one, axis=1, keepdims=True)
    base = jnp.zeros((8, 1), f32)
    for step in (1, 2, 3):
        base = base + jnp.where(
            lax.broadcasted_iota(jnp.int32, (8, 1), 0) >= step, jnp.roll(total, step, axis=0), 0.0
        )
    slot = jnp.where(one > 0.0, inside + base, -1.0).astype(jnp.int32)
    here = lax.broadcasted_iota(jnp.int32, (128, 128), 0)
    first = jnp.where(here < extra, here + 256, -2)
    second = jnp.where(here >= extra, here + (256 - extra), -2)
    for z in range(4):
        cells = slice(128 * z, 128 * z + 128)
        want = jnp.broadcast_to(slot[z : z + 1], (128, 128))
        for ref, start, names in ((low_ref, 0, here), (low_ref, 128, here + 128), (high_ref, 0, first), (high_ref, 128, second)):
            ref[start : start + 128, cells] = jnp.where(names == want, 1.0, 0.0).astype(bf16)


def crowded(p):
    taken = jnp.where((rows_of() < 4) & (p != 0.0), 1.0, 0.0)
    count = jnp.sum(jnp.sum(taken, axis=1, keepdims=True), axis=0, keepdims=True)
    count = jnp.broadcast_to(count, (8, 128))
    return jnp.where(jnp.maximum(count, 512.0 - count) > slots, 1.0, 0.0)


def pieces(x):
    high = x.astype(bf16)
    rest = x - high.astype(f32)
    middle = rest.astype(bf16)
    return high, middle, (rest - middle.astype(f32)).astype(bf16)


def stacked(x, half):
    return jnp.concatenate([part[half * i : half * i + half] for i in range(2) for part in pieces(x)], axis=0)


def summed(x, half):
    parts = [x[half * i : half * i + half] for i in range(6)]
    return [parts[3 * i] + (parts[3 * i + 1] + parts[3 * i + 2]) for i in range(2)]


def encode(comps, x_ref, first_row, low_ref, high_ref, message_ref):
    half = comps // 2
    x = jnp.concatenate(
        [stacked(x_ref[pl.ds(first_row + z, comps, stride=8)], half) for z in range(4)], axis=1
    )
    over = (((1,), (1,)), ((), ()))
    low = lax.dot_general(x, low_ref[...], over, preferred_element_type=f32)
    high = [
        lax.dot_general(
            x[3 * half * i : 3 * half * (i + 1)], high_ref[128 * i : 128 * i + 128], over, preferred_element_type=f32
        )
        for i in range(2)
    ]
    tail = jnp.zeros((half, 128), f32)
    for i, part in enumerate(summed(low, half)):
        message_ref[half * i : half * i + half] = part[:, :128]
        message_ref[comps + half * i : comps + half * i + half] = part[:, 128:]
    for part in high:
        tail = tail + (part[:half] + (part[half : 2 * half] + part[2 * half :]))
    message_ref[2 * comps : 2 * comps + half] = tail


def decode(comps, message_ref, low_ref, high_ref):
    half = comps // 2
    x = jnp.concatenate([stacked(message_ref[comps * i : comps * i + comps], half) for i in range(2)], axis=1)
    low = jnp.dot(x, low_ref[...], preferred_element_type=f32)
    tail = jnp.concatenate(pieces(message_ref[2 * comps : 2 * comps + half]), axis=0)
    found = []
    for i, part in enumerate(summed(low, half)):
        high = jnp.dot(tail, high_ref[128 * i : 128 * i + 128], preferred_element_type=f32)
        found.append(part + (high[:half] + (high[half : 2 * half] + high[2 * half :])))
    return jnp.concatenate(found, axis=0)


def add_azimuthal(comps, halo, coefficient, first_row, out_ref):
    for z in range(4):
        spots = pl.ds(first_row + z, comps, stride=8)
        out_ref[spots] = out_ref[spots] + coefficient[first_row + z : first_row + z + 1] * halo[:, 128 * z : 128 * z + 128]


def pack_sides(comps, last, x_ref, where_ref, rad_ref, ax_ref, radup_ref, raddn_ref):
    @pl.when(where_ref[0] == 0)
    def _():
        ax_ref[0 : 2 * comps] = x_ref[pl.ds(3, 2 * comps, stride=4)]

    @pl.when(where_ref[0] != 0)
    def _():
        ax_ref[0 : 2 * comps] = x_ref[pl.ds(0, 2 * comps, stride=4)]

    ends = columns(x_ref[...])
    radup_ref[:, 0 : 8 * comps] = jnp.where(rad_ref[0] < last, ends[0:1], 0.0)
    raddn_ref[:, 0 : 8 * comps] = jnp.where(rad_ref[0] > 0, ends[1:2], 0.0)


def columns(x):
    row, lane = rows_of(), lanes_of()
    take = jnp.where(((row == 0) & (lane == 127)) | ((row == 1) & (lane == 0)), 1.0, 0.0)
    return lax.dot_general(take, x, (((1,), (1,)), ((), ())), precision=exact, preferred_element_type=f32)


def put_columns(lower, upper):
    n = lower.shape[1]
    row, lane = rows_of(), lanes_of()
    which = lax.broadcasted_iota(jnp.int32, (8, n), 0)
    both = jnp.where(which == 0, lower, jnp.where(which == 1, upper, 0.0))
    place = jnp.where(((row == 0) & (lane == 0)) | ((row == 1) & (lane == 127)), 1.0, 0.0)
    return lax.dot_general(both, place, (((0,), (0,)), ((), ())), precision=exact, preferred_element_type=f32)


def first_rest(comps, last, where_ref, rad_ref, a_ref, speeds_ref, flags_ref, up_ref, up2_ref, ax_ref, radup_ref, raddn_ref):
    p, _ = faces(speeds_ref, flags_ref)
    half = comps // 2
    for c in range(half):
        up_ref[4 * c : 4 * c + 4] = a_ref[8 * c + 4 : 8 * c + 8]
        up2_ref[4 * c : 4 * c + 4] = a_ref[8 * (c + half) + 4 : 8 * (c + half) + 8]
    up_ref[4 * half :] = p[0]
    pack_sides(comps, last, a_ref, where_ref, rad_ref, ax_ref, radup_ref, raddn_ref)
    ax_ref[2 * comps : 2 * comps + 8] = pair_rows(p[1], 0, 4)
    radup_ref[:, 8 * comps :] = jnp.zeros((1, 128), f32)
    raddn_ref[:, 8 * comps :] = jnp.zeros((1, 128), f32)
    raddn_ref[:, 8 * comps : 8 * comps + 8] = jnp.where(rad_ref[0] > 0, columns(p[2])[1:2], 0.0)


def source(sections, x_ref, u_ref, growth_ref, transfer_ref, zones_ref, rate_ref, finish):
    def inner(k, s, x):
        term = transfer_ref[s] * ((x[k][1] - x[k][0]) if s + 1 < sections else -x[k][0])
        if k < 3:
            term = term + ((k + 1.0) * growth_ref[s]) * x[k + 1][0]
        return term

    def load(s):
        got = []
        for k in range(4):
            c = k * sections + s
            here = x_ref[8 * c : 8 * c + 8]
            got.append((here, x_ref[8 * c + 8 : 8 * c + 16] if s + 1 < sections else None))
        return got

    squares = jnp.zeros((8, 128), f32)
    product = jnp.zeros((8, 128), f32)
    for s in range(sections):
        x = load(s)
        for k in range(4):
            u = u_ref[k * sections + s].astype(f32)
            product = product + u * inner(k, s, x)
        squares = squares + u * u
    sigma = supersat_scale / (1.0 + crowding * squares)
    birth = jnp.zeros((8, 128), f32)
    for k in range(4):
        c = k * sections
        birth = birth + nucleus_moments[k] * x_ref[8 * c : 8 * c + 8]
    rate = jnp.zeros((8, 128), f32)
    for label in range(rate_ref.shape[0]):
        rate = jnp.where(zones_ref[...] == label, rate_ref[label], rate)
    slope = (-2.0 * crowding / supersat_scale) * sigma * sigma * (product + 2.0 * rate * sigma * birth)
    for s in range(sections):
        x = load(s)
        for k in range(4):
            c = k * sections + s
            term = sigma * inner(k, s, x)
            if k == 3:
                term = term + u_ref[c].astype(f32) * slope
            finish(c, x[k][0], term)


def first_local(
    sections,
    a_ref,
    u_ref,
    speeds_ref,
    flags_ref,
    zones_ref,
    growth_ref,
    transfer_ref,
    rate_ref,
    out_ref,
    dn_low_ref,
    dn_high_ref,
    up_low_ref,
    up_high_ref,
):
    p, q = faces(speeds_ref, flags_ref)
    local = Local(p, q)
    make_tables(p[0], False, dn_low_ref, dn_high_ref)
    make_tables(p[0], True, up_low_ref, up_high_ref)

    def finish(c, x, term):
        out_ref[8 * c : 8 * c + 8] = 0.5 * (x + local(x) + term)

    source(sections, a_ref, u_ref, growth_ref, transfer_ref, zones_ref, rate_ref, finish)


def second_local(
    sections,
    m_ref,
    a_ref,
    u_ref,
    below_ref,
    edge_ref,
    low_ref,
    high_ref,
    speeds_ref,
    flags_ref,
    zones_ref,
    growth_ref,
    transfer_ref,
    rate_ref,
    out_ref,
    bottom_ref,
):
    local = Local(*faces(speeds_ref, flags_ref))
    local.centre = local.centre + (edge_ref[3] - 1.0)

    def finish(c, x, term):
        out_ref[8 * c : 8 * c + 8] = 0.5 * a_ref[8 * c : 8 * c + 8] + (local(x) + term)

    source(sections, m_ref, u_ref, growth_ref, transfer_ref, zones_ref, rate_ref, finish)
    bottom_ref[...] = out_ref[...]
    add_azimuthal(4 * sections, decode(4 * sections, below_ref, low_ref, high_ref), edge_ref[0], 0, bottom_ref)


def from_below(c, below_ref):
    pair = below_ref[8 * (c // 2) : 8 * (c // 2) + 8]
    return pair if c % 2 == 0 else pltpu.roll(pair, 4, 0)


def from_above(c, above_ref):
    pair = above_ref[8 * (c // 2) : 8 * (c // 2) + 8]
    return pair if c % 2 == 1 else pltpu.roll(pair, 4, 0)


def add_axial(comps, scale, where_ref, axial, ax_ref, out_ref):
    several = jnp.concatenate([scale * axial] * (2 * comps // 8), axis=0)
    for start, index in ((3, 0), (0, 1)):

        @pl.when(where_ref[0] == index)
        def _():
            spots = pl.ds(start, 2 * comps, stride=4)
            out_ref[spots] = out_ref[spots] + several * ax_ref[0 : 2 * comps]


def first_top(
    comps,
    where_ref,
    part_ref,
    a_ref,
    above_ref,
    below_ref,
    ax_ref,
    radlo_ref,
    radhi_ref,
    speeds_ref,
    flags_ref,
    m_ref,
    edge_ref,
    up_ref,
    bad_ref,
    dn_low_ref,
    dn_high_ref,
    up_low_ref,
    up_high_ref,
):
    p, q = faces(speeds_ref, flags_ref)
    row, lane = rows_of(), lanes_of()
    upper = above_ref[4 * comps :]
    make_tables(upper, True, up_low_ref, up_high_ref)
    make_tables(upper, False, dn_low_ref, dn_high_ref)
    bad_ref[...] = crowded(p[0]) + crowded(upper) + crowded(below_ref[2 * comps :])
    low = jnp.where(row >= 4, 0.0, q[0])
    hrad = put_columns(radlo_ref[...], radhi_ref[...])
    lower_half = where_ref[0] == 0
    p_azim = jnp.where(row >= 4, pltpu.roll(upper, 4, 0), 0.0)
    pairs = jnp.where(lower_half, ax_ref[2 * comps : 2 * comps + 8], 0.0)
    p_axial = jnp.where(row == 3, pairs[0:1], jnp.where(row == 7, pairs[1:2], 0.0))
    p_rad = jnp.where(lane == 127, hrad[8 * comps : 8 * comps + 8], 0.0)
    axial = jnp.where(lower_half, pairs, pair_rows(q[1], 0, 4))
    rad = jnp.where(lane == 0, q[2], p_rad)
    centre = p_azim + p_axial + p_rad
    edge_ref[0] = jnp.where(row >= 4, p_azim, q[0])
    edge_ref[1] = axial
    edge_ref[2] = rad
    edge_ref[3] = centre
    for c in range(comps):
        spots = slice(8 * c, 8 * c + 8)
        halo = p_azim * from_above(c, above_ref)
        if c < comps // 2:
            halo = halo + low * from_below(c, below_ref)
        m_ref[spots] = part_ref[spots] + 0.5 * (halo + rad * hrad[spots] - centre * a_ref[spots])
    add_axial(comps, 0.5, where_ref, axial, ax_ref, m_ref)
    encode(comps, m_ref, 4, up_low_ref, up_high_ref, up_ref)


def first_bottom(
    comps,
    last,
    where_ref,
    rad_ref,
    part_ref,
    below_ref,
    edge_ref,
    bad_ref,
    low_ref,
    high_ref,
    m_ref,
    dn_ref,
    ax_ref,
    radup_ref,
    raddn_ref,
):
    azim = jnp.where(rows_of() >= 4, 0.0, 0.5 * edge_ref[0])
    for c in range(comps):
        m_ref[8 * c : 8 * c + 8] = part_ref[8 * c : 8 * c + 8]
        if c >= comps // 2:
            m_ref[8 * c : 8 * c + 8] = m_ref[8 * c : 8 * c + 8] + azim * from_below(c - comps // 2, below_ref)
    encode(comps, m_ref, 0, low_ref, high_ref, dn_ref)
    dn_ref[5 * comps // 2 :] = bad_ref[...]
    pack_sides(comps, last, m_ref, where_ref, rad_ref, ax_ref, radup_ref, raddn_ref)


def second_radial(comps, bottom_ref, radlo_ref, radhi_ref, edge_ref, full_ref):
    hrad = put_columns(radlo_ref[...], radhi_ref[...])
    rad = edge_ref[2]
    for c in range(comps):
        spots = slice(8 * c, 8 * c + 8)
        full_ref[spots] = bottom_ref[spots] + rad * hrad[spots]


def second_rest(
    comps,
    parts,
    where_ref,
    full_ref,
    above_ref,
    ax_ref,
    edge_ref,
    bad_ref,
    low_ref,
    high_ref,
    out_ref,
    again_ref,
    done_ref,
    sems,
):
    halo = decode(comps, above_ref, low_ref, high_ref)
    azim = edge_ref[0]
    done_ref[...] = full_ref[...]
    add_axial(comps, 1.0, where_ref, edge_ref[1], ax_ref, done_ref)
    size = comps // parts
    made = []
    for i in range(parts):
        for z in range(4):
            some = pl.ds(8 * size * i + 4 + z, size, stride=8)
            done_ref[some] = (
                done_ref[some] + azim[4 + z : 5 + z] * halo[size * i : size * i + size, 128 * z : 128 * z + 128]
            )
        spots = pl.ds(8 * size * i, 8 * size)
        made.append(pltpu.make_async_copy(done_ref.at[spots], out_ref.at[spots], sems.at[i]))
        made[-1].start()
    again_ref[0] = (jnp.max(bad_ref[...] + above_ref[5 * comps // 2 :]) > 0.0).astype(jnp.int32)
    for copy in made:
        copy.wait()


SPACES = {
    "v": pl.BlockSpec(memory_space=pltpu.VMEM),
    "s": pl.BlockSpec(memory_space=pltpu.SMEM),
    "h": pl.BlockSpec(memory_space=pltpu.HBM),
}


def call(body, ins, outs, shapes, cost, *operands, scratch=()):
    return pl.pallas_call(
        body,
        in_specs=[SPACES[s] for s in ins],
        out_specs=[SPACES[s] for s in outs],
        out_shape=[jax.ShapeDtypeStruct(s, f32) if isinstance(s, tuple) else s for s in shapes],
        scratch_shapes=scratch,
        cost_estimate=pl.CostEstimate(flops=cost, bytes_accessed=cost // 10, transcendentals=0),
        compiler_params=pltpu.CompilerParams(vmem_limit_bytes=32 * 1024 * 1024),
    )(*operands)


def shift(x, axis, step, wrap):
    size = lax.axis_size(axis)
    pairs = [(i, (i + step) % size) for i in range(size) if wrap or 0 <= i + step < size]
    return lax.ppermute(x, axis, pairs)


def sides(ax, radup, raddn):
    ax = lax.ppermute(ax, "axial", [(0, 1), (1, 0)])
    return ax, shift(radup, "rad", 1, True), shift(raddn, "rad", -1, True)


def shards(adjoint_final, state_start, state_middle, speeds, flags, zones, growth_rate, transfer_rate, nucleation_rate):
    shape = adjoint_final.shape
    moments, sections = shape[:2]
    comps = moments * sections
    assert moments == 4 and shape[2:] == (2, 4, 128) and comps % 4 == 0
    assert lax.axis_size("axial") == 2
    cells = 8 * comps
    half, rows = cells // 2, cells // 4
    a = adjoint_final.reshape(cells, 128)
    speeds2 = speeds.reshape(3, 8, 128)
    flags2 = flags.reshape(3, 8, 128)
    where = lax.axis_index("axial").reshape(1)
    place = (where, lax.axis_index("rad").reshape(1))
    last = lax.axis_size("rad") - 1
    rates = (zones.reshape(8, 128), growth_rate, transfer_rate, nucleation_rate)
    message = 5 * comps // 2
    tables = [jax.ShapeDtypeStruct((256, 512), bf16)] * 2

    keep = ((0, 2, 0), (0, -1, 0), (0, 0, 0), (0, 0, 0))
    after = ((comps, -1, 0), (0, -1, 0), (0, 0, 0), (0, 0, 0))
    dn = lax.pad(adjoint_final.reshape(comps, 2, 4, 128), 0.0, keep)
    dn = dn + lax.pad(speeds, 0.0, after) * lax.pad(flags, 0, after).astype(f32)
    above = shift(dn.reshape(half + 8, 128), "azim", -1, True)
    up, up2, *edges = call(
        functools.partial(first_rest, comps, last),
        "ssvvv",
        "vvvvv",
        [(half // 2 + 8, 128), (half // 2, 128), (rows + 8, 128), (1, cells + 128), (1, cells + 128)],
        2_000_000,
        *place,
        a,
        speeds2,
        flags2,
    )
    below, below2 = shift(up, "azim", 1, True), shift(up2, "azim", 1, True)
    edges = sides(*edges)
    part, *lower_tables = call(
        functools.partial(first_local, sections),
        "vvvvvsss",
        "vvvvv",
        [(cells, 128)] + 2 * tables,
        8_000_000,
        a,
        state_middle.reshape(comps, 8, 128),
        speeds2,
        flags2,
        *rates,
    )
    part, edge, up, bad, *upper_tables = call(
        functools.partial(first_top, comps),
        "s" + "v" * 9,
        "v" * 8,
        [(cells, 128), (4, 8, 128), (message, 128), (8, 128)] + 2 * tables,
        4_000_000,
        where,
        part,
        a,
        above,
        below,
        *edges,
        speeds2,
        flags2,
    )
    next_below = shift(up, "azim", 1, True)
    m, dn, *edges = call(
        functools.partial(first_bottom, comps, last),
        "ss" + "v" * 6,
        "v" * 5,
        [(cells, 128), (message + 8, 128), (rows, 128), (1, cells), (1, cells)],
        10_000,
        *place,
        part,
        below2,
        edge,
        bad,
        *lower_tables[:2],
    )
    next_above = shift(dn, "azim", -1, True)
    ax, radlo, radhi = sides(*edges)
    part, bottom = call(
        functools.partial(second_local, sections),
        "v" * 10 + "sss",
        "vv",
        [(cells, 128), (cells, 128)],
        300_000_000,
        m,
        a,
        state_start.reshape(comps, 8, 128),
        next_below,
        edge,
        *lower_tables[2:],
        speeds2,
        flags2,
        *rates,
    )
    (full,) = call(
        functools.partial(second_radial, comps),
        "v" * 4,
        "v",
        [(cells, 128)],
        1_000,
        bottom,
        radlo,
        radhi,
        edge,
    )
    out, again = call(
        functools.partial(second_rest, comps, 4),
        "s" + "v" * 7,
        "hs",
        [pltpu.HBM((cells, 128), f32), jax.ShapeDtypeStruct((1,), jnp.int32)],
        1_000_000,
        where,
        full,
        next_above,
        ax,
        edge,
        bad,
        *upper_tables[:2],
        scratch=[pltpu.VMEM((cells, 128), f32), pltpu.SemaphoreType.DMA((4,))],
    )

    def whole():
        rows_ = m.reshape(comps, 2, 4, 128)
        halo = jnp.stack([shift(rows_[:, 1], "azim", 1, True), shift(rows_[:, 0], "azim", -1, True)], axis=1)
        azimuthal = (edge[0].reshape(1, 2, 4, 128) * halo).reshape(comps, 8, 128)
        row, lane = jnp.arange(8).reshape(1, 8, 1), jnp.arange(128).reshape(1, 1, 128)
        two = jnp.repeat(ax.reshape(comps, 2, 128) * edge[1, :2], 4, axis=1)
        axial = jnp.where(row % 4 == 3 * (1 - where[0]), two, 0.0)
        lower, upper = radlo.reshape(comps, 8, 1), radhi.reshape(comps, 8, 1)
        radial = edge[2] * jnp.where(lane == 0, lower, jnp.where(lane == 127, upper, 0.0))
        return part + (azimuthal + axial + radial).reshape(cells, 128)

    again = again[0]
    if lax.axis_size("azim") != 4:
        again = lax.pmax(again.astype(f32), "azim").astype(jnp.int32)
    return lax.switch(again, (lambda: out, whole)).reshape(shape)


def solution(mesh):
    field = P(None, None, "azim", "axial", "rad")
    faces_spec = P(None, "azim", "axial", "rad")
    return jax.shard_map(
        shards,
        mesh=mesh,
        in_specs=(field, field, field, faces_spec, faces_spec, P("azim", "axial", "rad"), P(), P(), P()),
        out_specs=field,
        check_vma=False,
    )
```

```python
import functools

import jax
import jax.numpy as jnp
from jax import lax
from jax.experimental import pallas as pl
from jax.experimental.pallas import tpu as pltpu
from jax.sharding import PartitionSpec as P

supersat_scale = 1.5
crowding = 0.02
nucleus_moments = (1.0, 0.5, 0.25, 0.125)
f32 = jnp.float32
bf16 = jnp.bfloat16

slots = 320
extra = slots - 256


def rows_of():
    return lax.broadcasted_iota(jnp.int32, (8, 128), 0)


def lanes_of():
    return lax.broadcasted_iota(jnp.int32, (8, 128), 1)


def faces(speeds_ref, flags_ref):
    p, q = [], []
    for d in range(3):
        speed, upwind = speeds_ref[d], flags_ref[d].astype(f32)
        p.append(speed * upwind)
        q.append(speed * (1.0 - upwind))
    return p, q


class Local:
    def __init__(self, p, q):
        row, lane = rows_of(), lanes_of()
        z, top = row % 4, row >= 4
        self.azim = jnp.where(top, q[0], pltpu.roll(p[0], 4, 0))
        self.ax_up = jnp.where(z == 3, 0.0, pltpu.roll(p[1], 7, 0))
        self.ax_dn = jnp.where(z == 0, 0.0, q[1])
        self.rad_up = jnp.where(lane == 127, 0.0, pltpu.roll(p[2], 127, 1))
        self.rad_dn = jnp.where(lane == 0, 0.0, q[2])
        self.centre = self.azim + self.ax_up + q[1] + self.rad_up + q[2] + jnp.where(top, 0.0, q[0])

    def __call__(self, x):
        return (
            self.azim * pltpu.roll(x, 4, 0)
            + self.ax_up * pltpu.roll(x, 7, 0)
            + self.ax_dn * pltpu.roll(x, 1, 0)
            + self.rad_up * pltpu.roll(x, 127, 1)
            + self.rad_dn * pltpu.roll(x, 1, 1)
            - self.centre * x
        )


def pair_rows(x, first, second):
    return jnp.where(
        rows_of() % 2 == 0,
        jnp.broadcast_to(x[first : first + 1], (8, 128)),
        jnp.broadcast_to(x[second : second + 1], (8, 128)),
    )


def make_tables(p, where_zero, low_ref, high_ref):
    row, lane = rows_of(), lanes_of()
    taken = (p == 0.0) if where_zero else (p != 0.0)
    one = jnp.where(taken & (row < 4), 1.0, 0.0)
    before = lax.broadcasted_iota(jnp.int32, (128, 128), 0) < lax.broadcasted_iota(jnp.int32, (128, 128), 1)
    inside = jnp.dot(one.astype(bf16), jnp.where(before, 1.0, 0.0).astype(bf16), preferred_element_type=f32)
    total = jnp.sum(one, axis=1, keepdims=True)
    base = jnp.zeros((8, 1), f32)
    for step in (1, 2, 3):
        base = base + jnp.where(
            lax.broadcasted_iota(jnp.int32, (8, 1), 0) >= step, jnp.roll(total, step, axis=0), 0.0
        )
    slot = jnp.where(one > 0.0, inside + base, -1.0).astype(jnp.int32)
    here = lax.broadcasted_iota(jnp.int32, (128, 128), 0)
    first = jnp.where(here < extra, here + 256, -2)
    second = jnp.where(here >= extra, here + (256 - extra), -2)
    for z in range(4):
        cells = slice(128 * z, 128 * z + 128)
        want = jnp.broadcast_to(slot[z : z + 1], (128, 128))
        for ref, start, names in ((low_ref, 0, here), (low_ref, 128, here + 128), (high_ref, 0, first), (high_ref, 128, second)):
            ref[start : start + 128, cells] = jnp.where(names == want, 1.0, 0.0).astype(bf16)


def crowded(p):
    taken = jnp.where((rows_of() < 4) & (p != 0.0), 1.0, 0.0)
    count = jnp.sum(jnp.sum(taken, axis=1, keepdims=True), axis=0, keepdims=True)
    count = jnp.broadcast_to(count, (8, 128))
    return jnp.where(jnp.maximum(count, 512.0 - count) > slots, 1.0, 0.0)


def pieces(x):
    high = x.astype(bf16)
    rest = x - high.astype(f32)
    middle = rest.astype(bf16)
    return high, middle, (rest - middle.astype(f32)).astype(bf16)


def stacked(x, half):
    return jnp.concatenate([part[half * i : half * i + half] for i in range(2) for part in pieces(x)], axis=0)


def summed(x, half):
    parts = [x[half * i : half * i + half] for i in range(6)]
    return [parts[3 * i] + (parts[3 * i + 1] + parts[3 * i + 2]) for i in range(2)]


def encode(comps, x_ref, first_row, low_ref, high_ref, message_ref):
    half = comps // 2
    x = jnp.concatenate(
        [stacked(x_ref[pl.ds(first_row + z, comps, stride=8)], half) for z in range(4)], axis=1
    )
    over = (((1,), (1,)), ((), ()))
    low = lax.dot_general(x, low_ref[...], over, preferred_element_type=f32)
    high = [
        lax.dot_general(
            x[3 * half * i : 3 * half * (i + 1)], high_ref[128 * i : 128 * i + 128], over, preferred_element_type=f32
        )
        for i in range(2)
    ]
    tail = jnp.zeros((half, 128), f32)
    for i, part in enumerate(summed(low, half)):
        message_ref[half * i : half * i + half] = part[:, :128]
        message_ref[comps + half * i : comps + half * i + half] = part[:, 128:]
    for part in high:
        tail = tail + (part[:half] + (part[half : 2 * half] + part[2 * half :]))
    message_ref[2 * comps : 2 * comps + half] = tail


def decode(comps, message_ref, low_ref, high_ref):
    half = comps // 2
    x = jnp.concatenate([stacked(message_ref[comps * i : comps * i + comps], half) for i in range(2)], axis=1)
    low = jnp.dot(x, low_ref[...], preferred_element_type=f32)
    tail = jnp.concatenate(pieces(message_ref[2 * comps : 2 * comps + half]), axis=0)
    found = []
    for i, part in enumerate(summed(low, half)):
        high = jnp.dot(tail, high_ref[128 * i : 128 * i + 128], preferred_element_type=f32)
        found.append(part + (high[:half] + (high[half : 2 * half] + high[2 * half :])))
    return jnp.concatenate(found, axis=0)


def add_azimuthal(comps, halo, coefficient, first_row, out_ref):
    for z in range(4):
        spots = pl.ds(first_row + z, comps, stride=8)
        out_ref[spots] = out_ref[spots] + coefficient[first_row + z : first_row + z + 1] * halo[:, 128 * z : 128 * z + 128]


def pack_sides(comps, last, x_ref, where_ref, rad_ref, ax_ref, radup_ref, raddn_ref):
    @pl.when(where_ref[0] == 0)
    def _():
        ax_ref[0 : 2 * comps] = x_ref[pl.ds(3, 2 * comps, stride=4)]

    @pl.when(where_ref[0] != 0)
    def _():
        ax_ref[0 : 2 * comps] = x_ref[pl.ds(0, 2 * comps, stride=4)]

    ends = columns(x_ref[...])
    radup_ref[:, 0 : 8 * comps] = jnp.where(rad_ref[0] < last, ends[0:1], 0.0)
    raddn_ref[:, 0 : 8 * comps] = jnp.where(rad_ref[0] > 0, ends[1:2], 0.0)


def columns(x):
    row, lane = rows_of(), lanes_of()
    take = jnp.where(((row == 0) & (lane == 127)) | ((row == 1) & (lane == 0)), 1.0, 0.0).astype(bf16)
    high, middle, low = (
        lax.dot_general(take, part, (((1,), (1,)), ((), ())), preferred_element_type=f32) for part in pieces(x)
    )
    return high + (middle + low)


def put_columns(lower, upper):
    n = lower.shape[1]
    row, lane = rows_of(), lanes_of()
    which = lax.broadcasted_iota(jnp.int32, (8, n), 0)
    both = jnp.where(which == 0, lower, jnp.where(which == 1, upper, 0.0))
    place = jnp.where(((row == 0) & (lane == 0)) | ((row == 1) & (lane == 127)), 1.0, 0.0)
    parts = jnp.concatenate([part.astype(f32) for part in pieces(both)], axis=0).astype(bf16)
    places = jnp.concatenate([place] * 3, axis=0).astype(bf16)
    return lax.dot_general(parts, places, (((0,), (0,)), ((), ())), preferred_element_type=f32)


def first_rest(comps, last, where_ref, rad_ref, a_ref, speeds_ref, flags_ref, up_ref, ax_ref, radup_ref, raddn_ref):
    p, _ = faces(speeds_ref, flags_ref)
    for c in range(comps):
        up_ref[4 * c : 4 * c + 4] = a_ref[8 * c + 4 : 8 * c + 8]
    up_ref[4 * comps :] = p[0]
    pack_sides(comps, last, a_ref, where_ref, rad_ref, ax_ref, radup_ref, raddn_ref)
    ax_ref[2 * comps : 2 * comps + 8] = pair_rows(p[1], 0, 4)
    radup_ref[:, 8 * comps :] = jnp.zeros((1, 128), f32)
    raddn_ref[:, 8 * comps :] = jnp.zeros((1, 128), f32)
    raddn_ref[:, 8 * comps : 8 * comps + 8] = jnp.where(rad_ref[0] > 0, columns(p[2])[1:2], 0.0)


def source(sections, x_ref, u_ref, growth_ref, transfer_ref, zones_ref, rate_ref, finish):
    def inner(k, s, x):
        term = transfer_ref[s] * ((x[k][1] - x[k][0]) if s + 1 < sections else -x[k][0])
        if k < 3:
            term = term + ((k + 1.0) * growth_ref[s]) * x[k + 1][0]
        return term

    def load(s):
        got = []
        for k in range(4):
            c = k * sections + s
            here = x_ref[8 * c : 8 * c + 8]
            got.append((here, x_ref[8 * c + 8 : 8 * c + 16] if s + 1 < sections else None))
        return got

    squares = jnp.zeros((8, 128), f32)
    product = jnp.zeros((8, 128), f32)
    for s in range(sections):
        x = load(s)
        for k in range(4):
            u = u_ref[k * sections + s].astype(f32)
            product = product + u * inner(k, s, x)
        squares = squares + u * u
    sigma = supersat_scale / (1.0 + crowding * squares)
    birth = jnp.zeros((8, 128), f32)
    for k in range(4):
        c = k * sections
        birth = birth + nucleus_moments[k] * x_ref[8 * c : 8 * c + 8]
    rate = jnp.zeros((8, 128), f32)
    for label in range(rate_ref.shape[0]):
        rate = jnp.where(zones_ref[...] == label, rate_ref[label], rate)
    slope = (-2.0 * crowding / supersat_scale) * sigma * sigma * (product + 2.0 * rate * sigma * birth)
    for s in range(sections):
        x = load(s)
        for k in range(4):
            c = k * sections + s
            term = sigma * inner(k, s, x)
            if k == 3:
                term = term + u_ref[c].astype(f32) * slope
            finish(c, x[k][0], term)


def first_local(
    sections,
    a_ref,
    u_ref,
    speeds_ref,
    flags_ref,
    zones_ref,
    growth_ref,
    transfer_ref,
    rate_ref,
    out_ref,
    dn_low_ref,
    dn_high_ref,
    up_low_ref,
    up_high_ref,
):
    p, q = faces(speeds_ref, flags_ref)
    local = Local(p, q)
    make_tables(p[0], False, dn_low_ref, dn_high_ref)
    make_tables(p[0], True, up_low_ref, up_high_ref)

    def finish(c, x, term):
        out_ref[8 * c : 8 * c + 8] = 0.5 * (x + local(x) + term)

    source(sections, a_ref, u_ref, growth_ref, transfer_ref, zones_ref, rate_ref, finish)


def second_local(
    sections,
    m_ref,
    a_ref,
    u_ref,
    below_ref,
    edge_ref,
    low_ref,
    high_ref,
    speeds_ref,
    flags_ref,
    zones_ref,
    growth_ref,
    transfer_ref,
    rate_ref,
    out_ref,
    bottom_ref,
):
    local = Local(*faces(speeds_ref, flags_ref))
    local.centre = local.centre + (edge_ref[3] - 1.0)

    def finish(c, x, term):
        out_ref[8 * c : 8 * c + 8] = 0.5 * a_ref[8 * c : 8 * c + 8] + (local(x) + term)

    source(sections, m_ref, u_ref, growth_ref, transfer_ref, zones_ref, rate_ref, finish)
    bottom_ref[...] = out_ref[...]
    add_azimuthal(4 * sections, decode(4 * sections, below_ref, low_ref, high_ref), edge_ref[0], 0, bottom_ref)


def from_below(c, below_ref):
    pair = below_ref[8 * (c // 2) : 8 * (c // 2) + 8]
    return pair if c % 2 == 0 else pltpu.roll(pair, 4, 0)


def from_above(c, above_ref):
    pair = above_ref[8 * (c // 2) : 8 * (c // 2) + 8]
    return pair if c % 2 == 1 else pltpu.roll(pair, 4, 0)


def add_axial(comps, scale, where_ref, axial, ax_ref, out_ref):
    several = jnp.concatenate([scale * axial] * (2 * comps // 8), axis=0)
    for start, index in ((3, 0), (0, 1)):

        @pl.when(where_ref[0] == index)
        def _():
            spots = pl.ds(start, 2 * comps, stride=4)
            out_ref[spots] = out_ref[spots] + several * ax_ref[0 : 2 * comps]


def first_top(
    comps,
    where_ref,
    part_ref,
    a_ref,
    above_ref,
    ax_ref,
    radlo_ref,
    radhi_ref,
    speeds_ref,
    flags_ref,
    m_ref,
    edge_ref,
    up_ref,
    bad_ref,
    dn_low_ref,
    dn_high_ref,
    up_low_ref,
    up_high_ref,
):
    p, q = faces(speeds_ref, flags_ref)
    row, lane = rows_of(), lanes_of()
    upper = above_ref[4 * comps :]
    make_tables(upper, True, up_low_ref, up_high_ref)
    make_tables(upper, False, dn_low_ref, dn_high_ref)
    bad_ref[...] = crowded(p[0]) + crowded(upper)
    hrad = put_columns(radlo_ref[...], radhi_ref[...])
    lower_half = where_ref[0] == 0
    p_azim = jnp.where(row >= 4, pltpu.roll(upper, 4, 0), 0.0)
    pairs = jnp.where(lower_half, ax_ref[2 * comps : 2 * comps + 8], 0.0)
    p_axial = jnp.where(row == 3, pairs[0:1], jnp.where(row == 7, pairs[1:2], 0.0))
    p_rad = jnp.where(lane == 127, hrad[8 * comps : 8 * comps + 8], 0.0)
    axial = jnp.where(lower_half, pairs, pair_rows(q[1], 0, 4))
    rad = jnp.where(lane == 0, q[2], p_rad)
    centre = p_azim + p_axial + p_rad
    edge_ref[0] = jnp.where(row >= 4, p_azim, q[0])
    edge_ref[1] = axial
    edge_ref[2] = rad
    edge_ref[3] = centre
    for c in range(comps):
        spots = slice(8 * c, 8 * c + 8)
        m_ref[spots] = part_ref[spots] + 0.5 * (
            p_azim * from_above(c, above_ref) + rad * hrad[spots] - centre * a_ref[spots]
        )
    add_axial(comps, 0.5, where_ref, axial, ax_ref, m_ref)
    encode(comps, m_ref, 4, up_low_ref, up_high_ref, up_ref)


def first_bottom(
    comps,
    last,
    where_ref,
    rad_ref,
    part_ref,
    below_ref,
    edge_ref,
    bad_ref,
    low_ref,
    high_ref,
    m_ref,
    dn_ref,
    ax_ref,
    radup_ref,
    raddn_ref,
    worse_ref,
):
    azim = jnp.where(rows_of() >= 4, 0.0, 0.5 * edge_ref[0])
    for c in range(comps):
        m_ref[8 * c : 8 * c + 8] = part_ref[8 * c : 8 * c + 8] + azim * from_below(c, below_ref)
    encode(comps, m_ref, 0, low_ref, high_ref, dn_ref)
    worse_ref[...] = bad_ref[...] + crowded(below_ref[4 * comps :])
    dn_ref[5 * comps // 2 :] = worse_ref[...]
    pack_sides(comps, last, m_ref, where_ref, rad_ref, ax_ref, radup_ref, raddn_ref)


def second_radial(comps, bottom_ref, radlo_ref, radhi_ref, edge_ref, full_ref):
    hrad = put_columns(radlo_ref[...], radhi_ref[...])
    rad = edge_ref[2]
    for c in range(comps):
        spots = slice(8 * c, 8 * c + 8)
        full_ref[spots] = bottom_ref[spots] + rad * hrad[spots]


def second_rest(
    comps,
    parts,
    where_ref,
    full_ref,
    above_ref,
    ax_ref,
    edge_ref,
    bad_ref,
    low_ref,
    high_ref,
    out_ref,
    again_ref,
    done_ref,
    sems,
):
    again_ref[0] = (jnp.max(bad_ref[...] + above_ref[5 * comps // 2 :]) > 0.0).astype(jnp.int32)
    halo = decode(comps, above_ref, low_ref, high_ref)
    azim = edge_ref[0]
    done_ref[...] = full_ref[...]
    add_axial(comps, 1.0, where_ref, edge_ref[1], ax_ref, done_ref)
    size = comps // parts
    made = []
    for i in range(parts):
        for z in range(4):
            some = pl.ds(8 * size * i + 4 + z, size, stride=8)
            done_ref[some] = (
                done_ref[some] + azim[4 + z : 5 + z] * halo[size * i : size * i + size, 128 * z : 128 * z + 128]
            )
        spots = pl.ds(8 * size * i, 8 * size)
        made.append(pltpu.make_async_copy(done_ref.at[spots], out_ref.at[spots], sems.at[i]))
        made[-1].start()
    for copy in made:
        copy.wait()


SPACES = {
    "v": pl.BlockSpec(memory_space=pltpu.VMEM),
    "s": pl.BlockSpec(memory_space=pltpu.SMEM),
    "h": pl.BlockSpec(memory_space=pltpu.HBM),
}


def call(body, ins, outs, shapes, cost, *operands, scratch=()):
    return pl.pallas_call(
        body,
        in_specs=[SPACES[s] for s in ins],
        out_specs=[SPACES[s] for s in outs],
        out_shape=[jax.ShapeDtypeStruct(s, f32) if isinstance(s, tuple) else s for s in shapes],
        scratch_shapes=scratch,
        cost_estimate=pl.CostEstimate(flops=cost, bytes_accessed=cost // 10, transcendentals=0),
        compiler_params=pltpu.CompilerParams(vmem_limit_bytes=32 * 1024 * 1024),
    )(*operands)


def shift(x, axis, step, wrap):
    size = lax.axis_size(axis)
    pairs = [(i, (i + step) % size) for i in range(size) if wrap or 0 <= i + step < size]
    return lax.ppermute(x, axis, pairs)


def sides(ax, radup, raddn):
    ax = lax.ppermute(ax, "axial", [(0, 1), (1, 0)])
    return ax, shift(radup, "rad", 1, True), shift(raddn, "rad", -1, True)


def shards(adjoint_final, state_start, state_middle, speeds, flags, zones, growth_rate, transfer_rate, nucleation_rate):
    shape = adjoint_final.shape
    moments, sections = shape[:2]
    comps = moments * sections
    assert moments == 4 and shape[2:] == (2, 4, 128) and comps % 4 == 0
    assert lax.axis_size("axial") == 2
    cells = 8 * comps
    half, rows = cells // 2, cells // 4
    a = adjoint_final.reshape(cells, 128)
    speeds2 = speeds.reshape(3, 8, 128)
    flags2 = flags.reshape(3, 8, 128)
    where = lax.axis_index("axial").reshape(1)
    place = (where, lax.axis_index("rad").reshape(1))
    last = lax.axis_size("rad") - 1
    rates = (zones.reshape(8, 128), growth_rate, transfer_rate, nucleation_rate)
    message = 5 * comps // 2
    tables = [jax.ShapeDtypeStruct((256, 512), bf16)] * 2

    keep = ((0, 2, 0), (0, -1, 0), (0, 0, 0), (0, 0, 0))
    after = ((comps, -1, 0), (0, -1, 0), (0, 0, 0), (0, 0, 0))
    dn = lax.pad(adjoint_final.reshape(comps, 2, 4, 128), 0.0, keep)
    dn = dn + lax.pad(speeds, 0.0, after) * lax.pad(flags, 0, after).astype(f32)
    above = shift(dn.reshape(half + 8, 128), "azim", -1, True)
    up, *edges = call(
        functools.partial(first_rest, comps, last),
        "ssvvv",
        "vvvv",
        [(half + 8, 128), (rows + 8, 128), (1, cells + 128), (1, cells + 128)],
        2_000_000,
        *place,
        a,
        speeds2,
        flags2,
    )
    below = shift(up, "azim", 1, True)
    edges = sides(*edges)
    part, *lower_tables = call(
        functools.partial(first_local, sections),
        "vvvvvsss",
        "vvvvv",
        [(cells, 128)] + 2 * tables,
        8_000_000,
        a,
        state_middle.reshape(comps, 8, 128),
        speeds2,
        flags2,
        *rates,
    )
    part, edge, up, bad, *upper_tables = call(
        functools.partial(first_top, comps),
        "s" + "v" * 8,
        "v" * 8,
        [(cells, 128), (4, 8, 128), (message, 128), (8, 128)] + 2 * tables,
        4_000_000,
        where,
        part,
        a,
        above,
        *edges,
        speeds2,
        flags2,
    )
    next_below = shift(up, "azim", 1, True)
    m, dn, *edges, bad = call(
        functools.partial(first_bottom, comps, last),
        "ss" + "v" * 6,
        "v" * 6,
        [(cells, 128), (message + 8, 128), (rows, 128), (1, cells), (1, cells), (8, 128)],
        10_000,
        *place,
        part,
        below,
        edge,
        bad,
        *lower_tables[:2],
    )
    next_above = shift(dn, "azim", -1, True)
    ax, radlo, radhi = sides(*edges)
    part, bottom = call(
        functools.partial(second_local, sections),
        "v" * 10 + "sss",
        "vv",
        [(cells, 128), (cells, 128)],
        300_000_000,
        m,
        a,
        state_start.reshape(comps, 8, 128),
        next_below,
        edge,
        *lower_tables[2:],
        speeds2,
        flags2,
        *rates,
    )
    (full,) = call(
        functools.partial(second_radial, comps),
        "v" * 4,
        "v",
        [(cells, 128)],
        1_000,
        bottom,
        radlo,
        radhi,
        edge,
    )
    out, again = call(
        functools.partial(second_rest, comps, 4),
        "s" + "v" * 7,
        "hs",
        [pltpu.HBM((cells, 128), f32), jax.ShapeDtypeStruct((1,), jnp.int32)],
        1_000_000,
        where,
        full,
        next_above,
        ax,
        edge,
        bad,
        *upper_tables[:2],
        scratch=[pltpu.VMEM((cells, 128), f32), pltpu.SemaphoreType.DMA((4,))],
    )

    def whole():
        rows_ = m.reshape(comps, 2, 4, 128)
        halo = jnp.stack([shift(rows_[:, 1], "azim", 1, True), shift(rows_[:, 0], "azim", -1, True)], axis=1)
        azimuthal = (edge[0].reshape(1, 2, 4, 128) * halo).reshape(comps, 8, 128)
        row, lane = jnp.arange(8).reshape(1, 8, 1), jnp.arange(128).reshape(1, 1, 128)
        two = jnp.repeat(ax.reshape(comps, 2, 128) * edge[1, :2], 4, axis=1)
        axial = jnp.where(row % 4 == 3 * (1 - where[0]), two, 0.0)
        lower, upper = radlo.reshape(comps, 8, 1), radhi.reshape(comps, 8, 1)
        radial = edge[2] * jnp.where(lane == 0, lower, jnp.where(lane == 127, upper, 0.0))
        return part + (azimuthal + axial + radial).reshape(cells, 128)

    again = again[0]
    if lax.axis_size("azim") != 4:
        again = lax.pmax(again.astype(f32), "azim").astype(jnp.int32)
    return lax.switch(again, (lambda: out, whole)).reshape(shape)


def solution(mesh):
    field = P(None, None, "azim", "axial", "rad")
    faces_spec = P(None, "azim", "axial", "rad")
    return jax.shard_map(
        shards,
        mesh=mesh,
        in_specs=(field, field, field, faces_spec, faces_spec, P("azim", "axial", "rad"), P(), P(), P()),
        out_specs=field,
        check_vma=False,
    )
```

```python
import functools

import jax
import jax.numpy as jnp
from jax import lax
from jax.experimental import pallas as pl
from jax.experimental.pallas import tpu as pltpu
from jax.sharding import PartitionSpec as P

supersat_scale = 1.5
crowding = 0.02
nucleus_moments = (1.0, 0.5, 0.25, 0.125)
f32 = jnp.float32
bf16 = jnp.bfloat16

slots = 320
extra = slots - 256


def rows_of():
    return lax.broadcasted_iota(jnp.int32, (8, 128), 0)


def lanes_of():
    return lax.broadcasted_iota(jnp.int32, (8, 128), 1)


def faces(speeds_ref, flags_ref):
    p, q = [], []
    for d in range(3):
        speed, upwind = speeds_ref[d], flags_ref[d].astype(f32)
        p.append(speed * upwind)
        q.append(speed * (1.0 - upwind))
    return p, q


class Local:
    def __init__(self, p, q):
        row, lane = rows_of(), lanes_of()
        z, top = row % 4, row >= 4
        self.azim = jnp.where(top, q[0], pltpu.roll(p[0], 4, 0))
        self.ax_up = jnp.where(z == 3, 0.0, pltpu.roll(p[1], 7, 0))
        self.ax_dn = jnp.where(z == 0, 0.0, q[1])
        self.rad_up = jnp.where(lane == 127, 0.0, pltpu.roll(p[2], 127, 1))
        self.rad_dn = jnp.where(lane == 0, 0.0, q[2])
        self.centre = self.azim + self.ax_up + q[1] + self.rad_up + q[2] + jnp.where(top, 0.0, q[0])

    def __call__(self, x):
        return (
            self.azim * pltpu.roll(x, 4, 0)
            + self.ax_up * pltpu.roll(x, 7, 0)
            + self.ax_dn * pltpu.roll(x, 1, 0)
            + self.rad_up * pltpu.roll(x, 127, 1)
            + self.rad_dn * pltpu.roll(x, 1, 1)
            - self.centre * x
        )


def pair_rows(x, first, second):
    return jnp.where(
        rows_of() % 2 == 0,
        jnp.broadcast_to(x[first : first + 1], (8, 128)),
        jnp.broadcast_to(x[second : second + 1], (8, 128)),
    )


def make_tables(p, where_zero, low_ref, high_ref):
    row, lane = rows_of(), lanes_of()
    taken = (p == 0.0) if where_zero else (p != 0.0)
    one = jnp.where(taken & (row < 4), 1.0, 0.0)
    before = lax.broadcasted_iota(jnp.int32, (128, 128), 0) < lax.broadcasted_iota(jnp.int32, (128, 128), 1)
    inside = jnp.dot(one.astype(bf16), jnp.where(before, 1.0, 0.0).astype(bf16), preferred_element_type=f32)
    total = jnp.sum(one, axis=1, keepdims=True)
    base = jnp.zeros((8, 1), f32)
    for step in (1, 2, 3):
        base = base + jnp.where(
            lax.broadcasted_iota(jnp.int32, (8, 1), 0) >= step, jnp.roll(total, step, axis=0), 0.0
        )
    slot = jnp.where(one > 0.0, inside + base, -1.0).astype(jnp.int32)
    here = lax.broadcasted_iota(jnp.int32, (128, 128), 0)
    first = jnp.where(here < extra, here + 256, -2)
    second = jnp.where(here >= extra, here + (256 - extra), -2)
    for z in range(4):
        cells = slice(128 * z, 128 * z + 128)
        want = jnp.broadcast_to(slot[z : z + 1], (128, 128))
        for ref, start, names in ((low_ref, 0, here), (low_ref, 128, here + 128), (high_ref, 0, first), (high_ref, 128, second)):
            ref[start : start + 128, cells] = jnp.where(names == want, 1.0, 0.0).astype(bf16)


def crowded(p):
    taken = jnp.where((rows_of() < 4) & (p != 0.0), 1.0, 0.0)
    count = jnp.sum(jnp.sum(taken, axis=1, keepdims=True), axis=0, keepdims=True)
    count = jnp.broadcast_to(count, (8, 128))
    return jnp.where(jnp.maximum(count, 512.0 - count) > slots, 1.0, 0.0)


def pieces(x):
    high = x.astype(bf16)
    rest = x - high.astype(f32)
    middle = rest.astype(bf16)
    return high, middle, (rest - middle.astype(f32)).astype(bf16)


def stacked(x, half):
    return jnp.concatenate([part[half * i : half * i + half] for i in range(2) for part in pieces(x)], axis=0)


def summed(x, half):
    parts = [x[half * i : half * i + half] for i in range(6)]
    return [parts[3 * i] + (parts[3 * i + 1] + parts[3 * i + 2]) for i in range(2)]


def encode(comps, x_ref, first_row, low_ref, high_ref, message_ref):
    half = comps // 2
    x = jnp.concatenate(
        [stacked(x_ref[pl.ds(first_row + z, comps, stride=8)], half) for z in range(4)], axis=1
    )
    over = (((1,), (1,)), ((), ()))
    low = lax.dot_general(x, low_ref[...], over, preferred_element_type=f32)
    high = [
        lax.dot_general(
            x[3 * half * i : 3 * half * (i + 1)], high_ref[128 * i : 128 * i + 128], over, preferred_element_type=f32
        )
        for i in range(2)
    ]
    tail = jnp.zeros((half, 128), f32)
    for i, part in enumerate(summed(low, half)):
        message_ref[half * i : half * i + half] = part[:, :128]
        message_ref[comps + half * i : comps + half * i + half] = part[:, 128:]
    for part in high:
        tail = tail + (part[:half] + (part[half : 2 * half] + part[2 * half :]))
    message_ref[2 * comps : 2 * comps + half] = tail


def decode(comps, message_ref, low_ref, high_ref):
    half = comps // 2
    x = jnp.concatenate([stacked(message_ref[comps * i : comps * i + comps], half) for i in range(2)], axis=1)
    low = jnp.dot(x, low_ref[...], preferred_element_type=f32)
    tail = jnp.concatenate(pieces(message_ref[2 * comps : 2 * comps + half]), axis=0)
    found = []
    for i, part in enumerate(summed(low, half)):
        high = jnp.dot(tail, high_ref[128 * i : 128 * i + 128], preferred_element_type=f32)
        found.append(part + (high[:half] + (high[half : 2 * half] + high[2 * half :])))
    return jnp.concatenate(found, axis=0)


def spread(comps, halo, first_row, out_ref):
    for z in range(4):
        out_ref[pl.ds(first_row + z, comps, stride=8)] = halo[:, 128 * z : 128 * z + 128]


def pack_sides(comps, last, x_ref, where_ref, rad_ref, ax_ref, radup_ref, raddn_ref):
    @pl.when(where_ref[0] == 0)
    def _():
        ax_ref[0 : 2 * comps] = x_ref[pl.ds(3, 2 * comps, stride=4)]

    @pl.when(where_ref[0] != 0)
    def _():
        ax_ref[0 : 2 * comps] = x_ref[pl.ds(0, 2 * comps, stride=4)]

    ends = columns(x_ref[...])
    radup_ref[:, 0 : 8 * comps] = jnp.where(rad_ref[0] < last, ends[0:1], 0.0)
    raddn_ref[:, 0 : 8 * comps] = jnp.where(rad_ref[0] > 0, ends[1:2], 0.0)


def columns(x):
    row, lane = rows_of(), lanes_of()
    take = jnp.where(((row == 0) & (lane == 127)) | ((row == 1) & (lane == 0)), 1.0, 0.0).astype(bf16)
    high, middle, low = (
        lax.dot_general(take, part, (((1,), (1,)), ((), ())), preferred_element_type=f32) for part in pieces(x)
    )
    return high + (middle + low)


def put_columns(lower, upper):
    n = lower.shape[1]
    row, lane = rows_of(), lanes_of()
    which = lax.broadcasted_iota(jnp.int32, (8, n), 0)
    both = jnp.where(which == 0, lower, jnp.where(which == 1, upper, 0.0))
    place = jnp.where(((row == 0) & (lane == 0)) | ((row == 1) & (lane == 127)), 1.0, 0.0)
    parts = jnp.concatenate([part.astype(f32) for part in pieces(both)], axis=0).astype(bf16)
    places = jnp.concatenate([place] * 3, axis=0).astype(bf16)
    return lax.dot_general(parts, places, (((0,), (0,)), ((), ())), preferred_element_type=f32)


def first_rest(comps, last, where_ref, rad_ref, a_ref, speeds_ref, flags_ref, up_ref, ax_ref, radup_ref, raddn_ref):
    p, _ = faces(speeds_ref, flags_ref)
    for c in range(comps):
        up_ref[4 * c : 4 * c + 4] = a_ref[8 * c + 4 : 8 * c + 8]
    up_ref[4 * comps :] = p[0]
    pack_sides(comps, last, a_ref, where_ref, rad_ref, ax_ref, radup_ref, raddn_ref)
    ax_ref[2 * comps : 2 * comps + 8] = pair_rows(p[1], 0, 4)
    radup_ref[:, 8 * comps :] = jnp.zeros((1, 128), f32)
    raddn_ref[:, 8 * comps :] = jnp.zeros((1, 128), f32)
    raddn_ref[:, 8 * comps : 8 * comps + 8] = jnp.where(rad_ref[0] > 0, columns(p[2])[1:2], 0.0)


def source(sections, x_ref, u_ref, growth_ref, transfer_ref, zones_ref, rate_ref, finish):
    def inner(k, s, x):
        term = transfer_ref[s] * ((x[k][1] - x[k][0]) if s + 1 < sections else -x[k][0])
        if k < 3:
            term = term + ((k + 1.0) * growth_ref[s]) * x[k + 1][0]
        return term

    def load(s):
        got = []
        for k in range(4):
            c = k * sections + s
            here = x_ref[8 * c : 8 * c + 8]
            got.append((here, x_ref[8 * c + 8 : 8 * c + 16] if s + 1 < sections else None))
        return got

    squares = jnp.zeros((8, 128), f32)
    product = jnp.zeros((8, 128), f32)
    for s in range(sections):
        x = load(s)
        for k in range(4):
            u = u_ref[k * sections + s].astype(f32)
            product = product + u * inner(k, s, x)
        squares = squares + u * u
    sigma = supersat_scale / (1.0 + crowding * squares)
    birth = jnp.zeros((8, 128), f32)
    for k in range(4):
        c = k * sections
        birth = birth + nucleus_moments[k] * x_ref[8 * c : 8 * c + 8]
    rate = jnp.zeros((8, 128), f32)
    for label in range(rate_ref.shape[0]):
        rate = jnp.where(zones_ref[...] == label, rate_ref[label], rate)
    slope = (-2.0 * crowding / supersat_scale) * sigma * sigma * (product + 2.0 * rate * sigma * birth)
    for s in range(sections):
        x = load(s)
        for k in range(4):
            c = k * sections + s
            term = sigma * inner(k, s, x)
            if k == 3:
                term = term + u_ref[c].astype(f32) * slope
            finish(c, x[k][0], term)


def first_local(
    sections,
    a_ref,
    u_ref,
    speeds_ref,
    flags_ref,
    zones_ref,
    growth_ref,
    transfer_ref,
    rate_ref,
    out_ref,
    dn_low_ref,
    dn_high_ref,
    up_low_ref,
    up_high_ref,
):
    p, q = faces(speeds_ref, flags_ref)
    local = Local(p, q)
    make_tables(p[0], False, dn_low_ref, dn_high_ref)
    make_tables(p[0], True, up_low_ref, up_high_ref)

    def finish(c, x, term):
        out_ref[8 * c : 8 * c + 8] = 0.5 * (x + local(x) + term)

    source(sections, a_ref, u_ref, growth_ref, transfer_ref, zones_ref, rate_ref, finish)


def second_local(
    sections,
    m_ref,
    a_ref,
    u_ref,
    below_ref,
    edge_ref,
    low_ref,
    high_ref,
    speeds_ref,
    flags_ref,
    zones_ref,
    growth_ref,
    transfer_ref,
    rate_ref,
    out_ref,
    bottom_ref,
    halo_ref,
):
    local = Local(*faces(speeds_ref, flags_ref))
    local.centre = local.centre + (edge_ref[3] - 1.0)

    def finish(c, x, term):
        out_ref[8 * c : 8 * c + 8] = 0.5 * a_ref[8 * c : 8 * c + 8] + (local(x) + term)

    source(sections, m_ref, u_ref, growth_ref, transfer_ref, zones_ref, rate_ref, finish)
    spread(4 * sections, decode(4 * sections, below_ref, low_ref, high_ref), 0, halo_ref)
    azim, bottom = edge_ref[0], rows_of() < 4
    for c in range(4 * sections):
        spots = slice(8 * c, 8 * c + 8)
        bottom_ref[spots] = out_ref[spots] + jnp.where(bottom, azim * halo_ref[spots], 0.0)


def from_below(c, below_ref):
    pair = below_ref[8 * (c // 2) : 8 * (c // 2) + 8]
    return pair if c % 2 == 0 else pltpu.roll(pair, 4, 0)


def from_above(c, above_ref):
    pair = above_ref[8 * (c // 2) : 8 * (c // 2) + 8]
    return pair if c % 2 == 1 else pltpu.roll(pair, 4, 0)


def add_axial(comps, scale, where_ref, axial, ax_ref, out_ref):
    several = jnp.concatenate([scale * axial] * (2 * comps // 8), axis=0)
    for start, index in ((3, 0), (0, 1)):

        @pl.when(where_ref[0] == index)
        def _():
            spots = pl.ds(start, 2 * comps, stride=4)
            out_ref[spots] = out_ref[spots] + several * ax_ref[0 : 2 * comps]


def first_top(
    comps,
    where_ref,
    part_ref,
    a_ref,
    above_ref,
    ax_ref,
    radlo_ref,
    radhi_ref,
    speeds_ref,
    flags_ref,
    m_ref,
    edge_ref,
    up_ref,
    bad_ref,
    dn_low_ref,
    dn_high_ref,
    up_low_ref,
    up_high_ref,
):
    p, q = faces(speeds_ref, flags_ref)
    row, lane = rows_of(), lanes_of()
    upper = above_ref[4 * comps :]
    make_tables(upper, True, up_low_ref, up_high_ref)
    make_tables(upper, False, dn_low_ref, dn_high_ref)
    bad_ref[...] = crowded(p[0]) + crowded(upper)
    hrad = put_columns(radlo_ref[...], radhi_ref[...])
    lower_half = where_ref[0] == 0
    p_azim = jnp.where(row >= 4, pltpu.roll(upper, 4, 0), 0.0)
    pairs = jnp.where(lower_half, ax_ref[2 * comps : 2 * comps + 8], 0.0)
    p_axial = jnp.where(row == 3, pairs[0:1], jnp.where(row == 7, pairs[1:2], 0.0))
    p_rad = jnp.where(lane == 127, hrad[8 * comps : 8 * comps + 8], 0.0)
    axial = jnp.where(lower_half, pairs, pair_rows(q[1], 0, 4))
    rad = jnp.where(lane == 0, q[2], p_rad)
    centre = p_azim + p_axial + p_rad
    edge_ref[0] = jnp.where(row >= 4, p_azim, q[0])
    edge_ref[1] = axial
    edge_ref[2] = rad
    edge_ref[3] = centre
    for c in range(comps):
        spots = slice(8 * c, 8 * c + 8)
        m_ref[spots] = part_ref[spots] + 0.5 * (
            p_azim * from_above(c, above_ref) + rad * hrad[spots] - centre * a_ref[spots]
        )
    add_axial(comps, 0.5, where_ref, axial, ax_ref, m_ref)
    encode(comps, m_ref, 4, up_low_ref, up_high_ref, up_ref)


def first_bottom(
    comps,
    last,
    where_ref,
    rad_ref,
    part_ref,
    below_ref,
    edge_ref,
    bad_ref,
    low_ref,
    high_ref,
    m_ref,
    dn_ref,
    ax_ref,
    radup_ref,
    raddn_ref,
    worse_ref,
):
    azim = jnp.where(rows_of() >= 4, 0.0, 0.5 * edge_ref[0])
    for c in range(comps):
        m_ref[8 * c : 8 * c + 8] = part_ref[8 * c : 8 * c + 8] + azim * from_below(c, below_ref)
    encode(comps, m_ref, 0, low_ref, high_ref, dn_ref)
    worse_ref[...] = bad_ref[...] + crowded(below_ref[4 * comps :])
    dn_ref[5 * comps // 2 :] = worse_ref[...]
    pack_sides(comps, last, m_ref, where_ref, rad_ref, ax_ref, radup_ref, raddn_ref)


def second_radial(comps, bottom_ref, radlo_ref, radhi_ref, edge_ref, full_ref):
    hrad = put_columns(radlo_ref[...], radhi_ref[...])
    rad = edge_ref[2]
    for c in range(comps):
        spots = slice(8 * c, 8 * c + 8)
        full_ref[spots] = bottom_ref[spots] + rad * hrad[spots]


def second_rest(
    comps,
    parts,
    where_ref,
    full_ref,
    above_ref,
    ax_ref,
    edge_ref,
    bad_ref,
    low_ref,
    high_ref,
    out_ref,
    again_ref,
    halo_ref,
    side_ref,
    done_ref,
    sems,
):
    again_ref[0] = (jnp.max(bad_ref[...] + above_ref[5 * comps // 2 :]) > 0.0).astype(jnp.int32)
    spread(comps, decode(comps, above_ref, low_ref, high_ref), 4, halo_ref)
    several = jnp.concatenate([edge_ref[1]] * (2 * comps // 8), axis=0)
    for start, index in ((3, 0), (0, 1)):

        @pl.when(where_ref[0] == index)
        def _():
            side_ref[pl.ds(start, 2 * comps, stride=4)] = several * ax_ref[0 : 2 * comps]

    row = rows_of()
    azim, top, side = edge_ref[0], row >= 4, row % 4 == jnp.where(where_ref[0] == 0, 3, 0)
    size = comps // parts
    made = []
    for i in range(parts):
        for c in range(size * i, size * i + size):
            spots = slice(8 * c, 8 * c + 8)
            done_ref[spots] = (
                full_ref[spots] + jnp.where(top, azim * halo_ref[spots], 0.0) + jnp.where(side, side_ref[spots], 0.0)
            )
        spots = pl.ds(8 * size * i, 8 * size)
        made.append(pltpu.make_async_copy(done_ref.at[spots], out_ref.at[spots], sems.at[i]))
        made[-1].start()
    for copy in made:
        copy.wait()


SPACES = {
    "v": pl.BlockSpec(memory_space=pltpu.VMEM),
    "s": pl.BlockSpec(memory_space=pltpu.SMEM),
    "h": pl.BlockSpec(memory_space=pltpu.HBM),
}


def call(body, ins, outs, shapes, cost, *operands, scratch=()):
    return pl.pallas_call(
        body,
        in_specs=[SPACES[s] for s in ins],
        out_specs=[SPACES[s] for s in outs],
        out_shape=[jax.ShapeDtypeStruct(s, f32) if isinstance(s, tuple) else s for s in shapes],
        scratch_shapes=scratch,
        cost_estimate=pl.CostEstimate(flops=cost, bytes_accessed=cost // 10, transcendentals=0),
        compiler_params=pltpu.CompilerParams(vmem_limit_bytes=32 * 1024 * 1024),
    )(*operands)


def shift(x, axis, step, wrap):
    size = lax.axis_size(axis)
    pairs = [(i, (i + step) % size) for i in range(size) if wrap or 0 <= i + step < size]
    return lax.ppermute(x, axis, pairs)


def sides(ax, radup, raddn):
    ax = lax.ppermute(ax, "axial", [(0, 1), (1, 0)])
    return ax, shift(radup, "rad", 1, True), shift(raddn, "rad", -1, True)


def shards(adjoint_final, state_start, state_middle, speeds, flags, zones, growth_rate, transfer_rate, nucleation_rate):
    shape = adjoint_final.shape
    moments, sections = shape[:2]
    comps = moments * sections
    assert moments == 4 and shape[2:] == (2, 4, 128) and comps % 4 == 0
    assert lax.axis_size("axial") == 2
    cells = 8 * comps
    half, rows = cells // 2, cells // 4
    a = adjoint_final.reshape(cells, 128)
    speeds2 = speeds.reshape(3, 8, 128)
    flags2 = flags.reshape(3, 8, 128)
    where = lax.axis_index("axial").reshape(1)
    place = (where, lax.axis_index("rad").reshape(1))
    last = lax.axis_size("rad") - 1
    rates = (zones.reshape(8, 128), growth_rate, transfer_rate, nucleation_rate)
    message = 5 * comps // 2
    tables = [jax.ShapeDtypeStruct((256, 512), bf16)] * 2

    keep = ((0, 2, 0), (0, -1, 0), (0, 0, 0), (0, 0, 0))
    after = ((comps, -1, 0), (0, -1, 0), (0, 0, 0), (0, 0, 0))
    dn = lax.pad(adjoint_final.reshape(comps, 2, 4, 128), 0.0, keep)
    dn = dn + lax.pad(speeds, 0.0, after) * lax.pad(flags, 0, after).astype(f32)
    above = shift(dn.reshape(half + 8, 128), "azim", -1, True)
    up, *edges = call(
        functools.partial(first_rest, comps, last),
        "ssvvv",
        "vvvv",
        [(half + 8, 128), (rows + 8, 128), (1, cells + 128), (1, cells + 128)],
        2_000_000,
        *place,
        a,
        speeds2,
        flags2,
    )
    below = shift(up, "azim", 1, True)
    edges = sides(*edges)
    part, *lower_tables = call(
        functools.partial(first_local, sections),
        "vvvvvsss",
        "vvvvv",
        [(cells, 128)] + 2 * tables,
        8_000_000,
        a,
        state_middle.reshape(comps, 8, 128),
        speeds2,
        flags2,
        *rates,
    )
    part, edge, up, bad, *upper_tables = call(
        functools.partial(first_top, comps),
        "s" + "v" * 8,
        "v" * 8,
        [(cells, 128), (4, 8, 128), (message, 128), (8, 128)] + 2 * tables,
        4_000_000,
        where,
        part,
        a,
        above,
        *edges,
        speeds2,
        flags2,
    )
    next_below = shift(up, "azim", 1, True)
    m, dn, *edges, bad = call(
        functools.partial(first_bottom, comps, last),
        "ss" + "v" * 6,
        "v" * 6,
        [(cells, 128), (message + 8, 128), (rows, 128), (1, cells), (1, cells), (8, 128)],
        10_000,
        *place,
        part,
        below,
        edge,
        bad,
        *lower_tables[:2],
    )
    next_above = shift(dn, "azim", -1, True)
    ax, radlo, radhi = sides(*edges)
    part, bottom = call(
        functools.partial(second_local, sections),
        "v" * 10 + "sss",
        "vv",
        [(cells, 128), (cells, 128)],
        300_000_000,
        m,
        a,
        state_start.reshape(comps, 8, 128),
        next_below,
        edge,
        *lower_tables[2:],
        speeds2,
        flags2,
        *rates,
        scratch=[pltpu.VMEM((cells, 128), f32)],
    )
    (full,) = call(
        functools.partial(second_radial, comps),
        "v" * 4,
        "v",
        [(cells, 128)],
        1_000,
        bottom,
        radlo,
        radhi,
        edge,
    )
    out, again = call(
        functools.partial(second_rest, comps, 4),
        "s" + "v" * 7,
        "hs",
        [pltpu.HBM((cells, 128), f32), jax.ShapeDtypeStruct((1,), jnp.int32)],
        1_000_000,
        where,
        full,
        next_above,
        ax,
        edge,
        bad,
        *upper_tables[:2],
        scratch=[pltpu.VMEM((cells, 128), f32)] * 3 + [pltpu.SemaphoreType.DMA((4,))],
    )

    def whole():
        rows_ = m.reshape(comps, 2, 4, 128)
        halo = jnp.stack([shift(rows_[:, 1], "azim", 1, True), shift(rows_[:, 0], "azim", -1, True)], axis=1)
        azimuthal = (edge[0].reshape(1, 2, 4, 128) * halo).reshape(comps, 8, 128)
        row, lane = jnp.arange(8).reshape(1, 8, 1), jnp.arange(128).reshape(1, 1, 128)
        two = jnp.repeat(ax.reshape(comps, 2, 128) * edge[1, :2], 4, axis=1)
        axial = jnp.where(row % 4 == 3 * (1 - where[0]), two, 0.0)
        lower, upper = radlo.reshape(comps, 8, 1), radhi.reshape(comps, 8, 1)
        radial = edge[2] * jnp.where(lane == 0, lower, jnp.where(lane == 127, upper, 0.0))
        return part + (azimuthal + axial + radial).reshape(cells, 128)

    again = again[0]
    if lax.axis_size("azim") != 4:
        again = lax.pmax(again.astype(f32), "azim").astype(jnp.int32)
    return lax.switch(again, (lambda: out, whole)).reshape(shape)


def solution(mesh):
    field = P(None, None, "azim", "axial", "rad")
    faces_spec = P(None, "azim", "axial", "rad")
    return jax.shard_map(
        shards,
        mesh=mesh,
        in_specs=(field, field, field, faces_spec, faces_spec, P("azim", "axial", "rad"), P(), P(), P()),
        out_specs=field,
        check_vma=False,
    )
```

```python
import functools

import jax
import jax.numpy as jnp
from jax import lax
from jax.experimental import pallas as pl
from jax.experimental.pallas import tpu as pltpu
from jax.sharding import PartitionSpec as P

supersat_scale = 1.5
crowding = 0.02
nucleus_moments = (1.0, 0.5, 0.25, 0.125)
f32 = jnp.float32
bf16 = jnp.bfloat16

slots = 320
extra = slots - 256


def rows_of():
    return lax.broadcasted_iota(jnp.int32, (8, 128), 0)


def lanes_of():
    return lax.broadcasted_iota(jnp.int32, (8, 128), 1)


def faces(speeds_ref, flags_ref):
    p, q = [], []
    for d in range(3):
        speed, upwind = speeds_ref[d], flags_ref[d].astype(f32)
        p.append(speed * upwind)
        q.append(speed * (1.0 - upwind))
    return p, q


class Local:
    def __init__(self, p, q):
        row, lane = rows_of(), lanes_of()
        z, top = row % 4, row >= 4
        self.azim = jnp.where(top, q[0], pltpu.roll(p[0], 4, 0))
        self.ax_up = jnp.where(z == 3, 0.0, pltpu.roll(p[1], 7, 0))
        self.ax_dn = jnp.where(z == 0, 0.0, q[1])
        self.rad_up = jnp.where(lane == 127, 0.0, pltpu.roll(p[2], 127, 1))
        self.rad_dn = jnp.where(lane == 0, 0.0, q[2])
        self.centre = self.azim + self.ax_up + q[1] + self.rad_up + q[2] + jnp.where(top, 0.0, q[0])

    def __call__(self, x):
        return (
            self.azim * pltpu.roll(x, 4, 0)
            + self.ax_up * pltpu.roll(x, 7, 0)
            + self.ax_dn * pltpu.roll(x, 1, 0)
            + self.rad_up * pltpu.roll(x, 127, 1)
            + self.rad_dn * pltpu.roll(x, 1, 1)
            - self.centre * x
        )


def pair_rows(x, first, second):
    return jnp.where(
        rows_of() % 2 == 0,
        jnp.broadcast_to(x[first : first + 1], (8, 128)),
        jnp.broadcast_to(x[second : second + 1], (8, 128)),
    )


def make_tables(p, where_zero, low_ref, high_ref):
    row, lane = rows_of(), lanes_of()
    taken = (p == 0.0) if where_zero else (p != 0.0)
    one = jnp.where(taken & (row < 4), 1.0, 0.0)
    before = lax.broadcasted_iota(jnp.int32, (128, 128), 0) < lax.broadcasted_iota(jnp.int32, (128, 128), 1)
    inside = jnp.dot(one.astype(bf16), jnp.where(before, 1.0, 0.0).astype(bf16), preferred_element_type=f32)
    total = jnp.sum(one, axis=1, keepdims=True)
    base = jnp.zeros((8, 1), f32)
    for step in (1, 2, 3):
        base = base + jnp.where(
            lax.broadcasted_iota(jnp.int32, (8, 1), 0) >= step, jnp.roll(total, step, axis=0), 0.0
        )
    slot = jnp.where(one > 0.0, inside + base, -1.0).astype(jnp.int32)
    here = lax.broadcasted_iota(jnp.int32, (128, 128), 0)
    first = jnp.where(here < extra, here + 256, -2)
    second = jnp.where(here >= extra, here + (256 - extra), -2)
    for z in range(4):
        cells = slice(128 * z, 128 * z + 128)
        want = jnp.broadcast_to(slot[z : z + 1], (128, 128))
        for ref, start, names in ((low_ref, 0, here), (low_ref, 128, here + 128), (high_ref, 0, first), (high_ref, 128, second)):
            ref[start : start + 128, cells] = jnp.where(names == want, 1.0, 0.0).astype(bf16)


def crowded(p):
    taken = jnp.where((rows_of() < 4) & (p != 0.0), 1.0, 0.0)
    count = jnp.sum(jnp.sum(taken, axis=1, keepdims=True), axis=0, keepdims=True)
    count = jnp.broadcast_to(count, (8, 128))
    return jnp.where(jnp.maximum(count, 512.0 - count) > slots, 1.0, 0.0)


def pieces(x):
    high = x.astype(bf16)
    rest = x - high.astype(f32)
    middle = rest.astype(bf16)
    return high, middle, (rest - middle.astype(f32)).astype(bf16)


def stacked(x, half):
    return jnp.concatenate([part[half * i : half * i + half] for i in range(2) for part in pieces(x)], axis=0)


def summed(x, half):
    parts = [x[half * i : half * i + half] for i in range(6)]
    return [parts[3 * i] + (parts[3 * i + 1] + parts[3 * i + 2]) for i in range(2)]


def encode(comps, x_ref, first_row, low_ref, high_ref, message_ref):
    half = comps // 2
    x = jnp.concatenate(
        [stacked(x_ref[pl.ds(first_row + z, comps, stride=8)], half) for z in range(4)], axis=1
    )
    over = (((1,), (1,)), ((), ()))
    low = lax.dot_general(x, low_ref[...], over, preferred_element_type=f32)
    high = [
        lax.dot_general(
            x[3 * half * i : 3 * half * (i + 1)], high_ref[128 * i : 128 * i + 128], over, preferred_element_type=f32
        )
        for i in range(2)
    ]
    tail = jnp.zeros((half, 128), f32)
    for i, part in enumerate(summed(low, half)):
        message_ref[half * i : half * i + half] = part[:, :128]
        message_ref[comps + half * i : comps + half * i + half] = part[:, 128:]
    for part in high:
        tail = tail + (part[:half] + (part[half : 2 * half] + part[2 * half :]))
    message_ref[2 * comps : 2 * comps + half] = tail


def decode(comps, message_ref, low_ref, high_ref):
    half = comps // 2
    x = jnp.concatenate([stacked(message_ref[comps * i : comps * i + comps], half) for i in range(2)], axis=1)
    low = jnp.dot(x, low_ref[...], preferred_element_type=f32)
    tail = jnp.concatenate(pieces(message_ref[2 * comps : 2 * comps + half]), axis=0)
    found = []
    for i, part in enumerate(summed(low, half)):
        high = jnp.dot(tail, high_ref[128 * i : 128 * i + 128], preferred_element_type=f32)
        found.append(part + (high[:half] + (high[half : 2 * half] + high[2 * half :])))
    return jnp.concatenate(found, axis=0)


def add_azimuthal(comps, halo, coefficient, first_row, out_ref):
    for z in range(4):
        spots = pl.ds(first_row + z, comps, stride=8)
        out_ref[spots] = out_ref[spots] + coefficient[first_row + z : first_row + z + 1] * halo[:, 128 * z : 128 * z + 128]


def pack_sides(comps, last, x_ref, where_ref, rad_ref, ax_ref, radup_ref, raddn_ref):
    @pl.when(where_ref[0] == 0)
    def _():
        ax_ref[0 : 2 * comps] = x_ref[pl.ds(3, 2 * comps, stride=4)]

    @pl.when(where_ref[0] != 0)
    def _():
        ax_ref[0 : 2 * comps] = x_ref[pl.ds(0, 2 * comps, stride=4)]

    ends = columns(x_ref[...])
    radup_ref[:, 0 : 8 * comps] = jnp.where(rad_ref[0] < last, ends[0:1], 0.0)
    raddn_ref[:, 0 : 8 * comps] = jnp.where(rad_ref[0] > 0, ends[1:2], 0.0)


def columns(x):
    row, lane = rows_of(), lanes_of()
    take = jnp.where(((row == 0) & (lane == 127)) | ((row == 1) & (lane == 0)), 1.0, 0.0).astype(bf16)
    high, middle, low = (
        lax.dot_general(take, part, (((1,), (1,)), ((), ())), preferred_element_type=f32) for part in pieces(x)
    )
    return high + (middle + low)


def put_columns(lower, upper):
    n = lower.shape[1]
    row, lane = rows_of(), lanes_of()
    which = lax.broadcasted_iota(jnp.int32, (8, n), 0)
    both = jnp.where(which == 0, lower, jnp.where(which == 1, upper, 0.0))
    place = jnp.where(((row == 0) & (lane == 0)) | ((row == 1) & (lane == 127)), 1.0, 0.0)
    parts = jnp.concatenate([part.astype(f32) for part in pieces(both)], axis=0).astype(bf16)
    places = jnp.concatenate([place] * 3, axis=0).astype(bf16)
    return lax.dot_general(parts, places, (((0,), (0,)), ((), ())), preferred_element_type=f32)


def first_rest(comps, last, where_ref, rad_ref, a_ref, speeds_ref, flags_ref, up_ref, ax_ref, radup_ref, raddn_ref):
    p, _ = faces(speeds_ref, flags_ref)
    for c in range(comps):
        up_ref[4 * c : 4 * c + 4] = a_ref[8 * c + 4 : 8 * c + 8]
    up_ref[4 * comps :] = p[0]
    pack_sides(comps, last, a_ref, where_ref, rad_ref, ax_ref, radup_ref, raddn_ref)
    ax_ref[2 * comps : 2 * comps + 8] = pair_rows(p[1], 0, 4)
    radup_ref[:, 8 * comps :] = jnp.zeros((1, 128), f32)
    raddn_ref[:, 8 * comps :] = jnp.zeros((1, 128), f32)
    raddn_ref[:, 8 * comps : 8 * comps + 8] = jnp.where(rad_ref[0] > 0, columns(p[2])[1:2], 0.0)


def source(sections, x_ref, u_ref, growth_ref, transfer_ref, zones_ref, rate_ref, finish):
    def inner(k, s, x):
        term = transfer_ref[s] * ((x[k][1] - x[k][0]) if s + 1 < sections else -x[k][0])
        if k < 3:
            term = term + ((k + 1.0) * growth_ref[s]) * x[k + 1][0]
        return term

    def load(s):
        got = []
        for k in range(4):
            c = k * sections + s
            here = x_ref[8 * c : 8 * c + 8]
            got.append((here, x_ref[8 * c + 8 : 8 * c + 16] if s + 1 < sections else None))
        return got

    squares = jnp.zeros((8, 128), f32)
    product = jnp.zeros((8, 128), f32)
    for s in range(sections):
        x = load(s)
        for k in range(4):
            u = u_ref[k * sections + s].astype(f32)
            product = product + u * inner(k, s, x)
        squares = squares + u * u
    sigma = supersat_scale / (1.0 + crowding * squares)
    birth = jnp.zeros((8, 128), f32)
    for k in range(4):
        c = k * sections
        birth = birth + nucleus_moments[k] * x_ref[8 * c : 8 * c + 8]
    rate = jnp.zeros((8, 128), f32)
    for label in range(rate_ref.shape[0]):
        rate = jnp.where(zones_ref[...] == label, rate_ref[label], rate)
    slope = (-2.0 * crowding / supersat_scale) * sigma * sigma * (product + 2.0 * rate * sigma * birth)
    for s in range(sections):
        x = load(s)
        for k in range(4):
            c = k * sections + s
            term = sigma * inner(k, s, x)
            if k == 3:
                term = term + u_ref[c].astype(f32) * slope
            finish(c, x[k][0], term)


def first_local(
    sections,
    a_ref,
    u_ref,
    speeds_ref,
    flags_ref,
    zones_ref,
    growth_ref,
    transfer_ref,
    rate_ref,
    out_ref,
    dn_low_ref,
    dn_high_ref,
    up_low_ref,
    up_high_ref,
):
    p, q = faces(speeds_ref, flags_ref)
    local = Local(p, q)
    make_tables(p[0], False, dn_low_ref, dn_high_ref)
    make_tables(p[0], True, up_low_ref, up_high_ref)

    def finish(c, x, term):
        out_ref[8 * c : 8 * c + 8] = 0.5 * (x + local(x) + term)

    source(sections, a_ref, u_ref, growth_ref, transfer_ref, zones_ref, rate_ref, finish)


def second_local(
    sections,
    m_ref,
    a_ref,
    u_ref,
    below_ref,
    edge_ref,
    low_ref,
    high_ref,
    speeds_ref,
    flags_ref,
    zones_ref,
    growth_ref,
    transfer_ref,
    rate_ref,
    out_ref,
    bottom_ref,
):
    local = Local(*faces(speeds_ref, flags_ref))
    local.centre = local.centre + (edge_ref[3] - 1.0)

    def finish(c, x, term):
        out_ref[8 * c : 8 * c + 8] = 0.5 * a_ref[8 * c : 8 * c + 8] + (local(x) + term)

    source(sections, m_ref, u_ref, growth_ref, transfer_ref, zones_ref, rate_ref, finish)
    bottom_ref[...] = out_ref[...]
    add_azimuthal(4 * sections, decode(4 * sections, below_ref, low_ref, high_ref), edge_ref[0], 0, bottom_ref)


def from_below(c, below_ref):
    pair = below_ref[8 * (c // 2) : 8 * (c // 2) + 8]
    return pair if c % 2 == 0 else pltpu.roll(pair, 4, 0)


def from_above(c, above_ref):
    pair = above_ref[8 * (c // 2) : 8 * (c // 2) + 8]
    return pair if c % 2 == 1 else pltpu.roll(pair, 4, 0)


def add_axial(comps, scale, where_ref, axial, ax_ref, out_ref):
    several = jnp.concatenate([scale * axial] * (2 * comps // 8), axis=0)
    for start, index in ((3, 0), (0, 1)):

        @pl.when(where_ref[0] == index)
        def _():
            spots = pl.ds(start, 2 * comps, stride=4)
            out_ref[spots] = out_ref[spots] + several * ax_ref[0 : 2 * comps]


def first_top(
    comps,
    where_ref,
    part_ref,
    a_ref,
    above_ref,
    ax_ref,
    radlo_ref,
    radhi_ref,
    speeds_ref,
    flags_ref,
    m_ref,
    edge_ref,
    up_ref,
    bad_ref,
    dn_low_ref,
    dn_high_ref,
    up_low_ref,
    up_high_ref,
):
    p, q = faces(speeds_ref, flags_ref)
    row, lane = rows_of(), lanes_of()
    upper = above_ref[4 * comps :]
    make_tables(upper, True, up_low_ref, up_high_ref)
    make_tables(upper, False, dn_low_ref, dn_high_ref)
    bad_ref[...] = crowded(p[0]) + crowded(upper)
    hrad = put_columns(radlo_ref[...], radhi_ref[...])
    lower_half = where_ref[0] == 0
    p_azim = jnp.where(row >= 4, pltpu.roll(upper, 4, 0), 0.0)
    pairs = jnp.where(lower_half, ax_ref[2 * comps : 2 * comps + 8], 0.0)
    p_axial = jnp.where(row == 3, pairs[0:1], jnp.where(row == 7, pairs[1:2], 0.0))
    p_rad = jnp.where(lane == 127, hrad[8 * comps : 8 * comps + 8], 0.0)
    axial = jnp.where(lower_half, pairs, pair_rows(q[1], 0, 4))
    rad = jnp.where(lane == 0, q[2], p_rad)
    centre = p_azim + p_axial + p_rad
    edge_ref[0] = jnp.where(row >= 4, p_azim, q[0])
    edge_ref[1] = axial
    edge_ref[2] = rad
    edge_ref[3] = centre
    for c in range(comps):
        spots = slice(8 * c, 8 * c + 8)
        m_ref[spots] = part_ref[spots] + 0.5 * (
            p_azim * from_above(c, above_ref) + rad * hrad[spots] - centre * a_ref[spots]
        )
    add_axial(comps, 0.5, where_ref, axial, ax_ref, m_ref)
    encode(comps, m_ref, 4, up_low_ref, up_high_ref, up_ref)


def first_bottom(
    comps,
    last,
    where_ref,
    rad_ref,
    part_ref,
    below_ref,
    edge_ref,
    bad_ref,
    low_ref,
    high_ref,
    m_ref,
    dn_ref,
    ax_ref,
    radup_ref,
    raddn_ref,
    worse_ref,
):
    azim = jnp.where(rows_of() >= 4, 0.0, 0.5 * edge_ref[0])
    for c in range(comps):
        m_ref[8 * c : 8 * c + 8] = part_ref[8 * c : 8 * c + 8] + azim * from_below(c, below_ref)
    encode(comps, m_ref, 0, low_ref, high_ref, dn_ref)
    worse_ref[...] = bad_ref[...] + crowded(below_ref[4 * comps :])
    dn_ref[5 * comps // 2 :] = worse_ref[...]
    pack_sides(comps, last, m_ref, where_ref, rad_ref, ax_ref, radup_ref, raddn_ref)


def second_radial(comps, bottom_ref, radlo_ref, radhi_ref, edge_ref, full_ref):
    hrad = put_columns(radlo_ref[...], radhi_ref[...])
    rad = edge_ref[2]
    for c in range(comps):
        spots = slice(8 * c, 8 * c + 8)
        full_ref[spots] = bottom_ref[spots] + rad * hrad[spots]


def second_rest(
    comps,
    parts,
    where_ref,
    full_ref,
    above_ref,
    ax_ref,
    edge_ref,
    bad_ref,
    low_ref,
    high_ref,
    out_ref,
    again_ref,
    done_ref,
    sems,
):
    again_ref[...] = jnp.minimum(bad_ref[...] + above_ref[5 * comps // 2 :], 1.0).astype(jnp.int32)
    halo = decode(comps, above_ref, low_ref, high_ref)
    azim = edge_ref[0]
    done_ref[...] = full_ref[...]
    add_axial(comps, 1.0, where_ref, edge_ref[1], ax_ref, done_ref)
    size = comps // parts
    made = []
    for i in range(parts):
        for z in range(4):
            some = pl.ds(8 * size * i + 4 + z, size, stride=8)
            done_ref[some] = (
                done_ref[some] + azim[4 + z : 5 + z] * halo[size * i : size * i + size, 128 * z : 128 * z + 128]
            )
        spots = pl.ds(8 * size * i, 8 * size)
        made.append(pltpu.make_async_copy(done_ref.at[spots], out_ref.at[spots], sems.at[i]))
        made[-1].start()
    for copy in made:
        copy.wait()


SPACES = {
    "v": pl.BlockSpec(memory_space=pltpu.VMEM),
    "s": pl.BlockSpec(memory_space=pltpu.SMEM),
    "h": pl.BlockSpec(memory_space=pltpu.HBM),
}


def call(body, ins, outs, shapes, cost, *operands, scratch=()):
    return pl.pallas_call(
        body,
        in_specs=[SPACES[s] for s in ins],
        out_specs=[SPACES[s] for s in outs],
        out_shape=[jax.ShapeDtypeStruct(s, f32) if isinstance(s, tuple) else s for s in shapes],
        scratch_shapes=scratch,
        cost_estimate=pl.CostEstimate(flops=cost, bytes_accessed=cost // 10, transcendentals=0),
        compiler_params=pltpu.CompilerParams(vmem_limit_bytes=32 * 1024 * 1024),
    )(*operands)


def shift(x, axis, step, wrap):
    size = lax.axis_size(axis)
    pairs = [(i, (i + step) % size) for i in range(size) if wrap or 0 <= i + step < size]
    return lax.ppermute(x, axis, pairs)


def sides(ax, radup, raddn):
    ax = lax.ppermute(ax, "axial", [(0, 1), (1, 0)])
    return ax, shift(radup, "rad", 1, True), shift(raddn, "rad", -1, True)


def shards(adjoint_final, state_start, state_middle, speeds, flags, zones, growth_rate, transfer_rate, nucleation_rate):
    shape = adjoint_final.shape
    moments, sections = shape[:2]
    comps = moments * sections
    assert moments == 4 and shape[2:] == (2, 4, 128) and comps % 4 == 0
    assert lax.axis_size("axial") == 2
    cells = 8 * comps
    half, rows = cells // 2, cells // 4
    a = adjoint_final.reshape(cells, 128)
    speeds2 = speeds.reshape(3, 8, 128)
    flags2 = flags.reshape(3, 8, 128)
    where = lax.axis_index("axial").reshape(1)
    place = (where, lax.axis_index("rad").reshape(1))
    last = lax.axis_size("rad") - 1
    rates = (zones.reshape(8, 128), growth_rate, transfer_rate, nucleation_rate)
    message = 5 * comps // 2
    tables = [jax.ShapeDtypeStruct((256, 512), bf16)] * 2

    keep = ((0, 2, 0), (0, -1, 0), (0, 0, 0), (0, 0, 0))
    after = ((comps, -1, 0), (0, -1, 0), (0, 0, 0), (0, 0, 0))
    dn = lax.pad(adjoint_final.reshape(comps, 2, 4, 128), 0.0, keep)
    dn = dn + lax.pad(speeds, 0.0, after) * lax.pad(flags, 0, after).astype(f32)
    above = shift(dn.reshape(half + 8, 128), "azim", -1, True)
    up, *edges = call(
        functools.partial(first_rest, comps, last),
        "ssvvv",
        "vvvv",
        [(half + 8, 128), (rows + 8, 128), (1, cells + 128), (1, cells + 128)],
        2_000_000,
        *place,
        a,
        speeds2,
        flags2,
    )
    below = shift(up, "azim", 1, True)
    edges = sides(*edges)
    part, *lower_tables = call(
        functools.partial(first_local, sections),
        "vvvvvsss",
        "vvvvv",
        [(cells, 128)] + 2 * tables,
        8_000_000,
        a,
        state_middle.reshape(comps, 8, 128),
        speeds2,
        flags2,
        *rates,
    )
    part, edge, up, bad, *upper_tables = call(
        functools.partial(first_top, comps),
        "s" + "v" * 8,
        "v" * 8,
        [(cells, 128), (4, 8, 128), (message, 128), (8, 128)] + 2 * tables,
        4_000_000,
        where,
        part,
        a,
        above,
        *edges,
        speeds2,
        flags2,
    )
    next_below = shift(up, "azim", 1, True)
    m, dn, *edges, bad = call(
        functools.partial(first_bottom, comps, last),
        "ss" + "v" * 6,
        "v" * 6,
        [(cells, 128), (message + 8, 128), (rows, 128), (1, cells), (1, cells), (8, 128)],
        10_000,
        *place,
        part,
        below,
        edge,
        bad,
        *lower_tables[:2],
    )
    next_above = shift(dn, "azim", -1, True)
    ax, radlo, radhi = sides(*edges)
    part, bottom = call(
        functools.partial(second_local, sections),
        "v" * 10 + "sss",
        "vv",
        [(cells, 128), (cells, 128)],
        300_000_000,
        m,
        a,
        state_start.reshape(comps, 8, 128),
        next_below,
        edge,
        *lower_tables[2:],
        speeds2,
        flags2,
        *rates,
    )
    (full,) = call(
        functools.partial(second_radial, comps),
        "v" * 4,
        "v",
        [(cells, 128)],
        1_000,
        bottom,
        radlo,
        radhi,
        edge,
    )
    out, again = call(
        functools.partial(second_rest, comps, 4),
        "s" + "v" * 7,
        "hv",
        [pltpu.HBM((cells, 128), f32), jax.ShapeDtypeStruct((8, 128), jnp.int32)],
        1_000_000,
        where,
        full,
        next_above,
        ax,
        edge,
        bad,
        *upper_tables[:2],
        scratch=[pltpu.VMEM((cells, 128), f32), pltpu.SemaphoreType.DMA((4,))],
    )

    def whole():
        rows_ = m.reshape(comps, 2, 4, 128)
        halo = jnp.stack([shift(rows_[:, 1], "azim", 1, True), shift(rows_[:, 0], "azim", -1, True)], axis=1)
        azimuthal = (edge[0].reshape(1, 2, 4, 128) * halo).reshape(comps, 8, 128)
        row, lane = jnp.arange(8).reshape(1, 8, 1), jnp.arange(128).reshape(1, 1, 128)
        two = jnp.repeat(ax.reshape(comps, 2, 128) * edge[1, :2], 4, axis=1)
        axial = jnp.where(row % 4 == 3 * (1 - where[0]), two, 0.0)
        lower, upper = radlo.reshape(comps, 8, 1), radhi.reshape(comps, 8, 1)
        radial = edge[2] * jnp.where(lane == 0, lower, jnp.where(lane == 127, upper, 0.0))
        return part + (azimuthal + axial + radial).reshape(cells, 128)

    again = again[0, 0]
    if lax.axis_size("azim") != 4:
        again = lax.pmax(again.astype(f32), "azim").astype(jnp.int32)
    return lax.switch(again, (lambda: out, whole)).reshape(shape)


def solution(mesh):
    field = P(None, None, "azim", "axial", "rad")
    faces_spec = P(None, "azim", "axial", "rad")
    return jax.shard_map(
        shards,
        mesh=mesh,
        in_specs=(field, field, field, faces_spec, faces_spec, P("azim", "axial", "rad"), P(), P(), P()),
        out_specs=field,
        check_vma=False,
    )
```
